32 devices in a mesh: dp: 4 (over z), context: 2 (over y), experts: 4 (over x, core).
Axes of the slice: x: 2, y: 2, z: 4, core: 2. Of those that a mesh axis runs over, the one named last changes fastest.
Arguments:
- tokens: bfloat16 [12288, 768], P(('dp', 'context', 'experts')), may hold values from -6 to 6
- cotangent: bfloat16 [12288, 768], P(('dp', 'context', 'experts')), may hold values from -6 to 6
- routes: int32 [12288, 2], P(('dp', 'context', 'experts')), may hold values from 0 to 15, all different within a row; in each aligned block of 384 rows (0 to 383, 384 to 767, ...) at most 66 rows name the same one
- prompt_ids: int32 [64], P(('dp', 'context', 'experts')), may hold values from 0 to 1, as said below
- attn_gain: bfloat16 [768], P('dp'), may hold values from 0.5 to 1.5
- query_weight: bfloat16 [768, 768], P('dp'), may hold values from -0.21875 to 0.21875
- key_weight: bfloat16 [768, 768], P('dp'), may hold values from -0.21875 to 0.21875
- value_weight: bfloat16 [768, 768], P('dp'), may hold values from -0.21875 to 0.21875
- output_weight: bfloat16 [768, 768], P('dp'), may hold values from -2.5 to 2.5
- ffn_gain: bfloat16 [768], P('dp'), may hold values from 0.5 to 1.5
- router_weight: bfloat16 [768, 16], P('dp'), may hold values from -0.15625 to 0.15625
- shared_gate: bfloat16 [768, 2048], P('dp'), may hold values from -0.21875 to 0.21875
- shared_up: bfloat16 [768, 2048], P('dp'), may hold values from -0.21875 to 0.21875
- shared_down: bfloat16 [2048, 768], P('dp'), may hold values from -0.125 to 0.125
- expert_gate: bfloat16 [16, 768, 2048], P('experts'), may hold values from -0.21875 to 0.21875
- expert_up_weight: bfloat16 [16, 768, 2048], P('experts'), may hold values from -0.21875 to 0.21875
- expert_down: bfloat16 [16, 2048, 768], P('experts'), may hold values from -1.5 to 1.5
Outputs:
- layer_out: bfloat16 [12288, 768], P(('dp', 'context', 'experts'))
- grad_tokens: float32 [12288, 768], P(('dp', 'context', 'experts'))
- grad_attn_gain: float32 [768], P('dp')
- grad_query: float32 [768, 768], P('dp')
- grad_key: float32 [768, 768], P('dp')
- grad_value: float32 [768, 768], P('dp')
- grad_output: float32 [768, 768], P('dp')
- grad_ffn_gain: float32 [768], P('dp')
- grad_router: float32 [768, 16], P('dp')
- grad_shared_gate: float32 [768, 2048], P('dp')
- grad_shared_up: float32 [768, 2048], P('dp')
- grad_shared_down: float32 [2048, 768], P('dp')
- grad_expert_gate: float32 [16, 768, 2048], P('experts', None, ('dp', 'context'))
- grad_expert_up: float32 [16, 768, 2048], P('experts', None, ('dp', 'context'))
- grad_expert_down: float32 [16, 2048, 768], P('experts', ('dp', 'context'))
The draws below stay inside these ranges and needn't reach their ends.
Inputs may be any that keep to these rules, and one draw needn't show every extreme that they name: `routes`: among the 768 choices of the rows of one device, each expert is named at most 66 times; a row names 2 different experts. `prompt_ids`: in every block some continuation follows the prompt of another block of its group.
All inputs are finite; a program needn't handle non-finite values.
Results may differ from the reference program's by a relative error of at most 0.022.
Values may be sent and summed in bfloat16 or wider, within the bound.
No kernel may reach another device: no remote copies, remote signals or barrier semaphores. Data moves between devices by JAX's collectives and lax.ppermute only.
A program may use at most 256 MiB of HBM per device.

```python
import math
import jax
import jax.numpy as jnp
import numpy as np
from jax import lax

D = 768
HEADS = 12
HD = 64
FF = 2048
FFS = 2048
EXPERTS = 16
TOPK = 2
PROMPT = 256
CONT = 2
CLEN = 64
TOK_DEV = 384
CAP = 66
TOKENS = 12288
N_DP = 4
N_CONTEXT = 2
N_EXPERTS = 4
DEVICES = 32


def draw_prompt_ids(key, part):
    key = jax.random.fold_in(key, 7)
    key_base, key_slot = jax.random.split(key)
    base = jax.random.randint(key_base, (DEVICES, CONT), 0, N_CONTEXT)
    forced_slot = jax.random.randint(key_slot, (DEVICES,), 0, CONT)
    device_ids = jnp.arange(DEVICES)
    remote = (device_ids // N_EXPERTS % N_CONTEXT + 1) % N_CONTEXT
    picked = jnp.arange(CONT)[None, :] == forced_slot[:, None]
    chosen = jnp.where(picked, remote[:, None], base)
    return chosen.reshape(-1).astype(jnp.int32)


def steps_of(key, extent, cuts, least, largest):
    def one(axis_at, shards_of):
        heights = jax.random.uniform(jax.random.fold_in(jax.random.fold_in(key, 6), axis_at), (shards_of,), jnp.float32, least / len(cuts), largest / len(cuts))
        return jnp.repeat(jnp.exp(heights), extent[axis_at] // shards_of).reshape((-1,) + (1,) * (len(extent) - axis_at - 1))

    factor_of = one(*cuts[0])
    for cut in cuts[1:]:
        factor_of = factor_of * one(*cut)
    return factor_of


def shared_out(rng, own, number, rows, amount, top, bound, lean):
    sequence = jax.random.permutation(rng, amount)
    packed, ordinary = shares(amount, rows * top, bound, lean, True), shares(amount, rows * top, bound, lean, False)
    places = jnp.arange(amount)

    def named(tallies, turn):
        used = int((tallies > 0).sum())
        fixed = max(1, used // 4)
        shifted = fixed + (places - fixed + turn * (used - fixed)) % max(1, amount - fixed)
        return jnp.zeros((amount,), jnp.int32).at[sequence[jnp.where(places < fixed, places, shifted)]].set(jnp.asarray(tallies, jnp.int32))

    tallies = jnp.where(number % 4 == 0, named(packed, number // 4), named(ordinary, number - number // 4 - 1))
    mixed = jax.random.permutation(jax.random.fold_in(own, 3), amount)
    giver, taker = mixed[0:amount // 2 * 2:2], mixed[1:amount // 2 * 2:2]
    margin = jnp.minimum(tallies[giver] - 1, bound - tallies[taker]) // 2
    margin = jnp.where((giver == sequence[0]) | (taker == sequence[0]) | (tallies[taker] == 0), 0, jnp.maximum(margin, 0))
    shifted = jax.random.randint(jax.random.fold_in(own, 4), (amount // 2,), 0, 1 << 20) % (margin + 1)
    tallies = tallies.at[giver].add(-shifted).at[taker].add(shifted)
    labels = jnp.searchsorted(jnp.cumsum(tallies), jnp.arange(rows * top), side="right").astype(jnp.int32)
    grid = labels.reshape(top, rows).T
    grid = grid[jax.random.permutation(jax.random.fold_in(own, 1), rows)]
    turn = jax.random.randint(jax.random.fold_in(own, 2), (rows, 1), 0, top)
    return jnp.take_along_axis(grid, (jnp.arange(top)[None, :] + turn) % top, axis=1)


def shares(number_of, total, most, slope, full):
    loads = [(1 << 20) // math.isqrt(standing ** slope) + 1 for standing in range(1, number_of + 1)]
    largest = most if full else min(most, max(-(-total // number_of), total * loads[0] // sum(loads)))
    least = 1 if total - largest >= number_of - 1 else 0
    counts, surplus = [largest] + [least] * (number_of - 1), total - largest - least * (number_of - 1)
    while surplus > 0:
        free = [i for i in range(1, number_of) if counts[i] < largest] or [i for i in range(1, number_of) if counts[i] < most]
        pool, remaining = sum([loads[i] for i in free]), surplus
        for i in free:
            extra = min(most - counts[i], max(1, remaining * loads[i] // pool), surplus)
            counts[i] = counts[i] + extra
            surplus = surplus - extra
    return np.array(counts)


def centred(rng, extent, width, most, shards=(), dtype=jnp.bfloat16):
    result = jax.random.normal(rng, extent, jnp.float32) * width
    if len(shards) > 0:
        result = steps_of(rng, extent, shards, -0.22, 0.18) * result
    return jnp.clip(result, min=-most, max=most).astype(dtype)


def setup_inputs(seed: int = 0) -> dict:
    streams_of = jax.random.split(jax.random.key(seed), 18)
    tokens = centred(streams_of[0], (TOKENS, D), 1.0, 6.0, ((0, 32),))
    cotangent = centred(streams_of[1], (TOKENS, D), 1.0, 6.0, ((0, 32),))
    routes_keys = jax.random.split(jax.random.fold_in(streams_of[2], 1), TOKENS // TOK_DEV)
    routes_turns = jax.random.permutation(jax.random.fold_in(streams_of[2], 3), TOKENS // TOK_DEV)
    routes = jax.vmap(lambda own, number: shared_out(jax.random.fold_in(streams_of[2], 2), own, number, TOK_DEV, EXPERTS, TOPK, CAP, 0))(routes_keys, routes_turns).reshape((TOKENS, TOPK))
    prompt_ids = draw_prompt_ids(jax.random.fold_in(streams_of[17], 71), 0)
    attn_gain = jnp.clip(1.0 + 0.1 * jax.random.normal(streams_of[4], (D,), jnp.float32), 0.5, 1.5).astype(jnp.bfloat16)
    query_weight = centred(streams_of[5], (D, D), D ** -0.5, 0.21875, ((0, 4),))
    key_weight = centred(streams_of[6], (D, D), D ** -0.5, 0.21875, ((0, 4),))
    value_weight = centred(streams_of[7], (D, D), D ** -0.5, 0.21875, ((0, 4),))
    output_weight = centred(streams_of[8], (D, D), (max(D // 128, 2)) ** -0.5, 2.5, ((0, 4),))
    ffn_gain = jnp.clip(1.0 + 0.1 * jax.random.normal(streams_of[9], (D,), jnp.float32), 0.5, 1.5).astype(jnp.bfloat16)
    router_weight = centred(streams_of[10], (D, EXPERTS), (2 * D) ** -0.5, 0.15625, ((0, 4),))
    shared_gate = centred(streams_of[11], (D, FFS), D ** -0.5, 0.21875, ((0, 4),))
    shared_up = centred(streams_of[12], (D, FFS), D ** -0.5, 0.21875, ((0, 4),))
    shared_down = centred(streams_of[13], (FFS, D), FFS ** -0.5, 0.125, ((0, 4),))
    expert_gate = centred(streams_of[14], (EXPERTS, D, FF), D ** -0.5, 0.21875, ((0, 4),))
    expert_up_weight = centred(streams_of[15], (EXPERTS, D, FF), D ** -0.5, 0.21875, ((0, 4),))
    expert_down = centred(streams_of[16], (EXPERTS, FF, D), (max(FF // 128, 1)) ** -0.5, 1.5, ((0, 4),))
    return {"tokens": tokens, "cotangent": cotangent, "routes": routes, "prompt_ids": prompt_ids, "attn_gain": attn_gain, "query_weight": query_weight, "key_weight": key_weight, "value_weight": value_weight, "output_weight": output_weight, "ffn_gain": ffn_gain, "router_weight": router_weight, "shared_gate": shared_gate, "shared_up": shared_up, "shared_down": shared_down, "expert_gate": expert_gate, "expert_up_weight": expert_up_weight, "expert_down": expert_down}


EPS = 1e-06
HIGH = lax.Precision.HIGHEST

@jax.custom_vjp
def low(v):
    return lax.optimization_barrier(v.astype(jnp.bfloat16)).astype(jnp.float32)

@jax.custom_vjp
def low_back(v):
    return v

def low_keep(v):
    return (low(v), None)

def low_pass(kept, grad):
    return (grad,)

def back_keep(v):
    return (v, None)

def back_low(kept, grad):
    return (low(grad),)
low.defvjp(low_keep, low_pass)
low_back.defvjp(back_keep, back_low)

def matmul_high(left, right):
    return jnp.matmul(left, right, precision=HIGH)

def rotary_tables(tok_rows):
    row_ids = jnp.arange(tok_rows)
    position = jnp.where(row_ids < PROMPT, row_ids, PROMPT + (row_ids - PROMPT) % CLEN).astype(jnp.float32)
    frequency = 10000.0 ** (-2.0 * jnp.arange(HD // 2).astype(jnp.float32) / HD)
    angles = position[:, None] * frequency[None, :]
    return (jnp.cos(angles), jnp.sin(angles))

def rotate(values_in, cos_table, sin_table):
    shaped = values_in.reshape(values_in.shape[:-1] + (HEADS, HD))
    lower_half = shaped[..., :HD // 2]
    upper_half = shaped[..., HD // 2:]
    cos_part = cos_table[:, None, :]
    sin_part = sin_table[:, None, :]
    turned = jnp.concatenate([lower_half * cos_part - upper_half * sin_part, upper_half * cos_part + lower_half * sin_part], -1)
    return turned.reshape(values_in.shape)

def key_mask(context_index, prompt_pick, contexts):
    row_ids = jnp.arange(TOK_DEV)[:, None]
    col_ids = jnp.arange(contexts * PROMPT + CONT * CLEN)[None, :]
    prompt_row = row_ids < PROMPT
    cont_row = (row_ids - PROMPT) // CLEN
    within_row = (row_ids - PROMPT) % CLEN
    owner = lax.optimization_barrier(jnp.sum(prompt_pick[None, :] * (jnp.arange(CONT)[None, :] == cont_row), -1, keepdims=True))
    target = jnp.where(prompt_row, context_index, owner)
    prompt_keys = col_ids < contexts * PROMPT
    prompt_ok = prompt_keys & (col_ids // PROMPT == target) & (jnp.logical_not(prompt_row) | (col_ids % PROMPT <= row_ids))
    offset = col_ids - contexts * PROMPT
    cont_ok = jnp.logical_not(prompt_keys) & jnp.logical_not(prompt_row) & (offset // CLEN == cont_row) & (offset % CLEN <= within_row)
    return prompt_ok | cont_ok

def to_groups(array):
    shaped = array.reshape((N_DP, N_CONTEXT, N_EXPERTS) + array.shape[1:])
    moved = jnp.moveaxis(shaped, 2, 1)
    return moved.reshape((N_DP * N_EXPERTS, N_CONTEXT) + array.shape[1:])

def from_groups(array):
    shaped = array.reshape((N_DP, N_EXPERTS, N_CONTEXT) + array.shape[2:])
    moved = jnp.moveaxis(shaped, 2, 1)
    return moved.reshape((DEVICES,) + array.shape[2:])

def reference(tokens, cotangent, routes, prompt_ids, attn_gain, query_weight, key_weight, value_weight, output_weight, ffn_gain, router_weight, shared_gate, shared_up, shared_down, expert_gate, expert_up_weight, expert_down):
    cos_table, sin_table = rotary_tables(TOK_DEV)
    group_ids = to_groups(prompt_ids.reshape(DEVICES, CONT))

    def forward(inputs, dense, experts_w):
        gain_one, w_query, w_key, w_value, w_out, gain_two, w_router, w_sgate, w_sup, w_sdown = dense
        gate_all, up_all, down_all = experts_w

        def group_forward(pieces):
            block_in, prompt_pick = pieces
            inv_rms = lax.rsqrt(lax.optimization_barrier(jnp.mean(block_in * block_in, -1, keepdims=True)) + EPS)
            hidden1 = low(block_in * inv_rms * gain_one)
            query_all = low(rotate(low_back(matmul_high(hidden1, w_query)), cos_table, sin_table))
            key_all = low(rotate(low_back(matmul_high(hidden1, w_key)), cos_table, sin_table))
            value_all = low(low_back(matmul_high(hidden1, w_value)))
            prompt_keys = key_all[:, :PROMPT].reshape(N_CONTEXT * PROMPT, D)
            prompt_values = value_all[:, :PROMPT].reshape(N_CONTEXT * PROMPT, D)

            def one_block(query_rows, cont_keys, cont_values, own_pick, context_index):
                keys_h = jnp.concatenate([prompt_keys, cont_keys], 0).reshape(-1, HEADS, HD)
                values_h = jnp.concatenate([prompt_values, cont_values], 0).reshape(-1, HEADS, HD)
                query_h = query_rows.reshape(TOK_DEV, HEADS, HD)
                allowed = key_mask(context_index, own_pick, N_CONTEXT)
                scores = low_back(0.125 * jnp.einsum('qhd,khd->hqk', query_h, keys_h, precision=HIGH))
                scores = jnp.where(allowed[None], scores, -1e+30)
                attn_probs = jax.nn.softmax(scores, -1)
                attended = jnp.einsum('hqk,khd->qhd', low(attn_probs), values_h, precision=HIGH)
                attended = low(low_back(attended)).reshape(TOK_DEV, D)
                return low_back(matmul_high(attended, w_out))
            branch = jax.vmap(one_block)(query_all, key_all[:, PROMPT:], value_all[:, PROMPT:], prompt_pick, jnp.arange(N_CONTEXT))
            resid = block_in + branch
            inv_rms2 = lax.rsqrt(lax.optimization_barrier(jnp.mean(resid * resid, -1, keepdims=True)) + EPS)
            hidden2 = low(resid * inv_rms2 * gain_two)
            shared_gpre = low_back(matmul_high(hidden2, w_sgate))
            shared_upre = low_back(matmul_high(hidden2, w_sup))
            shared_act = low(jax.nn.silu(shared_gpre) * shared_upre)
            shared_res = low_back(matmul_high(shared_act, w_sdown))
            return (resid, hidden2, shared_res)
        resid_g, hidden_g, shared_g = lax.map(jax.checkpoint(group_forward), (to_groups(inputs.reshape(DEVICES, TOK_DEV, D)), group_ids))
        resid_rows = from_groups(resid_g).reshape(TOKENS, D)
        hidden_rows = from_groups(hidden_g).reshape(TOKENS, D)
        shared_rows = from_groups(shared_g).reshape(TOKENS, D)
        logits = low_back(matmul_high(hidden_rows, w_router))
        route_probs = jax.nn.softmax(logits, -1)
        route_hot = (routes[:, :, None] == jnp.arange(EXPERTS)[None, None, :]).astype(jnp.float32)
        gate_vals = lax.optimization_barrier(jnp.sum(route_probs[:, None, :] * route_hot, -1))
        flat_route = routes.reshape(DEVICES, TOK_DEV * TOPK)
        flat_hot = (flat_route[:, :, None] == jnp.arange(EXPERTS)[None, None, :]).astype(jnp.int32)
        slot_ids = lax.optimization_barrier(jnp.sum((jnp.cumsum(flat_hot, 1) - flat_hot) * flat_hot, -1))
        position = (jnp.arange(DEVICES)[:, None] * CAP + slot_ids).astype(jnp.int32)
        row_ids = jnp.arange(TOKENS * TOPK).reshape(DEVICES, TOK_DEV * TOPK).astype(jnp.int32)
        source = jnp.full((EXPERTS, DEVICES * CAP), TOKENS * TOPK, jnp.int32)
        source = source.at[flat_route.reshape(-1), position.reshape(-1)].set(row_ids.reshape(-1))
        copies = jnp.stack([low_back(hidden_rows) for pick_index in range(TOPK)], 1).reshape(TOKENS * TOPK, D)
        padded = jnp.concatenate([copies, jnp.zeros((1, D), jnp.float32)], 0)

        def expert_forward(pieces):
            index, gate_w, up_w, down_w = pieces
            inputs_e = padded[index]
            gate_pre = low_back(matmul_high(inputs_e, gate_w))
            up_pre = low_back(matmul_high(inputs_e, up_w))
            inner = low(jax.nn.silu(gate_pre) * up_pre)
            return low(low_back(matmul_high(inner, down_w)))
        expert_out = lax.map(jax.checkpoint(expert_forward), (source, gate_all, up_all, down_all))
        returned = expert_out[flat_route.reshape(TOKENS, TOPK), position.reshape(TOKENS, TOPK)]
        moe_out = lax.optimization_barrier(jnp.sum(gate_vals[:, :, None] * returned, 1))
        return resid_rows + shared_rows + moe_out
    dense = tuple((item.astype(jnp.float32) for item in (attn_gain, query_weight, key_weight, value_weight, output_weight, ffn_gain, router_weight, shared_gate, shared_up, shared_down)))
    experts_w = tuple((item.astype(jnp.float32) for item in (expert_gate, expert_up_weight, expert_down)))
    total, pullback = jax.vjp(forward, tokens.astype(jnp.float32), dense, experts_w)
    grad_in, grad_dense, grad_experts = pullback(cotangent.astype(jnp.float32))
    return (total.astype(jnp.bfloat16), grad_in, grad_dense[0], grad_dense[1], grad_dense[2], grad_dense[3], grad_dense[4], grad_dense[5], grad_dense[6], grad_dense[7], grad_dense[8], grad_dense[9], grad_experts[0], grad_experts[1], grad_experts[2])
```

```python
import functools

import jax
import jax.numpy as jnp
from jax import lax
from jax.sharding import PartitionSpec as P

from jax.experimental import pallas as pl
from jax.experimental.pallas import tpu as pltpu

D = 768
HEADS = 12
HD = 64
EXPERTS = 16
TOPK = 2
PROMPT = 256
CONT = 2
CLEN = 64
TOK_DEV = 384
CAP = 66


EPS = 1e-06


def rotary_tables(tok_rows):
    row_ids = jnp.arange(tok_rows)
    position = jnp.where(row_ids < PROMPT, row_ids, PROMPT + (row_ids - PROMPT) % CLEN).astype(
        jnp.float32
    )
    frequency = 10000.0 ** (-2.0 * jnp.arange(HD // 2).astype(jnp.float32) / HD)
    angles = position[:, None] * frequency[None, :]
    return (jnp.cos(angles), jnp.sin(angles))


def rotate(values_in, cos_table, sin_table):
    shaped = values_in.reshape(values_in.shape[:-1] + (HEADS, HD))
    lower_half = shaped[..., : HD // 2]
    upper_half = shaped[..., HD // 2 :]
    cos_part = cos_table[:, None, :]
    sin_part = sin_table[:, None, :]
    turned = jnp.concatenate(
        [
            lower_half * cos_part - upper_half * sin_part,
            upper_half * cos_part + lower_half * sin_part,
        ],
        -1,
    )
    return turned.reshape(values_in.shape)


def key_mask(context_index, prompt_pick, contexts):
    row_ids = jnp.arange(TOK_DEV)[:, None]
    col_ids = jnp.arange(contexts * PROMPT + CONT * CLEN)[None, :]
    prompt_row = row_ids < PROMPT
    cont_row = (row_ids - PROMPT) // CLEN
    within_row = (row_ids - PROMPT) % CLEN
    owner = jnp.sum(
        prompt_pick[None, :] * (jnp.arange(CONT)[None, :] == cont_row), -1, keepdims=True
    )
    target = jnp.where(prompt_row, context_index, owner)
    prompt_keys = col_ids < contexts * PROMPT
    prompt_ok = (
        prompt_keys
        & (col_ids // PROMPT == target)
        & (jnp.logical_not(prompt_row) | (col_ids % PROMPT <= row_ids))
    )
    offset = col_ids - contexts * PROMPT
    cont_ok = (
        jnp.logical_not(prompt_keys)
        & jnp.logical_not(prompt_row)
        & (offset // CLEN == cont_row)
        & (offset % CLEN <= within_row)
    )
    return prompt_ok | cont_ok


def inner_rows(left, right):
    return lax.dot_general(
        left, right, (((0,), (0,)), ((), ())), preferred_element_type=jnp.float32
    )


def times_transposed(left, right):
    return lax.dot_general(
        left, right, (((1,), (1,)), ((), ())), preferred_element_type=jnp.float32
    )


def swish_derivative(pre_act):
    sigma = jax.nn.sigmoid(pre_act)
    return sigma * (1.0 + pre_act * (1.0 - sigma))


def plain_body(
    tokens,
    cotangent,
    routes,
    prompt_ids,
    attn_gain,
    query_weight,
    key_weight,
    value_weight,
    output_weight,
    ffn_gain,
    router_weight,
    shared_gate,
    shared_up,
    shared_down,
    expert_gate,
    expert_up_weight,
    expert_down,
):
    contexts = lax.axis_size("context")
    context_here = lax.axis_index("context")
    gain_one, w_query, w_key, w_value, w_out, gain_two, w_router, w_sgate, w_sup, w_sdown = (
        lax.all_gather(attn_gain, "dp", axis=0, tiled=True),
        lax.all_gather(query_weight, "dp", axis=0, tiled=True),
        lax.all_gather(key_weight, "dp", axis=0, tiled=True),
        lax.all_gather(value_weight, "dp", axis=0, tiled=True),
        lax.all_gather(output_weight, "dp", axis=0, tiled=True),
        lax.all_gather(ffn_gain, "dp", axis=0, tiled=True),
        lax.all_gather(router_weight, "dp", axis=0, tiled=True),
        lax.all_gather(shared_gate, "dp", axis=0, tiled=True),
        lax.all_gather(shared_up, "dp", axis=0, tiled=True),
        lax.all_gather(shared_down, "dp", axis=0, tiled=True),
    )
    cos_table, sin_table = rotary_tables(TOK_DEV)
    inputs = tokens.astype(jnp.float32)
    inv_rms1 = lax.rsqrt(jnp.mean(inputs * inputs, -1, keepdims=True) + EPS)
    normed1 = inputs * inv_rms1
    gain1_f = gain_one.astype(jnp.float32)
    hidden1 = (normed1 * gain1_f).astype(jnp.bfloat16)
    query_f = jnp.dot(hidden1, w_query, preferred_element_type=jnp.float32)
    key_f = jnp.dot(hidden1, w_key, preferred_element_type=jnp.float32)
    value_f = jnp.dot(hidden1, w_value, preferred_element_type=jnp.float32)
    query_b = rotate(query_f, cos_table, sin_table).astype(jnp.bfloat16)
    key_b = rotate(key_f, cos_table, sin_table).astype(jnp.bfloat16)
    value_b = value_f.astype(jnp.bfloat16)
    prompt_keys, prompt_values = (
        lax.all_gather(key_b[:PROMPT], "context", axis=0, tiled=True),
        lax.all_gather(value_b[:PROMPT], "context", axis=0, tiled=True),
    )
    keys_h = jnp.concatenate([prompt_keys, key_b[PROMPT:]], 0).reshape(-1, HEADS, HD)
    values_h = jnp.concatenate([prompt_values, value_b[PROMPT:]], 0).reshape(-1, HEADS, HD)
    query_h = query_b.reshape(TOK_DEV, HEADS, HD)
    allowed = key_mask(context_here, prompt_ids, contexts)
    scores = jnp.where(
        allowed[None],
        0.125 * jnp.einsum("qhd,khd->hqk", query_h, keys_h, preferred_element_type=jnp.float32),
        -1e30,
    )
    row_max = jnp.max(scores, -1, keepdims=True)
    exp_scores = jnp.exp(scores - row_max)
    row_total = jnp.sum(exp_scores, -1, keepdims=True)
    log_total = row_max + jnp.log(row_total)
    attn_probs = (exp_scores / row_total).astype(jnp.bfloat16)
    attended = (
        jnp.einsum("hqk,khd->qhd", attn_probs, values_h, preferred_element_type=jnp.float32)
        .reshape(TOK_DEV, D)
        .astype(jnp.bfloat16)
    )
    resid = inputs + jnp.dot(attended, w_out, preferred_element_type=jnp.float32)
    inv_rms2 = lax.rsqrt(jnp.mean(resid * resid, -1, keepdims=True) + EPS)
    normed2 = resid * inv_rms2
    gain2_f = gain_two.astype(jnp.float32)
    hidden2 = (normed2 * gain2_f).astype(jnp.bfloat16)
    logits = jnp.dot(hidden2, w_router, preferred_element_type=jnp.float32)
    route_probs = jax.nn.softmax(logits, -1)
    route_hot = (routes[:, :, None] == jnp.arange(EXPERTS)[None, None, :]).astype(jnp.float32)
    gate_vals = jnp.sum(route_probs[:, None, :] * route_hot, -1)
    shared_gpre = jnp.dot(hidden2, w_sgate, preferred_element_type=jnp.float32)
    shared_upre = jnp.dot(hidden2, w_sup, preferred_element_type=jnp.float32)
    shared_act = (jax.nn.silu(shared_gpre) * shared_upre).astype(jnp.bfloat16)
    shared_res = jnp.dot(shared_act, w_sdown, preferred_element_type=jnp.float32)
    flat_route = routes.reshape(-1)
    flat_hot = (flat_route[:, None] == jnp.arange(EXPERTS)[None, :]).astype(jnp.int32)
    slot_ids = jnp.sum((jnp.cumsum(flat_hot, 0) - flat_hot) * flat_hot, -1)
    slot_index = flat_route * CAP + slot_ids
    send_rows = jnp.repeat(hidden2, TOPK, axis=0)
    outgoing = (
        jnp.zeros((EXPERTS * CAP, D), jnp.bfloat16)
        .at[slot_index]
        .set(send_rows)
        .reshape(EXPERTS, CAP, D)
    )
    received_rows = lax.all_to_all(outgoing, "experts", split_axis=0, concat_axis=1, tiled=True)
    expert_gate_preact = jnp.einsum(
        "mgx,mxp->mgp", received_rows, expert_gate, preferred_element_type=jnp.float32
    )
    expert_up_preact = jnp.einsum(
        "mgx,mxp->mgp", received_rows, expert_up_weight, preferred_element_type=jnp.float32
    )
    expert_activation = (jax.nn.silu(expert_gate_preact) * expert_up_preact).astype(jnp.bfloat16)
    expert_res = jnp.einsum(
        "erf,efd->erd", expert_activation, expert_down, preferred_element_type=jnp.float32
    ).astype(jnp.bfloat16)
    returned = lax.all_to_all(
        expert_res, "experts", split_axis=1, concat_axis=0, tiled=True
    ).reshape(EXPERTS * CAP, D)
    picked = returned[slot_index].astype(jnp.float32).reshape(TOK_DEV, TOPK, D)
    moe_out = jnp.sum(gate_vals[:, :, None] * picked, 1)
    layer_out = (resid + shared_res + moe_out).astype(jnp.bfloat16)
    gain_one, w_query, w_key, w_value, w_out, gain_two, w_router, w_sgate, w_sup, w_sdown = (
        lax.all_gather(attn_gain, "dp", axis=0, tiled=True),
        lax.all_gather(query_weight, "dp", axis=0, tiled=True),
        lax.all_gather(key_weight, "dp", axis=0, tiled=True),
        lax.all_gather(value_weight, "dp", axis=0, tiled=True),
        lax.all_gather(output_weight, "dp", axis=0, tiled=True),
        lax.all_gather(ffn_gain, "dp", axis=0, tiled=True),
        lax.all_gather(router_weight, "dp", axis=0, tiled=True),
        lax.all_gather(shared_gate, "dp", axis=0, tiled=True),
        lax.all_gather(shared_up, "dp", axis=0, tiled=True),
        lax.all_gather(shared_down, "dp", axis=0, tiled=True),
    )
    gain1_f = gain_one.astype(jnp.float32)
    gain2_f = gain_two.astype(jnp.float32)
    grad_total = cotangent.astype(jnp.float32)
    grad_gates = jnp.sum(grad_total[:, None, :] * picked, -1)
    grad_picked = (
        (gate_vals[:, :, None] * grad_total[:, None, :])
        .astype(jnp.bfloat16)
        .reshape(TOK_DEV * TOPK, D)
    )
    grad_back = (
        jnp.zeros((EXPERTS * CAP, D), jnp.bfloat16)
        .at[slot_index]
        .set(grad_picked)
        .reshape(EXPERTS, CAP, D)
    )
    grad_arrived = lax.all_to_all(grad_back, "experts", split_axis=0, concat_axis=1, tiled=True)
    grad_expert_activation = jnp.einsum(
        "erd,efd->erf", grad_arrived, expert_down, preferred_element_type=jnp.float32
    )
    grad_expert_gate_preact = (
        grad_expert_activation * expert_up_preact * swish_derivative(expert_gate_preact)
    ).astype(jnp.bfloat16)
    grad_expert_up_preact = (grad_expert_activation * jax.nn.silu(expert_gate_preact)).astype(
        jnp.bfloat16
    )
    expert_grad_down = jnp.einsum(
        "erf,erd->edf", expert_activation, grad_arrived, preferred_element_type=jnp.float32
    )
    expert_grad_gate = jnp.einsum(
        "xvb,xva->xba", received_rows, grad_expert_gate_preact, preferred_element_type=jnp.float32
    )
    expert_grad_up = jnp.einsum(
        "xvb,xva->xba", received_rows, grad_expert_up_preact, preferred_element_type=jnp.float32
    )
    grad_einputs = jnp.einsum(
        "cgj,clj->cgl", grad_expert_gate_preact, expert_gate, preferred_element_type=jnp.float32
    )
    grad_einputs = (
        grad_einputs
        + jnp.einsum(
            "cgj,clj->cgl",
            grad_expert_up_preact,
            expert_up_weight,
            preferred_element_type=jnp.float32,
        )
    ).astype(jnp.bfloat16)
    grad_returned = lax.all_to_all(
        grad_einputs, "experts", split_axis=1, concat_axis=0, tiled=True
    ).reshape(EXPERTS * CAP, D)
    grad_moe_in = jnp.sum(
        grad_returned[slot_index].astype(jnp.float32).reshape(TOK_DEV, TOPK, D), 1
    )
    grad_rprobs = jnp.sum(grad_gates[:, :, None] * route_hot, 1)
    grad_logits = (
        route_probs * (grad_rprobs - jnp.sum(route_probs * grad_rprobs, -1, keepdims=True))
    ).astype(jnp.bfloat16)
    grad_router_local = inner_rows(hidden2, grad_logits)
    grad_total_b = grad_total.astype(jnp.bfloat16)
    grad_sdown = inner_rows(shared_act, grad_total_b)
    grad_sact = times_transposed(grad_total_b, w_sdown)
    grad_sgpre = (grad_sact * shared_upre * swish_derivative(shared_gpre)).astype(jnp.bfloat16)
    grad_supre = (grad_sact * jax.nn.silu(shared_gpre)).astype(jnp.bfloat16)
    grad_sgate = inner_rows(hidden2, grad_sgpre)
    grad_sup = inner_rows(hidden2, grad_supre)
    grad_hidden2 = (
        grad_moe_in
        + times_transposed(grad_logits, w_router)
        + times_transposed(grad_sgpre, w_sgate)
        + times_transposed(grad_supre, w_sup)
    )
    grad_gain2 = jnp.sum(grad_hidden2 * normed2, 0)
    grad_normed2 = grad_hidden2 * gain2_f
    grad_resid = (
        inv_rms2 * (grad_normed2 - normed2 * jnp.mean(grad_normed2 * normed2, -1, keepdims=True))
        + grad_total
    )
    grad_branch = grad_resid.astype(jnp.bfloat16)
    grad_wout = inner_rows(attended, grad_branch)
    grad_attended = (
        times_transposed(grad_branch, w_out).astype(jnp.bfloat16).reshape(TOK_DEV, HEADS, HD)
    )
    scores_again = jnp.where(
        allowed[None],
        0.125 * jnp.einsum("qhd,khd->hqk", query_h, keys_h, preferred_element_type=jnp.float32),
        -1e30,
    )
    probs_f = jnp.exp(scores_again - log_total)
    probs_b = probs_f.astype(jnp.bfloat16)
    grad_pattn = jnp.einsum(
        "qhd,khd->hqk", grad_attended, values_h, preferred_element_type=jnp.float32
    )
    grad_scores = (
        probs_f * (grad_pattn - jnp.sum(probs_f * grad_pattn, -1, keepdims=True))
    ).astype(jnp.bfloat16)
    grad_query = 0.125 * jnp.einsum(
        "hqk,khd->qhd", grad_scores, keys_h, preferred_element_type=jnp.float32
    ).reshape(TOK_DEV, D)
    grad_keys = 0.125 * jnp.einsum(
        "hqk,qhd->khd", grad_scores, query_h, preferred_element_type=jnp.float32
    ).reshape(-1, D)
    grad_values = jnp.einsum(
        "hqk,qhd->khd", probs_b, grad_attended, preferred_element_type=jnp.float32
    ).reshape(-1, D)
    prompt_span = contexts * PROMPT
    grad_pkeys, grad_pvalues = (
        lax.psum_scatter(
            grad_keys[:prompt_span].astype(jnp.bfloat16), "context", scatter_dimension=0, tiled=True
        ).astype(jnp.float32),
        lax.psum_scatter(
            grad_values[:prompt_span].astype(jnp.bfloat16),
            "context",
            scatter_dimension=0,
            tiled=True,
        ).astype(jnp.float32),
    )
    grad_key_all = jnp.concatenate([grad_pkeys, grad_keys[prompt_span:]], 0)
    grad_value_all = jnp.concatenate([grad_pvalues, grad_values[prompt_span:]], 0)
    grad_qpre = rotate(grad_query, cos_table, -sin_table).astype(jnp.bfloat16)
    grad_kpre = rotate(grad_key_all, cos_table, -sin_table).astype(jnp.bfloat16)
    grad_vpre = grad_value_all.astype(jnp.bfloat16)
    grad_wquery = inner_rows(hidden1, grad_qpre)
    grad_wkey = inner_rows(hidden1, grad_kpre)
    grad_wvalue = inner_rows(hidden1, grad_vpre)
    grad_hidden1 = (
        times_transposed(grad_qpre, w_query)
        + times_transposed(grad_kpre, w_key)
        + times_transposed(grad_vpre, w_value)
    )
    grad_gain1 = jnp.sum(grad_hidden1 * normed1, 0)
    grad_normed1 = grad_hidden1 * gain1_f
    grad_inputs = (
        inv_rms1 * (grad_normed1 - normed1 * jnp.mean(grad_normed1 * normed1, -1, keepdims=True))
        + grad_resid
    )
    shares = (
        lax.psum_scatter(
            grad_gain1.astype(jnp.bfloat16), "dp", scatter_dimension=0, tiled=True
        ).astype(jnp.float32),
        lax.psum_scatter(
            grad_wquery.astype(jnp.bfloat16), "dp", scatter_dimension=0, tiled=True
        ).astype(jnp.float32),
        lax.psum_scatter(
            grad_wkey.astype(jnp.bfloat16), "dp", scatter_dimension=0, tiled=True
        ).astype(jnp.float32),
        lax.psum_scatter(
            grad_wvalue.astype(jnp.bfloat16), "dp", scatter_dimension=0, tiled=True
        ).astype(jnp.float32),
        lax.psum_scatter(
            grad_wout.astype(jnp.bfloat16), "dp", scatter_dimension=0, tiled=True
        ).astype(jnp.float32),
        lax.psum_scatter(
            grad_gain2.astype(jnp.bfloat16), "dp", scatter_dimension=0, tiled=True
        ).astype(jnp.float32),
        lax.psum_scatter(
            grad_router_local.astype(jnp.bfloat16), "dp", scatter_dimension=0, tiled=True
        ).astype(jnp.float32),
        lax.psum_scatter(
            grad_sgate.astype(jnp.bfloat16), "dp", scatter_dimension=0, tiled=True
        ).astype(jnp.float32),
        lax.psum_scatter(
            grad_sup.astype(jnp.bfloat16), "dp", scatter_dimension=0, tiled=True
        ).astype(jnp.float32),
        lax.psum_scatter(
            grad_sdown.astype(jnp.bfloat16), "dp", scatter_dimension=0, tiled=True
        ).astype(jnp.float32),
    )
    totals = (
        lax.psum(shares[0].astype(jnp.bfloat16), ("context", "experts")).astype(jnp.float32),
        lax.psum(shares[1].astype(jnp.bfloat16), ("context", "experts")).astype(jnp.float32),
        lax.psum(shares[2].astype(jnp.bfloat16), ("context", "experts")).astype(jnp.float32),
        lax.psum(shares[3].astype(jnp.bfloat16), ("context", "experts")).astype(jnp.float32),
        lax.psum(shares[4].astype(jnp.bfloat16), ("context", "experts")).astype(jnp.float32),
        lax.psum(shares[5].astype(jnp.bfloat16), ("context", "experts")).astype(jnp.float32),
        lax.psum(shares[6].astype(jnp.bfloat16), ("context", "experts")).astype(jnp.float32),
        lax.psum(shares[7].astype(jnp.bfloat16), ("context", "experts")).astype(jnp.float32),
        lax.psum(shares[8].astype(jnp.bfloat16), ("context", "experts")).astype(jnp.float32),
        lax.psum(shares[9].astype(jnp.bfloat16), ("context", "experts")).astype(jnp.float32),
    )
    summed_gate, summed_up, summed_down = (
        lax.psum_scatter(
            expert_grad_gate.astype(jnp.bfloat16),
            ("dp", "context"),
            scatter_dimension=2,
            tiled=True,
        ).astype(jnp.float32),
        lax.psum_scatter(
            expert_grad_up.astype(jnp.bfloat16), ("dp", "context"), scatter_dimension=2, tiled=True
        ).astype(jnp.float32),
        lax.psum_scatter(
            expert_grad_down.astype(jnp.bfloat16),
            ("dp", "context"),
            scatter_dimension=2,
            tiled=True,
        ).astype(jnp.float32),
    )
    summed_down = jnp.transpose(summed_down, (0, 2, 1))
    return (
        layer_out,
        grad_inputs,
        totals[0],
        totals[1],
        totals[2],
        totals[3],
        totals[4],
        totals[5],
        totals[6],
        totals[7],
        totals[8],
        totals[9],
        summed_gate,
        summed_up,
        summed_down,
    )


TUNED_MESH = {"dp": 4, "context": 2, "experts": 4}
AXES = ("dp", "context", "experts")
SLOT = 72
EXT = 16
ROWS = TOK_DEV + EXT
BF = jnp.bfloat16
F32 = jnp.float32
VMEM_LIMIT = 60 * 1024 * 1024


def moved(value, target):
    pairs = []
    for z in range(4):
        for y in range(2):
            for x in range(2):
                for c in range(2):
                    tz, ty, tx, tc = target(z, y, x, c)
                    pairs.append((((z * 2 + y) * 2 + x) * 2 + c, ((tz * 2 + ty) * 2 + tx) * 2 + tc))
    return lax.ppermute(value, AXES, pairs)


def over_core(value):
    return moved(value, lambda z, y, x, c: (z, y, x, 1 - c))


def over_x(value):
    return moved(value, lambda z, y, x, c: (z, y, 1 - x, c))


def over_a(value):
    return moved(value, lambda z, y, x, c: (z, y, 1 - x, c) if c == 0 else (z, 1 - y, x, c))


def over_b(value):
    return moved(value, lambda z, y, x, c: (z, 1 - y, x, c) if c == 0 else (z, y, 1 - x, c))


def over_z(value, step):
    return moved(value, lambda z, y, x, c: ((z + step) % 4, y, x, c))


def gather_blocks(block):
    column = jnp.stack([block] + [over_z(block, step) for step in (1, 2, 3)])
    first = over_a(column)
    second = over_b(column)
    third = over_b(first)
    mine = [column, first, second, third]
    return mine + [over_core(part) for part in mine]


def gather_rows(shard, core):
    half = shard.shape[0] // 2
    part = lax.dynamic_slice_in_dim(shard, core * half, half, 0)
    part = lax.all_gather(part, "dp", axis=0, tiled=False)
    other = over_core(part)
    both = jnp.where(core == 0, jnp.stack([part, other], 1), jnp.stack([other, part], 1))
    return both.reshape(-1, shard.shape[1])


def contract(left, right, left_dim, right_dim):
    return lax.dot_general(
        left, right, (((left_dim,), (right_dim,)), ((), ())), preferred_element_type=F32
    )


def one_hot_rows(rank_row):
    slots = lax.broadcasted_iota(jnp.int32, (SLOT, TOK_DEV), 0).astype(F32)
    return (slots == rank_row).astype(F32)


def swish_parts(pre_act):
    sigma = jax.nn.sigmoid(pre_act)
    return pre_act * sigma, sigma * (1.0 + pre_act * (1.0 - sigma))


def group_kernel(
    base_ref,
    h_ref,
    g_ref,
    wg_ref,
    wu_ref,
    wd_ref,
    moe_ref,
    dx_ref,
    rank_sc,
    prob_sc,
    x_sc,
    gd_sc,
    gate_sc,
    y_sc,
    acc_sc,
    dgate_sc,
    ysel_sc,
    dsel_sc,
    drp_sc,
):
    e = pl.program_id(0)
    f = pl.program_id(1)
    blocks = h_ref.shape[0]
    experts = pl.num_programs(0)
    base = base_ref[0]

    @pl.when((e == 0) & (f == 0))
    def _():
        for b in range(blocks):
            rank_sc[b] = g_ref[b, TOK_DEV:, :TOK_DEV].astype(F32)
            prob_sc[b] = h_ref[b, TOK_DEV:, :TOK_DEV].astype(F32) + h_ref[
                b, TOK_DEV:, TOK_DEV:
            ].astype(F32)
        drp_sc[...] = jnp.zeros_like(drp_sc)

    @pl.when(f == 0)
    def _():
        for pair in range(blocks // 2):
            rows_x, rows_g = [], []
            for b in (2 * pair, 2 * pair + 1):
                hot = one_hot_rows(rank_sc[b, pl.ds(base + e, 1), :])
                gate_sc[b * SLOT : (b + 1) * SLOT, :] = jnp.sum(
                    hot * prob_sc[b, pl.ds(base + e, 1), :], -1, keepdims=True
                )
                hot = hot.astype(BF)
                rows_x.append(jnp.dot(hot, h_ref[b, :TOK_DEV, :], preferred_element_type=F32))
                rows_g.append(jnp.dot(hot, g_ref[b, :TOK_DEV, :], preferred_element_type=F32))
            span = slice(pair * 2 * SLOT, (pair + 1) * 2 * SLOT)
            x_sc[span, :] = jnp.concatenate(rows_x, 0).astype(BF)
            gd_sc[span, :] = jnp.concatenate(rows_g, 0).astype(BF)
        y_sc[...] = jnp.zeros_like(y_sc)
        acc_sc[...] = jnp.zeros_like(acc_sc)
        dgate_sc[...] = jnp.zeros_like(dgate_sc)

    rows = x_sc[...]
    gate_pre = jnp.dot(rows, wg_ref[0], preferred_element_type=F32)
    up_pre = jnp.dot(rows, wu_ref[0], preferred_element_type=F32)
    back = contract(gd_sc[...], wd_ref[0], 1, 1)
    swish, slope = swish_parts(gate_pre)
    inner = (swish * up_pre).astype(BF)
    dgate_sc[...] += jnp.sum(back * inner.astype(F32), -1, keepdims=True)
    back = back * gate_sc[...]
    dgate_pre = (back * up_pre * slope).astype(BF)
    dup_pre = (back * swish).astype(BF)
    y_sc[...] += jnp.dot(inner, wd_ref[0], preferred_element_type=F32)
    acc_sc[...] += contract(dgate_pre, wg_ref[0], 1, 1) + contract(dup_pre, wu_ref[0], 1, 1)

    @pl.when(f == pl.num_programs(1) - 1)
    def _():
        for b in range(blocks):
            span = slice(b * SLOT, (b + 1) * SLOT)
            into = pl.ds(pl.multiple_of(e * SLOT, 8), SLOT)
            ysel_sc[b, into, :] = y_sc[span, :] * gate_sc[span, :]
            dsel_sc[b, into, :] = acc_sc[span, :]
            hot = one_hot_rows(rank_sc[b, pl.ds(base + e, 1), :])
            drp_sc[b, pl.ds(base + e, 1), :] = jnp.sum(hot * dgate_sc[span, :], 0, keepdims=True)

    @pl.when((f == pl.num_programs(1) - 1) & (e == experts - 1))
    def _():
        for b in range(blocks):
            hot = jnp.concatenate(
                [
                    one_hot_rows(rank_sc[b, pl.ds(base + i, 1), :])
                    for i in range(ysel_sc.shape[1] // SLOT)
                ],
                0,
            ).astype(BF)
            moe_ref[b] = contract(hot, ysel_sc[b].astype(BF), 0, 0).astype(BF)
            dx_ref[b, :TOK_DEV, :] = contract(hot, dsel_sc[b].astype(BF), 0, 0).astype(BF)
            high = drp_sc[b].astype(BF)
            dx_ref[b, TOK_DEV:, :TOK_DEV] = high
            dx_ref[b, TOK_DEV:, TOK_DEV:] = (drp_sc[b] - high.astype(F32)).astype(BF)


def group_experts(base, h_group, g_group, w_gate, w_up, w_down):
    blocks = h_group.shape[0]
    experts, _, ff = w_gate.shape
    tile = 512
    whole = lambda *shape: pl.BlockSpec(shape, lambda e, f, s: (0,) * len(shape))
    return pl.pallas_call(
        group_kernel,
        out_shape=(
            jax.ShapeDtypeStruct((blocks, TOK_DEV, D), BF),
            jax.ShapeDtypeStruct((blocks, ROWS, D), BF),
        ),
        grid_spec=pltpu.PrefetchScalarGridSpec(
            num_scalar_prefetch=1,
            grid=(experts, ff // tile),
            in_specs=[
                whole(blocks, ROWS, D),
                whole(blocks, ROWS, D),
                pl.BlockSpec((1, D, tile), lambda e, f, s: (e, 0, f)),
                pl.BlockSpec((1, D, tile), lambda e, f, s: (e, 0, f)),
                pl.BlockSpec((1, tile, D), lambda e, f, s: (e, f, 0)),
            ],
            out_specs=[whole(blocks, TOK_DEV, D), whole(blocks, ROWS, D)],
            scratch_shapes=[
                pltpu.VMEM((blocks, EXPERTS, TOK_DEV), F32),
                pltpu.VMEM((blocks, EXPERTS, TOK_DEV), F32),
                pltpu.VMEM((blocks * SLOT, D), BF),
                pltpu.VMEM((blocks * SLOT, D), BF),
                pltpu.VMEM((blocks * SLOT, 1), F32),
                pltpu.VMEM((blocks * SLOT, D), F32),
                pltpu.VMEM((blocks * SLOT, D), F32),
                pltpu.VMEM((blocks * SLOT, 1), F32),
                pltpu.VMEM((blocks, experts * SLOT, D), F32),
                pltpu.VMEM((blocks, experts * SLOT, D), F32),
                pltpu.VMEM((blocks, EXPERTS, TOK_DEV), F32),
            ],
        ),
        compiler_params=pltpu.CompilerParams(vmem_limit_bytes=VMEM_LIMIT),
        cost_estimate=pl.CostEstimate(
            flops=2 * 6 * experts * blocks * SLOT * D * ff,
            bytes_accessed=2 * 3 * experts * D * ff,
            transcendentals=0,
        ),
        name="group_experts",
    )(base, h_group, g_group, w_gate, w_up, w_down)


def shared_kernel(h_ref, g_ref, wg_ref, wu_ref, wd_ref, out_ref, dh_ref):
    @pl.when(pl.program_id(0) == 0)
    def _():
        out_ref[...] = jnp.zeros_like(out_ref)
        dh_ref[...] = jnp.zeros_like(dh_ref)

    gate_pre = jnp.dot(h_ref[...], wg_ref[...], preferred_element_type=F32)
    up_pre = jnp.dot(h_ref[...], wu_ref[...], preferred_element_type=F32)
    back = contract(g_ref[...], wd_ref[...], 1, 1)
    swish, slope = swish_parts(gate_pre)
    inner = (swish * up_pre).astype(BF)
    out_ref[...] += jnp.dot(inner, wd_ref[...], preferred_element_type=F32)
    dgate_pre = (back * up_pre * slope).astype(BF)
    dup_pre = (back * swish).astype(BF)
    dh_ref[...] += contract(dgate_pre, wg_ref[...], 1, 1) + contract(dup_pre, wu_ref[...], 1, 1)


def shared_rows(h2, grad, w_gate, w_up, w_down):
    tokens, ff = h2.shape[0], w_gate.shape[1]
    tile = 512
    rows = pl.BlockSpec((tokens, D), lambda f: (0, 0))
    return pl.pallas_call(
        shared_kernel,
        out_shape=(jax.ShapeDtypeStruct((tokens, D), F32),) * 2,
        grid=(ff // tile,),
        in_specs=[
            rows,
            rows,
            pl.BlockSpec((D, tile), lambda f: (0, f)),
            pl.BlockSpec((D, tile), lambda f: (0, f)),
            pl.BlockSpec((tile, D), lambda f: (f, 0)),
        ],
        out_specs=[rows, rows],
        compiler_params=pltpu.CompilerParams(vmem_limit_bytes=VMEM_LIMIT),
        cost_estimate=pl.CostEstimate(
            flops=2 * 6 * tokens * D * ff, bytes_accessed=2 * 3 * D * ff, transcendentals=0
        ),
        name="shared_rows",
    )(h2, grad, w_gate, w_up, w_down)


def start_half(part, h_parts, g_parts, h_buf, g_buf, sems):
    half = len(h_parts) // 2
    for i in range(half):
        per = h_parts[i].shape[0]
        for which, (parts, buf) in enumerate(((h_parts, h_buf), (g_parts, g_buf))):
            pltpu.make_async_copy(
                parts[part * half + i], buf.at[pl.ds(i * per, per)], sems.at[which, i]
            ).start()


def wait_part(part, i, h_parts, g_parts, h_buf, g_buf, sems):
    half = len(h_parts) // 2
    per = h_parts[i].shape[0]
    for which, (parts, buf) in enumerate(((h_parts, h_buf), (g_parts, g_buf))):
        pltpu.make_async_copy(
            parts[part * half + i], buf.at[pl.ds(i * per, per)], sems.at[which, i]
        ).wait()


def expert_slice_kernel(parts, pos_ref, *refs):
    h_parts, g_parts = refs[:parts], refs[parts : 2 * parts]
    wg_ref, wu_ref, wd_ref, og_ref, ou_ref, od_ref = refs[2 * parts : 2 * parts + 6]
    h_buf, g_buf, x_sc, gd_sc, gate_sc, rank_sc, prob_sc, sems = refs[2 * parts + 6 :]
    base = pos_ref[0]
    experts = wg_ref.shape[0]
    half = parts // 2
    per = h_parts[0].shape[0]

    def dispatch(pair, carry):
        both_x, both_g, both_gate = [], [], []
        for k in range(2):
            b = 2 * pair + k
            rank_sc[k] = g_buf[b, TOK_DEV:, :TOK_DEV].astype(F32)
            prob_sc[k] = h_buf[b, TOK_DEV:, :TOK_DEV].astype(F32) + h_buf[
                b, TOK_DEV:, TOK_DEV:
            ].astype(F32)
            hots, gates = [], []
            for i in range(experts):
                hot = one_hot_rows(rank_sc[k, pl.ds(base + i, 1), :])
                gates.append(
                    jnp.sum(hot * prob_sc[k, pl.ds(base + i, 1), :], -1, keepdims=True)
                )
                hots.append(hot)
            hot = jnp.concatenate(hots, 0).astype(BF)
            both_x.append(jnp.dot(hot, h_buf[b, :TOK_DEV, :], preferred_element_type=F32))
            both_g.append(jnp.dot(hot, g_buf[b, :TOK_DEV, :], preferred_element_type=F32))
            both_gate.append(gates)
        into = pl.ds(pl.multiple_of(pair * 2 * SLOT, 2 * SLOT), 2 * SLOT)
        for i in range(experts):
            span = slice(i * SLOT, (i + 1) * SLOT)
            x_sc[i, into, :] = jnp.concatenate([v[span] for v in both_x], 0).astype(BF)
            gd_sc[i, into, :] = jnp.concatenate([v[span] for v in both_g], 0).astype(BF)
            gate_sc[i, into, :] = jnp.concatenate([v[i] for v in both_gate], 0)
        return carry

    start_half(0, h_parts, g_parts, h_buf, g_buf, sems)
    for part in range(2):
        for i in range(half):
            wait_part(part, i, h_parts, g_parts, h_buf, g_buf, sems)
            lax.fori_loop(i * per // 2, (i + 1) * per // 2, dispatch, 0)
        if part == 0:
            start_half(1, h_parts, g_parts, h_buf, g_buf, sems)

        def products(i, carry, part=part):
            rows = x_sc[i]
            gate_pre = jnp.dot(rows, wg_ref[i], preferred_element_type=F32)
            up_pre = jnp.dot(rows, wu_ref[i], preferred_element_type=F32)
            back = contract(gd_sc[i], wd_ref[i], 1, 1) * gate_sc[i]
            swish, slope = swish_parts(gate_pre)
            inner = (swish * up_pre * gate_sc[i]).astype(BF)
            dgate_pre = (back * up_pre * slope).astype(BF)
            dup_pre = (back * swish).astype(BF)
            add_g = contract(rows, dgate_pre, 0, 0)
            add_u = contract(rows, dup_pre, 0, 0)
            add_d = contract(inner, gd_sc[i], 0, 0)
            if part == 0:
                og_ref[i], ou_ref[i], od_ref[i] = add_g, add_u, add_d
            else:
                og_ref[i] += add_g
                ou_ref[i] += add_u
                od_ref[i] += add_d
            return carry

        lax.fori_loop(0, experts, products, 0)


def expert_slice_grads(pos, h_parts, g_parts, w_gate, w_up, w_down, width):
    parts, per = len(h_parts), h_parts[0].shape[0]
    experts = w_gate.shape[0]
    blocks = parts * per // 2
    anywhere = pl.BlockSpec(memory_space=pl.ANY)
    return pl.pallas_call(
        functools.partial(expert_slice_kernel, parts),
        out_shape=(
            jax.ShapeDtypeStruct((experts, D, width), F32),
            jax.ShapeDtypeStruct((experts, D, width), F32),
            jax.ShapeDtypeStruct((experts, width, D), F32),
        ),
        grid_spec=pltpu.PrefetchScalarGridSpec(
            num_scalar_prefetch=1,
            grid=(1,),
            in_specs=[anywhere] * (2 * parts)
            + [
                pl.BlockSpec((experts, D, width), lambda i, s: (0, 0, s[1])),
                pl.BlockSpec((experts, D, width), lambda i, s: (0, 0, s[1])),
                pl.BlockSpec((experts, width, D), lambda i, s: (0, s[1], 0)),
            ],
            out_specs=[
                pl.BlockSpec((experts, D, width), lambda i, s: (0, 0, 0)),
                pl.BlockSpec((experts, D, width), lambda i, s: (0, 0, 0)),
                pl.BlockSpec((experts, width, D), lambda i, s: (0, 0, 0)),
            ],
            scratch_shapes=[
                pltpu.VMEM((blocks, ROWS, D), BF),
                pltpu.VMEM((blocks, ROWS, D), BF),
                pltpu.VMEM((experts, blocks * SLOT, D), BF),
                pltpu.VMEM((experts, blocks * SLOT, D), BF),
                pltpu.VMEM((experts, blocks * SLOT, 1), F32),
                pltpu.VMEM((2, EXPERTS, TOK_DEV), F32),
                pltpu.VMEM((2, EXPERTS, TOK_DEV), F32),
                pltpu.SemaphoreType.DMA((2, parts // 2)),
            ],
        ),
        compiler_params=pltpu.CompilerParams(vmem_limit_bytes=VMEM_LIMIT),
        cost_estimate=pl.CostEstimate(
            flops=2 * 2 * blocks * SLOT * experts * D * (6 * width + 2 * TOK_DEV),
            bytes_accessed=2 * 4 * blocks * ROWS * D + 18 * experts * D * width,
            transcendentals=0,
        ),
        name="expert_slice_grads",
    )(pos, *h_parts, *g_parts, w_gate, w_up, w_down)


def shared_slice_kernel(parts, pos_ref, *refs):
    h_parts, g_parts = refs[:parts], refs[parts : 2 * parts]
    wg_ref, wu_ref, wd_ref, og_ref, ou_ref, od_ref = refs[2 * parts : 2 * parts + 6]
    h_buf, g_buf, inner_sc, sems = refs[2 * parts + 6 :]
    half = parts // 2
    per = h_parts[0].shape[0]
    window = pl.ds(pl.multiple_of(pos_ref[0] * 128, 128), og_ref.shape[0])
    lanes = pl.ds(pl.multiple_of(pos_ref[1] * 128, 128), od_ref.shape[0])

    def two(buf, pair, cols=slice(None)):
        return jnp.concatenate([buf[2 * pair + k, :TOK_DEV, cols] for k in range(2)], 0)

    def products(pair, carry):
        rows, grads = two(h_buf, pair), two(g_buf, pair)
        gate_pre = jnp.dot(rows, wg_ref[...], preferred_element_type=F32)
        up_pre = jnp.dot(rows, wu_ref[...], preferred_element_type=F32)
        back = contract(grads, wd_ref[...], 1, 1)
        swish, slope = swish_parts(gate_pre)
        inner_sc[...] = (swish * up_pre).astype(BF)
        dgate_pre = (back * up_pre * slope).astype(BF)
        dup_pre = (back * swish).astype(BF)
        picked = two(h_buf, pair, window)
        og_ref[...] += contract(picked, dgate_pre, 0, 0)
        ou_ref[...] += contract(picked, dup_pre, 0, 0)
        od_ref[...] += contract(inner_sc[:, lanes], grads, 0, 0)
        return carry

    og_ref[...] = jnp.zeros_like(og_ref)
    ou_ref[...] = jnp.zeros_like(ou_ref)
    od_ref[...] = jnp.zeros_like(od_ref)
    start_half(0, h_parts, g_parts, h_buf, g_buf, sems)
    for part in range(2):
        for i in range(half):
            wait_part(part, i, h_parts, g_parts, h_buf, g_buf, sems)
            lax.fori_loop(i * per // 2, (i + 1) * per // 2, products, 0)
        if part == 0:
            start_half(1, h_parts, g_parts, h_buf, g_buf, sems)


def shared_slice_grads(pos, h_parts, g_parts, w_gate, w_up, w_down):
    parts, per = len(h_parts), h_parts[0].shape[0]
    blocks = parts * per // 2
    width = w_gate.shape[1]
    anywhere = pl.BlockSpec(memory_space=pl.ANY)
    whole = lambda *shape: pl.BlockSpec(shape, lambda i, s: (0,) * len(shape))
    return pl.pallas_call(
        functools.partial(shared_slice_kernel, parts),
        out_shape=(
            jax.ShapeDtypeStruct((256, width), F32),
            jax.ShapeDtypeStruct((256, width), F32),
            jax.ShapeDtypeStruct((128, D), F32),
        ),
        grid_spec=pltpu.PrefetchScalarGridSpec(
            num_scalar_prefetch=1,
            grid=(1,),
            in_specs=[anywhere] * (2 * parts)
            + [whole(D, width), whole(D, width), whole(width, D)],
            out_specs=[whole(256, width), whole(256, width), whole(128, D)],
            scratch_shapes=[
                pltpu.VMEM((blocks, ROWS, D), BF),
                pltpu.VMEM((blocks, ROWS, D), BF),
                pltpu.VMEM((2 * TOK_DEV, width), BF),
                pltpu.SemaphoreType.DMA((2, parts // 2)),
            ],
        ),
        compiler_params=pltpu.CompilerParams(vmem_limit_bytes=VMEM_LIMIT),
        cost_estimate=pl.CostEstimate(
            flops=2 * 2 * blocks * TOK_DEV * (3 * D * width + 512 * width + 128 * D),
            bytes_accessed=2 * 4 * blocks * ROWS * D,
            transcendentals=0,
        ),
        name="shared_slice_grads",
    )(pos, *h_parts, *g_parts, w_gate, w_up, w_down)


def pair_sum(kept, received):
    return (kept.astype(F32) + received.astype(F32)).astype(BF)


def halves(value, bit):
    width = value.shape[-1] // 2
    low, high = value[..., :width], value[..., width:]
    return jnp.where(bit == 0, low, high), jnp.where(bit == 0, high, low)


def rejoin(own, other, bit):
    return jnp.where(
        bit == 0, jnp.concatenate([own, other], -1), jnp.concatenate([other, own], -1)
    )


def reduce_dense(first, second, z, y, x, core):
    first, second = first.astype(BF), second.astype(BF)
    kept = jnp.where(core == 0, first, second)
    sent = jnp.where(core == 0, second, first)
    total = pair_sum(kept, over_core(sent))
    bit_a, bit_b = jnp.where(core == 0, x, y), jnp.where(core == 0, y, x)
    kept, sent = halves(total, bit_a)
    total = pair_sum(kept, over_a(sent))
    kept, sent = halves(total, bit_b)
    total = pair_sum(kept, over_b(sent))
    slabs = total.reshape(4, D // 4, -1)
    result = lax.dynamic_index_in_dim(slabs, z, 0, keepdims=False).astype(F32)
    for step in (1, 2, 3):
        out = lax.dynamic_index_in_dim(slabs, lax.rem(z + step, 4), 0, keepdims=False)
        result = result + over_z(out, step).astype(F32)
    result = result.astype(BF)
    result = rejoin(result, over_b(result), bit_b)
    result = rejoin(result, over_a(result), bit_a)
    other = over_core(result)
    return jnp.where(core == 0, result, other), jnp.where(core == 0, other, result)


def tuned_body(
    tokens,
    cotangent,
    routes,
    prompt_ids,
    attn_gain,
    query_weight,
    key_weight,
    value_weight,
    output_weight,
    ffn_gain,
    router_weight,
    shared_gate,
    shared_up,
    shared_down,
    expert_gate,
    expert_up_weight,
    expert_down,
):
    z, y, j = lax.axis_index("dp"), lax.axis_index("context"), lax.axis_index("experts")
    x, core = j // 2, j % 2
    contexts = 2

    expert_ids = jnp.arange(EXPERTS, dtype=jnp.int32)[:, None]
    route_t = routes.T
    member = (route_t[0:1] == expert_ids) | (route_t[1:2] == expert_ids)
    before = (jnp.arange(TOK_DEV)[:, None] < jnp.arange(TOK_DEV)[None, :]).astype(BF)
    ranks = jnp.dot(member.astype(BF), before, preferred_element_type=F32)
    ranks = jnp.where(member, ranks, -1.0).astype(BF)
    g_block = jnp.concatenate([cotangent, jnp.pad(ranks, ((0, 0), (0, D - TOK_DEV)))], 0)

    small = jnp.concatenate(
        [router_weight, attn_gain[:, None], ffn_gain[:, None], jnp.zeros((D // 4, 110), BF)], 1
    )
    w_in = gather_rows(
        jnp.concatenate([query_weight, key_weight, value_weight, small], 1), core
    )
    g_pair = jnp.stack([g_block, over_x(g_block)])
    g_group = jnp.concatenate([g_pair, over_core(g_pair)])
    w_out = gather_rows(output_weight, core)
    w_gateup = gather_rows(jnp.concatenate([shared_gate, shared_up], 1), core)
    w_sgate, w_sup = w_gateup[:, :2048], w_gateup[:, 2048:]
    w_sdown = gather_rows(shared_down, core)
    g_parts = gather_blocks(g_block)

    w_query, w_key, w_value = w_in[:, :D], w_in[:, D : 2 * D], w_in[:, 2 * D : 3 * D]
    w_router = w_in[:, 3 * D : 3 * D + EXPERTS]
    gain1_f = w_in[:, 3 * D + 16].astype(F32)
    gain2_f = w_in[:, 3 * D + 17].astype(F32)

    cos_table, sin_table = rotary_tables(TOK_DEV)
    inputs = tokens.astype(F32)
    inv_rms1 = lax.rsqrt(jnp.mean(inputs * inputs, -1, keepdims=True) + EPS)
    normed1 = inputs * inv_rms1
    hidden1 = (normed1 * gain1_f).astype(BF)
    query_f = jnp.dot(hidden1, w_query, preferred_element_type=F32)
    key_f = jnp.dot(hidden1, w_key, preferred_element_type=F32)
    value_f = jnp.dot(hidden1, w_value, preferred_element_type=F32)
    query_b = rotate(query_f, cos_table, sin_table).astype(BF)
    key_b = rotate(key_f, cos_table, sin_table).astype(BF)
    value_b = value_f.astype(BF)
    prompt_keys, prompt_values = (
        lax.all_gather(key_b[:PROMPT], "context", axis=0, tiled=True),
        lax.all_gather(value_b[:PROMPT], "context", axis=0, tiled=True),
    )
    keys_h = jnp.concatenate([prompt_keys, key_b[PROMPT:]], 0).reshape(-1, HEADS, HD)
    values_h = jnp.concatenate([prompt_values, value_b[PROMPT:]], 0).reshape(-1, HEADS, HD)
    query_h = query_b.reshape(TOK_DEV, HEADS, HD)
    allowed = key_mask(y, prompt_ids, contexts)
    scores = jnp.where(
        allowed[None],
        0.125 * jnp.einsum("qhd,khd->hqk", query_h, keys_h, preferred_element_type=F32),
        -1e30,
    )
    row_max = jnp.max(scores, -1, keepdims=True)
    exp_scores = jnp.exp(scores - row_max)
    row_total = jnp.sum(exp_scores, -1, keepdims=True)
    log_total = row_max + jnp.log(row_total)
    attn_probs = (exp_scores / row_total).astype(BF)
    attended = (
        jnp.einsum("hqk,khd->qhd", attn_probs, values_h, preferred_element_type=F32)
        .reshape(TOK_DEV, D)
        .astype(BF)
    )
    resid = inputs + jnp.dot(attended, w_out, preferred_element_type=F32)
    inv_rms2 = lax.rsqrt(jnp.mean(resid * resid, -1, keepdims=True) + EPS)
    normed2 = resid * inv_rms2
    hidden2 = (normed2 * gain2_f).astype(BF)
    logits_t = contract(w_router, hidden2, 0, 1)
    probs_t = jax.nn.softmax(logits_t, 0)
    probs_high = probs_t.astype(BF)
    probs_low = (probs_t - probs_high.astype(F32)).astype(BF)
    h_block = jnp.concatenate([hidden2, jnp.concatenate([probs_high, probs_low], 1)], 0)

    h_pair = jnp.stack([h_block, over_x(h_block)])
    h_group = jnp.concatenate([h_pair, over_core(h_pair)])
    shared_res, grad_shared_in = shared_rows(hidden2, cotangent, w_sgate, w_sup, w_sdown)
    base = (j * 4).astype(jnp.int32)
    moe_part, dx_part = group_experts(
        base[None], h_group, g_group, expert_gate, expert_up_weight, expert_down
    )
    h_parts = gather_blocks(h_block)

    def home(part):
        pair = pair_sum(part[:2], over_core(part[2:]))
        return pair[0].astype(F32) + over_x(pair[1]).astype(F32)

    dx_home = home(dx_part)
    moe_out = home(moe_part)
    layer_out = (resid + shared_res + moe_out).astype(BF)

    grad_total = cotangent.astype(F32)
    grad_rprobs = dx_home[TOK_DEV:, :TOK_DEV] + dx_home[TOK_DEV:, TOK_DEV:]
    grad_logits_t = (
        probs_t * (grad_rprobs - jnp.sum(probs_t * grad_rprobs, 0, keepdims=True))
    ).astype(BF)
    grad_router_local = contract(hidden2, grad_logits_t, 0, 1)
    grad_hidden2 = (
        dx_home[:TOK_DEV] + grad_shared_in + contract(grad_logits_t, w_router, 0, 1)
    )
    grad_gain2 = jnp.sum(grad_hidden2 * normed2, 0)
    grad_normed2 = grad_hidden2 * gain2_f
    grad_resid = (
        inv_rms2 * (grad_normed2 - normed2 * jnp.mean(grad_normed2 * normed2, -1, keepdims=True))
        + grad_total
    )
    grad_branch = grad_resid.astype(BF)
    grad_wout = inner_rows(attended, grad_branch)
    grad_attended = times_transposed(grad_branch, w_out).astype(BF).reshape(TOK_DEV, HEADS, HD)
    scores_again = jnp.where(
        allowed[None],
        0.125 * jnp.einsum("qhd,khd->hqk", query_h, keys_h, preferred_element_type=F32),
        -1e30,
    )
    probs_f = jnp.exp(scores_again - log_total)
    probs_b = probs_f.astype(BF)
    grad_pattn = jnp.einsum("qhd,khd->hqk", grad_attended, values_h, preferred_element_type=F32)
    grad_scores = (
        probs_f * (grad_pattn - jnp.sum(probs_f * grad_pattn, -1, keepdims=True))
    ).astype(BF)
    grad_query = 0.125 * jnp.einsum(
        "hqk,khd->qhd", grad_scores, keys_h, preferred_element_type=F32
    ).reshape(TOK_DEV, D)
    grad_keys = 0.125 * jnp.einsum(
        "hqk,qhd->khd", grad_scores, query_h, preferred_element_type=F32
    ).reshape(-1, D)
    grad_values = jnp.einsum(
        "hqk,qhd->khd", probs_b, grad_attended, preferred_element_type=F32
    ).reshape(-1, D)
    span = contexts * PROMPT
    grad_pkeys, grad_pvalues = (
        lax.psum_scatter(grad_keys[:span].astype(BF), "context", scatter_dimension=0, tiled=True),
        lax.psum_scatter(
            grad_values[:span].astype(BF), "context", scatter_dimension=0, tiled=True
        ),
    )
    grad_key_all = jnp.concatenate([grad_pkeys.astype(F32), grad_keys[span:]], 0)
    grad_value_all = jnp.concatenate([grad_pvalues.astype(F32), grad_values[span:]], 0)
    grad_qpre = rotate(grad_query, cos_table, -sin_table).astype(BF)
    grad_kpre = rotate(grad_key_all, cos_table, -sin_table).astype(BF)
    grad_vpre = grad_value_all.astype(BF)
    grad_wquery = inner_rows(hidden1, grad_qpre)
    grad_wkey = inner_rows(hidden1, grad_kpre)
    grad_wvalue = inner_rows(hidden1, grad_vpre)
    grad_hidden1 = (
        times_transposed(grad_qpre, w_query)
        + times_transposed(grad_kpre, w_key)
        + times_transposed(grad_vpre, w_value)
    )
    grad_gain1 = jnp.sum(grad_hidden1 * normed1, 0)
    grad_normed1 = grad_hidden1 * gain1_f
    grad_inputs = (
        inv_rms1 * (grad_normed1 - normed1 * jnp.mean(grad_normed1 * normed1, -1, keepdims=True))
        + grad_resid
    )

    sum_qk, sum_vo = reduce_dense(
        jnp.concatenate([grad_wquery, grad_wkey], 1),
        jnp.concatenate([grad_wvalue, grad_wout], 1),
        z,
        y,
        x,
        core,
    )
    sum_qk, sum_vo = sum_qk.astype(F32), sum_vo.astype(F32)
    extras = jnp.concatenate(
        [grad_router_local, grad_gain1[:, None], grad_gain2[:, None], jnp.zeros((D, 110), F32)], 1
    ).astype(BF)
    extras = lax.psum_scatter(extras, "dp", scatter_dimension=0, tiled=True)
    extras = lax.psum(extras, ("context", "experts")).astype(F32)

    plane = y * 4 + j
    columns = lambda w: lax.dynamic_index_in_dim(
        w.reshape(D, 4, 8, 64), plane, 2, keepdims=False
    ).reshape(D, 256)
    down_rows = lax.dynamic_index_in_dim(
        w_sdown.reshape(4, 8, 64, D), plane, 1, keepdims=False
    ).reshape(256, D)

    window = jnp.array([0, 1, 3, 4], jnp.int32)[z]
    s_gate, s_up, s_down = shared_slice_grads(
        jnp.stack([window, (z // 2).astype(jnp.int32)]),
        h_parts,
        g_parts,
        columns(w_sgate),
        columns(w_sup),
        down_rows,
    )
    lead = z * 192 - window * 128
    s_gateup = jnp.concatenate(
        [
            lax.dynamic_slice_in_dim(s_gate, lead, 192, 0),
            lax.dynamic_slice_in_dim(s_up, lead, 192, 0),
        ],
        1,
    ).astype(BF)
    s_down = lax.dynamic_slice_in_dim(s_down, (z % 2) * 64, 64, 0).astype(BF)
    s_gateup = lax.all_gather(s_gateup, ("context", "experts"), axis=0, tiled=False)
    s_down = lax.all_gather(s_down, ("context", "experts"), axis=0, tiled=True).astype(F32)
    s_gateup = s_gateup.reshape(8, 192, 2, 4, 64).transpose(2, 1, 3, 0, 4).reshape(2, 192, 2048)
    s_gateup = s_gateup.astype(F32)

    slice_index = (z * 2 + y).astype(jnp.int32)
    e_gate, e_up, e_down = expert_slice_grads(
        jnp.stack([base, slice_index]),
        h_parts,
        g_parts,
        expert_gate,
        expert_up_weight,
        expert_down,
        256,
    )
    return (
        layer_out,
        grad_inputs,
        extras[:, 16],
        sum_qk[:, :D],
        sum_qk[:, D:],
        sum_vo[:, :D],
        sum_vo[:, D:],
        extras[:, 17],
        extras[:, :16],
        s_gateup[0],
        s_gateup[1],
        s_down,
        e_gate,
        e_up,
        e_down,
    )


def solution(mesh):
    shape = dict(mesh.shape)
    tuned = shape == TUNED_MESH

    return jax.shard_map(
        tuned_body if tuned else plain_body,
        mesh=mesh,
        in_specs=(
            P(("dp", "context", "experts"), None),
            P(("dp", "context", "experts"), None),
            P(("dp", "context", "experts"), None),
            P(("dp", "context", "experts")),
            P("dp"),
            P("dp", None),
            P("dp", None),
            P("dp", None),
            P("dp", None),
            P("dp"),
            P("dp", None),
            P("dp", None),
            P("dp", None),
            P("dp", None),
            P("experts", None, None),
            P("experts", None, None),
            P("experts", None, None),
        ),
        out_specs=(
            P(("dp", "context", "experts"), None),
            P(("dp", "context", "experts"), None),
            P("dp"),
            P("dp", None),
            P("dp", None),
            P("dp", None),
            P("dp", None),
            P("dp"),
            P("dp", None),
            P("dp", None),
            P("dp", None),
            P("dp", None),
            P("experts", None, ("dp", "context")),
            P("experts", None, ("dp", "context")),
            P("experts", ("dp", "context"), None),
        ),
        check_vma=False,
    )
```

```python
import functools

import jax
import jax.numpy as jnp
from jax import lax
from jax.sharding import PartitionSpec as P

from jax.experimental import pallas as pl
from jax.experimental.pallas import tpu as pltpu

D = 768
HEADS = 12
HD = 64
EXPERTS = 16
TOPK = 2
PROMPT = 256
CONT = 2
CLEN = 64
TOK_DEV = 384
CAP = 66


EPS = 1e-06


def rotary_tables(tok_rows):
    row_ids = jnp.arange(tok_rows)
    position = jnp.where(row_ids < PROMPT, row_ids, PROMPT + (row_ids - PROMPT) % CLEN).astype(
        jnp.float32
    )
    frequency = 10000.0 ** (-2.0 * jnp.arange(HD // 2).astype(jnp.float32) / HD)
    angles = position[:, None] * frequency[None, :]
    return (jnp.cos(angles), jnp.sin(angles))


def rotate(values_in, cos_table, sin_table):
    shaped = values_in.reshape(values_in.shape[:-1] + (HEADS, HD))
    lower_half = shaped[..., : HD // 2]
    upper_half = shaped[..., HD // 2 :]
    cos_part = cos_table[:, None, :]
    sin_part = sin_table[:, None, :]
    turned = jnp.concatenate(
        [
            lower_half * cos_part - upper_half * sin_part,
            upper_half * cos_part + lower_half * sin_part,
        ],
        -1,
    )
    return turned.reshape(values_in.shape)


def key_mask(context_index, prompt_pick, contexts):
    row_ids = jnp.arange(TOK_DEV)[:, None]
    col_ids = jnp.arange(contexts * PROMPT + CONT * CLEN)[None, :]
    prompt_row = row_ids < PROMPT
    cont_row = (row_ids - PROMPT) // CLEN
    within_row = (row_ids - PROMPT) % CLEN
    owner = jnp.sum(
        prompt_pick[None, :] * (jnp.arange(CONT)[None, :] == cont_row), -1, keepdims=True
    )
    target = jnp.where(prompt_row, context_index, owner)
    prompt_keys = col_ids < contexts * PROMPT
    prompt_ok = (
        prompt_keys
        & (col_ids // PROMPT == target)
        & (jnp.logical_not(prompt_row) | (col_ids % PROMPT <= row_ids))
    )
    offset = col_ids - contexts * PROMPT
    cont_ok = (
        jnp.logical_not(prompt_keys)
        & jnp.logical_not(prompt_row)
        & (offset // CLEN == cont_row)
        & (offset % CLEN <= within_row)
    )
    return prompt_ok | cont_ok


def inner_rows(left, right):
    return lax.dot_general(
        left, right, (((0,), (0,)), ((), ())), preferred_element_type=jnp.float32
    )


def times_transposed(left, right):
    return lax.dot_general(
        left, right, (((1,), (1,)), ((), ())), preferred_element_type=jnp.float32
    )


def swish_derivative(pre_act):
    sigma = jax.nn.sigmoid(pre_act)
    return sigma * (1.0 + pre_act * (1.0 - sigma))


def plain_body(
    tokens,
    cotangent,
    routes,
    prompt_ids,
    attn_gain,
    query_weight,
    key_weight,
    value_weight,
    output_weight,
    ffn_gain,
    router_weight,
    shared_gate,
    shared_up,
    shared_down,
    expert_gate,
    expert_up_weight,
    expert_down,
):
    contexts = lax.axis_size("context")
    context_here = lax.axis_index("context")
    gain_one, w_query, w_key, w_value, w_out, gain_two, w_router, w_sgate, w_sup, w_sdown = (
        lax.all_gather(attn_gain, "dp", axis=0, tiled=True),
        lax.all_gather(query_weight, "dp", axis=0, tiled=True),
        lax.all_gather(key_weight, "dp", axis=0, tiled=True),
        lax.all_gather(value_weight, "dp", axis=0, tiled=True),
        lax.all_gather(output_weight, "dp", axis=0, tiled=True),
        lax.all_gather(ffn_gain, "dp", axis=0, tiled=True),
        lax.all_gather(router_weight, "dp", axis=0, tiled=True),
        lax.all_gather(shared_gate, "dp", axis=0, tiled=True),
        lax.all_gather(shared_up, "dp", axis=0, tiled=True),
        lax.all_gather(shared_down, "dp", axis=0, tiled=True),
    )
    cos_table, sin_table = rotary_tables(TOK_DEV)
    inputs = tokens.astype(jnp.float32)
    inv_rms1 = lax.rsqrt(jnp.mean(inputs * inputs, -1, keepdims=True) + EPS)
    normed1 = inputs * inv_rms1
    gain1_f = gain_one.astype(jnp.float32)
    hidden1 = (normed1 * gain1_f).astype(jnp.bfloat16)
    query_f = jnp.dot(hidden1, w_query, preferred_element_type=jnp.float32)
    key_f = jnp.dot(hidden1, w_key, preferred_element_type=jnp.float32)
    value_f = jnp.dot(hidden1, w_value, preferred_element_type=jnp.float32)
    query_b = rotate(query_f, cos_table, sin_table).astype(jnp.bfloat16)
    key_b = rotate(key_f, cos_table, sin_table).astype(jnp.bfloat16)
    value_b = value_f.astype(jnp.bfloat16)
    prompt_keys, prompt_values = (
        lax.all_gather(key_b[:PROMPT], "context", axis=0, tiled=True),
        lax.all_gather(value_b[:PROMPT], "context", axis=0, tiled=True),
    )
    keys_h = jnp.concatenate([prompt_keys, key_b[PROMPT:]], 0).reshape(-1, HEADS, HD)
    values_h = jnp.concatenate([prompt_values, value_b[PROMPT:]], 0).reshape(-1, HEADS, HD)
    query_h = query_b.reshape(TOK_DEV, HEADS, HD)
    allowed = key_mask(context_here, prompt_ids, contexts)
    scores = jnp.where(
        allowed[None],
        0.125 * jnp.einsum("qhd,khd->hqk", query_h, keys_h, preferred_element_type=jnp.float32),
        -1e30,
    )
    row_max = jnp.max(scores, -1, keepdims=True)
    exp_scores = jnp.exp(scores - row_max)
    row_total = jnp.sum(exp_scores, -1, keepdims=True)
    log_total = row_max + jnp.log(row_total)
    attn_probs = (exp_scores / row_total).astype(jnp.bfloat16)
    attended = (
        jnp.einsum("hqk,khd->qhd", attn_probs, values_h, preferred_element_type=jnp.float32)
        .reshape(TOK_DEV, D)
        .astype(jnp.bfloat16)
    )
    resid = inputs + jnp.dot(attended, w_out, preferred_element_type=jnp.float32)
    inv_rms2 = lax.rsqrt(jnp.mean(resid * resid, -1, keepdims=True) + EPS)
    normed2 = resid * inv_rms2
    gain2_f = gain_two.astype(jnp.float32)
    hidden2 = (normed2 * gain2_f).astype(jnp.bfloat16)
    logits = jnp.dot(hidden2, w_router, preferred_element_type=jnp.float32)
    route_probs = jax.nn.softmax(logits, -1)
    route_hot = (routes[:, :, None] == jnp.arange(EXPERTS)[None, None, :]).astype(jnp.float32)
    gate_vals = jnp.sum(route_probs[:, None, :] * route_hot, -1)
    shared_gpre = jnp.dot(hidden2, w_sgate, preferred_element_type=jnp.float32)
    shared_upre = jnp.dot(hidden2, w_sup, preferred_element_type=jnp.float32)
    shared_act = (jax.nn.silu(shared_gpre) * shared_upre).astype(jnp.bfloat16)
    shared_res = jnp.dot(shared_act, w_sdown, preferred_element_type=jnp.float32)
    flat_route = routes.reshape(-1)
    flat_hot = (flat_route[:, None] == jnp.arange(EXPERTS)[None, :]).astype(jnp.int32)
    slot_ids = jnp.sum((jnp.cumsum(flat_hot, 0) - flat_hot) * flat_hot, -1)
    slot_index = flat_route * CAP + slot_ids
    send_rows = jnp.repeat(hidden2, TOPK, axis=0)
    outgoing = (
        jnp.zeros((EXPERTS * CAP, D), jnp.bfloat16)
        .at[slot_index]
        .set(send_rows)
        .reshape(EXPERTS, CAP, D)
    )
    received_rows = lax.all_to_all(outgoing, "experts", split_axis=0, concat_axis=1, tiled=True)
    expert_gate_preact = jnp.einsum(
        "mgx,mxp->mgp", received_rows, expert_gate, preferred_element_type=jnp.float32
    )
    expert_up_preact = jnp.einsum(
        "mgx,mxp->mgp", received_rows, expert_up_weight, preferred_element_type=jnp.float32
    )
    expert_activation = (jax.nn.silu(expert_gate_preact) * expert_up_preact).astype(jnp.bfloat16)
    expert_res = jnp.einsum(
        "erf,efd->erd", expert_activation, expert_down, preferred_element_type=jnp.float32
    ).astype(jnp.bfloat16)
    returned = lax.all_to_all(
        expert_res, "experts", split_axis=1, concat_axis=0, tiled=True
    ).reshape(EXPERTS * CAP, D)
    picked = returned[slot_index].astype(jnp.float32).reshape(TOK_DEV, TOPK, D)
    moe_out = jnp.sum(gate_vals[:, :, None] * picked, 1)
    layer_out = (resid + shared_res + moe_out).astype(jnp.bfloat16)
    gain_one, w_query, w_key, w_value, w_out, gain_two, w_router, w_sgate, w_sup, w_sdown = (
        lax.all_gather(attn_gain, "dp", axis=0, tiled=True),
        lax.all_gather(query_weight, "dp", axis=0, tiled=True),
        lax.all_gather(key_weight, "dp", axis=0, tiled=True),
        lax.all_gather(value_weight, "dp", axis=0, tiled=True),
        lax.all_gather(output_weight, "dp", axis=0, tiled=True),
        lax.all_gather(ffn_gain, "dp", axis=0, tiled=True),
        lax.all_gather(router_weight, "dp", axis=0, tiled=True),
        lax.all_gather(shared_gate, "dp", axis=0, tiled=True),
        lax.all_gather(shared_up, "dp", axis=0, tiled=True),
        lax.all_gather(shared_down, "dp", axis=0, tiled=True),
    )
    gain1_f = gain_one.astype(jnp.float32)
    gain2_f = gain_two.astype(jnp.float32)
    grad_total = cotangent.astype(jnp.float32)
    grad_gates = jnp.sum(grad_total[:, None, :] * picked, -1)
    grad_picked = (
        (gate_vals[:, :, None] * grad_total[:, None, :])
        .astype(jnp.bfloat16)
        .reshape(TOK_DEV * TOPK, D)
    )
    grad_back = (
        jnp.zeros((EXPERTS * CAP, D), jnp.bfloat16)
        .at[slot_index]
        .set(grad_picked)
        .reshape(EXPERTS, CAP, D)
    )
    grad_arrived = lax.all_to_all(grad_back, "experts", split_axis=0, concat_axis=1, tiled=True)
    grad_expert_activation = jnp.einsum(
        "erd,efd->erf", grad_arrived, expert_down, preferred_element_type=jnp.float32
    )
    grad_expert_gate_preact = (
        grad_expert_activation * expert_up_preact * swish_derivative(expert_gate_preact)
    ).astype(jnp.bfloat16)
    grad_expert_up_preact = (grad_expert_activation * jax.nn.silu(expert_gate_preact)).astype(
        jnp.bfloat16
    )
    expert_grad_down = jnp.einsum(
        "erf,erd->edf", expert_activation, grad_arrived, preferred_element_type=jnp.float32
    )
    expert_grad_gate = jnp.einsum(
        "xvb,xva->xba", received_rows, grad_expert_gate_preact, preferred_element_type=jnp.float32
    )
    expert_grad_up = jnp.einsum(
        "xvb,xva->xba", received_rows, grad_expert_up_preact, preferred_element_type=jnp.float32
    )
    grad_einputs = jnp.einsum(
        "cgj,clj->cgl", grad_expert_gate_preact, expert_gate, preferred_element_type=jnp.float32
    )
    grad_einputs = (
        grad_einputs
        + jnp.einsum(
            "cgj,clj->cgl",
            grad_expert_up_preact,
            expert_up_weight,
            preferred_element_type=jnp.float32,
        )
    ).astype(jnp.bfloat16)
    grad_returned = lax.all_to_all(
        grad_einputs, "experts", split_axis=1, concat_axis=0, tiled=True
    ).reshape(EXPERTS * CAP, D)
    grad_moe_in = jnp.sum(
        grad_returned[slot_index].astype(jnp.float32).reshape(TOK_DEV, TOPK, D), 1
    )
    grad_rprobs = jnp.sum(grad_gates[:, :, None] * route_hot, 1)
    grad_logits = (
        route_probs * (grad_rprobs - jnp.sum(route_probs * grad_rprobs, -1, keepdims=True))
    ).astype(jnp.bfloat16)
    grad_router_local = inner_rows(hidden2, grad_logits)
    grad_total_b = grad_total.astype(jnp.bfloat16)
    grad_sdown = inner_rows(shared_act, grad_total_b)
    grad_sact = times_transposed(grad_total_b, w_sdown)
    grad_sgpre = (grad_sact * shared_upre * swish_derivative(shared_gpre)).astype(jnp.bfloat16)
    grad_supre = (grad_sact * jax.nn.silu(shared_gpre)).astype(jnp.bfloat16)
    grad_sgate = inner_rows(hidden2, grad_sgpre)
    grad_sup = inner_rows(hidden2, grad_supre)
    grad_hidden2 = (
        grad_moe_in
        + times_transposed(grad_logits, w_router)
        + times_transposed(grad_sgpre, w_sgate)
        + times_transposed(grad_supre, w_sup)
    )
    grad_gain2 = jnp.sum(grad_hidden2 * normed2, 0)
    grad_normed2 = grad_hidden2 * gain2_f
    grad_resid = (
        inv_rms2 * (grad_normed2 - normed2 * jnp.mean(grad_normed2 * normed2, -1, keepdims=True))
        + grad_total
    )
    grad_branch = grad_resid.astype(jnp.bfloat16)
    grad_wout = inner_rows(attended, grad_branch)
    grad_attended = (
        times_transposed(grad_branch, w_out).astype(jnp.bfloat16).reshape(TOK_DEV, HEADS, HD)
    )
    scores_again = jnp.where(
        allowed[None],
        0.125 * jnp.einsum("qhd,khd->hqk", query_h, keys_h, preferred_element_type=jnp.float32),
        -1e30,
    )
    probs_f = jnp.exp(scores_again - log_total)
    probs_b = probs_f.astype(jnp.bfloat16)
    grad_pattn = jnp.einsum(
        "qhd,khd->hqk", grad_attended, values_h, preferred_element_type=jnp.float32
    )
    grad_scores = (
        probs_f * (grad_pattn - jnp.sum(probs_f * grad_pattn, -1, keepdims=True))
    ).astype(jnp.bfloat16)
    grad_query = 0.125 * jnp.einsum(
        "hqk,khd->qhd", grad_scores, keys_h, preferred_element_type=jnp.float32
    ).reshape(TOK_DEV, D)
    grad_keys = 0.125 * jnp.einsum(
        "hqk,qhd->khd", grad_scores, query_h, preferred_element_type=jnp.float32
    ).reshape(-1, D)
    grad_values = jnp.einsum(
        "hqk,qhd->khd", probs_b, grad_attended, preferred_element_type=jnp.float32
    ).reshape(-1, D)
    prompt_span = contexts * PROMPT
    grad_pkeys, grad_pvalues = (
        lax.psum_scatter(
            grad_keys[:prompt_span].astype(jnp.bfloat16), "context", scatter_dimension=0, tiled=True
        ).astype(jnp.float32),
        lax.psum_scatter(
            grad_values[:prompt_span].astype(jnp.bfloat16),
            "context",
            scatter_dimension=0,
            tiled=True,
        ).astype(jnp.float32),
    )
    grad_key_all = jnp.concatenate([grad_pkeys, grad_keys[prompt_span:]], 0)
    grad_value_all = jnp.concatenate([grad_pvalues, grad_values[prompt_span:]], 0)
    grad_qpre = rotate(grad_query, cos_table, -sin_table).astype(jnp.bfloat16)
    grad_kpre = rotate(grad_key_all, cos_table, -sin_table).astype(jnp.bfloat16)
    grad_vpre = grad_value_all.astype(jnp.bfloat16)
    grad_wquery = inner_rows(hidden1, grad_qpre)
    grad_wkey = inner_rows(hidden1, grad_kpre)
    grad_wvalue = inner_rows(hidden1, grad_vpre)
    grad_hidden1 = (
        times_transposed(grad_qpre, w_query)
        + times_transposed(grad_kpre, w_key)
        + times_transposed(grad_vpre, w_value)
    )
    grad_gain1 = jnp.sum(grad_hidden1 * normed1, 0)
    grad_normed1 = grad_hidden1 * gain1_f
    grad_inputs = (
        inv_rms1 * (grad_normed1 - normed1 * jnp.mean(grad_normed1 * normed1, -1, keepdims=True))
        + grad_resid
    )
    shares = (
        lax.psum_scatter(
            grad_gain1.astype(jnp.bfloat16), "dp", scatter_dimension=0, tiled=True
        ).astype(jnp.float32),
        lax.psum_scatter(
            grad_wquery.astype(jnp.bfloat16), "dp", scatter_dimension=0, tiled=True
        ).astype(jnp.float32),
        lax.psum_scatter(
            grad_wkey.astype(jnp.bfloat16), "dp", scatter_dimension=0, tiled=True
        ).astype(jnp.float32),
        lax.psum_scatter(
            grad_wvalue.astype(jnp.bfloat16), "dp", scatter_dimension=0, tiled=True
        ).astype(jnp.float32),
        lax.psum_scatter(
            grad_wout.astype(jnp.bfloat16), "dp", scatter_dimension=0, tiled=True
        ).astype(jnp.float32),
        lax.psum_scatter(
            grad_gain2.astype(jnp.bfloat16), "dp", scatter_dimension=0, tiled=True
        ).astype(jnp.float32),
        lax.psum_scatter(
            grad_router_local.astype(jnp.bfloat16), "dp", scatter_dimension=0, tiled=True
        ).astype(jnp.float32),
        lax.psum_scatter(
            grad_sgate.astype(jnp.bfloat16), "dp", scatter_dimension=0, tiled=True
        ).astype(jnp.float32),
        lax.psum_scatter(
            grad_sup.astype(jnp.bfloat16), "dp", scatter_dimension=0, tiled=True
        ).astype(jnp.float32),
        lax.psum_scatter(
            grad_sdown.astype(jnp.bfloat16), "dp", scatter_dimension=0, tiled=True
        ).astype(jnp.float32),
    )
    totals = (
        lax.psum(shares[0].astype(jnp.bfloat16), ("context", "experts")).astype(jnp.float32),
        lax.psum(shares[1].astype(jnp.bfloat16), ("context", "experts")).astype(jnp.float32),
        lax.psum(shares[2].astype(jnp.bfloat16), ("context", "experts")).astype(jnp.float32),
        lax.psum(shares[3].astype(jnp.bfloat16), ("context", "experts")).astype(jnp.float32),
        lax.psum(shares[4].astype(jnp.bfloat16), ("context", "experts")).astype(jnp.float32),
        lax.psum(shares[5].astype(jnp.bfloat16), ("context", "experts")).astype(jnp.float32),
        lax.psum(shares[6].astype(jnp.bfloat16), ("context", "experts")).astype(jnp.float32),
        lax.psum(shares[7].astype(jnp.bfloat16), ("context", "experts")).astype(jnp.float32),
        lax.psum(shares[8].astype(jnp.bfloat16), ("context", "experts")).astype(jnp.float32),
        lax.psum(shares[9].astype(jnp.bfloat16), ("context", "experts")).astype(jnp.float32),
    )
    summed_gate, summed_up, summed_down = (
        lax.psum_scatter(
            expert_grad_gate.astype(jnp.bfloat16),
            ("dp", "context"),
            scatter_dimension=2,
            tiled=True,
        ).astype(jnp.float32),
        lax.psum_scatter(
            expert_grad_up.astype(jnp.bfloat16), ("dp", "context"), scatter_dimension=2, tiled=True
        ).astype(jnp.float32),
        lax.psum_scatter(
            expert_grad_down.astype(jnp.bfloat16),
            ("dp", "context"),
            scatter_dimension=2,
            tiled=True,
        ).astype(jnp.float32),
    )
    summed_down = jnp.transpose(summed_down, (0, 2, 1))
    return (
        layer_out,
        grad_inputs,
        totals[0],
        totals[1],
        totals[2],
        totals[3],
        totals[4],
        totals[5],
        totals[6],
        totals[7],
        totals[8],
        totals[9],
        summed_gate,
        summed_up,
        summed_down,
    )


TUNED_MESH = {"dp": 4, "context": 2, "experts": 4}
AXES = ("dp", "context", "experts")
SLOT = 72
EXT = 16
ROWS = TOK_DEV + EXT
BF = jnp.bfloat16
F32 = jnp.float32
VMEM_LIMIT = 60 * 1024 * 1024


def moved(value, target):
    pairs = []
    for z in range(4):
        for y in range(2):
            for x in range(2):
                for c in range(2):
                    tz, ty, tx, tc = target(z, y, x, c)
                    pairs.append((((z * 2 + y) * 2 + x) * 2 + c, ((tz * 2 + ty) * 2 + tx) * 2 + tc))
    return lax.ppermute(value, AXES, pairs)


def over_core(value):
    return moved(value, lambda z, y, x, c: (z, y, x, 1 - c))


def over_x(value):
    return moved(value, lambda z, y, x, c: (z, y, 1 - x, c))


def over_a(value):
    return moved(value, lambda z, y, x, c: (z, y, 1 - x, c) if c == 0 else (z, 1 - y, x, c))


def over_b(value):
    return moved(value, lambda z, y, x, c: (z, 1 - y, x, c) if c == 0 else (z, y, 1 - x, c))


def over_z(value, step):
    return moved(value, lambda z, y, x, c: ((z + step) % 4, y, x, c))


def contract(left, right, left_dim, right_dim):
    return lax.dot_general(
        left, right, (((left_dim,), (right_dim,)), ((), ())), preferred_element_type=F32
    )


def one_hot_rows(rank_row):
    slots = lax.broadcasted_iota(jnp.int32, (SLOT, TOK_DEV), 0).astype(F32)
    return (slots == rank_row).astype(F32)


def swish_parts(pre_act):
    sigma = jax.nn.sigmoid(pre_act)
    return pre_act * sigma, sigma * (1.0 + pre_act * (1.0 - sigma))


def group_kernel(
    blocks,
    base_ref,
    *refs,
):
    h_refs, g_refs = refs[:blocks], refs[blocks : 2 * blocks]
    wg_ref, wu_ref, wd_ref, moe_ref, moe_far_ref, dx_ref, dx_far_ref = refs[2 * blocks : 2 * blocks + 7]
    (
        rank_sc,
        prob_sc,
        x_sc,
        gd_sc,
        gate_sc,
        y_sc,
        acc_sc,
        dgate_sc,
        ysel_sc,
        dsel_sc,
        drp_sc,
    ) = refs[2 * blocks + 7 :]
    e = pl.program_id(0)
    f = pl.program_id(1)
    experts = pl.num_programs(0)
    base = base_ref[0]

    @pl.when((e == 0) & (f == 0))
    def _():
        for b in range(blocks):
            rank_sc[b] = g_refs[b][TOK_DEV:, :TOK_DEV].astype(F32)
            prob_sc[b] = h_refs[b][TOK_DEV:, :TOK_DEV].astype(F32) + h_refs[b][
                TOK_DEV:, TOK_DEV:
            ].astype(F32)
        drp_sc[...] = jnp.zeros_like(drp_sc)

    @pl.when(f == 0)
    def _():
        for pair in range(blocks // 2):
            rows_x, rows_g = [], []
            for b in (2 * pair, 2 * pair + 1):
                hot = one_hot_rows(rank_sc[b, pl.ds(base + e, 1), :])
                gate_sc[b * SLOT : (b + 1) * SLOT, :] = jnp.sum(
                    hot * prob_sc[b, pl.ds(base + e, 1), :], -1, keepdims=True
                )
                hot = hot.astype(BF)
                rows_x.append(jnp.dot(hot, h_refs[b][:TOK_DEV, :], preferred_element_type=F32))
                rows_g.append(jnp.dot(hot, g_refs[b][:TOK_DEV, :], preferred_element_type=F32))
            span = slice(pair * 2 * SLOT, (pair + 1) * 2 * SLOT)
            x_sc[span, :] = jnp.concatenate(rows_x, 0).astype(BF)
            gd_sc[span, :] = jnp.concatenate(rows_g, 0).astype(BF)
        y_sc[...] = jnp.zeros_like(y_sc)
        acc_sc[...] = jnp.zeros_like(acc_sc)
        dgate_sc[...] = jnp.zeros_like(dgate_sc)

    rows = x_sc[...]
    gate_pre = jnp.dot(rows, wg_ref[0], preferred_element_type=F32)
    up_pre = jnp.dot(rows, wu_ref[0], preferred_element_type=F32)
    back = contract(gd_sc[...], wd_ref[0], 1, 1)
    swish, slope = swish_parts(gate_pre)
    inner = (swish * up_pre).astype(BF)
    dgate_sc[...] += jnp.sum(back * inner.astype(F32), -1, keepdims=True)
    back = back * gate_sc[...]
    dgate_pre = (back * up_pre * slope).astype(BF)
    dup_pre = (back * swish).astype(BF)
    y_sc[...] += jnp.dot(inner, wd_ref[0], preferred_element_type=F32)
    acc_sc[...] += contract(dgate_pre, wg_ref[0], 1, 1) + contract(dup_pre, wu_ref[0], 1, 1)

    @pl.when(f == pl.num_programs(1) - 1)
    def _():
        for b in range(blocks):
            span = slice(b * SLOT, (b + 1) * SLOT)
            into = pl.ds(pl.multiple_of(e * SLOT, 8), SLOT)
            ysel_sc[b, into, :] = y_sc[span, :] * gate_sc[span, :]
            dsel_sc[b, into, :] = acc_sc[span, :]
            hot = one_hot_rows(rank_sc[b, pl.ds(base + e, 1), :])
            drp_sc[b, pl.ds(base + e, 1), :] = jnp.sum(hot * dgate_sc[span, :], 0, keepdims=True)

    @pl.when((f == pl.num_programs(1) - 1) & (e == experts - 1))
    def _():
        for b in range(blocks):
            moe_out, dx_out, at = (
                (moe_ref, dx_ref, b) if b < blocks // 2 else (moe_far_ref, dx_far_ref, b - blocks // 2)
            )
            hot = jnp.concatenate(
                [
                    one_hot_rows(rank_sc[b, pl.ds(base + i, 1), :])
                    for i in range(ysel_sc.shape[1] // SLOT)
                ],
                0,
            ).astype(BF)
            moe_out[at] = contract(hot, ysel_sc[b].astype(BF), 0, 0).astype(BF)
            dx_out[at, :TOK_DEV, :] = contract(hot, dsel_sc[b].astype(BF), 0, 0).astype(BF)
            high = drp_sc[b].astype(BF)
            dx_out[at, TOK_DEV:, :TOK_DEV] = high
            dx_out[at, TOK_DEV:, TOK_DEV:] = (drp_sc[b] - high.astype(F32)).astype(BF)


def group_experts(base, h_group, g_group, w_gate, w_up, w_down):
    blocks = len(h_group)
    experts, _, ff = w_gate.shape
    tile = 512
    whole = lambda *shape: pl.BlockSpec(shape, lambda e, f, s: (0,) * len(shape))
    moe_shape, dx_shape = (blocks // 2, TOK_DEV, D), (blocks // 2, ROWS, D)
    return pl.pallas_call(
        functools.partial(group_kernel, blocks),
        out_shape=tuple(
            jax.ShapeDtypeStruct(s, BF) for s in (moe_shape, moe_shape, dx_shape, dx_shape)
        ),
        grid_spec=pltpu.PrefetchScalarGridSpec(
            num_scalar_prefetch=1,
            grid=(experts, ff // tile),
            in_specs=[whole(ROWS, D)] * (2 * blocks)
            + [
                pl.BlockSpec((1, D, tile), lambda e, f, s: (e, 0, f)),
                pl.BlockSpec((1, D, tile), lambda e, f, s: (e, 0, f)),
                pl.BlockSpec((1, tile, D), lambda e, f, s: (e, f, 0)),
            ],
            out_specs=[whole(*moe_shape)] * 2 + [whole(*dx_shape)] * 2,
            scratch_shapes=[
                pltpu.VMEM((blocks, EXPERTS, TOK_DEV), F32),
                pltpu.VMEM((blocks, EXPERTS, TOK_DEV), F32),
                pltpu.VMEM((blocks * SLOT, D), BF),
                pltpu.VMEM((blocks * SLOT, D), BF),
                pltpu.VMEM((blocks * SLOT, 1), F32),
                pltpu.VMEM((blocks * SLOT, D), F32),
                pltpu.VMEM((blocks * SLOT, D), F32),
                pltpu.VMEM((blocks * SLOT, 1), F32),
                pltpu.VMEM((blocks, experts * SLOT, D), F32),
                pltpu.VMEM((blocks, experts * SLOT, D), F32),
                pltpu.VMEM((blocks, EXPERTS, TOK_DEV), F32),
            ],
        ),
        compiler_params=pltpu.CompilerParams(vmem_limit_bytes=VMEM_LIMIT),
        cost_estimate=pl.CostEstimate(
            flops=2 * 6 * experts * blocks * SLOT * D * ff,
            bytes_accessed=2 * 3 * experts * D * ff,
            transcendentals=0,
        ),
        name="group_experts",
    )(base, *h_group, *g_group, w_gate, w_up, w_down)


def shared_kernel(parts, h_ref, g_ref, *refs):
    bufs = refs[:parts]
    out_ref, dh_ref, gu_sc, down_sc, sems = refs[parts:]
    copies = []
    for k, buf in enumerate(bufs):
        mine = [pltpu.make_async_copy(buf.at[:, :, :512], gu_sc.at[k], sems.at[k, 3])]
        for i in range(3):
            mine.append(
                pltpu.make_async_copy(
                    buf.at[:, 64 * i : 64 * (i + 1), 512:],
                    down_sc.at[k, :, :, 256 * i : 256 * (i + 1)],
                    sems.at[k, i],
                )
            )
        copies.append(mine)
        for one in mine:
            one.start()
    for k in range(parts):
        for one in copies[k]:
            one.wait()
        gate_up = gu_sc[k].reshape(D, 512)
        w_gate, w_up, w_down = gate_up[:, :256], gate_up[:, 256:], down_sc[k].reshape(256, D)
        gate_pre = jnp.dot(h_ref[:TOK_DEV, :], w_gate, preferred_element_type=F32)
        up_pre = jnp.dot(h_ref[:TOK_DEV, :], w_up, preferred_element_type=F32)
        back = contract(g_ref[...], w_down, 1, 1)
        swish, slope = swish_parts(gate_pre)
        inner = (swish * up_pre).astype(BF)
        out = jnp.dot(inner, w_down, preferred_element_type=F32)
        dgate_pre = (back * up_pre * slope).astype(BF)
        dup_pre = (back * swish).astype(BF)
        dh = contract(dgate_pre, w_gate, 1, 1) + contract(dup_pre, w_up, 1, 1)
        if k == 0:
            out_ref[...] = out
            dh_ref[...] = dh
        else:
            out_ref[...] += out
            dh_ref[...] += dh


def shared_rows(h_block, grad, bufs):
    parts = len(bufs)
    rows = jax.ShapeDtypeStruct((TOK_DEV, D), F32)
    vmem = pl.BlockSpec(memory_space=pltpu.VMEM)
    return pl.pallas_call(
        functools.partial(shared_kernel, parts),
        out_shape=(rows, rows),
        in_specs=[vmem, vmem] + [pl.BlockSpec(memory_space=pl.ANY)] * parts,
        out_specs=(vmem, vmem),
        scratch_shapes=[
            pltpu.VMEM((parts, 4, D // 4, 512), BF),
            pltpu.VMEM((parts, 4, 64, D), BF),
            pltpu.SemaphoreType.DMA((parts, 4)),
        ],
        compiler_params=pltpu.CompilerParams(vmem_limit_bytes=VMEM_LIMIT),
        cost_estimate=pl.CostEstimate(
            flops=2 * 6 * TOK_DEV * D * 2048, bytes_accessed=6 * D * 2048, transcendentals=0
        ),
        name="shared_rows",
    )(h_block, grad, *bufs)


def start_half(part, h_parts, g_parts, h_buf, g_buf, sems):
    half = len(h_parts) // 2
    for i in range(half):
        per = h_parts[i].shape[0]
        for which, (parts, buf) in enumerate(((h_parts, h_buf), (g_parts, g_buf))):
            pltpu.make_async_copy(
                parts[part * half + i], buf.at[pl.ds(i * per, per)], sems.at[which, i]
            ).start()


def wait_part(part, i, h_parts, g_parts, h_buf, g_buf, sems):
    half = len(h_parts) // 2
    per = h_parts[i].shape[0]
    for which, (parts, buf) in enumerate(((h_parts, h_buf), (g_parts, g_buf))):
        pltpu.make_async_copy(
            parts[part * half + i], buf.at[pl.ds(i * per, per)], sems.at[which, i]
        ).wait()


def expert_slice_kernel(parts, pos_ref, *refs):
    h_parts, g_parts = refs[:parts], refs[parts : 2 * parts]
    wg_ref, wu_ref, wd_ref, og_ref, ou_ref, od_ref = refs[2 * parts : 2 * parts + 6]
    h_buf, g_buf, x_sc, gd_sc, gate_sc, rank_sc, prob_sc, sems = refs[2 * parts + 6 :]
    base = pos_ref[0]
    experts = wg_ref.shape[0]
    half = parts // 2
    per = h_parts[0].shape[0]

    def dispatch(pair, carry):
        both_x, both_g, both_gate = [], [], []
        for k in range(2):
            b = 2 * pair + k
            rank_sc[k] = g_buf[b, TOK_DEV:, :TOK_DEV].astype(F32)
            prob_sc[k] = h_buf[b, TOK_DEV:, :TOK_DEV].astype(F32) + h_buf[
                b, TOK_DEV:, TOK_DEV:
            ].astype(F32)
            hots, gates = [], []
            for i in range(experts):
                hot = one_hot_rows(rank_sc[k, pl.ds(base + i, 1), :])
                gates.append(
                    jnp.sum(hot * prob_sc[k, pl.ds(base + i, 1), :], -1, keepdims=True)
                )
                hots.append(hot)
            hot = jnp.concatenate(hots, 0).astype(BF)
            both_x.append(jnp.dot(hot, h_buf[b, :TOK_DEV, :], preferred_element_type=F32))
            both_g.append(jnp.dot(hot, g_buf[b, :TOK_DEV, :], preferred_element_type=F32))
            both_gate.append(gates)
        into = pl.ds(pl.multiple_of(pair * 2 * SLOT, 2 * SLOT), 2 * SLOT)
        for i in range(experts):
            span = slice(i * SLOT, (i + 1) * SLOT)
            x_sc[i, into, :] = jnp.concatenate([v[span] for v in both_x], 0).astype(BF)
            gd_sc[i, into, :] = jnp.concatenate([v[span] for v in both_g], 0).astype(BF)
            gate_sc[i, into, :] = jnp.concatenate([v[i] for v in both_gate], 0)
        return carry

    start_half(0, h_parts, g_parts, h_buf, g_buf, sems)
    for part in range(2):
        for i in range(half):
            wait_part(part, i, h_parts, g_parts, h_buf, g_buf, sems)
            lax.fori_loop(i * per // 2, (i + 1) * per // 2, dispatch, 0)
        if part == 0:
            start_half(1, h_parts, g_parts, h_buf, g_buf, sems)

        def products(i, carry, part=part):
            rows = x_sc[i]
            gate_pre = jnp.dot(rows, wg_ref[i], preferred_element_type=F32)
            up_pre = jnp.dot(rows, wu_ref[i], preferred_element_type=F32)
            back = contract(gd_sc[i], wd_ref[i], 1, 1) * gate_sc[i]
            swish, slope = swish_parts(gate_pre)
            inner = (swish * up_pre * gate_sc[i]).astype(BF)
            dgate_pre = (back * up_pre * slope).astype(BF)
            dup_pre = (back * swish).astype(BF)
            add_g = contract(rows, dgate_pre, 0, 0)
            add_u = contract(rows, dup_pre, 0, 0)
            add_d = contract(inner, gd_sc[i], 0, 0)
            if part == 0:
                og_ref[i], ou_ref[i], od_ref[i] = add_g, add_u, add_d
            else:
                og_ref[i] += add_g
                ou_ref[i] += add_u
                od_ref[i] += add_d
            return carry

        lax.fori_loop(0, experts, products, 0)


def expert_slice_grads(pos, h_parts, g_parts, w_gate, w_up, w_down, width):
    parts, per = len(h_parts), h_parts[0].shape[0]
    experts = w_gate.shape[0]
    blocks = parts * per // 2
    anywhere = pl.BlockSpec(memory_space=pl.ANY)
    return pl.pallas_call(
        functools.partial(expert_slice_kernel, parts),
        out_shape=(
            jax.ShapeDtypeStruct((experts, D, width), F32),
            jax.ShapeDtypeStruct((experts, D, width), F32),
            jax.ShapeDtypeStruct((experts, width, D), F32),
        ),
        grid_spec=pltpu.PrefetchScalarGridSpec(
            num_scalar_prefetch=1,
            grid=(1,),
            in_specs=[anywhere] * (2 * parts)
            + [
                pl.BlockSpec((experts, D, width), lambda i, s: (0, 0, s[1])),
                pl.BlockSpec((experts, D, width), lambda i, s: (0, 0, s[1])),
                pl.BlockSpec((experts, width, D), lambda i, s: (0, s[1], 0)),
            ],
            out_specs=[
                pl.BlockSpec((experts, D, width), lambda i, s: (0, 0, 0)),
                pl.BlockSpec((experts, D, width), lambda i, s: (0, 0, 0)),
                pl.BlockSpec((experts, width, D), lambda i, s: (0, 0, 0)),
            ],
            scratch_shapes=[
                pltpu.VMEM((blocks, ROWS, D), BF),
                pltpu.VMEM((blocks, ROWS, D), BF),
                pltpu.VMEM((experts, blocks * SLOT, D), BF),
                pltpu.VMEM((experts, blocks * SLOT, D), BF),
                pltpu.VMEM((experts, blocks * SLOT, 1), F32),
                pltpu.VMEM((2, EXPERTS, TOK_DEV), F32),
                pltpu.VMEM((2, EXPERTS, TOK_DEV), F32),
                pltpu.SemaphoreType.DMA((2, parts // 2)),
            ],
        ),
        compiler_params=pltpu.CompilerParams(vmem_limit_bytes=VMEM_LIMIT),
        cost_estimate=pl.CostEstimate(
            flops=2 * 2 * blocks * SLOT * experts * D * (6 * width + 2 * TOK_DEV),
            bytes_accessed=2 * 4 * blocks * ROWS * D + 18 * experts * D * width,
            transcendentals=0,
        ),
        name="expert_slice_grads",
    )(pos, *h_parts, *g_parts, w_gate, w_up, w_down)


def shared_slice_kernel(parts, pos_ref, *refs):
    h_parts, g_parts = refs[:parts], refs[parts : 2 * parts]
    w_ref, og_ref, ou_ref, od_ref = refs[2 * parts : 2 * parts + 4]
    h_buf, g_buf, inner_sc, wg_ref, wu_ref, wd_ref, sems = refs[2 * parts + 4 :]
    wg_ref[...] = w_ref[:, :, :256].reshape(D, 256)
    wu_ref[...] = w_ref[:, :, 256:512].reshape(D, 256)
    for i in range(3):
        wd_ref[:, 256 * i : 256 * (i + 1)] = w_ref[:, 64 * i : 64 * (i + 1), 512:].reshape(256, 256)
    half = parts // 2
    per = h_parts[0].shape[0]
    window = pl.ds(pl.multiple_of(pos_ref[0] * 128, 128), og_ref.shape[0])
    lanes = pl.ds(pl.multiple_of(pos_ref[1] * 128, 128), od_ref.shape[0])

    def two(buf, pair, cols=slice(None)):
        return jnp.concatenate([buf[2 * pair + k, :TOK_DEV, cols] for k in range(2)], 0)

    def products(pair, carry):
        rows, grads = two(h_buf, pair), two(g_buf, pair)
        gate_pre = jnp.dot(rows, wg_ref[...], preferred_element_type=F32)
        up_pre = jnp.dot(rows, wu_ref[...], preferred_element_type=F32)
        back = contract(grads, wd_ref[...], 1, 1)
        swish, slope = swish_parts(gate_pre)
        inner_sc[...] = (swish * up_pre).astype(BF)
        dgate_pre = (back * up_pre * slope).astype(BF)
        dup_pre = (back * swish).astype(BF)
        picked = two(h_buf, pair, window)
        og_ref[...] += contract(picked, dgate_pre, 0, 0)
        ou_ref[...] += contract(picked, dup_pre, 0, 0)
        od_ref[...] += contract(inner_sc[:, lanes], grads, 0, 0)
        return carry

    og_ref[...] = jnp.zeros_like(og_ref)
    ou_ref[...] = jnp.zeros_like(ou_ref)
    od_ref[...] = jnp.zeros_like(od_ref)
    start_half(0, h_parts, g_parts, h_buf, g_buf, sems)
    for part in range(2):
        for i in range(half):
            wait_part(part, i, h_parts, g_parts, h_buf, g_buf, sems)
            lax.fori_loop(i * per // 2, (i + 1) * per // 2, products, 0)
        if part == 0:
            start_half(1, h_parts, g_parts, h_buf, g_buf, sems)


def shared_slice_grads(pos, h_parts, g_parts, weights):
    parts, per = len(h_parts), h_parts[0].shape[0]
    blocks = parts * per // 2
    width = 256
    anywhere = pl.BlockSpec(memory_space=pl.ANY)
    whole = lambda *shape: pl.BlockSpec(shape, lambda i, s: (0,) * len(shape))
    return pl.pallas_call(
        functools.partial(shared_slice_kernel, parts),
        out_shape=(
            jax.ShapeDtypeStruct((256, width), F32),
            jax.ShapeDtypeStruct((256, width), F32),
            jax.ShapeDtypeStruct((128, D), F32),
        ),
        grid_spec=pltpu.PrefetchScalarGridSpec(
            num_scalar_prefetch=1,
            grid=(1,),
            in_specs=[anywhere] * (2 * parts)
            + [whole(4, D // 4, D)],
            out_specs=[whole(256, width), whole(256, width), whole(128, D)],
            scratch_shapes=[
                pltpu.VMEM((blocks, ROWS, D), BF),
                pltpu.VMEM((blocks, ROWS, D), BF),
                pltpu.VMEM((2 * TOK_DEV, width), BF),
                pltpu.VMEM((D, width), BF),
                pltpu.VMEM((D, width), BF),
                pltpu.VMEM((width, D), BF),
                pltpu.SemaphoreType.DMA((2, parts // 2)),
            ],
        ),
        compiler_params=pltpu.CompilerParams(vmem_limit_bytes=VMEM_LIMIT),
        cost_estimate=pl.CostEstimate(
            flops=2 * 2 * blocks * TOK_DEV * (3 * D * width + 512 * width + 128 * D),
            bytes_accessed=2 * 4 * blocks * ROWS * D,
            transcendentals=0,
        ),
        name="shared_slice_grads",
    )(pos, *h_parts, *g_parts, weights)


def pair_sum(kept, received):
    return (kept.astype(F32) + received.astype(F32)).astype(BF)


def halves(value, bit):
    width = value.shape[-1] // 2
    low, high = value[..., :width], value[..., width:]
    return jnp.where(bit == 0, low, high), jnp.where(bit == 0, high, low)


def rejoin(own, other, bit):
    return jnp.where(
        bit == 0, jnp.concatenate([own, other], -1), jnp.concatenate([other, own], -1)
    )


def lane_halves():
    lane = lax.broadcasted_iota(jnp.int32, (1, 128), 1)
    return [(lane < 64).astype(F32).astype(BF), (lane >= 64).astype(F32).astype(BF)]


def pick_lanes(first, second):
    lane = lax.broadcasted_iota(jnp.int32, first.shape, 1)
    return jnp.where(lane < 64, first, second)


def turned(value, cos, sin):
    lane = lax.broadcasted_iota(jnp.int32, value.shape, 1)
    partner = jnp.where(lane % 64 < 32, pltpu.roll(value, 96, 1), pltpu.roll(value, 32, 1))
    return value * cos + partner * sin


def causal_mask(rows):
    row = lax.broadcasted_iota(jnp.int32, (rows, rows), 0)
    col = lax.broadcasted_iota(jnp.int32, (rows, rows), 1)
    return row, col


def unit_rms(value):
    return lax.rsqrt(jnp.mean(value * value, -1, keepdims=True) + EPS)


def softmax_of(first, second=None):
    top = jnp.max(first, -1, keepdims=True)
    if second is not None:
        top = jnp.maximum(top, jnp.max(second, -1, keepdims=True))
    first = jnp.exp(first - top)
    total = jnp.sum(first, -1, keepdims=True)
    if second is None:
        return first * (1.0 / total)
    second = jnp.exp(second - top)
    scale = 1.0 / (total + jnp.sum(second, -1, keepdims=True))
    return first * scale, second * scale


def attention_kernel(place_ref, *refs):
    w_parts = refs[:8]
    (
        own_ref,
        far_ref,
        gain1_ref,
        gain2_ref,
        router_ref,
        cos_ref,
        sin_ref,
        w_ref,
        q_ref,
        k_ref,
        v_ref,
        h1_ref,
        o_ref,
        x1_ref,
        h2_ref,
        h_sc,
        sems,
    ) = refs[8:]
    copies = []
    for part in range(8):
        for slot in range(4):
            rows = pl.ds(pl.multiple_of(place_ref[8 + slot] * 192, 192), 192)
            copies.append(
                pltpu.make_async_copy(
                    w_parts[part].at[slot, :192, :],
                    w_ref.at[place_ref[part], rows, :],
                    sems.at[part, slot],
                )
            )
    for one in copies:
        one.start()
    inputs = own_ref[:TOK_DEV, :].astype(F32)
    h_sc[:TOK_DEV, :] = (inputs * unit_rms(inputs) * gain1_ref[...]).astype(BF)
    far = far_ref[:TOK_DEV, :].astype(F32)
    h_sc[TOK_DEV:, :] = (far * unit_rms(far) * gain1_ref[...]).astype(BF)
    h1_ref[...] = h_sc[:TOK_DEV, :]
    for one in copies:
        one.wait()
    for i in range(6):
        out_ref = (q_ref, k_ref, v_ref)[i // 2]
        product = jnp.dot(h_sc[...], w_ref[i], preferred_element_type=F32)
        for slab in range(3):
            at = (i % 2) * 384 + slab * 128
            for half in range(2):
                rows = slice(half * TOK_DEV, (half + 1) * TOK_DEV)
                value = product[rows, slab * 128 : (slab + 1) * 128]
                if i < 4:
                    value = turned(value, cos_ref[...], sin_ref[...])
                out_ref[rows, at : at + 128] = value.astype(BF)
    masks = lane_halves()
    row, col = causal_mask(PROMPT)
    prompt_ok = col <= row
    row, col = causal_mask(CONT * CLEN)
    cont_ok = (row // CLEN == col // CLEN) & (col <= row)
    row = lax.broadcasted_iota(jnp.int32, (CONT * CLEN, 1), 0)
    reads_far = jnp.where(row < CLEN, place_ref[12], place_ref[13]).astype(F32)
    own_c = slice(PROMPT, TOK_DEV)
    far_p = slice(TOK_DEV, TOK_DEV + PROMPT)

    def heads(pair, carry):
        cols = pl.ds(pl.multiple_of(pair * 128, 128), 128)
        q_p, k_p, v_p = q_ref[:PROMPT, cols], k_ref[:PROMPT, cols], v_ref[:PROMPT, cols]
        q_c, k_c, v_c = q_ref[own_c, cols], k_ref[own_c, cols], v_ref[own_c, cols]
        k_f, v_f = k_ref[far_p, cols], v_ref[far_p, cols]
        out_p, out_c = [], []
        for mask in masks:
            score = jnp.where(prompt_ok, 0.125 * contract(q_p * mask, k_p, 1, 1), -1e30)
            out_p.append(
                jnp.dot(softmax_of(score).astype(BF), v_p, preferred_element_type=F32)
            )
            query = q_c * mask
            near, far = contract(query, k_p, 1, 1), contract(query, k_f, 1, 1)
            first = 0.125 * jnp.where(reads_far > 0.5, far, near)
            second = jnp.where(cont_ok, 0.125 * contract(query, k_c, 1, 1), -1e30)
            first, second = softmax_of(first, second)
            out_c.append(
                jnp.dot((first * (1.0 - reads_far)).astype(BF), v_p, preferred_element_type=F32)
                + jnp.dot((first * reads_far).astype(BF), v_f, preferred_element_type=F32)
                + jnp.dot(second.astype(BF), v_c, preferred_element_type=F32)
            )
        o_ref[:PROMPT, cols] = pick_lanes(*out_p).astype(BF)
        o_ref[own_c, cols] = pick_lanes(*out_c).astype(BF)
        return carry

    lax.fori_loop(0, HEADS // 2, heads, 0)
    for i in range(2):
        cols = slice(384 * i, 384 * (i + 1))
        x1_ref[:, cols] = own_ref[:TOK_DEV, cols].astype(F32) + jnp.dot(
            o_ref[...], w_ref[6 + i], preferred_element_type=F32
        )
    resid = x1_ref[...]
    hidden = (resid * unit_rms(resid) * gain2_ref[...]).astype(BF)
    h2_ref[:TOK_DEV, :] = hidden
    logits = contract(router_ref[...], hidden, 1, 1)
    logits = jnp.exp(logits - jnp.max(logits, 0, keepdims=True))
    probs = logits / jnp.sum(logits, 0, keepdims=True)
    high = probs.astype(BF)
    h2_ref[TOK_DEV:, :TOK_DEV] = high
    h2_ref[TOK_DEV:, TOK_DEV:] = (probs - high.astype(F32)).astype(BF)


def attention_forward(place, w_parts, own, far, gain1, gain2, router_t, cos, sin):
    vmem = pl.BlockSpec(memory_space=pltpu.VMEM)
    shape = jax.ShapeDtypeStruct
    return pl.pallas_call(
        attention_kernel,
        out_shape=(
            shape((8, D, 384), BF),
            shape((2 * TOK_DEV, D), BF),
            shape((2 * TOK_DEV, D), BF),
            shape((2 * TOK_DEV, D), BF),
            shape((TOK_DEV, D), BF),
            shape((TOK_DEV, D), BF),
            shape((TOK_DEV, D), F32),
            shape((ROWS, D), BF),
        ),
        in_specs=[pl.BlockSpec(memory_space=pltpu.SMEM)]
        + [pl.BlockSpec(memory_space=pl.ANY)] * 8
        + [vmem] * 7,
        out_specs=(vmem,) * 8,
        scratch_shapes=[
            pltpu.VMEM((2 * TOK_DEV, D), BF),
            pltpu.SemaphoreType.DMA((8, 4)),
        ],
        compiler_params=pltpu.CompilerParams(vmem_limit_bytes=VMEM_LIMIT),
        cost_estimate=pl.CostEstimate(
            flops=2 * 2 * TOK_DEV * D * 4 * D, bytes_accessed=8 * 2 * D * D, transcendentals=0
        ),
        name="attention_forward",
    )(place, *w_parts, own, far, gain1, gain2, router_t, cos, sin)


def branch_kernel(
    dx_a_ref,
    dx_b_ref,
    dsh_ref,
    h2_ref,
    x1_ref,
    g_ref,
    gain2_ref,
    router_ref,
    o_ref,
    w_ref,
    dx1_ref,
    do_ref,
    do_c_ref,
    gwo_ref,
    grouter_ref,
    ggain_ref,
):
    tail = dx_a_ref[TOK_DEV:, :].astype(F32) + dx_b_ref[TOK_DEV:, :].astype(F32)
    drp = tail[:, :TOK_DEV] + tail[:, TOK_DEV:]
    probs = h2_ref[TOK_DEV:, :TOK_DEV].astype(F32) + h2_ref[TOK_DEV:, TOK_DEV:].astype(F32)
    dlogits = (probs * (drp - jnp.sum(probs * drp, 0, keepdims=True))).astype(BF)
    hidden = h2_ref[:TOK_DEV, :]
    grouter_ref[...] = jnp.dot(dlogits, hidden, preferred_element_type=F32)
    dh2 = (
        dx_a_ref[:TOK_DEV, :].astype(F32)
        + dx_b_ref[:TOK_DEV, :].astype(F32)
        + dsh_ref[...]
        + contract(dlogits, router_ref[...], 0, 0)
    )
    resid = x1_ref[...]
    scale = unit_rms(resid)
    normed = resid * scale
    ggain_ref[...] = jnp.sum(dh2 * normed, 0, keepdims=True)
    dnormed = dh2 * gain2_ref[...]
    dx1 = scale * (dnormed - normed * jnp.mean(dnormed * normed, -1, keepdims=True)) + g_ref[
        ...
    ].astype(F32)
    dx1_ref[...] = dx1
    datt = dx1.astype(BF)
    do_ref[...] = (
        contract(datt[:, :384], w_ref[0], 1, 1) + contract(datt[:, 384:], w_ref[1], 1, 1)
    ).astype(BF)
    do_c_ref[...] = do_ref[PROMPT:, :]
    gwo_ref[...] = contract(o_ref[...], datt, 0, 0).astype(BF)


def branch_backward(dx_a, dx_b, dsh, h_block, x1, grad, gain2, router_t, o, w_all):
    shape = jax.ShapeDtypeStruct
    whole = lambda *dims: pl.BlockSpec(dims, lambda i: (0,) * len(dims))
    rows = whole(TOK_DEV, D)
    return pl.pallas_call(
        branch_kernel,
        grid=(1,),
        out_shape=(
            shape((TOK_DEV, D), F32),
            shape((TOK_DEV, D), BF),
            shape((TOK_DEV - PROMPT, D), BF),
            shape((D, D), BF),
            shape((EXPERTS, D), F32),
            shape((1, D), F32),
        ),
        in_specs=[
            whole(ROWS, D),
            whole(ROWS, D),
            rows,
            whole(ROWS, D),
            rows,
            rows,
            whole(1, D),
            whole(EXPERTS, D),
            rows,
            pl.BlockSpec((2, D, 384), lambda i: (3, 0, 0)),
        ],
        out_specs=(
            rows,
            rows,
            whole(TOK_DEV - PROMPT, D),
            whole(D, D),
            whole(EXPERTS, D),
            whole(1, D),
        ),
        compiler_params=pltpu.CompilerParams(vmem_limit_bytes=VMEM_LIMIT),
        cost_estimate=pl.CostEstimate(
            flops=2 * 2 * TOK_DEV * D * D, bytes_accessed=12 * TOK_DEV * D, transcendentals=0
        ),
        name="branch_backward",
    )(dx_a, dx_b, dsh, h_block, x1, grad, gain2, router_t, o, w_all)


def attention_back_kernel(
    flags_ref,
    q_ref,
    k_ref,
    v_ref,
    do_ref,
    do_far_ref,
    h1_ref,
    w_ref,
    own_ref,
    gain1_ref,
    cos_ref,
    sin_ref,
    dx1_ref,
    gwo_ref,
    gtok_ref,
    gqk_ref,
    gvo_ref,
    ggain_ref,
    dq_sc,
    dk_sc,
    dv_sc,
    low_sc,
):
    masks = lane_halves()
    row, col = causal_mask(PROMPT)
    prompt_ok = col <= row
    cont_ok = (row // CLEN == col // CLEN) & (col <= row)
    row = lax.broadcasted_iota(jnp.int32, (4 * CLEN, 1), 0) // CLEN
    near = jnp.where(
        row < 2,
        jnp.where(row == 0, flags_ref[0], flags_ref[1]),
        jnp.where(row == 2, flags_ref[2], flags_ref[3]),
    ).astype(F32)
    own_c = slice(PROMPT, TOK_DEV)
    far_p = slice(TOK_DEV, TOK_DEV + PROMPT)
    far_c = slice(TOK_DEV + PROMPT, 2 * TOK_DEV)
    cont = CONT * CLEN

    def either(own_near, far_own):
        return jnp.concatenate(
            [jnp.where(near[:cont] > 0.5, own_near[:cont], far_own), own_near[cont:]], 0
        )

    def heads(pair, carry):
        cols = pl.ds(pl.multiple_of(pair * 128, 128), 128)
        q_p, k_p, v_p = q_ref[:PROMPT, cols], k_ref[:PROMPT, cols], v_ref[:PROMPT, cols]
        k_f, v_f = k_ref[far_p, cols], v_ref[far_p, cols]
        q_c, k_c, v_c = q_ref[own_c, cols], k_ref[own_c, cols], v_ref[own_c, cols]
        do_p, do_c = do_ref[:PROMPT, cols], do_ref[own_c, cols]
        q_4 = jnp.concatenate([q_c, q_ref[far_c, cols]], 0)
        k_4 = jnp.concatenate([k_c, k_ref[far_c, cols]], 0)
        v_4 = jnp.concatenate([v_c, v_ref[far_c, cols]], 0)
        do_4 = jnp.concatenate([do_c, do_far_ref[:, cols]], 0)
        q_all = jnp.concatenate([q_p, q_4], 0)
        do_all = jnp.concatenate([do_p, do_4], 0)
        dq_p, dq_c, dk_p, dk_c, dv_p, dv_c = [], [], [], [], [], []
        for mask in masks:
            score = jnp.where(prompt_ok, 0.125 * contract(q_p * mask, k_p, 1, 1), -1e30)
            prob = softmax_of(score)
            dprob = contract(do_p * mask, v_p, 1, 1)
            ds = (prob * (dprob - jnp.sum(prob * dprob, -1, keepdims=True))).astype(BF)
            query, grad = q_4 * mask, do_4 * mask
            first = 0.125 * either(
                contract(query, k_p, 1, 1), contract(query[:cont], k_f, 1, 1)
            )
            second = jnp.where(cont_ok, 0.125 * contract(query, k_4, 1, 1), -1e30)
            first, second = softmax_of(first, second)
            dfirst = either(contract(grad, v_p, 1, 1), contract(grad[:cont], v_f, 1, 1))
            dsecond = contract(grad, v_4, 1, 1)
            mean = jnp.sum(first * dfirst, -1, keepdims=True) + jnp.sum(
                second * dsecond, -1, keepdims=True
            )
            ds1 = first * (dfirst - mean)
            ds2 = (second * (dsecond - mean)).astype(BF)[:cont, :cont]
            ds_near = (ds1 * near).astype(BF)
            ds_far = (ds1 * (1.0 - near)).astype(BF)[:cont]
            p_near = (first * near).astype(BF)
            p_own = second.astype(BF)[:cont, :cont]
            dq_p.append(jnp.dot(ds, k_p, preferred_element_type=F32))
            dq_c.append(
                jnp.dot(ds_near[:cont], k_p, preferred_element_type=F32)
                + jnp.dot(ds_far, k_f, preferred_element_type=F32)
                + jnp.dot(ds2, k_c, preferred_element_type=F32)
            )
            dk_p.append(contract(jnp.concatenate([ds, ds_near], 0), q_all, 0, 0))
            dv_p.append(contract(jnp.concatenate([prob.astype(BF), p_near], 0), do_all, 0, 0))
            dk_c.append(contract(ds2, q_c, 0, 0))
            dv_c.append(contract(p_own, do_c, 0, 0))
        for out, prompt_part, cont_part in (
            (dq_sc, dq_p, dq_c),
            (dk_sc, dk_p, dk_c),
            (dv_sc, dv_p, dv_c),
        ):
            out[:PROMPT, cols] = pick_lanes(*prompt_part)
            out[own_c, cols] = pick_lanes(*cont_part)
        return carry

    lax.fori_loop(0, HEADS // 2, heads, 0)
    dh1 = None
    for i, source in enumerate((dq_sc, dk_sc, dv_sc)):
        for slab in range(6):
            cols = slice(slab * 128, (slab + 1) * 128)
            value = source[:, cols]
            if i < 2:
                value = turned(0.125 * value, cos_ref[...], -sin_ref[...])
            low_sc[:, cols] = value.astype(BF)
        grads = low_sc[...]
        product = contract(h1_ref[...], grads, 0, 0).astype(BF)
        out_ref, at = ((gqk_ref, 0), (gqk_ref, D), (gvo_ref, 0))[i]
        for z in range(4):
            out_ref[z, : D // 4, at : at + D] = product[z * (D // 4) : (z + 1) * (D // 4), :]
        for half in range(2):
            part = contract(grads[:, 384 * half : 384 * (half + 1)], w_ref[2 * i + half], 1, 1)
            dh1 = part if dh1 is None else dh1 + part
    for z in range(4):
        gvo_ref[z, : D // 4, D:] = gwo_ref[z * (D // 4) : (z + 1) * (D // 4), :]
        gqk_ref[z, D // 4 :, :] = jnp.zeros((EXT, 2 * D), BF)
        gvo_ref[z, D // 4 :, :] = jnp.zeros((EXT, 2 * D), BF)
    inputs = own_ref[:TOK_DEV, :].astype(F32)
    scale = unit_rms(inputs)
    normed = inputs * scale
    ggain_ref[...] = jnp.sum(dh1 * normed, 0, keepdims=True)
    dnormed = dh1 * gain1_ref[...]
    gtok_ref[...] = (
        scale * (dnormed - normed * jnp.mean(dnormed * normed, -1, keepdims=True)) + dx1_ref[...]
    )


def attention_backward(flags, q, k, v, do, do_far, h1, w_all, own, gain1, cos, sin, dx1, gwo):
    shape = jax.ShapeDtypeStruct
    whole = lambda *dims: pl.BlockSpec(dims, lambda i: (0,) * len(dims))
    rows = whole(TOK_DEV, D)
    both = whole(2 * TOK_DEV, D)
    packed = (4, D // 4 + EXT, 2 * D)
    return pl.pallas_call(
        attention_back_kernel,
        grid=(1,),
        out_shape=(
            shape((TOK_DEV, D), F32),
            shape(packed, BF),
            shape(packed, BF),
            shape((1, D), F32),
        ),
        in_specs=[
            pl.BlockSpec(memory_space=pltpu.SMEM),
            both,
            both,
            both,
            rows,
            whole(TOK_DEV - PROMPT, D),
            rows,
            whole(6, D, 384),
            whole(ROWS, D),
            whole(1, D),
            whole(TOK_DEV, 128),
            whole(TOK_DEV, 128),
            rows,
            whole(D, D),
        ],
        out_specs=(rows, whole(*packed), whole(*packed), whole(1, D)),
        scratch_shapes=[
            pltpu.VMEM((TOK_DEV, D), F32),
            pltpu.VMEM((TOK_DEV, D), F32),
            pltpu.VMEM((TOK_DEV, D), F32),
            pltpu.VMEM((TOK_DEV, D), BF),
        ],
        compiler_params=pltpu.CompilerParams(vmem_limit_bytes=VMEM_LIMIT),
        cost_estimate=pl.CostEstimate(
            flops=2 * 8 * TOK_DEV * D * D, bytes_accessed=40 * TOK_DEV * D, transcendentals=0
        ),
        name="attention_backward",
    )(flags, q, k, v, do, do_far, h1, w_all, own, gain1, cos, sin, dx1, gwo)


def after(value, *earlier):
    return lax.optimization_barrier((value, earlier))[0]


def spread(column):
    first = over_a(column)
    second = over_b(column)
    third = over_b(first)
    return [column, first, second, third]


def with_core(parts):
    return parts + [over_core(part) for part in parts]


def reduce_dense(first, second, z, y, x, core):
    kept = jnp.where(core == 0, first, second)
    sent = jnp.where(core == 0, second, first)
    total = pair_sum(kept, over_core(sent))
    bit_a, bit_b = jnp.where(core == 0, x, y), jnp.where(core == 0, y, x)
    kept, sent = halves(total, bit_a)
    total = pair_sum(kept, over_a(sent))
    kept, sent = halves(total, bit_b)
    total = pair_sum(kept, over_b(sent))
    result = lax.dynamic_index_in_dim(total, z, 0, keepdims=False).astype(F32)
    for step in (1, 2, 3):
        out = lax.dynamic_index_in_dim(total, lax.rem(z + step, 4), 0, keepdims=False)
        result = result + over_z(out, step).astype(F32)
    result = result.astype(BF)
    result = rejoin(result, over_b(result), bit_b)
    result = rejoin(result, over_a(result), bit_a)
    other = over_core(result)
    return jnp.where(core == 0, result, other), jnp.where(core == 0, other, result)


def tuned_body(
    tokens,
    cotangent,
    routes,
    prompt_ids,
    attn_gain,
    query_weight,
    key_weight,
    value_weight,
    output_weight,
    ffn_gain,
    router_weight,
    shared_gate,
    shared_up,
    shared_down,
    expert_gate,
    expert_up_weight,
    expert_down,
):
    z, y, j = lax.axis_index("dp"), lax.axis_index("context"), lax.axis_index("experts")
    x, core = j // 2, j % 2
    plane = y * 4 + j
    shard = D // 4

    dense = jnp.concatenate([query_weight, key_weight, value_weight, output_weight], 1)
    dense = lax.dynamic_slice_in_dim(dense, plane * 384, 384, 1)
    gains = jnp.concatenate(
        [attn_gain[None], ffn_gain[None], jnp.zeros((EXT - 2, shard), BF)], 0
    )
    dense = jnp.concatenate([dense, jnp.concatenate([router_weight.T, gains], 1)], 0)
    dense = jnp.stack([dense] + [over_z(dense, step) for step in (1, 2, 3)])
    dense_parts = with_core(spread(dense))

    ids = jnp.broadcast_to(prompt_ids.astype(BF)[:, None], (CONT, D))
    own = jnp.concatenate([tokens, ids, jnp.zeros((EXT - CONT, D), BF)], 0)
    far = moved(own, lambda z, y, x, c: (z, 1 - y, x, c))
    far_ids = far[TOK_DEV : TOK_DEV + CONT, 0].astype(jnp.int32)

    expert_ids = jnp.arange(EXPERTS, dtype=jnp.int32)[:, None]
    route_t = routes.T
    member = (route_t[0:1] == expert_ids) | (route_t[1:2] == expert_ids)
    before = (jnp.arange(TOK_DEV)[:, None] < jnp.arange(TOK_DEV)[None, :]).astype(BF)
    ranks = jnp.dot(member.astype(BF), before, preferred_element_type=F32)
    ranks = jnp.where(member, ranks, -1.0).astype(BF)
    g_block = jnp.concatenate([cotangent, jnp.pad(ranks, ((0, 0), (0, D - TOK_DEV)))], 0)
    g_near = [g_block, over_x(g_block)]
    g_group = with_core(g_near)

    units = lambda w: lax.dynamic_index_in_dim(
        w.reshape(shard, 4, 8, 64), plane, 2, keepdims=False
    ).reshape(shard, 256)
    down = lax.dynamic_slice_in_dim(shared_down, plane * 64, 64, 0)
    down = jnp.concatenate([down[:, 256 * i : 256 * (i + 1)] for i in range(3)], 0)
    shared = jnp.concatenate([units(shared_gate), units(shared_up), down], 1)
    shared = lax.all_gather(shared, "dp", axis=0, tiled=False)
    shared_parts = with_core(spread(shared))

    g_column = lax.all_gather(g_block, "dp", axis=0, tiled=False)
    g_parts = with_core(spread(g_column))

    slots = dense[:, shard:, :]
    slots = jnp.stack([slots[0], slots[3], slots[2], slots[1]])
    small = lax.dynamic_slice_in_dim(
        jnp.concatenate([slots, slots], 0), lax.rem(4 - z, 4), 4, 0
    )
    router_t = small[:, :, :shard].transpose(1, 0, 2).reshape(EXPERTS, D)
    gain1 = small[:, 0, shard:].reshape(1, D).astype(F32)
    gain2 = small[:, 1, shard:].reshape(1, D).astype(F32)

    cos_table, sin_table = rotary_tables(TOK_DEV)
    cos = jnp.tile(cos_table, (1, 4))
    sin = jnp.tile(jnp.concatenate([-sin_table, sin_table], 1), (1, 2))
    flip_a, flip_b = jnp.where(core == 0, 2, 4), jnp.where(core == 0, 4, 2)
    flips = [0 * core, flip_a, flip_b, 0 * core + 6]
    flips = flips + [1 + flips[0], 1 + flip_b, 1 + flip_a, 1 + flips[3]]
    place = [jnp.bitwise_xor(plane, flip) for flip in flips]
    place += [lax.rem(z + 4 - slot, 4) for slot in range(4)]
    place += [(prompt_ids[m] != y) for m in range(CONT)]
    place = jnp.stack([v.astype(jnp.int32) for v in place])
    w_all, q, k, v, h1, o, x1, h_block = attention_forward(
        place, dense_parts, own, far, gain1, gain2, router_t, cos, sin
    )

    h_near = [h_block, over_x(h_block)]
    h_group = with_core(h_near)
    h_column = lax.all_gather(h_block, "dp", axis=0, tiled=False)
    base = (j * 4).astype(jnp.int32)
    moe_near, moe_far, dx_near, dx_far = group_experts(
        base[None], h_group, g_group, expert_gate, expert_up_weight, expert_down
    )
    shared_out, shared_dh = shared_rows(h_block, cotangent, shared_parts)
    h_parts = with_core(spread(h_column))

    dx_pair = pair_sum(dx_near, over_core(dx_far))
    dx_there = over_x(dx_pair[1])
    dx1, do, do_c, gwo, grad_router_t, grad_gain2 = branch_backward(
        dx_pair[0], dx_there, shared_dh, h_block, x1, cotangent, gain2, router_t, o, w_all
    )
    do_far = moved(do_c, lambda z, y, x, c: (z, 1 - y, x, c))
    flags = jnp.concatenate([prompt_ids == y, far_ids == y]).astype(jnp.int32)
    grad_inputs, gqk, gvo, grad_gain1 = attention_backward(
        flags, q, k, v, do, do_far, h1, w_all, own, gain1, cos, sin, dx1, gwo
    )
    moe_pair = pair_sum(moe_near, over_core(moe_far))
    moe_out = moe_pair[0].astype(F32) + over_x(moe_pair[1]).astype(F32)
    layer_out = (x1 + shared_out + moe_out).astype(BF)

    extras = jnp.concatenate([grad_gain1, grad_gain2, jnp.zeros((EXT - 2, D), F32)], 0)
    extras = jnp.stack([grad_router_t, extras]).astype(BF).reshape(2, EXT, 4, shard)
    extras = extras.transpose(2, 1, 0, 3).reshape(4, EXT, 2 * shard)
    gqk = lax.dynamic_update_slice(gqk, extras, (0, shard, 0))
    sum_qk, sum_vo = reduce_dense(gqk, gvo, z, y, x, core)
    extras = sum_qk[shard:, : 2 * shard].astype(F32)
    sum_qk, sum_vo = sum_qk[:shard].astype(F32), sum_vo[:shard].astype(F32)

    window = jnp.array([0, 1, 3, 4], jnp.int32)[z]
    s_gate, s_up, s_down = shared_slice_grads(
        jnp.stack([window, (z // 2).astype(jnp.int32)]), h_parts, g_parts, shared
    )
    lead = z * 192 - window * 128
    s_down = lax.dynamic_slice_in_dim(s_down, (z % 2) * 64, 64, 0)
    mine = jnp.concatenate(
        [
            lax.dynamic_slice_in_dim(s_gate, lead, 192, 0),
            lax.dynamic_slice_in_dim(s_up, lead, 192, 0),
            jnp.concatenate([s_down[:, 256 * i : 256 * (i + 1)] for i in range(3)], 0),
        ],
        1,
    ).astype(BF)
    every = lax.all_gather(mine, ("context", "experts"), axis=0, tiled=False)
    s_gateup = (
        every[:, :, :512].reshape(8, shard, 2, 4, 64).transpose(2, 1, 3, 0, 4)
    ).reshape(2, shard, 2048)
    s_gateup = s_gateup.astype(F32)
    s_down = jnp.concatenate(
        [every[:, 64 * i : 64 * (i + 1), 512:].reshape(512, 256) for i in range(3)], 1
    ).astype(F32)

    slice_index = (z * 2 + y).astype(jnp.int32)
    e_gate, e_up, e_down = expert_slice_grads(
        jnp.stack([base, slice_index]),
        h_parts,
        g_parts,
        expert_gate,
        expert_up_weight,
        expert_down,
        256,
    )
    return (
        layer_out,
        grad_inputs,
        extras[0, shard:],
        sum_qk[:, :D],
        sum_qk[:, D:],
        sum_vo[:, :D],
        sum_vo[:, D:],
        extras[1, shard:],
        extras[:, :shard].T,
        s_gateup[0],
        s_gateup[1],
        s_down,
        e_gate,
        e_up,
        e_down,
    )


def solution(mesh):
    tuned = dict(mesh.shape) == TUNED_MESH

    return jax.shard_map(
        tuned_body if tuned else plain_body,
        mesh=mesh,
        in_specs=(
            P(("dp", "context", "experts"), None),
            P(("dp", "context", "experts"), None),
            P(("dp", "context", "experts"), None),
            P(("dp", "context", "experts")),
            P("dp"),
            P("dp", None),
            P("dp", None),
            P("dp", None),
            P("dp", None),
            P("dp"),
            P("dp", None),
            P("dp", None),
            P("dp", None),
            P("dp", None),
            P("experts", None, None),
            P("experts", None, None),
            P("experts", None, None),
        ),
        out_specs=(
            P(("dp", "context", "experts"), None),
            P(("dp", "context", "experts"), None),
            P("dp"),
            P("dp", None),
            P("dp", None),
            P("dp", None),
            P("dp", None),
            P("dp"),
            P("dp", None),
            P("dp", None),
            P("dp", None),
            P("dp", None),
            P("experts", None, ("dp", "context")),
            P("experts", None, ("dp", "context")),
            P("experts", ("dp", "context"), None),
        ),
        check_vma=False,
    )
```

```python
import functools

import jax
import jax.numpy as jnp
from jax import lax
from jax.sharding import PartitionSpec as P

from jax.experimental import pallas as pl
from jax.experimental.pallas import tpu as pltpu

D = 768
HEADS = 12
HD = 64
EXPERTS = 16
TOPK = 2
PROMPT = 256
CONT = 2
CLEN = 64
TOK_DEV = 384
CAP = 66


EPS = 1e-06


def rotary_tables(tok_rows):
    row_ids = jnp.arange(tok_rows)
    position = jnp.where(row_ids < PROMPT, row_ids, PROMPT + (row_ids - PROMPT) % CLEN).astype(
        jnp.float32
    )
    frequency = 10000.0 ** (-2.0 * jnp.arange(HD // 2).astype(jnp.float32) / HD)
    angles = position[:, None] * frequency[None, :]
    return (jnp.cos(angles), jnp.sin(angles))


def rotate(values_in, cos_table, sin_table):
    shaped = values_in.reshape(values_in.shape[:-1] + (HEADS, HD))
    lower_half = shaped[..., : HD // 2]
    upper_half = shaped[..., HD // 2 :]
    cos_part = cos_table[:, None, :]
    sin_part = sin_table[:, None, :]
    turned = jnp.concatenate(
        [
            lower_half * cos_part - upper_half * sin_part,
            upper_half * cos_part + lower_half * sin_part,
        ],
        -1,
    )
    return turned.reshape(values_in.shape)


def key_mask(context_index, prompt_pick, contexts):
    row_ids = jnp.arange(TOK_DEV)[:, None]
    col_ids = jnp.arange(contexts * PROMPT + CONT * CLEN)[None, :]
    prompt_row = row_ids < PROMPT
    cont_row = (row_ids - PROMPT) // CLEN
    within_row = (row_ids - PROMPT) % CLEN
    owner = jnp.sum(
        prompt_pick[None, :] * (jnp.arange(CONT)[None, :] == cont_row), -1, keepdims=True
    )
    target = jnp.where(prompt_row, context_index, owner)
    prompt_keys = col_ids < contexts * PROMPT
    prompt_ok = (
        prompt_keys
        & (col_ids // PROMPT == target)
        & (jnp.logical_not(prompt_row) | (col_ids % PROMPT <= row_ids))
    )
    offset = col_ids - contexts * PROMPT
    cont_ok = (
        jnp.logical_not(prompt_keys)
        & jnp.logical_not(prompt_row)
        & (offset // CLEN == cont_row)
        & (offset % CLEN <= within_row)
    )
    return prompt_ok | cont_ok


def inner_rows(left, right):
    return lax.dot_general(
        left, right, (((0,), (0,)), ((), ())), preferred_element_type=jnp.float32
    )


def times_transposed(left, right):
    return lax.dot_general(
        left, right, (((1,), (1,)), ((), ())), preferred_element_type=jnp.float32
    )


def swish_derivative(pre_act):
    sigma = jax.nn.sigmoid(pre_act)
    return sigma * (1.0 + pre_act * (1.0 - sigma))


def plain_body(
    tokens,
    cotangent,
    routes,
    prompt_ids,
    attn_gain,
    query_weight,
    key_weight,
    value_weight,
    output_weight,
    ffn_gain,
    router_weight,
    shared_gate,
    shared_up,
    shared_down,
    expert_gate,
    expert_up_weight,
    expert_down,
):
    contexts = lax.axis_size("context")
    context_here = lax.axis_index("context")
    gain_one, w_query, w_key, w_value, w_out, gain_two, w_router, w_sgate, w_sup, w_sdown = (
        lax.all_gather(attn_gain, "dp", axis=0, tiled=True),
        lax.all_gather(query_weight, "dp", axis=0, tiled=True),
        lax.all_gather(key_weight, "dp", axis=0, tiled=True),
        lax.all_gather(value_weight, "dp", axis=0, tiled=True),
        lax.all_gather(output_weight, "dp", axis=0, tiled=True),
        lax.all_gather(ffn_gain, "dp", axis=0, tiled=True),
        lax.all_gather(router_weight, "dp", axis=0, tiled=True),
        lax.all_gather(shared_gate, "dp", axis=0, tiled=True),
        lax.all_gather(shared_up, "dp", axis=0, tiled=True),
        lax.all_gather(shared_down, "dp", axis=0, tiled=True),
    )
    cos_table, sin_table = rotary_tables(TOK_DEV)
    inputs = tokens.astype(jnp.float32)
    inv_rms1 = lax.rsqrt(jnp.mean(inputs * inputs, -1, keepdims=True) + EPS)
    normed1 = inputs * inv_rms1
    gain1_f = gain_one.astype(jnp.float32)
    hidden1 = (normed1 * gain1_f).astype(jnp.bfloat16)
    query_f = jnp.dot(hidden1, w_query, preferred_element_type=jnp.float32)
    key_f = jnp.dot(hidden1, w_key, preferred_element_type=jnp.float32)
    value_f = jnp.dot(hidden1, w_value, preferred_element_type=jnp.float32)
    query_b = rotate(query_f, cos_table, sin_table).astype(jnp.bfloat16)
    key_b = rotate(key_f, cos_table, sin_table).astype(jnp.bfloat16)
    value_b = value_f.astype(jnp.bfloat16)
    prompt_keys, prompt_values = (
        lax.all_gather(key_b[:PROMPT], "context", axis=0, tiled=True),
        lax.all_gather(value_b[:PROMPT], "context", axis=0, tiled=True),
    )
    keys_h = jnp.concatenate([prompt_keys, key_b[PROMPT:]], 0).reshape(-1, HEADS, HD)
    values_h = jnp.concatenate([prompt_values, value_b[PROMPT:]], 0).reshape(-1, HEADS, HD)
    query_h = query_b.reshape(TOK_DEV, HEADS, HD)
    allowed = key_mask(context_here, prompt_ids, contexts)
    scores = jnp.where(
        allowed[None],
        0.125 * jnp.einsum("qhd,khd->hqk", query_h, keys_h, preferred_element_type=jnp.float32),
        -1e30,
    )
    row_max = jnp.max(scores, -1, keepdims=True)
    exp_scores = jnp.exp(scores - row_max)
    row_total = jnp.sum(exp_scores, -1, keepdims=True)
    log_total = row_max + jnp.log(row_total)
    attn_probs = (exp_scores / row_total).astype(jnp.bfloat16)
    attended = (
        jnp.einsum("hqk,khd->qhd", attn_probs, values_h, preferred_element_type=jnp.float32)
        .reshape(TOK_DEV, D)
        .astype(jnp.bfloat16)
    )
    resid = inputs + jnp.dot(attended, w_out, preferred_element_type=jnp.float32)
    inv_rms2 = lax.rsqrt(jnp.mean(resid * resid, -1, keepdims=True) + EPS)
    normed2 = resid * inv_rms2
    gain2_f = gain_two.astype(jnp.float32)
    hidden2 = (normed2 * gain2_f).astype(jnp.bfloat16)
    logits = jnp.dot(hidden2, w_router, preferred_element_type=jnp.float32)
    route_probs = jax.nn.softmax(logits, -1)
    route_hot = (routes[:, :, None] == jnp.arange(EXPERTS)[None, None, :]).astype(jnp.float32)
    gate_vals = jnp.sum(route_probs[:, None, :] * route_hot, -1)
    shared_gpre = jnp.dot(hidden2, w_sgate, preferred_element_type=jnp.float32)
    shared_upre = jnp.dot(hidden2, w_sup, preferred_element_type=jnp.float32)
    shared_act = (jax.nn.silu(shared_gpre) * shared_upre).astype(jnp.bfloat16)
    shared_res = jnp.dot(shared_act, w_sdown, preferred_element_type=jnp.float32)
    flat_route = routes.reshape(-1)
    flat_hot = (flat_route[:, None] == jnp.arange(EXPERTS)[None, :]).astype(jnp.int32)
    slot_ids = jnp.sum((jnp.cumsum(flat_hot, 0) - flat_hot) * flat_hot, -1)
    slot_index = flat_route * CAP + slot_ids
    send_rows = jnp.repeat(hidden2, TOPK, axis=0)
    outgoing = (
        jnp.zeros((EXPERTS * CAP, D), jnp.bfloat16)
        .at[slot_index]
        .set(send_rows)
        .reshape(EXPERTS, CAP, D)
    )
    received_rows = lax.all_to_all(outgoing, "experts", split_axis=0, concat_axis=1, tiled=True)
    expert_gate_preact = jnp.einsum(
        "mgx,mxp->mgp", received_rows, expert_gate, preferred_element_type=jnp.float32
    )
    expert_up_preact = jnp.einsum(
        "mgx,mxp->mgp", received_rows, expert_up_weight, preferred_element_type=jnp.float32
    )
    expert_activation = (jax.nn.silu(expert_gate_preact) * expert_up_preact).astype(jnp.bfloat16)
    expert_res = jnp.einsum(
        "erf,efd->erd", expert_activation, expert_down, preferred_element_type=jnp.float32
    ).astype(jnp.bfloat16)
    returned = lax.all_to_all(
        expert_res, "experts", split_axis=1, concat_axis=0, tiled=True
    ).reshape(EXPERTS * CAP, D)
    picked = returned[slot_index].astype(jnp.float32).reshape(TOK_DEV, TOPK, D)
    moe_out = jnp.sum(gate_vals[:, :, None] * picked, 1)
    layer_out = (resid + shared_res + moe_out).astype(jnp.bfloat16)
    gain_one, w_query, w_key, w_value, w_out, gain_two, w_router, w_sgate, w_sup, w_sdown = (
        lax.all_gather(attn_gain, "dp", axis=0, tiled=True),
        lax.all_gather(query_weight, "dp", axis=0, tiled=True),
        lax.all_gather(key_weight, "dp", axis=0, tiled=True),
        lax.all_gather(value_weight, "dp", axis=0, tiled=True),
        lax.all_gather(output_weight, "dp", axis=0, tiled=True),
        lax.all_gather(ffn_gain, "dp", axis=0, tiled=True),
        lax.all_gather(router_weight, "dp", axis=0, tiled=True),
        lax.all_gather(shared_gate, "dp", axis=0, tiled=True),
        lax.all_gather(shared_up, "dp", axis=0, tiled=True),
        lax.all_gather(shared_down, "dp", axis=0, tiled=True),
    )
    gain1_f = gain_one.astype(jnp.float32)
    gain2_f = gain_two.astype(jnp.float32)
    grad_total = cotangent.astype(jnp.float32)
    grad_gates = jnp.sum(grad_total[:, None, :] * picked, -1)
    grad_picked = (
        (gate_vals[:, :, None] * grad_total[:, None, :])
        .astype(jnp.bfloat16)
        .reshape(TOK_DEV * TOPK, D)
    )
    grad_back = (
        jnp.zeros((EXPERTS * CAP, D), jnp.bfloat16)
        .at[slot_index]
        .set(grad_picked)
        .reshape(EXPERTS, CAP, D)
    )
    grad_arrived = lax.all_to_all(grad_back, "experts", split_axis=0, concat_axis=1, tiled=True)
    grad_expert_activation = jnp.einsum(
        "erd,efd->erf", grad_arrived, expert_down, preferred_element_type=jnp.float32
    )
    grad_expert_gate_preact = (
        grad_expert_activation * expert_up_preact * swish_derivative(expert_gate_preact)
    ).astype(jnp.bfloat16)
    grad_expert_up_preact = (grad_expert_activation * jax.nn.silu(expert_gate_preact)).astype(
        jnp.bfloat16
    )
    expert_grad_down = jnp.einsum(
        "erf,erd->edf", expert_activation, grad_arrived, preferred_element_type=jnp.float32
    )
    expert_grad_gate = jnp.einsum(
        "xvb,xva->xba", received_rows, grad_expert_gate_preact, preferred_element_type=jnp.float32
    )
    expert_grad_up = jnp.einsum(
        "xvb,xva->xba", received_rows, grad_expert_up_preact, preferred_element_type=jnp.float32
    )
    grad_einputs = jnp.einsum(
        "cgj,clj->cgl", grad_expert_gate_preact, expert_gate, preferred_element_type=jnp.float32
    )
    grad_einputs = (
        grad_einputs
        + jnp.einsum(
            "cgj,clj->cgl",
            grad_expert_up_preact,
            expert_up_weight,
            preferred_element_type=jnp.float32,
        )
    ).astype(jnp.bfloat16)
    grad_returned = lax.all_to_all(
        grad_einputs, "experts", split_axis=1, concat_axis=0, tiled=True
    ).reshape(EXPERTS * CAP, D)
    grad_moe_in = jnp.sum(
        grad_returned[slot_index].astype(jnp.float32).reshape(TOK_DEV, TOPK, D), 1
    )
    grad_rprobs = jnp.sum(grad_gates[:, :, None] * route_hot, 1)
    grad_logits = (
        route_probs * (grad_rprobs - jnp.sum(route_probs * grad_rprobs, -1, keepdims=True))
    ).astype(jnp.bfloat16)
    grad_router_local = inner_rows(hidden2, grad_logits)
    grad_total_b = grad_total.astype(jnp.bfloat16)
    grad_sdown = inner_rows(shared_act, grad_total_b)
    grad_sact = times_transposed(grad_total_b, w_sdown)
    grad_sgpre = (grad_sact * shared_upre * swish_derivative(shared_gpre)).astype(jnp.bfloat16)
    grad_supre = (grad_sact * jax.nn.silu(shared_gpre)).astype(jnp.bfloat16)
    grad_sgate = inner_rows(hidden2, grad_sgpre)
    grad_sup = inner_rows(hidden2, grad_supre)
    grad_hidden2 = (
        grad_moe_in
        + times_transposed(grad_logits, w_router)
        + times_transposed(grad_sgpre, w_sgate)
        + times_transposed(grad_supre, w_sup)
    )
    grad_gain2 = jnp.sum(grad_hidden2 * normed2, 0)
    grad_normed2 = grad_hidden2 * gain2_f
    grad_resid = (
        inv_rms2 * (grad_normed2 - normed2 * jnp.mean(grad_normed2 * normed2, -1, keepdims=True))
        + grad_total
    )
    grad_branch = grad_resid.astype(jnp.bfloat16)
    grad_wout = inner_rows(attended, grad_branch)
    grad_attended = (
        times_transposed(grad_branch, w_out).astype(jnp.bfloat16).reshape(TOK_DEV, HEADS, HD)
    )
    scores_again = jnp.where(
        allowed[None],
        0.125 * jnp.einsum("qhd,khd->hqk", query_h, keys_h, preferred_element_type=jnp.float32),
        -1e30,
    )
    probs_f = jnp.exp(scores_again - log_total)
    probs_b = probs_f.astype(jnp.bfloat16)
    grad_pattn = jnp.einsum(
        "qhd,khd->hqk", grad_attended, values_h, preferred_element_type=jnp.float32
    )
    grad_scores = (
        probs_f * (grad_pattn - jnp.sum(probs_f * grad_pattn, -1, keepdims=True))
    ).astype(jnp.bfloat16)
    grad_query = 0.125 * jnp.einsum(
        "hqk,khd->qhd", grad_scores, keys_h, preferred_element_type=jnp.float32
    ).reshape(TOK_DEV, D)
    grad_keys = 0.125 * jnp.einsum(
        "hqk,qhd->khd", grad_scores, query_h, preferred_element_type=jnp.float32
    ).reshape(-1, D)
    grad_values = jnp.einsum(
        "hqk,qhd->khd", probs_b, grad_attended, preferred_element_type=jnp.float32
    ).reshape(-1, D)
    prompt_span = contexts * PROMPT
    grad_pkeys, grad_pvalues = (
        lax.psum_scatter(
            grad_keys[:prompt_span].astype(jnp.bfloat16), "context", scatter_dimension=0, tiled=True
        ).astype(jnp.float32),
        lax.psum_scatter(
            grad_values[:prompt_span].astype(jnp.bfloat16),
            "context",
            scatter_dimension=0,
            tiled=True,
        ).astype(jnp.float32),
    )
    grad_key_all = jnp.concatenate([grad_pkeys, grad_keys[prompt_span:]], 0)
    grad_value_all = jnp.concatenate([grad_pvalues, grad_values[prompt_span:]], 0)
    grad_qpre = rotate(grad_query, cos_table, -sin_table).astype(jnp.bfloat16)
    grad_kpre = rotate(grad_key_all, cos_table, -sin_table).astype(jnp.bfloat16)
    grad_vpre = grad_value_all.astype(jnp.bfloat16)
    grad_wquery = inner_rows(hidden1, grad_qpre)
    grad_wkey = inner_rows(hidden1, grad_kpre)
    grad_wvalue = inner_rows(hidden1, grad_vpre)
    grad_hidden1 = (
        times_transposed(grad_qpre, w_query)
        + times_transposed(grad_kpre, w_key)
        + times_transposed(grad_vpre, w_value)
    )
    grad_gain1 = jnp.sum(grad_hidden1 * normed1, 0)
    grad_normed1 = grad_hidden1 * gain1_f
    grad_inputs = (
        inv_rms1 * (grad_normed1 - normed1 * jnp.mean(grad_normed1 * normed1, -1, keepdims=True))
        + grad_resid
    )
    shares = (
        lax.psum_scatter(
            grad_gain1.astype(jnp.bfloat16), "dp", scatter_dimension=0, tiled=True
        ).astype(jnp.float32),
        lax.psum_scatter(
            grad_wquery.astype(jnp.bfloat16), "dp", scatter_dimension=0, tiled=True
        ).astype(jnp.float32),
        lax.psum_scatter(
            grad_wkey.astype(jnp.bfloat16), "dp", scatter_dimension=0, tiled=True
        ).astype(jnp.float32),
        lax.psum_scatter(
            grad_wvalue.astype(jnp.bfloat16), "dp", scatter_dimension=0, tiled=True
        ).astype(jnp.float32),
        lax.psum_scatter(
            grad_wout.astype(jnp.bfloat16), "dp", scatter_dimension=0, tiled=True
        ).astype(jnp.float32),
        lax.psum_scatter(
            grad_gain2.astype(jnp.bfloat16), "dp", scatter_dimension=0, tiled=True
        ).astype(jnp.float32),
        lax.psum_scatter(
            grad_router_local.astype(jnp.bfloat16), "dp", scatter_dimension=0, tiled=True
        ).astype(jnp.float32),
        lax.psum_scatter(
            grad_sgate.astype(jnp.bfloat16), "dp", scatter_dimension=0, tiled=True
        ).astype(jnp.float32),
        lax.psum_scatter(
            grad_sup.astype(jnp.bfloat16), "dp", scatter_dimension=0, tiled=True
        ).astype(jnp.float32),
        lax.psum_scatter(
            grad_sdown.astype(jnp.bfloat16), "dp", scatter_dimension=0, tiled=True
        ).astype(jnp.float32),
    )
    totals = (
        lax.psum(shares[0].astype(jnp.bfloat16), ("context", "experts")).astype(jnp.float32),
        lax.psum(shares[1].astype(jnp.bfloat16), ("context", "experts")).astype(jnp.float32),
        lax.psum(shares[2].astype(jnp.bfloat16), ("context", "experts")).astype(jnp.float32),
        lax.psum(shares[3].astype(jnp.bfloat16), ("context", "experts")).astype(jnp.float32),
        lax.psum(shares[4].astype(jnp.bfloat16), ("context", "experts")).astype(jnp.float32),
        lax.psum(shares[5].astype(jnp.bfloat16), ("context", "experts")).astype(jnp.float32),
        lax.psum(shares[6].astype(jnp.bfloat16), ("context", "experts")).astype(jnp.float32),
        lax.psum(shares[7].astype(jnp.bfloat16), ("context", "experts")).astype(jnp.float32),
        lax.psum(shares[8].astype(jnp.bfloat16), ("context", "experts")).astype(jnp.float32),
        lax.psum(shares[9].astype(jnp.bfloat16), ("context", "experts")).astype(jnp.float32),
    )
    summed_gate, summed_up, summed_down = (
        lax.psum_scatter(
            expert_grad_gate.astype(jnp.bfloat16),
            ("dp", "context"),
            scatter_dimension=2,
            tiled=True,
        ).astype(jnp.float32),
        lax.psum_scatter(
            expert_grad_up.astype(jnp.bfloat16), ("dp", "context"), scatter_dimension=2, tiled=True
        ).astype(jnp.float32),
        lax.psum_scatter(
            expert_grad_down.astype(jnp.bfloat16),
            ("dp", "context"),
            scatter_dimension=2,
            tiled=True,
        ).astype(jnp.float32),
    )
    summed_down = jnp.transpose(summed_down, (0, 2, 1))
    return (
        layer_out,
        grad_inputs,
        totals[0],
        totals[1],
        totals[2],
        totals[3],
        totals[4],
        totals[5],
        totals[6],
        totals[7],
        totals[8],
        totals[9],
        summed_gate,
        summed_up,
        summed_down,
    )


TUNED_MESH = {"dp": 4, "context": 2, "experts": 4}
AXES = ("dp", "context", "experts")
SLOT = 72
EXT = 16
ROWS = TOK_DEV + EXT
BF = jnp.bfloat16
F32 = jnp.float32
VMEM_LIMIT = 60 * 1024 * 1024


def microseconds(time):
    return pl.CostEstimate(flops=0, bytes_accessed=int(time * 0.4e6), transcendentals=0)


def moved(value, target):
    pairs = []
    for z in range(4):
        for y in range(2):
            for x in range(2):
                for c in range(2):
                    tz, ty, tx, tc = target(z, y, x, c)
                    pairs.append((((z * 2 + y) * 2 + x) * 2 + c, ((tz * 2 + ty) * 2 + tx) * 2 + tc))
    return lax.ppermute(value, AXES, pairs)


def over_core(value):
    return moved(value, lambda z, y, x, c: (z, y, x, 1 - c))


def over_x(value):
    return moved(value, lambda z, y, x, c: (z, y, 1 - x, c))


def over_a(value):
    return moved(value, lambda z, y, x, c: (z, y, 1 - x, c) if c == 0 else (z, 1 - y, x, c))


def over_b(value):
    return moved(value, lambda z, y, x, c: (z, 1 - y, x, c) if c == 0 else (z, y, 1 - x, c))


def over_z(value, step):
    return moved(value, lambda z, y, x, c: ((z + step) % 4, y, x, c))


def contract(left, right, left_dim, right_dim):
    return lax.dot_general(
        left, right, (((left_dim,), (right_dim,)), ((), ())), preferred_element_type=F32
    )


def one_hot_rows(rank_row):
    slots = lax.broadcasted_iota(jnp.int32, (SLOT, TOK_DEV), 0).astype(F32)
    return (slots == rank_row).astype(F32)


def swish_parts(pre_act):
    sigma = jax.nn.sigmoid(pre_act)
    return pre_act * sigma, sigma * (1.0 + pre_act * (1.0 - sigma))


def group_kernel(
    blocks,
    more,
    base_ref,
    *refs,
):
    h_refs, g_refs = refs[:blocks], refs[blocks : 2 * blocks]
    refs = refs[2 * blocks :]
    more_refs, refs = refs[:more], refs[more:]
    wg_ref, wu_ref, wd_ref, moe_ref, moe_far_ref, dx_ref, dx_far_ref = refs[:7]
    (
        rank_sc,
        prob_sc,
        x_sc,
        gd_sc,
        gate_sc,
        y_sc,
        acc_sc,
        dgate_sc,
        ysel_sc,
        dsel_sc,
        drp_sc,
    ) = refs[7:18]
    e = pl.program_id(0)
    f = pl.program_id(1)
    experts = pl.num_programs(0)
    base = base_ref[0]
    copies = [
        pltpu.make_async_copy(source, into, refs[-1].at[i])
        for i, (source, into) in enumerate(zip(more_refs, refs[18:]))
    ]

    @pl.when((e == 0) & (f == 0))
    def _():
        for one in copies:
            one.start()
        for b in range(blocks):
            rank_sc[b] = g_refs[b][TOK_DEV:, :TOK_DEV].astype(F32)
            prob_sc[b] = h_refs[b][TOK_DEV:, :TOK_DEV].astype(F32) + h_refs[b][
                TOK_DEV:, TOK_DEV:
            ].astype(F32)
        drp_sc[...] = jnp.zeros_like(drp_sc)

    @pl.when(f == 0)
    def _():
        for pair in range(blocks // 2):
            rows_x, rows_g = [], []
            for b in (2 * pair, 2 * pair + 1):
                hot = one_hot_rows(rank_sc[b, pl.ds(base + e, 1), :])
                gate_sc[b * SLOT : (b + 1) * SLOT, :] = jnp.sum(
                    hot * prob_sc[b, pl.ds(base + e, 1), :], -1, keepdims=True
                )
                hot = hot.astype(BF)
                rows_x.append(jnp.dot(hot, h_refs[b][:TOK_DEV, :], preferred_element_type=F32))
                rows_g.append(jnp.dot(hot, g_refs[b][:TOK_DEV, :], preferred_element_type=F32))
            span = slice(pair * 2 * SLOT, (pair + 1) * 2 * SLOT)
            x_sc[span, :] = jnp.concatenate(rows_x, 0).astype(BF)
            gd_sc[span, :] = jnp.concatenate(rows_g, 0).astype(BF)
        y_sc[...] = jnp.zeros_like(y_sc)
        acc_sc[...] = jnp.zeros_like(acc_sc)
        dgate_sc[...] = jnp.zeros_like(dgate_sc)

    rows = x_sc[...]
    gate_pre = jnp.dot(rows, wg_ref[0], preferred_element_type=F32)
    up_pre = jnp.dot(rows, wu_ref[0], preferred_element_type=F32)
    back = contract(gd_sc[...], wd_ref[0], 1, 1)
    swish, slope = swish_parts(gate_pre)
    inner = (swish * up_pre).astype(BF)
    dgate_sc[...] += jnp.sum(back * inner.astype(F32), -1, keepdims=True)
    back = back * gate_sc[...]
    dgate_pre = (back * up_pre * slope).astype(BF)
    dup_pre = (back * swish).astype(BF)
    y_sc[...] += jnp.dot(inner, wd_ref[0], preferred_element_type=F32)
    acc_sc[...] += contract(dgate_pre, wg_ref[0], 1, 1) + contract(dup_pre, wu_ref[0], 1, 1)

    @pl.when(f == pl.num_programs(1) - 1)
    def _():
        for b in range(blocks):
            span = slice(b * SLOT, (b + 1) * SLOT)
            into = pl.ds(pl.multiple_of(e * SLOT, 8), SLOT)
            ysel_sc[b, into, :] = y_sc[span, :] * gate_sc[span, :]
            dsel_sc[b, into, :] = acc_sc[span, :]
            hot = one_hot_rows(rank_sc[b, pl.ds(base + e, 1), :])
            drp_sc[b, pl.ds(base + e, 1), :] = jnp.sum(hot * dgate_sc[span, :], 0, keepdims=True)

    @pl.when((f == pl.num_programs(1) - 1) & (e == experts - 1))
    def _():
        for one in copies:
            one.wait()
        for b in range(blocks):
            side, at = divmod(b, blocks // 2)
            moe_out, dx_out = ((moe_ref, dx_ref), (moe_far_ref, dx_far_ref))[side]
            hot = jnp.concatenate(
                [
                    one_hot_rows(rank_sc[b, pl.ds(base + i, 1), :])
                    for i in range(ysel_sc.shape[1] // SLOT)
                ],
                0,
            ).astype(BF)
            moe = contract(hot, ysel_sc[b].astype(BF), 0, 0)
            dx = contract(hot, dsel_sc[b].astype(BF), 0, 0)
            drp = drp_sc[b]
            if more:
                shared = refs[18 + 2 * at : 20 + 2 * at]
                before = refs[22 + side], refs[24 + side]
                moe = moe + shared[0][side] + before[0][at].astype(F32)
                dx = dx + shared[1][side] + before[1][at, :TOK_DEV, :].astype(F32)
                drp = drp + before[1][at, TOK_DEV:, :TOK_DEV].astype(F32)
                drp = drp + before[1][at, TOK_DEV:, TOK_DEV:].astype(F32)
            moe_out[at] = moe.astype(BF)
            dx_out[at, :TOK_DEV, :] = dx.astype(BF)
            high = drp.astype(BF)
            dx_out[at, TOK_DEV:, :TOK_DEV] = high
            dx_out[at, TOK_DEV:, TOK_DEV:] = (drp - high.astype(F32)).astype(BF)


def group_experts(base, first, experts, h_group, g_group, more, w_gate, w_up, w_down):
    blocks = len(h_group)
    ff = w_gate.shape[2]
    tile = 512
    whole = lambda *shape: pl.BlockSpec(shape, lambda e, f, s: (0,) * len(shape))
    moe_shape, dx_shape = (blocks // 2, TOK_DEV, D), (blocks // 2, ROWS, D)
    return pl.pallas_call(
        functools.partial(group_kernel, blocks, len(more)),
        out_shape=tuple(
            jax.ShapeDtypeStruct(s, BF) for s in (moe_shape, moe_shape, dx_shape, dx_shape)
        ),
        grid_spec=pltpu.PrefetchScalarGridSpec(
            num_scalar_prefetch=1,
            grid=(experts, ff // tile),
            in_specs=[whole(ROWS, D)] * (2 * blocks)
            + [pl.BlockSpec(memory_space=pl.ANY)] * len(more)
            + [
                pl.BlockSpec((1, D, tile), lambda e, f, s: (first + e, 0, f)),
                pl.BlockSpec((1, D, tile), lambda e, f, s: (first + e, 0, f)),
                pl.BlockSpec((1, tile, D), lambda e, f, s: (first + e, f, 0)),
            ],
            out_specs=[whole(*moe_shape)] * 2 + [whole(*dx_shape)] * 2,
            scratch_shapes=[
                pltpu.VMEM((blocks, EXPERTS, TOK_DEV), F32),
                pltpu.VMEM((blocks, EXPERTS, TOK_DEV), F32),
                pltpu.VMEM((blocks * SLOT, D), BF),
                pltpu.VMEM((blocks * SLOT, D), BF),
                pltpu.VMEM((blocks * SLOT, 1), F32),
                pltpu.VMEM((blocks * SLOT, D), F32),
                pltpu.VMEM((blocks * SLOT, D), F32),
                pltpu.VMEM((blocks * SLOT, 1), F32),
                pltpu.VMEM((blocks, experts * SLOT, D), F32),
                pltpu.VMEM((blocks, experts * SLOT, D), F32),
                pltpu.VMEM((blocks, EXPERTS, TOK_DEV), F32),
            ]
            + [pltpu.VMEM(v.shape, v.dtype) for v in more]
            + [pltpu.SemaphoreType.DMA((max(1, len(more)),))],
        ),
        compiler_params=pltpu.CompilerParams(vmem_limit_bytes=VMEM_LIMIT),
        cost_estimate=microseconds(21),
        name="group_experts",
    )(base, *h_group, *g_group, *more, w_gate, w_up, w_down)


def shared_kernel(h_a_ref, h_b_ref, g_a_ref, g_b_ref, w_a_ref, w_b_ref, out_ref, dh_ref, h_sc, g_sc):
    for k, (h_ref, g_ref) in enumerate(((h_a_ref, g_a_ref), (h_b_ref, g_b_ref))):
        h_sc[k * TOK_DEV : (k + 1) * TOK_DEV, :] = h_ref[:TOK_DEV, :]
        g_sc[k * TOK_DEV : (k + 1) * TOK_DEV, :] = g_ref[:TOK_DEV, :]
    for k, w_ref in enumerate((w_a_ref, w_b_ref)):
        w_gate, w_up = w_ref[:, :, :256].reshape(D, 256), w_ref[:, :, 256:512].reshape(D, 256)
        w_down = jnp.concatenate(
            [w_ref[:, 64 * i : 64 * (i + 1), 512:].reshape(256, 256) for i in range(3)], 1
        )
        gate_pre = jnp.dot(h_sc[...], w_gate, preferred_element_type=F32)
        up_pre = jnp.dot(h_sc[...], w_up, preferred_element_type=F32)
        back = contract(g_sc[...], w_down, 1, 1)
        swish, slope = swish_parts(gate_pre)
        inner = (swish * up_pre).astype(BF)
        out = jnp.dot(inner, w_down, preferred_element_type=F32)
        dgate_pre = (back * up_pre * slope).astype(BF)
        dup_pre = (back * swish).astype(BF)
        dh = contract(dgate_pre, w_gate, 1, 1) + contract(dup_pre, w_up, 1, 1)
        for b in range(2):
            rows = slice(b * TOK_DEV, (b + 1) * TOK_DEV)
            out_ref[b] = out[rows] if k == 0 else out_ref[b] + out[rows]
            dh_ref[b] = dh[rows] if k == 0 else dh_ref[b] + dh[rows]


def shared_rows(h_pair, g_pair, w_own, w_far):
    rows = jax.ShapeDtypeStruct((2, TOK_DEV, D), F32)
    vmem = pl.BlockSpec(memory_space=pltpu.VMEM)
    return pl.pallas_call(
        shared_kernel,
        out_shape=(rows, rows),
        in_specs=[vmem] * 6,
        out_specs=(vmem, vmem),
        scratch_shapes=[
            pltpu.VMEM((2 * TOK_DEV, D), BF),
            pltpu.VMEM((2 * TOK_DEV, D), BF),
        ],
        compiler_params=pltpu.CompilerParams(vmem_limit_bytes=VMEM_LIMIT),
        cost_estimate=microseconds(8),
        name="shared_rows",
    )(*h_pair, *g_pair, w_own, w_far)


def start_parts(h_parts, g_parts, h_buf, g_buf, sems):
    per = h_parts[0].shape[0]
    copies = []
    for i in range(len(h_parts)):
        into = pl.ds(i * per, per)
        copies.append(
            (
                pltpu.make_async_copy(h_parts[i], h_buf.at[into], sems.at[0, i]),
                pltpu.make_async_copy(g_parts[i], g_buf.at[into], sems.at[1, i]),
            )
        )
    for pair in copies:
        for one in pair:
            one.start()
    return copies


def expert_slice_kernel(parts, more, pos_ref, *refs):
    h_parts, g_parts = refs[:parts], refs[parts : 2 * parts]
    weights = refs[2 * parts : 2 * parts + 3]
    refs = refs[2 * parts + 3 :]
    sums, refs = refs[: 3 * more], refs[3 * more :]
    og_ref, ou_ref, od_ref, h_buf, g_buf, x_sc, gd_sc, rank_sc, prob_sc = refs[:9]
    wg_ref, wu_ref, wd_ref, sems, w_sems = refs[9:]
    base = pos_ref[0]
    experts, _, width = wg_ref.shape
    per = h_parts[0].shape[0]
    copies = start_parts(h_parts, g_parts, h_buf, g_buf, sems)
    cols = pl.ds(pl.multiple_of(pos_ref[1] * width, width), width)
    loads = [
        pltpu.make_async_copy(weights[0].at[:, :, cols], wg_ref, w_sems.at[0]),
        pltpu.make_async_copy(weights[1].at[:, :, cols], wu_ref, w_sems.at[1]),
        pltpu.make_async_copy(weights[2].at[:, cols, :], wd_ref, w_sems.at[2]),
    ]
    for i in range(3 * more):
        loads.append(
            pltpu.make_async_copy(sums[i], (og_ref, ou_ref, od_ref)[i], w_sems.at[3 + i])
        )
    for one in loads:
        one.start()

    def dispatch(pair, carry):
        both_x, both_g = [], []
        for k in range(2):
            b = 2 * pair + k
            rank_sc[k] = g_buf[b, TOK_DEV:, :TOK_DEV].astype(F32)
            prob_sc[k] = h_buf[b, TOK_DEV:, :TOK_DEV].astype(F32) + h_buf[
                b, TOK_DEV:, TOK_DEV:
            ].astype(F32)
            hots, gates = [], []
            for i in range(experts):
                hot = one_hot_rows(rank_sc[k, pl.ds(base + i, 1), :])
                gates.append(
                    jnp.sum(hot * prob_sc[k, pl.ds(base + i, 1), :], -1, keepdims=True)
                )
                hots.append(hot)
            hot = jnp.concatenate(hots, 0).astype(BF)
            both_x.append(jnp.dot(hot, h_buf[b, :TOK_DEV, :], preferred_element_type=F32))
            both_g.append(
                jnp.dot(hot, g_buf[b, :TOK_DEV, :], preferred_element_type=F32)
                * jnp.concatenate(gates, 0)
            )
        into = pl.ds(pl.multiple_of(pair * 2 * SLOT, 2 * SLOT), 2 * SLOT)
        for i in range(experts):
            span = slice(i * SLOT, (i + 1) * SLOT)
            x_sc[i, into, :] = jnp.concatenate([v[span] for v in both_x], 0).astype(BF)
            gd_sc[i, into, :] = jnp.concatenate([v[span] for v in both_g], 0).astype(BF)
        return carry

    for i in range(parts):
        for one in copies[i]:
            one.wait()
        lax.fori_loop(i * per // 2, (i + 1) * per // 2, dispatch, 0)
    for one in loads:
        one.wait()

    def products(i, carry):
        rows = x_sc[i]
        gate_pre = jnp.dot(rows, wg_ref[i], preferred_element_type=F32)
        up_pre = jnp.dot(rows, wu_ref[i], preferred_element_type=F32)
        back = contract(gd_sc[i], wd_ref[i], 1, 1)
        swish, slope = swish_parts(gate_pre)
        inner = (swish * up_pre).astype(BF)
        dgate_pre = (back * up_pre * slope).astype(BF)
        dup_pre = (back * swish).astype(BF)
        add_g = contract(rows, dgate_pre, 0, 0)
        add_u = contract(rows, dup_pre, 0, 0)
        add_d = contract(inner, gd_sc[i], 0, 0)
        if more:
            og_ref[i] += add_g
            ou_ref[i] += add_u
            od_ref[i] += add_d
        else:
            og_ref[i], ou_ref[i], od_ref[i] = add_g, add_u, add_d
        return carry

    lax.fori_loop(0, experts, products, 0)


def expert_slice_grads(pos, h_parts, g_parts, w_gate, w_up, w_down, width, sums=()):
    parts, per = len(h_parts), h_parts[0].shape[0]
    experts = w_gate.shape[0]
    blocks = parts * per
    shapes = ((experts, D, width), (experts, D, width), (experts, width, D))
    vmem = pl.BlockSpec(memory_space=pltpu.VMEM)
    anywhere = pl.BlockSpec(memory_space=pl.ANY)
    return pl.pallas_call(
        functools.partial(expert_slice_kernel, parts, len(sums) // 3),
        out_shape=tuple(jax.ShapeDtypeStruct(s, F32) for s in shapes),
        in_specs=[pl.BlockSpec(memory_space=pltpu.SMEM)]
        + [anywhere] * (2 * parts + 3 + len(sums)),
        out_specs=(vmem,) * 3,
        scratch_shapes=[
            pltpu.VMEM((blocks, ROWS, D), BF),
            pltpu.VMEM((blocks, ROWS, D), BF),
            pltpu.VMEM((experts, blocks * SLOT, D), BF),
            pltpu.VMEM((experts, blocks * SLOT, D), BF),
            pltpu.VMEM((2, EXPERTS, TOK_DEV), F32),
            pltpu.VMEM((2, EXPERTS, TOK_DEV), F32),
        ]
        + [pltpu.VMEM(s, BF) for s in shapes]
        + [
            pltpu.SemaphoreType.DMA((2, parts)),
            pltpu.SemaphoreType.DMA((6,)),
        ],
        compiler_params=pltpu.CompilerParams(vmem_limit_bytes=VMEM_LIMIT),
        cost_estimate=microseconds(31),
        name="expert_slice_grads",
    )(pos, *h_parts, *g_parts, w_gate, w_up, w_down, *sums)


def shared_slice_kernel(parts, more, pos_ref, *refs):
    h_parts, g_parts = refs[:parts], refs[parts : 2 * parts]
    w_ref = refs[2 * parts]
    refs = refs[2 * parts + 1 :]
    sums, refs = refs[: 3 * more], refs[3 * more :]
    og_ref, ou_ref, od_ref, h_buf, g_buf, inner_sc, wg_ref, wu_ref, wd_ref, sems = refs
    per = h_parts[0].shape[0]
    copies = start_parts(h_parts, g_parts, h_buf, g_buf, sems)
    wg_ref[...] = w_ref[:, :, :256].reshape(D, 256)
    wu_ref[...] = w_ref[:, :, 256:512].reshape(D, 256)
    for i in range(3):
        wd_ref[:, 256 * i : 256 * (i + 1)] = w_ref[:, 64 * i : 64 * (i + 1), 512:].reshape(256, 256)
    window = pl.ds(pl.multiple_of(pos_ref[0] * 128, 128), og_ref.shape[0])
    lanes = pl.ds(pl.multiple_of(pos_ref[1] * 128, 128), od_ref.shape[0])
    for i, out_ref in enumerate((og_ref, ou_ref, od_ref)):
        out_ref[...] = sums[i][...] if more else jnp.zeros_like(out_ref)

    def two(buf, pair, cols=slice(None)):
        return jnp.concatenate([buf[2 * pair + k, :TOK_DEV, cols] for k in range(2)], 0)

    def products(pair, carry):
        rows, grads = two(h_buf, pair), two(g_buf, pair)
        gate_pre = jnp.dot(rows, wg_ref[...], preferred_element_type=F32)
        up_pre = jnp.dot(rows, wu_ref[...], preferred_element_type=F32)
        back = contract(grads, wd_ref[...], 1, 1)
        swish, slope = swish_parts(gate_pre)
        inner_sc[...] = (swish * up_pre).astype(BF)
        dgate_pre = (back * up_pre * slope).astype(BF)
        dup_pre = (back * swish).astype(BF)
        picked = two(h_buf, pair, window)
        og_ref[...] += contract(picked, dgate_pre, 0, 0)
        ou_ref[...] += contract(picked, dup_pre, 0, 0)
        od_ref[...] += contract(inner_sc[:, lanes], grads, 0, 0)
        return carry

    for i in range(parts):
        for one in copies[i]:
            one.wait()
        lax.fori_loop(i * per // 2, (i + 1) * per // 2, products, 0)


def shared_slice_grads(pos, h_parts, g_parts, weights, sums=()):
    parts, per = len(h_parts), h_parts[0].shape[0]
    blocks = parts * per
    width = 256
    vmem = pl.BlockSpec(memory_space=pltpu.VMEM)
    anywhere = pl.BlockSpec(memory_space=pl.ANY)
    return pl.pallas_call(
        functools.partial(shared_slice_kernel, parts, len(sums) // 3),
        out_shape=(
            jax.ShapeDtypeStruct((256, width), F32),
            jax.ShapeDtypeStruct((256, width), F32),
            jax.ShapeDtypeStruct((128, D), F32),
        ),
        in_specs=[pl.BlockSpec(memory_space=pltpu.SMEM)]
        + [anywhere] * (2 * parts)
        + [vmem] * (1 + len(sums)),
        out_specs=(vmem,) * 3,
        scratch_shapes=[
            pltpu.VMEM((blocks, ROWS, D), BF),
            pltpu.VMEM((blocks, ROWS, D), BF),
            pltpu.VMEM((2 * TOK_DEV, width), BF),
            pltpu.VMEM((D, width), BF),
            pltpu.VMEM((D, width), BF),
            pltpu.VMEM((width, D), BF),
            pltpu.SemaphoreType.DMA((2, parts)),
        ],
        compiler_params=pltpu.CompilerParams(vmem_limit_bytes=VMEM_LIMIT),
        cost_estimate=microseconds(20),
        name="shared_slice_grads",
    )(pos, *h_parts, *g_parts, weights, *sums)


def pair_sum(kept, received):
    return (kept.astype(F32) + received.astype(F32)).astype(BF)


def halves(value, bit):
    width = value.shape[-1] // 2
    low, high = value[..., :width], value[..., width:]
    return jnp.where(bit == 0, low, high), jnp.where(bit == 0, high, low)


def rejoin(own, other, bit):
    return jnp.where(
        bit == 0, jnp.concatenate([own, other], -1), jnp.concatenate([other, own], -1)
    )


def lane_halves():
    lane = lax.broadcasted_iota(jnp.int32, (1, 128), 1)
    return [(lane < 64).astype(F32).astype(BF), (lane >= 64).astype(F32).astype(BF)]


def pick_lanes(first, second):
    lane = lax.broadcasted_iota(jnp.int32, first.shape, 1)
    return jnp.where(lane < 64, first, second)


def turned(value, cos, sin):
    lane = lax.broadcasted_iota(jnp.int32, value.shape, 1)
    partner = jnp.where(lane % 64 < 32, pltpu.roll(value, 96, 1), pltpu.roll(value, 32, 1))
    return value * cos + partner * sin


def causal_mask(rows):
    row = lax.broadcasted_iota(jnp.int32, (rows, rows), 0)
    col = lax.broadcasted_iota(jnp.int32, (rows, rows), 1)
    return row, col


def unit_rms(value):
    return lax.rsqrt(jnp.mean(value * value, -1, keepdims=True) + EPS)


def softmax_of(first, second=None):
    top = jnp.max(first, -1, keepdims=True)
    if second is not None:
        top = jnp.maximum(top, jnp.max(second, -1, keepdims=True))
    first = jnp.exp(first - top)
    total = jnp.sum(first, -1, keepdims=True)
    if second is None:
        return first * (1.0 / total)
    second = jnp.exp(second - top)
    scale = 1.0 / (total + jnp.sum(second, -1, keepdims=True))
    return first * scale, second * scale


def attention_kernel(place_ref, *refs):
    w_parts = refs[:8]
    (
        own_ref,
        far_ref,
        gain1_ref,
        gain2_ref,
        router_ref,
        cos_ref,
        sin_ref,
        w_ref,
        q_ref,
        k_ref,
        v_ref,
        h1_ref,
        o_ref,
        x1_ref,
        h2_ref,
        h_sc,
        sems,
    ) = refs[8:]
    copies = []
    for part in range(8):
        for slot in range(4):
            rows = pl.ds(pl.multiple_of(place_ref[8 + slot] * 192, 192), 192)
            copies.append(
                pltpu.make_async_copy(
                    w_parts[part].at[slot, :192, :],
                    w_ref.at[place_ref[part], rows, :],
                    sems.at[part, slot],
                )
            )
    for one in copies:
        one.start()
    inputs = own_ref[:TOK_DEV, :].astype(F32)
    h_sc[:TOK_DEV, :] = (inputs * unit_rms(inputs) * gain1_ref[...]).astype(BF)
    far = far_ref[:TOK_DEV, :].astype(F32)
    h_sc[TOK_DEV:, :] = (far * unit_rms(far) * gain1_ref[...]).astype(BF)
    h1_ref[...] = h_sc[:TOK_DEV, :]
    for one in copies:
        one.wait()
    for i in range(6):
        out_ref = (q_ref, k_ref, v_ref)[i // 2]
        product = jnp.dot(h_sc[...], w_ref[i], preferred_element_type=F32)
        for slab in range(3):
            at = (i % 2) * 384 + slab * 128
            for half in range(2):
                rows = slice(half * TOK_DEV, (half + 1) * TOK_DEV)
                value = product[rows, slab * 128 : (slab + 1) * 128]
                if i < 4:
                    value = turned(value, cos_ref[...], sin_ref[...])
                out_ref[rows, at : at + 128] = value.astype(BF)
    masks = lane_halves()
    row, col = causal_mask(PROMPT)
    prompt_ok = col <= row
    row, col = causal_mask(CONT * CLEN)
    cont_ok = (row // CLEN == col // CLEN) & (col <= row)
    row = lax.broadcasted_iota(jnp.int32, (CONT * CLEN, 1), 0)
    reads_far = jnp.where(row < CLEN, place_ref[12], place_ref[13]).astype(F32)
    own_c = slice(PROMPT, TOK_DEV)
    far_p = slice(TOK_DEV, TOK_DEV + PROMPT)

    def heads(pair, carry):
        cols = pl.ds(pl.multiple_of(pair * 128, 128), 128)
        q_p, k_p, v_p = q_ref[:PROMPT, cols], k_ref[:PROMPT, cols], v_ref[:PROMPT, cols]
        q_c, k_c, v_c = q_ref[own_c, cols], k_ref[own_c, cols], v_ref[own_c, cols]
        k_f, v_f = k_ref[far_p, cols], v_ref[far_p, cols]
        out_p, out_c = [], []
        for mask in masks:
            score = jnp.where(prompt_ok, 0.125 * contract(q_p * mask, k_p, 1, 1), -1e30)
            out_p.append(
                jnp.dot(softmax_of(score).astype(BF), v_p, preferred_element_type=F32)
            )
            query = q_c * mask
            near, far = contract(query, k_p, 1, 1), contract(query, k_f, 1, 1)
            first = 0.125 * jnp.where(reads_far > 0.5, far, near)
            second = jnp.where(cont_ok, 0.125 * contract(query, k_c, 1, 1), -1e30)
            first, second = softmax_of(first, second)
            out_c.append(
                jnp.dot((first * (1.0 - reads_far)).astype(BF), v_p, preferred_element_type=F32)
                + jnp.dot((first * reads_far).astype(BF), v_f, preferred_element_type=F32)
                + jnp.dot(second.astype(BF), v_c, preferred_element_type=F32)
            )
        o_ref[:PROMPT, cols] = pick_lanes(*out_p).astype(BF)
        o_ref[own_c, cols] = pick_lanes(*out_c).astype(BF)
        return carry

    lax.fori_loop(0, HEADS // 2, heads, 0)
    for i in range(2):
        cols = slice(384 * i, 384 * (i + 1))
        x1_ref[:, cols] = own_ref[:TOK_DEV, cols].astype(F32) + jnp.dot(
            o_ref[...], w_ref[6 + i], preferred_element_type=F32
        )
    resid = x1_ref[...]
    hidden = (resid * unit_rms(resid) * gain2_ref[...]).astype(BF)
    h2_ref[:TOK_DEV, :] = hidden
    logits = contract(router_ref[...], hidden, 1, 1)
    logits = jnp.exp(logits - jnp.max(logits, 0, keepdims=True))
    probs = logits / jnp.sum(logits, 0, keepdims=True)
    high = probs.astype(BF)
    h2_ref[TOK_DEV:, :TOK_DEV] = high
    h2_ref[TOK_DEV:, TOK_DEV:] = (probs - high.astype(F32)).astype(BF)


def attention_forward(place, w_parts, own, far, gain1, gain2, router_t, cos, sin):
    vmem = pl.BlockSpec(memory_space=pltpu.VMEM)
    shape = jax.ShapeDtypeStruct
    return pl.pallas_call(
        attention_kernel,
        out_shape=(
            shape((8, D, 384), BF),
            shape((2 * TOK_DEV, D), BF),
            shape((2 * TOK_DEV, D), BF),
            shape((2 * TOK_DEV, D), BF),
            shape((TOK_DEV, D), BF),
            shape((TOK_DEV, D), BF),
            shape((TOK_DEV, D), F32),
            shape((ROWS, D), BF),
        ),
        in_specs=[pl.BlockSpec(memory_space=pltpu.SMEM)]
        + [pl.BlockSpec(memory_space=pl.ANY)] * 8
        + [vmem] * 7,
        out_specs=(vmem,) * 8,
        scratch_shapes=[
            pltpu.VMEM((2 * TOK_DEV, D), BF),
            pltpu.SemaphoreType.DMA((8, 4)),
        ],
        compiler_params=pltpu.CompilerParams(vmem_limit_bytes=VMEM_LIMIT),
        cost_estimate=microseconds(20),
        name="attention_forward",
    )(place, *w_parts, own, far, gain1, gain2, router_t, cos, sin)


def branch_kernel(
    dx_a_ref,
    dx_b_ref,
    h2_ref,
    x1_ref,
    g_ref,
    gain2_ref,
    router_ref,
    o_ref,
    w_ref,
    dx1_ref,
    do_ref,
    do_c_ref,
    gwo_ref,
    grouter_ref,
    ggain_ref,
):
    tail = dx_a_ref[TOK_DEV:, :].astype(F32) + dx_b_ref[TOK_DEV:, :].astype(F32)
    drp = tail[:, :TOK_DEV] + tail[:, TOK_DEV:]
    probs = h2_ref[TOK_DEV:, :TOK_DEV].astype(F32) + h2_ref[TOK_DEV:, TOK_DEV:].astype(F32)
    dlogits = (probs * (drp - jnp.sum(probs * drp, 0, keepdims=True))).astype(BF)
    hidden = h2_ref[:TOK_DEV, :]
    grouter_ref[...] = jnp.dot(dlogits, hidden, preferred_element_type=F32)
    dh2 = (
        dx_a_ref[:TOK_DEV, :].astype(F32)
        + dx_b_ref[:TOK_DEV, :].astype(F32)
        + contract(dlogits, router_ref[...], 0, 0)
    )
    resid = x1_ref[...]
    scale = unit_rms(resid)
    normed = resid * scale
    ggain_ref[...] = jnp.sum(dh2 * normed, 0, keepdims=True)
    dnormed = dh2 * gain2_ref[...]
    dx1 = scale * (dnormed - normed * jnp.mean(dnormed * normed, -1, keepdims=True)) + g_ref[
        ...
    ].astype(F32)
    dx1_ref[...] = dx1
    datt = dx1.astype(BF)
    do_ref[...] = (
        contract(datt[:, :384], w_ref[0], 1, 1) + contract(datt[:, 384:], w_ref[1], 1, 1)
    ).astype(BF)
    do_c_ref[...] = do_ref[PROMPT:, :]
    gwo_ref[...] = contract(o_ref[...], datt, 0, 0).astype(BF)


def branch_backward(dx_a, dx_b, h_block, x1, grad, gain2, router_t, o, w_all):
    shape = jax.ShapeDtypeStruct
    whole = lambda *dims: pl.BlockSpec(dims, lambda i: (0,) * len(dims))
    rows = whole(TOK_DEV, D)
    return pl.pallas_call(
        branch_kernel,
        grid=(1,),
        out_shape=(
            shape((TOK_DEV, D), F32),
            shape((TOK_DEV, D), BF),
            shape((TOK_DEV - PROMPT, D), BF),
            shape((D, D), BF),
            shape((EXPERTS, D), F32),
            shape((1, D), F32),
        ),
        in_specs=[
            whole(ROWS, D),
            whole(ROWS, D),
            whole(ROWS, D),
            rows,
            rows,
            whole(1, D),
            whole(EXPERTS, D),
            rows,
            pl.BlockSpec((2, D, 384), lambda i: (3, 0, 0)),
        ],
        out_specs=(
            rows,
            rows,
            whole(TOK_DEV - PROMPT, D),
            whole(D, D),
            whole(EXPERTS, D),
            whole(1, D),
        ),
        compiler_params=pltpu.CompilerParams(vmem_limit_bytes=VMEM_LIMIT),
        cost_estimate=microseconds(6),
        name="branch_backward",
    )(dx_a, dx_b, h_block, x1, grad, gain2, router_t, o, w_all)


def attention_back_kernel(
    flags_ref,
    q_ref,
    k_ref,
    v_ref,
    do_ref,
    do_far_ref,
    h1_ref,
    w_ref,
    own_ref,
    gain1_ref,
    cos_ref,
    sin_ref,
    dx1_ref,
    gwo_ref,
    grouter_ref,
    ggain2_ref,
    gtok_ref,
    keep_ref,
    send_ref,
    dq_sc,
    dk_sc,
    dv_sc,
    low_sc,
):
    masks = lane_halves()
    row, col = causal_mask(PROMPT)
    prompt_ok = col <= row
    cont_ok = (row // CLEN == col // CLEN) & (col <= row)
    row = lax.broadcasted_iota(jnp.int32, (4 * CLEN, 1), 0) // CLEN
    near = jnp.where(
        row < 2,
        jnp.where(row == 0, flags_ref[0], flags_ref[1]),
        jnp.where(row == 2, flags_ref[2], flags_ref[3]),
    ).astype(F32)
    own_c = slice(PROMPT, TOK_DEV)
    far_p = slice(TOK_DEV, TOK_DEV + PROMPT)
    far_c = slice(TOK_DEV + PROMPT, 2 * TOK_DEV)
    cont = CONT * CLEN

    def either(own_near, far_own):
        return jnp.concatenate(
            [jnp.where(near[:cont] > 0.5, own_near[:cont], far_own), own_near[cont:]], 0
        )

    def heads(pair, carry):
        cols = pl.ds(pl.multiple_of(pair * 128, 128), 128)
        q_p, k_p, v_p = q_ref[:PROMPT, cols], k_ref[:PROMPT, cols], v_ref[:PROMPT, cols]
        k_f, v_f = k_ref[far_p, cols], v_ref[far_p, cols]
        q_c, k_c, v_c = q_ref[own_c, cols], k_ref[own_c, cols], v_ref[own_c, cols]
        do_p, do_c = do_ref[:PROMPT, cols], do_ref[own_c, cols]
        q_4 = jnp.concatenate([q_c, q_ref[far_c, cols]], 0)
        k_4 = jnp.concatenate([k_c, k_ref[far_c, cols]], 0)
        v_4 = jnp.concatenate([v_c, v_ref[far_c, cols]], 0)
        do_4 = jnp.concatenate([do_c, do_far_ref[:, cols]], 0)
        q_all = jnp.concatenate([q_p, q_4], 0)
        do_all = jnp.concatenate([do_p, do_4], 0)
        dq_p, dq_c, dk_p, dk_c, dv_p, dv_c = [], [], [], [], [], []
        for mask in masks:
            score = jnp.where(prompt_ok, 0.125 * contract(q_p * mask, k_p, 1, 1), -1e30)
            prob = softmax_of(score)
            dprob = contract(do_p * mask, v_p, 1, 1)
            ds = (prob * (dprob - jnp.sum(prob * dprob, -1, keepdims=True))).astype(BF)
            query, grad = q_4 * mask, do_4 * mask
            first = 0.125 * either(
                contract(query, k_p, 1, 1), contract(query[:cont], k_f, 1, 1)
            )
            second = jnp.where(cont_ok, 0.125 * contract(query, k_4, 1, 1), -1e30)
            first, second = softmax_of(first, second)
            dfirst = either(contract(grad, v_p, 1, 1), contract(grad[:cont], v_f, 1, 1))
            dsecond = contract(grad, v_4, 1, 1)
            mean = jnp.sum(first * dfirst, -1, keepdims=True) + jnp.sum(
                second * dsecond, -1, keepdims=True
            )
            ds1 = first * (dfirst - mean)
            ds2 = (second * (dsecond - mean)).astype(BF)[:cont, :cont]
            ds_near = (ds1 * near).astype(BF)
            ds_far = (ds1 * (1.0 - near)).astype(BF)[:cont]
            p_near = (first * near).astype(BF)
            p_own = second.astype(BF)[:cont, :cont]
            dq_p.append(jnp.dot(ds, k_p, preferred_element_type=F32))
            dq_c.append(
                jnp.dot(ds_near[:cont], k_p, preferred_element_type=F32)
                + jnp.dot(ds_far, k_f, preferred_element_type=F32)
                + jnp.dot(ds2, k_c, preferred_element_type=F32)
            )
            dk_p.append(contract(jnp.concatenate([ds, ds_near], 0), q_all, 0, 0))
            dv_p.append(contract(jnp.concatenate([prob.astype(BF), p_near], 0), do_all, 0, 0))
            dk_c.append(contract(ds2, q_c, 0, 0))
            dv_c.append(contract(p_own, do_c, 0, 0))
        for out, prompt_part, cont_part in (
            (dq_sc, dq_p, dq_c),
            (dk_sc, dk_p, dk_c),
            (dv_sc, dv_p, dv_c),
        ):
            out[:PROMPT, cols] = pick_lanes(*prompt_part)
            out[own_c, cols] = pick_lanes(*cont_part)
        return carry

    lax.fori_loop(0, HEADS // 2, heads, 0)

    def put(owner, at, product):
        for z in range(4):
            rows = product[z * (D // 4) : (z + 1) * (D // 4), :]

            @pl.when(flags_ref[4] == owner)
            def _():
                keep_ref[z, : D // 4, at : at + D] = rows

            @pl.when(flags_ref[4] != owner)
            def _():
                send_ref[z, : D // 4, at : at + D] = rows

    dh1 = None
    for i, source in enumerate((dq_sc, dk_sc, dv_sc)):
        for slab in range(6):
            cols = slice(slab * 128, (slab + 1) * 128)
            value = source[:, cols]
            if i < 2:
                value = turned(0.125 * value, cos_ref[...], -sin_ref[...])
            low_sc[:, cols] = value.astype(BF)
        grads = low_sc[...]
        product = contract(h1_ref[...], grads, 0, 0).astype(BF)
        put(i // 2, (i % 2) * D, product)
        for half in range(2):
            part = contract(grads[:, 384 * half : 384 * (half + 1)], w_ref[2 * i + half], 1, 1)
            dh1 = part if dh1 is None else dh1 + part
    put(1, D, gwo_ref[...])
    inputs = own_ref[:TOK_DEV, :].astype(F32)
    scale = unit_rms(inputs)
    normed = inputs * scale
    ggain1 = jnp.sum(dh1 * normed, 0, keepdims=True)
    gains = jnp.concatenate([ggain1, ggain2_ref[...], jnp.zeros((EXT - 2, D), F32)], 0)
    keep_ref[:, D // 4 :, :] = jnp.zeros((4, EXT, 2 * D), BF)
    send_ref[:, D // 4 :, :] = jnp.zeros((4, EXT, 2 * D), BF)
    for z in range(4):
        cols = slice(z * (D // 4), (z + 1) * (D // 4))
        extras = jnp.concatenate([grouter_ref[:, cols], gains[:, cols]], 1).astype(BF)

        @pl.when(flags_ref[4] == 0)
        def _():
            keep_ref[z, D // 4 :, : 2 * (D // 4)] = extras

        @pl.when(flags_ref[4] != 0)
        def _():
            send_ref[z, D // 4 :, : 2 * (D // 4)] = extras

    dnormed = dh1 * gain1_ref[...]
    gtok_ref[...] = (
        scale * (dnormed - normed * jnp.mean(dnormed * normed, -1, keepdims=True)) + dx1_ref[...]
    )


def attention_backward(
    flags, q, k, v, do, do_far, h1, w_all, own, gain1, cos, sin, dx1, gwo, grouter, ggain2
):
    shape = jax.ShapeDtypeStruct
    whole = lambda *dims: pl.BlockSpec(dims, lambda i: (0,) * len(dims))
    rows = whole(TOK_DEV, D)
    both = whole(2 * TOK_DEV, D)
    packed = (4, D // 4 + EXT, 2 * D)
    return pl.pallas_call(
        attention_back_kernel,
        grid=(1,),
        out_shape=(
            shape((TOK_DEV, D), F32),
            shape(packed, BF),
            shape(packed, BF),
        ),
        in_specs=[
            pl.BlockSpec(memory_space=pltpu.SMEM),
            both,
            both,
            both,
            rows,
            whole(TOK_DEV - PROMPT, D),
            rows,
            whole(6, D, 384),
            whole(ROWS, D),
            whole(1, D),
            whole(TOK_DEV, 128),
            whole(TOK_DEV, 128),
            rows,
            whole(D, D),
            whole(EXPERTS, D),
            whole(1, D),
        ],
        out_specs=(rows, whole(*packed), whole(*packed)),
        scratch_shapes=[
            pltpu.VMEM((TOK_DEV, D), F32),
            pltpu.VMEM((TOK_DEV, D), F32),
            pltpu.VMEM((TOK_DEV, D), F32),
            pltpu.VMEM((TOK_DEV, D), BF),
        ],
        compiler_params=pltpu.CompilerParams(vmem_limit_bytes=VMEM_LIMIT),
        cost_estimate=microseconds(23),
        name="attention_backward",
    )(flags, q, k, v, do, do_far, h1, w_all, own, gain1, cos, sin, dx1, gwo, grouter, ggain2)


def after(value, *earlier):
    return lax.optimization_barrier((value, earlier))[0]


def place_kernel(every_ref, gate_ref, up_ref, down_ref):
    for out_ref, at in ((gate_ref, 0), (up_ref, 256)):
        for k in range(4):
            for p in range(0, 8, 2):
                pair = [
                    every_ref[p + i, :, at + 64 * k : at + 64 * (k + 1)].astype(F32)
                    for i in range(2)
                ]
                to = 512 * k + 64 * p
                out_ref[:, to : to + 128] = jnp.concatenate(pair, 1)
    for p in range(8):
        for i in range(3):
            down_ref[64 * p : 64 * (p + 1), 256 * i : 256 * (i + 1)] = every_ref[
                p, 64 * i : 64 * (i + 1), 512:
            ].astype(F32)


def place_shared(every):
    vmem = pl.BlockSpec(memory_space=pltpu.VMEM)
    return pl.pallas_call(
        place_kernel,
        out_shape=(
            jax.ShapeDtypeStruct((D // 4, 2048), F32),
            jax.ShapeDtypeStruct((D // 4, 2048), F32),
            jax.ShapeDtypeStruct((512, D), F32),
        ),
        in_specs=[vmem],
        out_specs=(vmem,) * 3,
        compiler_params=pltpu.CompilerParams(vmem_limit_bytes=VMEM_LIMIT),
        cost_estimate=microseconds(4),
        name="place_shared",
    )(every)


def reduce_step(total, over, bit):
    kept, sent = halves(total, bit)
    return kept, over(sent)


def reduce_dp(total, z):
    result = lax.dynamic_index_in_dim(total, z, 0, keepdims=False).astype(F32)
    for step in (1, 2, 3):
        out = lax.dynamic_index_in_dim(total, lax.rem(z + step, 4), 0, keepdims=False)
        result = result + over_z(out, step).astype(F32)
    return result.astype(BF)


def tuned_body(
    tokens,
    cotangent,
    routes,
    prompt_ids,
    attn_gain,
    query_weight,
    key_weight,
    value_weight,
    output_weight,
    ffn_gain,
    router_weight,
    shared_gate,
    shared_up,
    shared_down,
    expert_gate,
    expert_up_weight,
    expert_down,
):
    z, y, j = lax.axis_index("dp"), lax.axis_index("context"), lax.axis_index("experts")
    x, core = j // 2, j % 2
    plane = y * 4 + j
    shard = D // 4

    dense = jnp.concatenate([query_weight, key_weight, value_weight, output_weight], 1)
    dense = lax.dynamic_slice_in_dim(dense, plane * 384, 384, 1)
    gains = jnp.concatenate(
        [attn_gain[None], ffn_gain[None], jnp.zeros((EXT - 2, shard), BF)], 0
    )
    dense = jnp.concatenate([dense, jnp.concatenate([router_weight.T, gains], 1)], 0)
    dense_z = [over_z(dense, step) for step in (1, 2, 3)]

    ids = jnp.broadcast_to(prompt_ids.astype(BF)[:, None], (CONT, D))
    own = jnp.concatenate([tokens, ids, jnp.zeros((EXT - CONT, D), BF)], 0)
    far = moved(own, lambda z, y, x, c: (z, 1 - y, x, c))
    dense = jnp.stack([dense] + after(dense_z, far))
    dense_a, dense_b = over_a(dense), over_b(dense)
    dense_c = over_b(after(dense_a, dense_b))
    dense_parts = [dense, dense_a, dense_b, dense_c]
    dense_parts = dense_parts + [over_core(part) for part in dense_parts]
    far_ids = far[TOK_DEV : TOK_DEV + CONT, 0].astype(jnp.int32)

    expert_ids = jnp.arange(EXPERTS, dtype=jnp.int32)[:, None]
    route_t = routes.T
    member = (route_t[0:1] == expert_ids) | (route_t[1:2] == expert_ids)
    before = (jnp.arange(TOK_DEV)[:, None] < jnp.arange(TOK_DEV)[None, :]).astype(BF)
    ranks = jnp.dot(member.astype(BF), before, preferred_element_type=F32)
    ranks = jnp.where(member, ranks, -1.0).astype(BF)
    g_block = jnp.concatenate([cotangent, jnp.pad(ranks, ((0, 0), (0, D - TOK_DEV)))], 0)
    g_near = after(g_block, dense_c)
    g_a, g_b = over_a(g_near), over_b(g_near)
    g_x = jnp.where(core == 0, g_a, g_b)
    g_group = [g_block, g_x, over_core(g_block), over_core(g_x)]

    units = lambda w: lax.dynamic_index_in_dim(
        w.reshape(shard, 4, 8, 64), plane, 2, keepdims=False
    ).reshape(shard, 256)
    down = lax.dynamic_slice_in_dim(shared_down, plane * 64, 64, 0)
    down = jnp.concatenate([down[:, 256 * i : 256 * (i + 1)] for i in range(3)], 0)
    shared = jnp.concatenate([units(shared_gate), units(shared_up), down], 1)
    shared = lax.all_gather(after(shared, dense), "dp", axis=0, tiled=False)
    shared_far = moved(after(shared, dense_c), lambda z, y, x, c: (z, 1 - y, x, c))

    g_column = lax.all_gather(after(g_block, dense_a), "dp", axis=0, tiled=False)

    slots = dense[:, shard:, :]
    slots = jnp.stack([slots[0], slots[3], slots[2], slots[1]])
    small = lax.dynamic_slice_in_dim(
        jnp.concatenate([slots, slots], 0), lax.rem(4 - z, 4), 4, 0
    )
    router_t = small[:, :, :shard].transpose(1, 0, 2).reshape(EXPERTS, D)
    gain1 = small[:, 0, shard:].reshape(1, D).astype(F32)
    gain2 = small[:, 1, shard:].reshape(1, D).astype(F32)

    cos_table, sin_table = rotary_tables(TOK_DEV)
    cos = jnp.tile(cos_table, (1, 4))
    sin = jnp.tile(jnp.concatenate([-sin_table, sin_table], 1), (1, 2))
    flip_a, flip_b = jnp.where(core == 0, 2, 4), jnp.where(core == 0, 4, 2)
    flips = [0 * core, flip_a, flip_b, 0 * core + 6]
    flips = flips + [1 + flips[0], 1 + flip_b, 1 + flip_a, 1 + flips[3]]
    place = [jnp.bitwise_xor(plane, flip) for flip in flips]
    place += [lax.rem(z + 4 - slot, 4) for slot in range(4)]
    place += [(prompt_ids[m] != y) for m in range(CONT)]
    place = jnp.stack([v.astype(jnp.int32) for v in place])
    cos = after(cos, shared)
    w_all, q, k, v, h1, o, x1, h_block = attention_forward(
        place, dense_parts, own, far, gain1, gain2, router_t, cos, sin
    )

    h_block, x1 = after((h_block, x1), g_a, g_b)
    h_x = over_x(h_block)
    h_group = [h_block, h_x, over_core(h_block), over_core(h_x)]
    h_column = lax.all_gather(h_block, "dp", axis=0, tiled=False)
    experts_w = (expert_gate, expert_up_weight, expert_down)
    base = (j * 4).astype(jnp.int32)
    part = group_experts(base[None], 0, 2, h_group, g_group, (), *experts_w)
    near, far_group, part = after((h_group[::2], h_group[1::2], part), shared_far)
    more = shared_rows(near, g_group[::2], shared, shared_far)
    more += shared_rows(far_group, g_group[1::2], shared, shared_far)
    g_first = over_a(after(g_column, part))
    moe_near, moe_far, dx_near, dx_far = group_experts(
        base[None] + 2, 2, 2, h_group, g_group, (*more, *part), *experts_w
    )
    moe_near, moe_far, dx_near, dx_far = after((moe_near, moe_far, dx_near, dx_far), g_first)
    g_second = lax.all_gather(after(g_b, dx_near), "dp", axis=0, tiled=False)

    dx_pair = pair_sum(dx_near, over_core(dx_far))
    dx_there = over_x(dx_pair[1])
    window = jnp.array([0, 1, 3, 4], jnp.int32)[z]
    s_pos = jnp.stack([window, (z // 2).astype(jnp.int32)])
    e_pos = jnp.stack([base, (z * 2 + y).astype(jnp.int32)])
    h_column, g_column = after((h_column, g_column), dx_pair)
    h_core, g_core = [over_core(h_column)], [over_core(g_column)]
    s_sums = shared_slice_grads(
        s_pos, [h_column, h_core[0]], [g_column, g_core[0]], shared
    )
    gain2 = after(gain2, s_sums)
    dx1, do, do_c, gwo, grad_router_t, grad_gain2 = branch_backward(
        dx_pair[0], dx_there, h_block, x1, cotangent, gain2, router_t, o, w_all
    )
    do_far = moved(do_c, lambda z, y, x, c: (z, 1 - y, x, c))
    h_column, g_column, g_first = after((h_column, g_column, g_first), do_far)
    h_first = over_a(h_column)
    g_core.append(over_core(g_first))
    flags = jnp.concatenate([prompt_ids == y, far_ids == y, core[None] != 0]).astype(jnp.int32)
    grad_inputs, keep, send = attention_backward(
        flags,
        q,
        k,
        v,
        do,
        do_far,
        h1,
        w_all,
        own,
        gain1,
        cos,
        sin,
        dx1,
        gwo,
        grad_router_t,
        grad_gain2,
    )
    grad_inputs, keep, send = after(
        (grad_inputs, keep, send), h_first, g_core, g_second
    )
    g_third = lax.all_gather(after(over_b(after(g_a, near)), keep), "dp", axis=0, tiled=False)
    bit_a, bit_b = jnp.where(core == 0, x, y), jnp.where(core == 0, y, x)
    total = pair_sum(keep, over_core(send))
    h_core.append(over_core(h_first))
    kept, there = reduce_step(total, over_a, bit_a)

    h_parts, g_parts = [h_column, h_first] + h_core, [g_column, g_first] + g_core
    s_sums = shared_slice_grads(
        s_pos, [h_first, h_core[1]], [g_first, g_core[1]], shared, s_sums
    )
    s_sums, kept = after((s_sums, kept), there)
    kept, there = reduce_step(pair_sum(kept, there), over_b, bit_b)
    h_second, h_third = over_b(after(h_column, s_sums)), over_b(after(h_first, s_sums))
    e_sums = expert_slice_grads(after(e_pos, s_sums), h_parts, g_parts, *experts_w, 256)
    e_sums, kept, g_second, g_third = after(
        (e_sums, kept, g_second, g_third), there, h_second, h_third
    )
    z_own = pair_sum(kept, there)
    z_parts = [
        over_z(lax.dynamic_index_in_dim(z_own, lax.rem(z + step, 4), 0, keepdims=False), step)
        for step in (1, 2, 3)
    ]
    h_parts, g_parts = [h_second, h_third], [g_second, g_third]
    h_parts = h_parts + [over_core(part) for part in h_parts]
    g_parts = g_parts + [over_core(part) for part in g_parts]
    s_sums = shared_slice_grads(s_pos, h_parts, g_parts, shared, s_sums)
    s_gate, s_up, s_down = after(s_sums, z_parts)
    total = lax.dynamic_index_in_dim(z_own, z, 0, keepdims=False).astype(F32)
    for part in z_parts:
        total = total + part.astype(F32)
    total = after(total.astype(BF), s_gate)
    moe_near, moe_far = after((moe_near, moe_far), s_gate)
    moe_pair = pair_sum(moe_near, over_core(moe_far))
    moe_there = over_x(moe_pair[1])
    half_a, half_b = over_a(total), over_b(total)
    opposite = moved(total, lambda z, y, x, c: (z, 1 - y, 1 - x, c))
    lead = z * 192 - window * 128
    s_down = lax.dynamic_slice_in_dim(s_down, (z % 2) * 64, 64, 0)
    mine = jnp.concatenate(
        [
            lax.dynamic_slice_in_dim(s_gate, lead, 192, 0),
            lax.dynamic_slice_in_dim(s_up, lead, 192, 0),
            jnp.concatenate([s_down[:, 256 * i : 256 * (i + 1)] for i in range(3)], 0),
        ],
        1,
    ).astype(BF)
    every = lax.all_gather(mine, ("context", "experts"), axis=0, tiled=False)
    e_gate, e_up, e_down = expert_slice_grads(e_pos, h_parts, g_parts, *experts_w, 256, e_sums)
    e_gate, total = after((e_gate, total), half_a, half_b, opposite, moe_there, every)
    layer_out = (x1 + (moe_pair[0].astype(F32) + moe_there.astype(F32))).astype(BF)
    total = rejoin(rejoin(total, half_b, bit_b), rejoin(half_a, opposite, bit_b), bit_a)
    other = over_core(total)
    sum_qk, sum_vo = jnp.where(core == 0, total, other), jnp.where(core == 0, other, total)
    extras = sum_qk[shard:, : 2 * shard].astype(F32)
    sum_qk, sum_vo = sum_qk[:shard].astype(F32), sum_vo[:shard].astype(F32)

    s_gate, s_up, s_down = place_shared(every)
    return (
        layer_out,
        grad_inputs,
        extras[0, shard:],
        sum_qk[:, :D],
        sum_qk[:, D:],
        sum_vo[:, :D],
        sum_vo[:, D:],
        extras[1, shard:],
        extras[:, :shard].T,
        s_gate,
        s_up,
        s_down,
        e_gate,
        e_up,
        e_down,
    )


def solution(mesh):
    tuned = dict(mesh.shape) == TUNED_MESH

    return jax.shard_map(
        tuned_body if tuned else plain_body,
        mesh=mesh,
        in_specs=(
            P(("dp", "context", "experts"), None),
            P(("dp", "context", "experts"), None),
            P(("dp", "context", "experts"), None),
            P(("dp", "context", "experts")),
            P("dp"),
            P("dp", None),
            P("dp", None),
            P("dp", None),
            P("dp", None),
            P("dp"),
            P("dp", None),
            P("dp", None),
            P("dp", None),
            P("dp", None),
            P("experts", None, None),
            P("experts", None, None),
            P("experts", None, None),
        ),
        out_specs=(
            P(("dp", "context", "experts"), None),
            P(("dp", "context", "experts"), None),
            P("dp"),
            P("dp", None),
            P("dp", None),
            P("dp", None),
            P("dp", None),
            P("dp"),
            P("dp", None),
            P("dp", None),
            P("dp", None),
            P("dp", None),
            P("experts", None, ("dp", "context")),
            P("experts", None, ("dp", "context")),
            P("experts", ("dp", "context"), None),
        ),
        check_vma=False,
    )
```

```python
import functools

import jax
import jax.numpy as jnp
import numpy as np
from jax import lax
from jax.sharding import PartitionSpec as P

from jax.experimental import pallas as pl
from jax.experimental.pallas import tpu as pltpu

D = 768
HEADS = 12
HD = 64
EXPERTS = 16
TOPK = 2
PROMPT = 256
CONT = 2
CLEN = 64
TOK_DEV = 384
CAP = 66


EPS = 1e-06


def rotary_tables(tok_rows):
    row_ids = jnp.arange(tok_rows)
    position = jnp.where(row_ids < PROMPT, row_ids, PROMPT + (row_ids - PROMPT) % CLEN).astype(
        jnp.float32
    )
    frequency = 10000.0 ** (-2.0 * jnp.arange(HD // 2).astype(jnp.float32) / HD)
    angles = position[:, None] * frequency[None, :]
    return (jnp.cos(angles), jnp.sin(angles))


def rotate(values_in, cos_table, sin_table):
    shaped = values_in.reshape(values_in.shape[:-1] + (HEADS, HD))
    lower_half = shaped[..., : HD // 2]
    upper_half = shaped[..., HD // 2 :]
    cos_part = cos_table[:, None, :]
    sin_part = sin_table[:, None, :]
    turned = jnp.concatenate(
        [
            lower_half * cos_part - upper_half * sin_part,
            upper_half * cos_part + lower_half * sin_part,
        ],
        -1,
    )
    return turned.reshape(values_in.shape)


def key_mask(context_index, prompt_pick, contexts):
    row_ids = jnp.arange(TOK_DEV)[:, None]
    col_ids = jnp.arange(contexts * PROMPT + CONT * CLEN)[None, :]
    prompt_row = row_ids < PROMPT
    cont_row = (row_ids - PROMPT) // CLEN
    within_row = (row_ids - PROMPT) % CLEN
    owner = jnp.sum(
        prompt_pick[None, :] * (jnp.arange(CONT)[None, :] == cont_row), -1, keepdims=True
    )
    target = jnp.where(prompt_row, context_index, owner)
    prompt_keys = col_ids < contexts * PROMPT
    prompt_ok = (
        prompt_keys
        & (col_ids // PROMPT == target)
        & (jnp.logical_not(prompt_row) | (col_ids % PROMPT <= row_ids))
    )
    offset = col_ids - contexts * PROMPT
    cont_ok = (
        jnp.logical_not(prompt_keys)
        & jnp.logical_not(prompt_row)
        & (offset // CLEN == cont_row)
        & (offset % CLEN <= within_row)
    )
    return prompt_ok | cont_ok


def inner_rows(left, right):
    return lax.dot_general(
        left, right, (((0,), (0,)), ((), ())), preferred_element_type=jnp.float32
    )


def times_transposed(left, right):
    return lax.dot_general(
        left, right, (((1,), (1,)), ((), ())), preferred_element_type=jnp.float32
    )


def swish_derivative(pre_act):
    sigma = jax.nn.sigmoid(pre_act)
    return sigma * (1.0 + pre_act * (1.0 - sigma))


def plain_body(
    tokens,
    cotangent,
    routes,
    prompt_ids,
    attn_gain,
    query_weight,
    key_weight,
    value_weight,
    output_weight,
    ffn_gain,
    router_weight,
    shared_gate,
    shared_up,
    shared_down,
    expert_gate,
    expert_up_weight,
    expert_down,
):
    contexts = lax.axis_size("context")
    context_here = lax.axis_index("context")
    gain_one, w_query, w_key, w_value, w_out, gain_two, w_router, w_sgate, w_sup, w_sdown = (
        lax.all_gather(attn_gain, "dp", axis=0, tiled=True),
        lax.all_gather(query_weight, "dp", axis=0, tiled=True),
        lax.all_gather(key_weight, "dp", axis=0, tiled=True),
        lax.all_gather(value_weight, "dp", axis=0, tiled=True),
        lax.all_gather(output_weight, "dp", axis=0, tiled=True),
        lax.all_gather(ffn_gain, "dp", axis=0, tiled=True),
        lax.all_gather(router_weight, "dp", axis=0, tiled=True),
        lax.all_gather(shared_gate, "dp", axis=0, tiled=True),
        lax.all_gather(shared_up, "dp", axis=0, tiled=True),
        lax.all_gather(shared_down, "dp", axis=0, tiled=True),
    )
    cos_table, sin_table = rotary_tables(TOK_DEV)
    inputs = tokens.astype(jnp.float32)
    inv_rms1 = lax.rsqrt(jnp.mean(inputs * inputs, -1, keepdims=True) + EPS)
    normed1 = inputs * inv_rms1
    gain1_f = gain_one.astype(jnp.float32)
    hidden1 = (normed1 * gain1_f).astype(jnp.bfloat16)
    query_f = jnp.dot(hidden1, w_query, preferred_element_type=jnp.float32)
    key_f = jnp.dot(hidden1, w_key, preferred_element_type=jnp.float32)
    value_f = jnp.dot(hidden1, w_value, preferred_element_type=jnp.float32)
    query_b = rotate(query_f, cos_table, sin_table).astype(jnp.bfloat16)
    key_b = rotate(key_f, cos_table, sin_table).astype(jnp.bfloat16)
    value_b = value_f.astype(jnp.bfloat16)
    prompt_keys, prompt_values = (
        lax.all_gather(key_b[:PROMPT], "context", axis=0, tiled=True),
        lax.all_gather(value_b[:PROMPT], "context", axis=0, tiled=True),
    )
    keys_h = jnp.concatenate([prompt_keys, key_b[PROMPT:]], 0).reshape(-1, HEADS, HD)
    values_h = jnp.concatenate([prompt_values, value_b[PROMPT:]], 0).reshape(-1, HEADS, HD)
    query_h = query_b.reshape(TOK_DEV, HEADS, HD)
    allowed = key_mask(context_here, prompt_ids, contexts)
    scores = jnp.where(
        allowed[None],
        0.125 * jnp.einsum("qhd,khd->hqk", query_h, keys_h, preferred_element_type=jnp.float32),
        -1e30,
    )
    row_max = jnp.max(scores, -1, keepdims=True)
    exp_scores = jnp.exp(scores - row_max)
    row_total = jnp.sum(exp_scores, -1, keepdims=True)
    log_total = row_max + jnp.log(row_total)
    attn_probs = (exp_scores / row_total).astype(jnp.bfloat16)
    attended = (
        jnp.einsum("hqk,khd->qhd", attn_probs, values_h, preferred_element_type=jnp.float32)
        .reshape(TOK_DEV, D)
        .astype(jnp.bfloat16)
    )
    resid = inputs + jnp.dot(attended, w_out, preferred_element_type=jnp.float32)
    inv_rms2 = lax.rsqrt(jnp.mean(resid * resid, -1, keepdims=True) + EPS)
    normed2 = resid * inv_rms2
    gain2_f = gain_two.astype(jnp.float32)
    hidden2 = (normed2 * gain2_f).astype(jnp.bfloat16)
    logits = jnp.dot(hidden2, w_router, preferred_element_type=jnp.float32)
    route_probs = jax.nn.softmax(logits, -1)
    route_hot = (routes[:, :, None] == jnp.arange(EXPERTS)[None, None, :]).astype(jnp.float32)
    gate_vals = jnp.sum(route_probs[:, None, :] * route_hot, -1)
    shared_gpre = jnp.dot(hidden2, w_sgate, preferred_element_type=jnp.float32)
    shared_upre = jnp.dot(hidden2, w_sup, preferred_element_type=jnp.float32)
    shared_act = (jax.nn.silu(shared_gpre) * shared_upre).astype(jnp.bfloat16)
    shared_res = jnp.dot(shared_act, w_sdown, preferred_element_type=jnp.float32)
    flat_route = routes.reshape(-1)
    flat_hot = (flat_route[:, None] == jnp.arange(EXPERTS)[None, :]).astype(jnp.int32)
    slot_ids = jnp.sum((jnp.cumsum(flat_hot, 0) - flat_hot) * flat_hot, -1)
    slot_index = flat_route * CAP + slot_ids
    send_rows = jnp.repeat(hidden2, TOPK, axis=0)
    outgoing = (
        jnp.zeros((EXPERTS * CAP, D), jnp.bfloat16)
        .at[slot_index]
        .set(send_rows)
        .reshape(EXPERTS, CAP, D)
    )
    received_rows = lax.all_to_all(outgoing, "experts", split_axis=0, concat_axis=1, tiled=True)
    expert_gate_preact = jnp.einsum(
        "mgx,mxp->mgp", received_rows, expert_gate, preferred_element_type=jnp.float32
    )
    expert_up_preact = jnp.einsum(
        "mgx,mxp->mgp", received_rows, expert_up_weight, preferred_element_type=jnp.float32
    )
    expert_activation = (jax.nn.silu(expert_gate_preact) * expert_up_preact).astype(jnp.bfloat16)
    expert_res = jnp.einsum(
        "erf,efd->erd", expert_activation, expert_down, preferred_element_type=jnp.float32
    ).astype(jnp.bfloat16)
    returned = lax.all_to_all(
        expert_res, "experts", split_axis=1, concat_axis=0, tiled=True
    ).reshape(EXPERTS * CAP, D)
    picked = returned[slot_index].astype(jnp.float32).reshape(TOK_DEV, TOPK, D)
    moe_out = jnp.sum(gate_vals[:, :, None] * picked, 1)
    layer_out = (resid + shared_res + moe_out).astype(jnp.bfloat16)
    gain_one, w_query, w_key, w_value, w_out, gain_two, w_router, w_sgate, w_sup, w_sdown = (
        lax.all_gather(attn_gain, "dp", axis=0, tiled=True),
        lax.all_gather(query_weight, "dp", axis=0, tiled=True),
        lax.all_gather(key_weight, "dp", axis=0, tiled=True),
        lax.all_gather(value_weight, "dp", axis=0, tiled=True),
        lax.all_gather(output_weight, "dp", axis=0, tiled=True),
        lax.all_gather(ffn_gain, "dp", axis=0, tiled=True),
        lax.all_gather(router_weight, "dp", axis=0, tiled=True),
        lax.all_gather(shared_gate, "dp", axis=0, tiled=True),
        lax.all_gather(shared_up, "dp", axis=0, tiled=True),
        lax.all_gather(shared_down, "dp", axis=0, tiled=True),
    )
    gain1_f = gain_one.astype(jnp.float32)
    gain2_f = gain_two.astype(jnp.float32)
    grad_total = cotangent.astype(jnp.float32)
    grad_gates = jnp.sum(grad_total[:, None, :] * picked, -1)
    grad_picked = (
        (gate_vals[:, :, None] * grad_total[:, None, :])
        .astype(jnp.bfloat16)
        .reshape(TOK_DEV * TOPK, D)
    )
    grad_back = (
        jnp.zeros((EXPERTS * CAP, D), jnp.bfloat16)
        .at[slot_index]
        .set(grad_picked)
        .reshape(EXPERTS, CAP, D)
    )
    grad_arrived = lax.all_to_all(grad_back, "experts", split_axis=0, concat_axis=1, tiled=True)
    grad_expert_activation = jnp.einsum(
        "erd,efd->erf", grad_arrived, expert_down, preferred_element_type=jnp.float32
    )
    grad_expert_gate_preact = (
        grad_expert_activation * expert_up_preact * swish_derivative(expert_gate_preact)
    ).astype(jnp.bfloat16)
    grad_expert_up_preact = (grad_expert_activation * jax.nn.silu(expert_gate_preact)).astype(
        jnp.bfloat16
    )
    expert_grad_down = jnp.einsum(
        "erf,erd->edf", expert_activation, grad_arrived, preferred_element_type=jnp.float32
    )
    expert_grad_gate = jnp.einsum(
        "xvb,xva->xba", received_rows, grad_expert_gate_preact, preferred_element_type=jnp.float32
    )
    expert_grad_up = jnp.einsum(
        "xvb,xva->xba", received_rows, grad_expert_up_preact, preferred_element_type=jnp.float32
    )
    grad_einputs = jnp.einsum(
        "cgj,clj->cgl", grad_expert_gate_preact, expert_gate, preferred_element_type=jnp.float32
    )
    grad_einputs = (
        grad_einputs
        + jnp.einsum(
            "cgj,clj->cgl",
            grad_expert_up_preact,
            expert_up_weight,
            preferred_element_type=jnp.float32,
        )
    ).astype(jnp.bfloat16)
    grad_returned = lax.all_to_all(
        grad_einputs, "experts", split_axis=1, concat_axis=0, tiled=True
    ).reshape(EXPERTS * CAP, D)
    grad_moe_in = jnp.sum(
        grad_returned[slot_index].astype(jnp.float32).reshape(TOK_DEV, TOPK, D), 1
    )
    grad_rprobs = jnp.sum(grad_gates[:, :, None] * route_hot, 1)
    grad_logits = (
        route_probs * (grad_rprobs - jnp.sum(route_probs * grad_rprobs, -1, keepdims=True))
    ).astype(jnp.bfloat16)
    grad_router_local = inner_rows(hidden2, grad_logits)
    grad_total_b = grad_total.astype(jnp.bfloat16)
    grad_sdown = inner_rows(shared_act, grad_total_b)
    grad_sact = times_transposed(grad_total_b, w_sdown)
    grad_sgpre = (grad_sact * shared_upre * swish_derivative(shared_gpre)).astype(jnp.bfloat16)
    grad_supre = (grad_sact * jax.nn.silu(shared_gpre)).astype(jnp.bfloat16)
    grad_sgate = inner_rows(hidden2, grad_sgpre)
    grad_sup = inner_rows(hidden2, grad_supre)
    grad_hidden2 = (
        grad_moe_in
        + times_transposed(grad_logits, w_router)
        + times_transposed(grad_sgpre, w_sgate)
        + times_transposed(grad_supre, w_sup)
    )
    grad_gain2 = jnp.sum(grad_hidden2 * normed2, 0)
    grad_normed2 = grad_hidden2 * gain2_f
    grad_resid = (
        inv_rms2 * (grad_normed2 - normed2 * jnp.mean(grad_normed2 * normed2, -1, keepdims=True))
        + grad_total
    )
    grad_branch = grad_resid.astype(jnp.bfloat16)
    grad_wout = inner_rows(attended, grad_branch)
    grad_attended = (
        times_transposed(grad_branch, w_out).astype(jnp.bfloat16).reshape(TOK_DEV, HEADS, HD)
    )
    scores_again = jnp.where(
        allowed[None],
        0.125 * jnp.einsum("qhd,khd->hqk", query_h, keys_h, preferred_element_type=jnp.float32),
        -1e30,
    )
    probs_f = jnp.exp(scores_again - log_total)
    probs_b = probs_f.astype(jnp.bfloat16)
    grad_pattn = jnp.einsum(
        "qhd,khd->hqk", grad_attended, values_h, preferred_element_type=jnp.float32
    )
    grad_scores = (
        probs_f * (grad_pattn - jnp.sum(probs_f * grad_pattn, -1, keepdims=True))
    ).astype(jnp.bfloat16)
    grad_query = 0.125 * jnp.einsum(
        "hqk,khd->qhd", grad_scores, keys_h, preferred_element_type=jnp.float32
    ).reshape(TOK_DEV, D)
    grad_keys = 0.125 * jnp.einsum(
        "hqk,qhd->khd", grad_scores, query_h, preferred_element_type=jnp.float32
    ).reshape(-1, D)
    grad_values = jnp.einsum(
        "hqk,qhd->khd", probs_b, grad_attended, preferred_element_type=jnp.float32
    ).reshape(-1, D)
    prompt_span = contexts * PROMPT
    grad_pkeys, grad_pvalues = (
        lax.psum_scatter(
            grad_keys[:prompt_span].astype(jnp.bfloat16), "context", scatter_dimension=0, tiled=True
        ).astype(jnp.float32),
        lax.psum_scatter(
            grad_values[:prompt_span].astype(jnp.bfloat16),
            "context",
            scatter_dimension=0,
            tiled=True,
        ).astype(jnp.float32),
    )
    grad_key_all = jnp.concatenate([grad_pkeys, grad_keys[prompt_span:]], 0)
    grad_value_all = jnp.concatenate([grad_pvalues, grad_values[prompt_span:]], 0)
    grad_qpre = rotate(grad_query, cos_table, -sin_table).astype(jnp.bfloat16)
    grad_kpre = rotate(grad_key_all, cos_table, -sin_table).astype(jnp.bfloat16)
    grad_vpre = grad_value_all.astype(jnp.bfloat16)
    grad_wquery = inner_rows(hidden1, grad_qpre)
    grad_wkey = inner_rows(hidden1, grad_kpre)
    grad_wvalue = inner_rows(hidden1, grad_vpre)
    grad_hidden1 = (
        times_transposed(grad_qpre, w_query)
        + times_transposed(grad_kpre, w_key)
        + times_transposed(grad_vpre, w_value)
    )
    grad_gain1 = jnp.sum(grad_hidden1 * normed1, 0)
    grad_normed1 = grad_hidden1 * gain1_f
    grad_inputs = (
        inv_rms1 * (grad_normed1 - normed1 * jnp.mean(grad_normed1 * normed1, -1, keepdims=True))
        + grad_resid
    )
    shares = (
        lax.psum_scatter(
            grad_gain1.astype(jnp.bfloat16), "dp", scatter_dimension=0, tiled=True
        ).astype(jnp.float32),
        lax.psum_scatter(
            grad_wquery.astype(jnp.bfloat16), "dp", scatter_dimension=0, tiled=True
        ).astype(jnp.float32),
        lax.psum_scatter(
            grad_wkey.astype(jnp.bfloat16), "dp", scatter_dimension=0, tiled=True
        ).astype(jnp.float32),
        lax.psum_scatter(
            grad_wvalue.astype(jnp.bfloat16), "dp", scatter_dimension=0, tiled=True
        ).astype(jnp.float32),
        lax.psum_scatter(
            grad_wout.astype(jnp.bfloat16), "dp", scatter_dimension=0, tiled=True
        ).astype(jnp.float32),
        lax.psum_scatter(
            grad_gain2.astype(jnp.bfloat16), "dp", scatter_dimension=0, tiled=True
        ).astype(jnp.float32),
        lax.psum_scatter(
            grad_router_local.astype(jnp.bfloat16), "dp", scatter_dimension=0, tiled=True
        ).astype(jnp.float32),
        lax.psum_scatter(
            grad_sgate.astype(jnp.bfloat16), "dp", scatter_dimension=0, tiled=True
        ).astype(jnp.float32),
        lax.psum_scatter(
            grad_sup.astype(jnp.bfloat16), "dp", scatter_dimension=0, tiled=True
        ).astype(jnp.float32),
        lax.psum_scatter(
            grad_sdown.astype(jnp.bfloat16), "dp", scatter_dimension=0, tiled=True
        ).astype(jnp.float32),
    )
    totals = (
        lax.psum(shares[0].astype(jnp.bfloat16), ("context", "experts")).astype(jnp.float32),
        lax.psum(shares[1].astype(jnp.bfloat16), ("context", "experts")).astype(jnp.float32),
        lax.psum(shares[2].astype(jnp.bfloat16), ("context", "experts")).astype(jnp.float32),
        lax.psum(shares[3].astype(jnp.bfloat16), ("context", "experts")).astype(jnp.float32),
        lax.psum(shares[4].astype(jnp.bfloat16), ("context", "experts")).astype(jnp.float32),
        lax.psum(shares[5].astype(jnp.bfloat16), ("context", "experts")).astype(jnp.float32),
        lax.psum(shares[6].astype(jnp.bfloat16), ("context", "experts")).astype(jnp.float32),
        lax.psum(shares[7].astype(jnp.bfloat16), ("context", "experts")).astype(jnp.float32),
        lax.psum(shares[8].astype(jnp.bfloat16), ("context", "experts")).astype(jnp.float32),
        lax.psum(shares[9].astype(jnp.bfloat16), ("context", "experts")).astype(jnp.float32),
    )
    summed_gate, summed_up, summed_down = (
        lax.psum_scatter(
            expert_grad_gate.astype(jnp.bfloat16),
            ("dp", "context"),
            scatter_dimension=2,
            tiled=True,
        ).astype(jnp.float32),
        lax.psum_scatter(
            expert_grad_up.astype(jnp.bfloat16), ("dp", "context"), scatter_dimension=2, tiled=True
        ).astype(jnp.float32),
        lax.psum_scatter(
            expert_grad_down.astype(jnp.bfloat16),
            ("dp", "context"),
            scatter_dimension=2,
            tiled=True,
        ).astype(jnp.float32),
    )
    summed_down = jnp.transpose(summed_down, (0, 2, 1))
    return (
        layer_out,
        grad_inputs,
        totals[0],
        totals[1],
        totals[2],
        totals[3],
        totals[4],
        totals[5],
        totals[6],
        totals[7],
        totals[8],
        totals[9],
        summed_gate,
        summed_up,
        summed_down,
    )


TUNED_MESH = {"dp": 4, "context": 2, "experts": 4}
AXES = ("dp", "context", "experts")
SLOT = 72
EXT = 16
ROWS = TOK_DEV + EXT
BF = jnp.bfloat16
F32 = jnp.float32
VMEM_LIMIT = 60 * 1024 * 1024


def microseconds(time):
    return pl.CostEstimate(flops=0, bytes_accessed=int(time * 0.4e6), transcendentals=0)


def moved(value, target):
    pairs = []
    for z in range(4):
        for y in range(2):
            for x in range(2):
                for c in range(2):
                    tz, ty, tx, tc = target(z, y, x, c)
                    pairs.append((((z * 2 + y) * 2 + x) * 2 + c, ((tz * 2 + ty) * 2 + tx) * 2 + tc))
    return lax.ppermute(value, AXES, pairs)


def over_core(value):
    return moved(value, lambda z, y, x, c: (z, y, x, 1 - c))


def over_x(value):
    return moved(value, lambda z, y, x, c: (z, y, 1 - x, c))


def over_a(value):
    return moved(value, lambda z, y, x, c: (z, y, 1 - x, c) if c == 0 else (z, 1 - y, x, c))


def over_b(value):
    return moved(value, lambda z, y, x, c: (z, 1 - y, x, c) if c == 0 else (z, y, 1 - x, c))


def over_z(value, step):
    return moved(value, lambda z, y, x, c: ((z + step) % 4, y, x, c))


def contract(left, right, left_dim, right_dim):
    return lax.dot_general(
        left, right, (((left_dim,), (right_dim,)), ((), ())), preferred_element_type=F32
    )


def one_hot_rows(rank_row):
    slots = lax.broadcasted_iota(jnp.int32, (SLOT, TOK_DEV), 0).astype(F32)
    return (slots == rank_row).astype(F32)


def swish_parts(pre_act):
    sigma = jax.nn.sigmoid(pre_act)
    return pre_act * sigma, sigma * (1.0 + pre_act * (1.0 - sigma))


def group_kernel(
    blocks,
    more,
    base_ref,
    *refs,
):
    h_refs, g_refs = refs[:blocks], refs[blocks : 2 * blocks]
    refs = refs[2 * blocks :]
    more_refs, refs = refs[:more], refs[more:]
    wg_ref, wu_ref, wd_ref = refs[:3]
    moe_refs, dx_refs, refs = refs[3 : 3 + blocks], refs[3 + blocks : 3 + 2 * blocks], refs[3 + 2 * blocks :]
    (
        rank_sc,
        prob_sc,
        x_sc,
        gd_sc,
        gate_sc,
        y_sc,
        acc_sc,
        dgate_sc,
        ysel_sc,
        dsel_sc,
        drp_sc,
    ) = refs[:11]
    e = pl.program_id(0)
    f = pl.program_id(1)
    experts = pl.num_programs(0)
    base = base_ref[0]
    copies = [
        pltpu.make_async_copy(source, into, refs[-1].at[i])
        for i, (source, into) in enumerate(zip(more_refs, refs[11:]))
    ]

    @pl.when((e == 0) & (f == 0))
    def _():
        for one in copies:
            one.start()
        for b in range(blocks):
            rank_sc[b] = g_refs[b][TOK_DEV:, :TOK_DEV].astype(F32)
            prob_sc[b] = h_refs[b][TOK_DEV:, :TOK_DEV].astype(F32) + h_refs[b][
                TOK_DEV:, TOK_DEV:
            ].astype(F32)
        drp_sc[...] = jnp.zeros_like(drp_sc)

    @pl.when(f == 0)
    def _():
        for pair in range(blocks // 2):
            rows_x, rows_g = [], []
            for b in (2 * pair, 2 * pair + 1):
                hot = one_hot_rows(rank_sc[b, pl.ds(base + e, 1), :])
                gate_sc[b * SLOT : (b + 1) * SLOT, :] = jnp.sum(
                    hot * prob_sc[b, pl.ds(base + e, 1), :], -1, keepdims=True
                )
                hot = hot.astype(BF)
                rows_x.append(jnp.dot(hot, h_refs[b][:TOK_DEV, :], preferred_element_type=F32))
                rows_g.append(jnp.dot(hot, g_refs[b][:TOK_DEV, :], preferred_element_type=F32))
            span = slice(pair * 2 * SLOT, (pair + 1) * 2 * SLOT)
            x_sc[span, :] = jnp.concatenate(rows_x, 0).astype(BF)
            gd_sc[span, :] = jnp.concatenate(rows_g, 0).astype(BF)
        y_sc[...] = jnp.zeros_like(y_sc)
        acc_sc[...] = jnp.zeros_like(acc_sc)
        dgate_sc[...] = jnp.zeros_like(dgate_sc)

    rows = x_sc[...]
    gate_pre = jnp.dot(rows, wg_ref[0], preferred_element_type=F32)
    up_pre = jnp.dot(rows, wu_ref[0], preferred_element_type=F32)
    back = contract(gd_sc[...], wd_ref[0], 1, 1)
    swish, slope = swish_parts(gate_pre)
    inner = (swish * up_pre).astype(BF)
    dgate_sc[...] += jnp.sum(back * inner.astype(F32), -1, keepdims=True)
    back = back * gate_sc[...]
    dgate_pre = (back * up_pre * slope).astype(BF)
    dup_pre = (back * swish).astype(BF)
    y_sc[...] += jnp.dot(inner, wd_ref[0], preferred_element_type=F32)
    acc_sc[...] += contract(dgate_pre, wg_ref[0], 1, 1) + contract(dup_pre, wu_ref[0], 1, 1)

    @pl.when(f == pl.num_programs(1) - 1)
    def _():
        for b in range(blocks):
            span = slice(b * SLOT, (b + 1) * SLOT)
            into = pl.ds(pl.multiple_of(e * SLOT, 8), SLOT)
            ysel_sc[b, into, :] = y_sc[span, :] * gate_sc[span, :]
            dsel_sc[b, into, :] = acc_sc[span, :]
            hot = one_hot_rows(rank_sc[b, pl.ds(base + e, 1), :])
            drp_sc[b, pl.ds(base + e, 1), :] = jnp.sum(hot * dgate_sc[span, :], 0, keepdims=True)

    @pl.when((f == pl.num_programs(1) - 1) & (e == experts - 1))
    def _():
        for one in copies:
            one.wait()
        for b in range(blocks):
            side, at = divmod(b, blocks // 2)
            moe_out, dx_out = moe_refs[b], dx_refs[b]
            hot = jnp.concatenate(
                [
                    one_hot_rows(rank_sc[b, pl.ds(base + i, 1), :])
                    for i in range(ysel_sc.shape[1] // SLOT)
                ],
                0,
            ).astype(BF)
            moe = contract(hot, ysel_sc[b].astype(BF), 0, 0)
            dx = contract(hot, dsel_sc[b].astype(BF), 0, 0)
            drp = drp_sc[b]
            if more:
                shared = refs[11 + 2 * at : 13 + 2 * at]
                moe_before, dx_before = refs[15 + b], refs[15 + blocks + b]
                moe = moe + shared[0][side] + moe_before[...].astype(F32)
                dx = dx + shared[1][side] + dx_before[:TOK_DEV, :].astype(F32)
                drp = drp + dx_before[TOK_DEV:, :TOK_DEV].astype(F32)
                drp = drp + dx_before[TOK_DEV:, TOK_DEV:].astype(F32)
            moe_out[...] = moe.astype(BF)
            dx_out[:TOK_DEV, :] = dx.astype(BF)
            high = drp.astype(BF)
            dx_out[TOK_DEV:, :TOK_DEV] = high
            dx_out[TOK_DEV:, TOK_DEV:] = (drp - high.astype(F32)).astype(BF)


def group_experts(base, first, experts, h_group, g_group, more, w_gate, w_up, w_down):
    blocks = len(h_group)
    ff = w_gate.shape[2]
    tile = 512
    whole = lambda *shape: pl.BlockSpec(shape, lambda e, f, s: (0,) * len(shape))
    results = [(TOK_DEV, D)] * blocks + [(ROWS, D)] * blocks
    return pl.pallas_call(
        functools.partial(group_kernel, blocks, len(more)),
        out_shape=tuple(jax.ShapeDtypeStruct(s, BF) for s in results),
        grid_spec=pltpu.PrefetchScalarGridSpec(
            num_scalar_prefetch=1,
            grid=(experts, ff // tile),
            in_specs=[whole(ROWS, D)] * (2 * blocks)
            + [pl.BlockSpec(memory_space=pl.ANY)] * len(more)
            + [
                pl.BlockSpec((1, D, tile), lambda e, f, s: (first + e, 0, f)),
                pl.BlockSpec((1, D, tile), lambda e, f, s: (first + e, 0, f)),
                pl.BlockSpec((1, tile, D), lambda e, f, s: (first + e, f, 0)),
            ],
            out_specs=[whole(*s) for s in results],
            scratch_shapes=[
                pltpu.VMEM((blocks, EXPERTS, TOK_DEV), F32),
                pltpu.VMEM((blocks, EXPERTS, TOK_DEV), F32),
                pltpu.VMEM((blocks * SLOT, D), BF),
                pltpu.VMEM((blocks * SLOT, D), BF),
                pltpu.VMEM((blocks * SLOT, 1), F32),
                pltpu.VMEM((blocks * SLOT, D), F32),
                pltpu.VMEM((blocks * SLOT, D), F32),
                pltpu.VMEM((blocks * SLOT, 1), F32),
                pltpu.VMEM((blocks, experts * SLOT, D), F32),
                pltpu.VMEM((blocks, experts * SLOT, D), F32),
                pltpu.VMEM((blocks, EXPERTS, TOK_DEV), F32),
            ]
            + [pltpu.VMEM(v.shape, v.dtype) for v in more]
            + [pltpu.SemaphoreType.DMA((max(1, len(more)),))],
        ),
        compiler_params=pltpu.CompilerParams(vmem_limit_bytes=VMEM_LIMIT),
        cost_estimate=microseconds(21),
        name="group_experts",
    )(base, *h_group, *g_group, *more, w_gate, w_up, w_down)


def shared_kernel(h_a_ref, h_b_ref, g_a_ref, g_b_ref, w_a_ref, w_b_ref, out_ref, dh_ref, h_sc, g_sc):
    for k, (h_ref, g_ref) in enumerate(((h_a_ref, g_a_ref), (h_b_ref, g_b_ref))):
        h_sc[k * TOK_DEV : (k + 1) * TOK_DEV, :] = h_ref[:TOK_DEV, :]
        g_sc[k * TOK_DEV : (k + 1) * TOK_DEV, :] = g_ref[:TOK_DEV, :]
    for k, w_ref in enumerate((w_a_ref, w_b_ref)):
        w_gate, w_up = w_ref[:, :, :256].reshape(D, 256), w_ref[:, :, 256:512].reshape(D, 256)
        w_down = jnp.concatenate(
            [w_ref[:, 64 * i : 64 * (i + 1), 512:].reshape(256, 256) for i in range(3)], 1
        )
        gate_pre = jnp.dot(h_sc[...], w_gate, preferred_element_type=F32)
        up_pre = jnp.dot(h_sc[...], w_up, preferred_element_type=F32)
        back = contract(g_sc[...], w_down, 1, 1)
        swish, slope = swish_parts(gate_pre)
        inner = (swish * up_pre).astype(BF)
        out = jnp.dot(inner, w_down, preferred_element_type=F32)
        dgate_pre = (back * up_pre * slope).astype(BF)
        dup_pre = (back * swish).astype(BF)
        dh = contract(dgate_pre, w_gate, 1, 1) + contract(dup_pre, w_up, 1, 1)
        for b in range(2):
            rows = slice(b * TOK_DEV, (b + 1) * TOK_DEV)
            out_ref[b] = out[rows] if k == 0 else out_ref[b] + out[rows]
            dh_ref[b] = dh[rows] if k == 0 else dh_ref[b] + dh[rows]


def shared_rows(h_pair, g_pair, w_own, w_far):
    rows = jax.ShapeDtypeStruct((2, TOK_DEV, D), F32)
    vmem = pl.BlockSpec(memory_space=pltpu.VMEM)
    return pl.pallas_call(
        shared_kernel,
        out_shape=(rows, rows),
        in_specs=[vmem] * 6,
        out_specs=(vmem, vmem),
        scratch_shapes=[
            pltpu.VMEM((2 * TOK_DEV, D), BF),
            pltpu.VMEM((2 * TOK_DEV, D), BF),
        ],
        compiler_params=pltpu.CompilerParams(vmem_limit_bytes=VMEM_LIMIT),
        cost_estimate=microseconds(8),
        name="shared_rows",
    )(*h_pair, *g_pair, w_own, w_far)


def start_parts(h_parts, g_parts, h_buf, g_buf, sems):
    per = h_parts[0].shape[0]
    copies = []
    for i in range(len(h_parts)):
        into = pl.ds(i * per, per)
        copies.append(
            (
                pltpu.make_async_copy(h_parts[i], h_buf.at[into], sems.at[0, i]),
                pltpu.make_async_copy(g_parts[i], g_buf.at[into], sems.at[1, i]),
            )
        )
    for pair in copies:
        for one in pair:
            one.start()
    return copies


def expert_slice_kernel(parts, more, pos_ref, *refs):
    h_parts, g_parts = refs[:parts], refs[parts : 2 * parts]
    weights = refs[2 * parts : 2 * parts + 3]
    refs = refs[2 * parts + 3 :]
    sums, refs = refs[: 3 * more], refs[3 * more :]
    og_ref, ou_ref, od_ref, h_buf, g_buf, x_sc, gd_sc, rank_sc, prob_sc = refs[:9]
    wg_ref, wu_ref, wd_ref, sems, w_sems = refs[9:]
    base = pos_ref[0]
    experts, _, width = wg_ref.shape
    per = h_parts[0].shape[0]
    copies = start_parts(h_parts, g_parts, h_buf, g_buf, sems)
    cols = pl.ds(pl.multiple_of(pos_ref[1] * width, width), width)
    loads = [
        pltpu.make_async_copy(weights[0].at[:, :, cols], wg_ref, w_sems.at[0]),
        pltpu.make_async_copy(weights[1].at[:, :, cols], wu_ref, w_sems.at[1]),
        pltpu.make_async_copy(weights[2].at[:, cols, :], wd_ref, w_sems.at[2]),
    ]
    for i in range(3 * more):
        loads.append(
            pltpu.make_async_copy(sums[i], (og_ref, ou_ref, od_ref)[i], w_sems.at[3 + i])
        )
    for one in loads:
        one.start()

    def dispatch(pair, carry):
        both_x, both_g = [], []
        for k in range(2):
            b = 2 * pair + k
            rank_sc[k] = g_buf[b, TOK_DEV:, :TOK_DEV].astype(F32)
            prob_sc[k] = h_buf[b, TOK_DEV:, :TOK_DEV].astype(F32) + h_buf[
                b, TOK_DEV:, TOK_DEV:
            ].astype(F32)
            hots, gates = [], []
            for i in range(experts):
                hot = one_hot_rows(rank_sc[k, pl.ds(base + i, 1), :])
                gates.append(
                    jnp.sum(hot * prob_sc[k, pl.ds(base + i, 1), :], -1, keepdims=True)
                )
                hots.append(hot)
            hot = jnp.concatenate(hots, 0).astype(BF)
            both_x.append(jnp.dot(hot, h_buf[b, :TOK_DEV, :], preferred_element_type=F32))
            both_g.append(
                jnp.dot(hot, g_buf[b, :TOK_DEV, :], preferred_element_type=F32)
                * jnp.concatenate(gates, 0)
            )
        into = pl.ds(pl.multiple_of(pair * 2 * SLOT, 2 * SLOT), 2 * SLOT)
        for i in range(experts):
            span = slice(i * SLOT, (i + 1) * SLOT)
            x_sc[i, into, :] = jnp.concatenate([v[span] for v in both_x], 0).astype(BF)
            gd_sc[i, into, :] = jnp.concatenate([v[span] for v in both_g], 0).astype(BF)
        return carry

    for i in range(parts):
        for one in copies[i]:
            one.wait()
        lax.fori_loop(i * per // 2, (i + 1) * per // 2, dispatch, 0)
    for one in loads:
        one.wait()

    def products(i, carry):
        rows = x_sc[i]
        gate_pre = jnp.dot(rows, wg_ref[i], preferred_element_type=F32)
        up_pre = jnp.dot(rows, wu_ref[i], preferred_element_type=F32)
        back = contract(gd_sc[i], wd_ref[i], 1, 1)
        swish, slope = swish_parts(gate_pre)
        inner = (swish * up_pre).astype(BF)
        dgate_pre = (back * up_pre * slope).astype(BF)
        dup_pre = (back * swish).astype(BF)
        add_g = contract(rows, dgate_pre, 0, 0)
        add_u = contract(rows, dup_pre, 0, 0)
        add_d = contract(inner, gd_sc[i], 0, 0)
        if more:
            og_ref[i] += add_g
            ou_ref[i] += add_u
            od_ref[i] += add_d
        else:
            og_ref[i], ou_ref[i], od_ref[i] = add_g, add_u, add_d
        return carry

    lax.fori_loop(0, experts, products, 0)


def expert_slice_grads(pos, h_parts, g_parts, w_gate, w_up, w_down, width, sums=()):
    parts, per = len(h_parts), h_parts[0].shape[0]
    experts = w_gate.shape[0]
    blocks = parts * per
    shapes = ((experts, D, width), (experts, D, width), (experts, width, D))
    vmem = pl.BlockSpec(memory_space=pltpu.VMEM)
    anywhere = pl.BlockSpec(memory_space=pl.ANY)
    return pl.pallas_call(
        functools.partial(expert_slice_kernel, parts, len(sums) // 3),
        out_shape=tuple(jax.ShapeDtypeStruct(s, F32) for s in shapes),
        in_specs=[pl.BlockSpec(memory_space=pltpu.SMEM)]
        + [anywhere] * (2 * parts + 3 + len(sums)),
        out_specs=(vmem,) * 3,
        scratch_shapes=[
            pltpu.VMEM((blocks, ROWS, D), BF),
            pltpu.VMEM((blocks, ROWS, D), BF),
            pltpu.VMEM((experts, blocks * SLOT, D), BF),
            pltpu.VMEM((experts, blocks * SLOT, D), BF),
            pltpu.VMEM((2, EXPERTS, TOK_DEV), F32),
            pltpu.VMEM((2, EXPERTS, TOK_DEV), F32),
        ]
        + [pltpu.VMEM(s, BF) for s in shapes]
        + [
            pltpu.SemaphoreType.DMA((2, parts)),
            pltpu.SemaphoreType.DMA((6,)),
        ],
        compiler_params=pltpu.CompilerParams(vmem_limit_bytes=VMEM_LIMIT),
        cost_estimate=microseconds(31),
        name="expert_slice_grads",
    )(pos, *h_parts, *g_parts, w_gate, w_up, w_down, *sums)


def shared_slice_kernel(parts, more, pos_ref, *refs):
    h_parts, g_parts = refs[:parts], refs[parts : 2 * parts]
    w_ref = refs[2 * parts]
    refs = refs[2 * parts + 1 :]
    sums, refs = refs[: 3 * more], refs[3 * more :]
    og_ref, ou_ref, od_ref, h_buf, g_buf, inner_sc, wg_ref, wu_ref, wd_ref, sems = refs
    per = h_parts[0].shape[0]
    copies = start_parts(h_parts, g_parts, h_buf, g_buf, sems)
    wg_ref[...] = w_ref[:, :, :256].reshape(D, 256)
    wu_ref[...] = w_ref[:, :, 256:512].reshape(D, 256)
    for i in range(3):
        wd_ref[:, 256 * i : 256 * (i + 1)] = w_ref[:, 64 * i : 64 * (i + 1), 512:].reshape(256, 256)
    window = pl.ds(pl.multiple_of(pos_ref[0] * 128, 128), og_ref.shape[0])
    lanes = pl.ds(pl.multiple_of(pos_ref[1] * 128, 128), od_ref.shape[0])
    for i, out_ref in enumerate((og_ref, ou_ref, od_ref)):
        out_ref[...] = sums[i][...] if more else jnp.zeros_like(out_ref)

    def two(buf, pair, cols=slice(None)):
        return jnp.concatenate([buf[2 * pair + k, :TOK_DEV, cols] for k in range(2)], 0)

    def products(pair, carry):
        rows, grads = two(h_buf, pair), two(g_buf, pair)
        gate_pre = jnp.dot(rows, wg_ref[...], preferred_element_type=F32)
        up_pre = jnp.dot(rows, wu_ref[...], preferred_element_type=F32)
        back = contract(grads, wd_ref[...], 1, 1)
        swish, slope = swish_parts(gate_pre)
        inner_sc[...] = (swish * up_pre).astype(BF)
        dgate_pre = (back * up_pre * slope).astype(BF)
        dup_pre = (back * swish).astype(BF)
        picked = two(h_buf, pair, window)
        og_ref[...] += contract(picked, dgate_pre, 0, 0)
        ou_ref[...] += contract(picked, dup_pre, 0, 0)
        od_ref[...] += contract(inner_sc[:, lanes], grads, 0, 0)
        return carry

    for i in range(parts):
        for one in copies[i]:
            one.wait()
        lax.fori_loop(i * per // 2, (i + 1) * per // 2, products, 0)


def shared_slice_grads(pos, h_parts, g_parts, weights, sums=()):
    parts, per = len(h_parts), h_parts[0].shape[0]
    blocks = parts * per
    width = 256
    vmem = pl.BlockSpec(memory_space=pltpu.VMEM)
    anywhere = pl.BlockSpec(memory_space=pl.ANY)
    return pl.pallas_call(
        functools.partial(shared_slice_kernel, parts, len(sums) // 3),
        out_shape=(
            jax.ShapeDtypeStruct((256, width), F32),
            jax.ShapeDtypeStruct((256, width), F32),
            jax.ShapeDtypeStruct((128, D), F32),
        ),
        in_specs=[pl.BlockSpec(memory_space=pltpu.SMEM)]
        + [anywhere] * (2 * parts)
        + [vmem] * (1 + len(sums)),
        out_specs=(vmem,) * 3,
        scratch_shapes=[
            pltpu.VMEM((blocks, ROWS, D), BF),
            pltpu.VMEM((blocks, ROWS, D), BF),
            pltpu.VMEM((2 * TOK_DEV, width), BF),
            pltpu.VMEM((D, width), BF),
            pltpu.VMEM((D, width), BF),
            pltpu.VMEM((width, D), BF),
            pltpu.SemaphoreType.DMA((2, parts)),
        ],
        compiler_params=pltpu.CompilerParams(vmem_limit_bytes=VMEM_LIMIT),
        cost_estimate=microseconds(20),
        name="shared_slice_grads",
    )(pos, *h_parts, *g_parts, weights, *sums)


def pair_sum(kept, received):
    return (kept.astype(F32) + received.astype(F32)).astype(BF)


def halves(value, bit):
    width = value.shape[-1] // 2
    low, high = value[..., :width], value[..., width:]
    return jnp.where(bit == 0, low, high), jnp.where(bit == 0, high, low)


def rejoin(own, other, bit):
    return jnp.where(
        bit == 0, jnp.concatenate([own, other], -1), jnp.concatenate([other, own], -1)
    )


def lane_halves():
    lane = lax.broadcasted_iota(jnp.int32, (1, 128), 1)
    return [(lane < 64).astype(F32).astype(BF), (lane >= 64).astype(F32).astype(BF)]


def pick_lanes(first, second):
    lane = lax.broadcasted_iota(jnp.int32, first.shape, 1)
    return jnp.where(lane < 64, first, second)


def turned(value, cos, sin):
    lane = lax.broadcasted_iota(jnp.int32, value.shape, 1)
    partner = jnp.where(lane % 64 < 32, pltpu.roll(value, 96, 1), pltpu.roll(value, 32, 1))
    return value * cos + partner * sin


def causal_mask(rows):
    row = lax.broadcasted_iota(jnp.int32, (rows, rows), 0)
    col = lax.broadcasted_iota(jnp.int32, (rows, rows), 1)
    return row, col


def unit_rms(value):
    return lax.rsqrt(jnp.mean(value * value, -1, keepdims=True) + EPS)


def softmax_of(first, second=None):
    top = jnp.max(first, -1, keepdims=True)
    if second is not None:
        top = jnp.maximum(top, jnp.max(second, -1, keepdims=True))
    first = jnp.exp(first - top)
    total = jnp.sum(first, -1, keepdims=True)
    if second is None:
        return first * (1.0 / total)
    second = jnp.exp(second - top)
    scale = 1.0 / (total + jnp.sum(second, -1, keepdims=True))
    return first * scale, second * scale


def attention_kernel(place_ref, *refs):
    w_parts = refs[:8]
    (
        h1_ref,
        own_ref,
        far_ref,
        gain1_ref,
        gain2_ref,
        router_ref,
        cos_ref,
        sin_ref,
        w_ref,
        q_ref,
        k_ref,
        v_ref,
        o_ref,
        x1_ref,
        h2_ref,
        h_sc,
        sems,
    ) = refs[8:]
    copies = []
    for part in range(8):
        for slot in range(4):
            rows = pl.ds(pl.multiple_of(place_ref[8 + slot] * 192, 192), 192)
            copies.append(
                pltpu.make_async_copy(
                    w_parts[part].at[slot, :192, :],
                    w_ref.at[place_ref[part], rows, :],
                    sems.at[part, slot],
                )
            )
    for one in copies:
        one.start()
    h_sc[:TOK_DEV, :] = h1_ref[...]
    far = far_ref[:TOK_DEV, :].astype(F32)
    h_sc[TOK_DEV:, :] = (far * unit_rms(far) * gain1_ref[...]).astype(BF)
    for one in copies:
        one.wait()
    for i in range(6):
        out_ref = (q_ref, k_ref, v_ref)[i // 2]
        product = jnp.dot(h_sc[...], w_ref[i], preferred_element_type=F32)
        for slab in range(3):
            at = (i % 2) * 384 + slab * 128
            for half in range(2):
                rows = slice(half * TOK_DEV, (half + 1) * TOK_DEV)
                value = product[rows, slab * 128 : (slab + 1) * 128]
                if i < 4:
                    value = turned(value, cos_ref[...], sin_ref[...])
                out_ref[rows, at : at + 128] = value.astype(BF)
    masks = lane_halves()
    row, col = causal_mask(PROMPT)
    prompt_ok = col <= row
    row, col = causal_mask(CONT * CLEN)
    cont_ok = (row // CLEN == col // CLEN) & (col <= row)
    row = lax.broadcasted_iota(jnp.int32, (CONT * CLEN, 1), 0)
    reads_far = jnp.where(row < CLEN, place_ref[12], place_ref[13]).astype(F32)
    own_c = slice(PROMPT, TOK_DEV)
    far_p = slice(TOK_DEV, TOK_DEV + PROMPT)

    def heads(pair, carry):
        cols = pl.ds(pl.multiple_of(pair * 128, 128), 128)
        q_p, k_p, v_p = q_ref[:PROMPT, cols], k_ref[:PROMPT, cols], v_ref[:PROMPT, cols]
        q_c, k_c, v_c = q_ref[own_c, cols], k_ref[own_c, cols], v_ref[own_c, cols]
        k_f, v_f = k_ref[far_p, cols], v_ref[far_p, cols]
        out_p, out_c = [], []
        for mask in masks:
            score = jnp.where(prompt_ok, 0.125 * contract(q_p * mask, k_p, 1, 1), -1e30)
            out_p.append(
                jnp.dot(softmax_of(score).astype(BF), v_p, preferred_element_type=F32)
            )
            query = q_c * mask
            near, far = contract(query, k_p, 1, 1), contract(query, k_f, 1, 1)
            first = 0.125 * jnp.where(reads_far > 0.5, far, near)
            second = jnp.where(cont_ok, 0.125 * contract(query, k_c, 1, 1), -1e30)
            first, second = softmax_of(first, second)
            out_c.append(
                jnp.dot((first * (1.0 - reads_far)).astype(BF), v_p, preferred_element_type=F32)
                + jnp.dot((first * reads_far).astype(BF), v_f, preferred_element_type=F32)
                + jnp.dot(second.astype(BF), v_c, preferred_element_type=F32)
            )
        o_ref[:PROMPT, cols] = pick_lanes(*out_p).astype(BF)
        o_ref[own_c, cols] = pick_lanes(*out_c).astype(BF)
        return carry

    lax.fori_loop(0, HEADS // 2, heads, 0)
    for i in range(2):
        cols = slice(384 * i, 384 * (i + 1))
        x1_ref[:, cols] = own_ref[:TOK_DEV, cols].astype(F32) + jnp.dot(
            o_ref[...], w_ref[6 + i], preferred_element_type=F32
        )
    resid = x1_ref[...]
    hidden = (resid * unit_rms(resid) * gain2_ref[...]).astype(BF)
    h2_ref[:TOK_DEV, :] = hidden
    logits = contract(router_ref[...], hidden, 1, 1)
    logits = jnp.exp(logits - jnp.max(logits, 0, keepdims=True))
    probs = logits / jnp.sum(logits, 0, keepdims=True)
    high = probs.astype(BF)
    h2_ref[TOK_DEV:, :TOK_DEV] = high
    h2_ref[TOK_DEV:, TOK_DEV:] = (probs - high.astype(F32)).astype(BF)


def attention_forward(place, w_parts, h1, own, far, gain1, gain2, router_t, cos, sin):
    vmem = pl.BlockSpec(memory_space=pltpu.VMEM)
    shape = jax.ShapeDtypeStruct
    return pl.pallas_call(
        attention_kernel,
        out_shape=(
            shape((8, D, 384), BF),
            shape((2 * TOK_DEV, D), BF),
            shape((2 * TOK_DEV, D), BF),
            shape((2 * TOK_DEV, D), BF),
            shape((TOK_DEV, D), BF),
            shape((TOK_DEV, D), F32),
            shape((ROWS, D), BF),
        ),
        in_specs=[pl.BlockSpec(memory_space=pltpu.SMEM)]
        + [pl.BlockSpec(memory_space=pl.ANY)] * 8
        + [vmem] * 8,
        out_specs=(vmem,) * 7,
        scratch_shapes=[
            pltpu.VMEM((2 * TOK_DEV, D), BF),
            pltpu.SemaphoreType.DMA((8, 4)),
        ],
        compiler_params=pltpu.CompilerParams(vmem_limit_bytes=VMEM_LIMIT),
        cost_estimate=microseconds(20),
        name="attention_forward",
    )(place, *w_parts, h1, own, far, gain1, gain2, router_t, cos, sin)


def branch_kernel(*refs):
    dx_refs, refs = refs[:3], refs[3:]
    (
        h2_ref,
        x1_ref,
        g_ref,
        gain2_ref,
        router_ref,
        w_ref,
        dx1_ref,
        do_ref,
        do_c_ref,
        grouter_ref,
        ggain_ref,
    ) = refs
    dx = dx_refs[0][...].astype(F32) + dx_refs[1][...].astype(F32) + dx_refs[2][...].astype(F32)
    drp = dx[TOK_DEV:, :TOK_DEV] + dx[TOK_DEV:, TOK_DEV:]
    probs = h2_ref[TOK_DEV:, :TOK_DEV].astype(F32) + h2_ref[TOK_DEV:, TOK_DEV:].astype(F32)
    dlogits = (probs * (drp - jnp.sum(probs * drp, 0, keepdims=True))).astype(BF)
    hidden = h2_ref[:TOK_DEV, :]
    grouter_ref[...] = jnp.dot(dlogits, hidden, preferred_element_type=F32)
    dh2 = (
        dx[:TOK_DEV]
        + contract(dlogits, router_ref[...], 0, 0)
    )
    resid = x1_ref[...]
    scale = unit_rms(resid)
    normed = resid * scale
    ggain_ref[...] = jnp.sum(dh2 * normed, 0, keepdims=True)
    dnormed = dh2 * gain2_ref[...]
    dx1 = scale * (dnormed - normed * jnp.mean(dnormed * normed, -1, keepdims=True)) + g_ref[
        ...
    ].astype(F32)
    dx1_ref[...] = dx1
    datt = dx1.astype(BF)
    do_ref[...] = (
        contract(datt[:, :384], w_ref[0], 1, 1) + contract(datt[:, 384:], w_ref[1], 1, 1)
    ).astype(BF)
    do_c_ref[...] = do_ref[PROMPT:, :]


def branch_backward(dx, h_block, x1, grad, gain2, router_t, w_all):
    shape = jax.ShapeDtypeStruct
    whole = lambda *dims: pl.BlockSpec(dims, lambda i: (0,) * len(dims))
    rows = whole(TOK_DEV, D)
    return pl.pallas_call(
        branch_kernel,
        grid=(1,),
        out_shape=(
            shape((TOK_DEV, D), F32),
            shape((TOK_DEV, D), BF),
            shape((TOK_DEV - PROMPT, D), BF),
            shape((EXPERTS, D), F32),
            shape((1, D), F32),
        ),
        in_specs=[
            whole(ROWS, D),
            whole(ROWS, D),
            whole(ROWS, D),
            whole(ROWS, D),
            rows,
            rows,
            whole(1, D),
            whole(EXPERTS, D),
            pl.BlockSpec((2, D, 384), lambda i: (3, 0, 0)),
        ],
        out_specs=(
            rows,
            rows,
            whole(TOK_DEV - PROMPT, D),
            whole(EXPERTS, D),
            whole(1, D),
        ),
        compiler_params=pltpu.CompilerParams(vmem_limit_bytes=VMEM_LIMIT),
        cost_estimate=microseconds(6),
        name="branch_backward",
    )(*dx, h_block, x1, grad, gain2, router_t, w_all)


def attention_back_kernel(
    flags_ref,
    q_ref,
    k_ref,
    v_ref,
    do_ref,
    do_far_ref,
    h1_ref,
    w_ref,
    own_ref,
    gain1_ref,
    cos_ref,
    sin_ref,
    dx1_ref,
    gwo_ref,
    grouter_ref,
    ggain2_ref,
    gtok_ref,
    keep_ref,
    send_ref,
    dq_sc,
    dk_sc,
    dv_sc,
    low_sc,
):
    masks = lane_halves()
    row, col = causal_mask(PROMPT)
    prompt_ok = col <= row
    cont_ok = (row // CLEN == col // CLEN) & (col <= row)
    row = lax.broadcasted_iota(jnp.int32, (4 * CLEN, 1), 0) // CLEN
    near = jnp.where(
        row < 2,
        jnp.where(row == 0, flags_ref[0], flags_ref[1]),
        jnp.where(row == 2, flags_ref[2], flags_ref[3]),
    ).astype(F32)
    own_c = slice(PROMPT, TOK_DEV)
    far_p = slice(TOK_DEV, TOK_DEV + PROMPT)
    far_c = slice(TOK_DEV + PROMPT, 2 * TOK_DEV)
    cont = CONT * CLEN

    def either(own_near, far_own):
        return jnp.concatenate(
            [jnp.where(near[:cont] > 0.5, own_near[:cont], far_own), own_near[cont:]], 0
        )

    def heads(pair, carry):
        cols = pl.ds(pl.multiple_of(pair * 128, 128), 128)
        q_p, k_p, v_p = q_ref[:PROMPT, cols], k_ref[:PROMPT, cols], v_ref[:PROMPT, cols]
        k_f, v_f = k_ref[far_p, cols], v_ref[far_p, cols]
        q_c, k_c, v_c = q_ref[own_c, cols], k_ref[own_c, cols], v_ref[own_c, cols]
        do_p, do_c = do_ref[:PROMPT, cols], do_ref[own_c, cols]
        q_4 = jnp.concatenate([q_c, q_ref[far_c, cols]], 0)
        k_4 = jnp.concatenate([k_c, k_ref[far_c, cols]], 0)
        v_4 = jnp.concatenate([v_c, v_ref[far_c, cols]], 0)
        do_4 = jnp.concatenate([do_c, do_far_ref[:, cols]], 0)
        q_all = jnp.concatenate([q_p, q_4], 0)
        do_all = jnp.concatenate([do_p, do_4], 0)
        dq_p, dq_c, dk_p, dk_c, dv_p, dv_c = [], [], [], [], [], []
        for mask in masks:
            score = jnp.where(prompt_ok, 0.125 * contract(q_p * mask, k_p, 1, 1), -1e30)
            prob = softmax_of(score)
            dprob = contract(do_p * mask, v_p, 1, 1)
            ds = (prob * (dprob - jnp.sum(prob * dprob, -1, keepdims=True))).astype(BF)
            query, grad = q_4 * mask, do_4 * mask
            first = 0.125 * either(
                contract(query, k_p, 1, 1), contract(query[:cont], k_f, 1, 1)
            )
            second = jnp.where(cont_ok, 0.125 * contract(query, k_4, 1, 1), -1e30)
            first, second = softmax_of(first, second)
            dfirst = either(contract(grad, v_p, 1, 1), contract(grad[:cont], v_f, 1, 1))
            dsecond = contract(grad, v_4, 1, 1)
            mean = jnp.sum(first * dfirst, -1, keepdims=True) + jnp.sum(
                second * dsecond, -1, keepdims=True
            )
            ds1 = first * (dfirst - mean)
            ds2 = (second * (dsecond - mean)).astype(BF)[:cont, :cont]
            ds_near = (ds1 * near).astype(BF)
            ds_far = (ds1 * (1.0 - near)).astype(BF)[:cont]
            p_near = (first * near).astype(BF)
            p_own = second.astype(BF)[:cont, :cont]
            dq_p.append(jnp.dot(ds, k_p, preferred_element_type=F32))
            dq_c.append(
                jnp.dot(ds_near[:cont], k_p, preferred_element_type=F32)
                + jnp.dot(ds_far, k_f, preferred_element_type=F32)
                + jnp.dot(ds2, k_c, preferred_element_type=F32)
            )
            dk_p.append(contract(jnp.concatenate([ds, ds_near], 0), q_all, 0, 0))
            dv_p.append(contract(jnp.concatenate([prob.astype(BF), p_near], 0), do_all, 0, 0))
            dk_c.append(contract(ds2, q_c, 0, 0))
            dv_c.append(contract(p_own, do_c, 0, 0))
        for out, prompt_part, cont_part in (
            (dq_sc, dq_p, dq_c),
            (dk_sc, dk_p, dk_c),
            (dv_sc, dv_p, dv_c),
        ):
            out[:PROMPT, cols] = pick_lanes(*prompt_part)
            out[own_c, cols] = pick_lanes(*cont_part)
        return carry

    lax.fori_loop(0, HEADS // 2, heads, 0)

    def put(owner, at, product):
        for z in range(4):
            rows = product[z * (D // 4) : (z + 1) * (D // 4), :]

            @pl.when(flags_ref[4] == owner)
            def _():
                keep_ref[z, : D // 4, at : at + D] = rows

            @pl.when(flags_ref[4] != owner)
            def _():
                send_ref[z, : D // 4, at : at + D] = rows

    dh1 = None
    for i, source in enumerate((dq_sc, dk_sc, dv_sc)):
        for slab in range(6):
            cols = slice(slab * 128, (slab + 1) * 128)
            value = source[:, cols]
            if i < 2:
                value = turned(0.125 * value, cos_ref[...], -sin_ref[...])
            low_sc[:, cols] = value.astype(BF)
        grads = low_sc[...]
        product = contract(h1_ref[...], grads, 0, 0).astype(BF)
        put(i // 2, (i % 2) * D, product)
        for half in range(2):
            part = contract(grads[:, 384 * half : 384 * (half + 1)], w_ref[2 * i + half], 1, 1)
            dh1 = part if dh1 is None else dh1 + part
    put(1, D, gwo_ref[...])
    inputs = own_ref[:TOK_DEV, :].astype(F32)
    scale = unit_rms(inputs)
    normed = inputs * scale
    ggain1 = jnp.sum(dh1 * normed, 0, keepdims=True)
    gains = jnp.concatenate([ggain1, ggain2_ref[...], jnp.zeros((EXT - 2, D), F32)], 0)
    keep_ref[:, D // 4 :, :] = jnp.zeros((4, EXT, 2 * D), BF)
    send_ref[:, D // 4 :, :] = jnp.zeros((4, EXT, 2 * D), BF)
    for z in range(4):
        cols = slice(z * (D // 4), (z + 1) * (D // 4))
        extras = jnp.concatenate([grouter_ref[:, cols], gains[:, cols]], 1).astype(BF)

        @pl.when(flags_ref[4] == 0)
        def _():
            keep_ref[z, D // 4 :, : 2 * (D // 4)] = extras

        @pl.when(flags_ref[4] != 0)
        def _():
            send_ref[z, D // 4 :, : 2 * (D // 4)] = extras

    dnormed = dh1 * gain1_ref[...]
    gtok_ref[...] = (
        scale * (dnormed - normed * jnp.mean(dnormed * normed, -1, keepdims=True)) + dx1_ref[...]
    )


def attention_backward(
    flags, q, k, v, do, do_far, h1, w_all, own, gain1, cos, sin, dx1, gwo, grouter, ggain2
):
    shape = jax.ShapeDtypeStruct
    whole = lambda *dims: pl.BlockSpec(dims, lambda i: (0,) * len(dims))
    rows = whole(TOK_DEV, D)
    both = whole(2 * TOK_DEV, D)
    packed = (4, D // 4 + EXT, 2 * D)
    return pl.pallas_call(
        attention_back_kernel,
        grid=(1,),
        out_shape=(
            shape((TOK_DEV, D), F32),
            shape(packed, BF),
            shape(packed, BF),
        ),
        in_specs=[
            pl.BlockSpec(memory_space=pltpu.SMEM),
            both,
            both,
            both,
            rows,
            whole(TOK_DEV - PROMPT, D),
            rows,
            whole(6, D, 384),
            rows,
            whole(1, D),
            whole(TOK_DEV, 128),
            whole(TOK_DEV, 128),
            rows,
            whole(D, D),
            whole(EXPERTS, D),
            whole(1, D),
        ],
        out_specs=(rows, whole(*packed), whole(*packed)),
        scratch_shapes=[
            pltpu.VMEM((TOK_DEV, D), F32),
            pltpu.VMEM((TOK_DEV, D), F32),
            pltpu.VMEM((TOK_DEV, D), F32),
            pltpu.VMEM((TOK_DEV, D), BF),
        ],
        compiler_params=pltpu.CompilerParams(vmem_limit_bytes=VMEM_LIMIT),
        cost_estimate=microseconds(23),
        name="attention_backward",
    )(flags, q, k, v, do, do_far, h1, w_all, own, gain1, cos, sin, dx1, gwo, grouter, ggain2)


def after(value, *earlier):
    return lax.optimization_barrier((value, earlier))[0]


def over_y(value):
    return moved(value, lambda z, y, x, c: (z, 1 - y, x, c))


def beside(results, moving):
    return lax.optimization_barrier((results, moving))


def norm_kernel(rows_ref, gain_ref, out_ref):
    rows = rows_ref[...].astype(F32)
    out_ref[...] = (rows * unit_rms(rows) * gain_ref[...]).astype(BF)


def norm_rows(rows, gain):
    return pl.pallas_call(
        norm_kernel,
        out_shape=jax.ShapeDtypeStruct(rows.shape, BF),
        compiler_params=pltpu.CompilerParams(vmem_limit_bytes=VMEM_LIMIT),
        cost_estimate=microseconds(2),
        name="norm_rows",
    )(rows, gain)


def place_kernel(every_ref, gate_ref, up_ref, down_ref):
    for out_ref, at in ((gate_ref, 0), (up_ref, 256)):
        for k in range(4):
            for p in range(0, 8, 2):
                pair = [
                    every_ref[p + i, :, at + 64 * k : at + 64 * (k + 1)].astype(F32)
                    for i in range(2)
                ]
                to = 512 * k + 64 * p
                out_ref[:, to : to + 128] = jnp.concatenate(pair, 1)
    for p in range(8):
        for i in range(3):
            down_ref[64 * p : 64 * (p + 1), 256 * i : 256 * (i + 1)] = every_ref[
                p, 64 * i : 64 * (i + 1), 512:
            ].astype(F32)


def place_shared(every):
    vmem = pl.BlockSpec(memory_space=pltpu.VMEM)
    return pl.pallas_call(
        place_kernel,
        out_shape=(
            jax.ShapeDtypeStruct((D // 4, 2048), F32),
            jax.ShapeDtypeStruct((D // 4, 2048), F32),
            jax.ShapeDtypeStruct((512, D), F32),
        ),
        in_specs=[vmem],
        out_specs=(vmem,) * 3,
        compiler_params=pltpu.CompilerParams(vmem_limit_bytes=VMEM_LIMIT),
        cost_estimate=microseconds(4),
        name="place_shared",
    )(every)


OTHERS = (
    over_x,
    over_y,
    lambda value: moved(value, lambda z, y, x, c: (z, 1 - y, 1 - x, c)),
)


def plane_pieces(value, x, y):
    width = value.shape[-1] // 4
    quarters = [value[..., width * i : width * (i + 1)] for i in range(4)]

    def pick(column, row):
        left = jnp.where(column == 0, quarters[0], quarters[1])
        right = jnp.where(column == 0, quarters[2], quarters[3])
        return jnp.where(row == 0, left, right)

    return [pick(x, y), pick(1 - x, y), pick(x, 1 - y), pick(1 - x, 1 - y)]


def lane_tables():
    row = np.arange(TOK_DEV)
    position = np.where(row < PROMPT, row, PROMPT + (row - PROMPT) % CLEN).astype(np.float32)
    frequency = (10000.0 ** (-2.0 * np.arange(HD // 2) / HD)).astype(np.float32)
    angles = (position[:, None] * frequency[None, :]).astype(np.float64)
    cos, sin = np.cos(angles).astype(np.float32), np.sin(angles).astype(np.float32)
    return jnp.asarray(np.tile(cos, (1, 4))), jnp.asarray(np.tile(np.concatenate([-sin, sin], 1), (1, 2)))


def tuned_body(
    tokens,
    cotangent,
    routes,
    prompt_ids,
    attn_gain,
    query_weight,
    key_weight,
    value_weight,
    output_weight,
    ffn_gain,
    router_weight,
    shared_gate,
    shared_up,
    shared_down,
    expert_gate,
    expert_up_weight,
    expert_down,
):
    z, y, j = lax.axis_index("dp"), lax.axis_index("context"), lax.axis_index("experts")
    x, core = j // 2, j % 2
    plane = y * 4 + j
    shard = D // 4

    dense = jnp.concatenate([query_weight, key_weight, value_weight, output_weight], 1)
    dense = lax.dynamic_slice_in_dim(dense, plane * 384, 384, 1)
    gains = jnp.concatenate(
        [attn_gain[None], ffn_gain[None], jnp.zeros((EXT - 2, shard), BF)], 0
    )
    dense = jnp.concatenate([dense, jnp.concatenate([router_weight.T, gains], 1)], 0)
    dense_z = [over_z(dense, step) for step in (1, 2, 3)]

    far = over_y(tokens)
    ids = jnp.broadcast_to(prompt_ids.astype(BF)[:, None], (CONT, 128))
    far_ids = over_y(ids)
    dense = jnp.stack([dense] + after(dense_z, far, far_ids))
    slots = dense[:, shard:, :]
    slots = jnp.stack([slots[0], slots[3], slots[2], slots[1]])
    small = lax.dynamic_slice_in_dim(
        jnp.concatenate([slots, slots], 0), lax.rem(4 - z, 4), 4, 0
    )
    router_t = small[:, :, :shard].transpose(1, 0, 2).reshape(EXPERTS, D)
    gain1 = small[:, 0, shard:].reshape(1, D).astype(F32)
    gain2 = small[:, 1, shard:].reshape(1, D).astype(F32)
    flip_a, flip_b = jnp.where(core == 0, 2, 4), jnp.where(core == 0, 4, 2)
    flips = [0 * core, flip_a, flip_b, 0 * core + 6]
    flips = flips + [1 + flips[0], 1 + flip_b, 1 + flip_a, 1 + flips[3]]
    place = [jnp.bitwise_xor(plane, flip) for flip in flips]
    place += [lax.rem(z + 4 - slot, 4) for slot in range(4)]
    place += [(prompt_ids[m] != y) for m in range(CONT)]
    place = jnp.stack([v.astype(jnp.int32) for v in place])
    cos, sin = lane_tables()
    gain1, place, gain2, router_t, cos, sin = after((gain1, place, gain2, router_t, cos, sin))
    h1 = norm_rows(tokens, gain1)
    h1, dense_parts = beside(h1, (over_a(dense), over_b(dense)))
    dense_parts = [dense, *dense_parts, over_b(dense_parts[0])]
    dense_parts = dense_parts + [over_core(part) for part in dense_parts]

    expert_ids = jnp.arange(EXPERTS, dtype=jnp.int32)[:, None]
    route_t = routes.T
    member = (route_t[0:1] == expert_ids) | (route_t[1:2] == expert_ids)
    before = (jnp.arange(TOK_DEV)[:, None] < jnp.arange(TOK_DEV)[None, :]).astype(BF)
    ranks = jnp.dot(member.astype(BF), before, preferred_element_type=F32)
    ranks = jnp.where(member, ranks, -1.0).astype(BF)
    g_block = jnp.concatenate([cotangent, jnp.pad(ranks, ((0, 0), (0, D - TOK_DEV)))], 0)
    g_near = after(g_block, h1)
    g_x = over_x(g_near)
    g_group = [g_block, g_x, over_core(g_near), over_core(g_x)]

    units = lambda w: lax.dynamic_index_in_dim(
        w.reshape(shard, 4, 8, 64), plane, 2, keepdims=False
    ).reshape(shard, 256)
    down = lax.dynamic_slice_in_dim(shared_down, plane * 64, 64, 0)
    down = jnp.concatenate([down[:, 256 * i : 256 * (i + 1)] for i in range(3)], 0)
    shared = jnp.concatenate([units(shared_gate), units(shared_up), down], 1)
    shared = lax.all_gather(after(shared, dense), "dp", axis=0, tiled=False)
    shared_far = over_y(after(shared, h1))

    g_column = lax.all_gather(after(g_block, dense), "dp", axis=0, tiled=False)

    place = after(place, shared)
    flags = jnp.concatenate([prompt_ids == y, far_ids[:, 0].astype(jnp.int32) == y, core[None] != 0]).astype(jnp.int32)
    w_all, q, k, v, o, x1, h_block = attention_forward(
        place, dense_parts, h1, tokens, far, gain1, gain2, router_t, cos, sin
    )
    (h_block, x1), (g_x, shared_far) = beside((h_block, x1), (g_x, shared_far))
    g_group = [g_block, g_x, over_core(g_block), over_core(g_x)]

    h_x = over_x(h_block)
    h_near, g_near = [h_block, over_core(h_block)], [g_block, g_group[2]]
    h_column = lax.all_gather(h_block, "dp", axis=0, tiled=False)
    experts_w = (expert_gate, expert_up_weight, expert_down)
    base = (j * 4).astype(jnp.int32)
    more = shared_rows(h_near, g_near, shared, shared_far)
    more, (h_x, g_y) = beside(more, (h_x, over_y(after(g_block, h_block))))
    h_far, g_far = [h_x, over_core(h_x)], [g_x, g_group[3]]
    h_group = [h_near[0], h_far[0], h_near[1], h_far[1]]
    part = group_experts(base[None], 0, 2, h_group, g_group, (), *experts_w)
    (part, h_far), h_b = beside((part, h_far), over_b(after(h_block, h_x)))
    g_first = over_a(after(g_column, h_x))
    more = more + shared_rows(h_far, g_far, shared, shared_far)
    more, g_first = beside(more, g_first)
    g_second = jnp.where(core == 0, g_y, g_x)
    g_second = lax.all_gather(after(g_second, h_x), "dp", axis=0, tiled=False)
    results = group_experts(
        base[None] + 2, 2, 2, h_group, g_group, (*more, *part), *experts_w
    )
    g_third = over_b(g_first)
    results, (g_third, g_core) = beside(
        results, (g_third, [over_core(g_column), over_core(g_first)])
    )
    moe, dx = results[:4], results[4:]
    dx_x = pair_sum(dx[1], over_core(dx[3]))
    dx = [dx[0], over_core(dx[2]), over_x(dx_x)]
    h_column = after(h_column, dx_x)
    h_core = [over_core(h_column)]
    window = jnp.array([0, 1, 3, 4], jnp.int32)[z]
    s_pos = jnp.stack([window, (z // 2).astype(jnp.int32)])
    e_pos = jnp.stack([base, (z * 2 + y).astype(jnp.int32)])
    s_sums = shared_slice_grads(
        s_pos, [h_column, h_core[0]], [g_column, g_core[0]], shared
    )
    s_sums, dx = beside(s_sums, dx)
    dx1, do, do_c, grad_router_t, grad_gain2 = branch_backward(
        dx, h_block, x1, cotangent, gain2, router_t, w_all
    )
    gwo = inner_rows(o, dx1.astype(BF)).astype(BF)
    gwo, do_far = beside(gwo, over_y(do_c))
    h_first = over_a(after(h_column, do_far))
    h_second = lax.all_gather(after(h_b, do_far), "dp", axis=0, tiled=False)
    grad_inputs, keep, send = attention_backward(
        flags,
        q,
        k,
        v,
        do,
        do_far,
        h1,
        w_all,
        tokens,
        gain1,
        cos,
        sin,
        dx1,
        gwo,
        grad_router_t,
        grad_gain2,
    )
    (grad_inputs, keep, send), (h_first, g_second) = beside(
        (grad_inputs, keep, send), (h_first, g_second)
    )
    h_core.append(over_core(h_first))
    h_third = over_b(after(h_first, keep))
    h_parts, g_parts = [h_column, h_first] + h_core, [g_column, g_first] + g_core[:2]
    e_pos = after(e_pos, keep)
    e_sums = expert_slice_grads(e_pos, h_parts, g_parts, *experts_w, 256)
    (e_sums, keep), (send, h_second, h_third, g_far) = beside(
        (e_sums, keep),
        (over_core(send), h_second, h_third, [over_core(after(v, keep)) for v in (g_second, g_third)]),
    )
    h_far = [over_core(h_second), over_core(h_third)]
    h_parts, g_parts = [h_second, h_third] + h_far, [g_second, g_third] + g_far
    pieces = plane_pieces(pair_sum(keep, send), x, y)
    h_parts, pieces = after((h_parts, pieces))
    s_sums = shared_slice_grads(
        s_pos, [h_first, h_core[1], *h_parts], [g_first, g_core[1], *g_parts], shared, s_sums
    )
    (s_sums, pieces), there = beside(
        (s_sums, pieces), [over(piece) for over, piece in zip(OTHERS, pieces[1:])]
    )
    s_gate, s_up, s_down = s_sums
    z_own = pieces[0].astype(F32)
    for piece in there:
        z_own = z_own + piece.astype(F32)
    z_own = z_own.astype(BF)
    z_parts = [
        lax.dynamic_index_in_dim(z_own, lax.rem(z + step, 4), 0, keepdims=False)
        for step in (0, 1, 2, 3)
    ]
    moe = after(moe, s_gate)
    moe_x = pair_sum(moe[1], over_core(moe[3]))
    moe_core = over_core(moe[2])

    lead = z * 192 - window * 128
    s_down = lax.dynamic_slice_in_dim(s_down, (z % 2) * 64, 64, 0)
    mine = jnp.concatenate(
        [
            lax.dynamic_slice_in_dim(s_gate, lead, 192, 0),
            lax.dynamic_slice_in_dim(s_up, lead, 192, 0),
            jnp.concatenate([s_down[:, 256 * i : 256 * (i + 1)] for i in range(3)], 0),
        ],
        1,
    ).astype(BF)
    mine, z_parts, moe_x, moe_core, h_parts, g_parts = after(
        (mine, z_parts, moe_x, moe_core, h_parts, g_parts)
    )
    every = lax.all_gather(mine, ("context", "experts"), axis=0, tiled=False)
    moving = ([over_z(z_parts[step], step) for step in (1, 2, 3)], over_x(moe_x), every)
    e_gate, e_up, e_down = expert_slice_grads(e_pos, h_parts, g_parts, *experts_w, 256, e_sums)
    (e_gate, e_up, e_down), (there, moe_there, every) = beside((e_gate, e_up, e_down), moving)
    total = z_parts[0].astype(F32)
    for part in there:
        total = total + part.astype(F32)
    total = total.astype(BF)
    total_parts = [over(total) for over in OTHERS]
    layer_out = (
        x1 + (moe[0].astype(F32) + moe_core.astype(F32) + moe_there.astype(F32))
    ).astype(BF)
    s_gate, s_up, s_down = place_shared(every)
    (layer_out, s_gate), total_parts = beside((layer_out, s_gate), total_parts)
    beside_x = rejoin(total, total_parts[0], x)
    total = rejoin(beside_x, rejoin(total_parts[1], total_parts[2], x), y)
    other = over_core(total)
    sum_qk, sum_vo = jnp.where(core == 0, total, other), jnp.where(core == 0, other, total)
    extras = sum_qk[shard:, : 2 * shard].astype(F32)
    sum_qk, sum_vo = sum_qk[:shard].astype(F32), sum_vo[:shard].astype(F32)

    return (
        layer_out,
        grad_inputs,
        extras[0, shard:],
        sum_qk[:, :D],
        sum_qk[:, D:],
        sum_vo[:, :D],
        sum_vo[:, D:],
        extras[1, shard:],
        extras[:, :shard].T,
        s_gate,
        s_up,
        s_down,
        e_gate,
        e_up,
        e_down,
    )


def solution(mesh):
    tuned = dict(mesh.shape) == TUNED_MESH

    return jax.shard_map(
        tuned_body if tuned else plain_body,
        mesh=mesh,
        in_specs=(
            P(("dp", "context", "experts"), None),
            P(("dp", "context", "experts"), None),
            P(("dp", "context", "experts"), None),
            P(("dp", "context", "experts")),
            P("dp"),
            P("dp", None),
            P("dp", None),
            P("dp", None),
            P("dp", None),
            P("dp"),
            P("dp", None),
            P("dp", None),
            P("dp", None),
            P("dp", None),
            P("experts", None, None),
            P("experts", None, None),
            P("experts", None, None),
        ),
        out_specs=(
            P(("dp", "context", "experts"), None),
            P(("dp", "context", "experts"), None),
            P("dp"),
            P("dp", None),
            P("dp", None),
            P("dp", None),
            P("dp", None),
            P("dp"),
            P("dp", None),
            P("dp", None),
            P("dp", None),
            P("dp", None),
            P("experts", None, ("dp", "context")),
            P("experts", None, ("dp", "context")),
            P("experts", ("dp", "context"), None),
        ),
        check_vma=False,
    )
```

```python
import functools

import jax
import jax.numpy as jnp
import numpy as np
from jax import lax
from jax.sharding import PartitionSpec as P

from jax.experimental import pallas as pl
from jax.experimental.pallas import tpu as pltpu

D = 768
HEADS = 12
HD = 64
EXPERTS = 16
TOPK = 2
PROMPT = 256
CONT = 2
CLEN = 64
TOK_DEV = 384
CAP = 66


EPS = 1e-06


def rotary_tables(tok_rows):
    row_ids = jnp.arange(tok_rows)
    position = jnp.where(row_ids < PROMPT, row_ids, PROMPT + (row_ids - PROMPT) % CLEN).astype(
        jnp.float32
    )
    frequency = 10000.0 ** (-2.0 * jnp.arange(HD // 2).astype(jnp.float32) / HD)
    angles = position[:, None] * frequency[None, :]
    return (jnp.cos(angles), jnp.sin(angles))


def rotate(values_in, cos_table, sin_table):
    shaped = values_in.reshape(values_in.shape[:-1] + (HEADS, HD))
    lower_half = shaped[..., : HD // 2]
    upper_half = shaped[..., HD // 2 :]
    cos_part = cos_table[:, None, :]
    sin_part = sin_table[:, None, :]
    turned = jnp.concatenate(
        [
            lower_half * cos_part - upper_half * sin_part,
            upper_half * cos_part + lower_half * sin_part,
        ],
        -1,
    )
    return turned.reshape(values_in.shape)


def key_mask(context_index, prompt_pick, contexts):
    row_ids = jnp.arange(TOK_DEV)[:, None]
    col_ids = jnp.arange(contexts * PROMPT + CONT * CLEN)[None, :]
    prompt_row = row_ids < PROMPT
    cont_row = (row_ids - PROMPT) // CLEN
    within_row = (row_ids - PROMPT) % CLEN
    owner = jnp.sum(
        prompt_pick[None, :] * (jnp.arange(CONT)[None, :] == cont_row), -1, keepdims=True
    )
    target = jnp.where(prompt_row, context_index, owner)
    prompt_keys = col_ids < contexts * PROMPT
    prompt_ok = (
        prompt_keys
        & (col_ids // PROMPT == target)
        & (jnp.logical_not(prompt_row) | (col_ids % PROMPT <= row_ids))
    )
    offset = col_ids - contexts * PROMPT
    cont_ok = (
        jnp.logical_not(prompt_keys)
        & jnp.logical_not(prompt_row)
        & (offset // CLEN == cont_row)
        & (offset % CLEN <= within_row)
    )
    return prompt_ok | cont_ok


def inner_rows(left, right):
    return lax.dot_general(
        left, right, (((0,), (0,)), ((), ())), preferred_element_type=jnp.float32
    )


def times_transposed(left, right):
    return lax.dot_general(
        left, right, (((1,), (1,)), ((), ())), preferred_element_type=jnp.float32
    )


def swish_derivative(pre_act):
    sigma = jax.nn.sigmoid(pre_act)
    return sigma * (1.0 + pre_act * (1.0 - sigma))


def plain_body(
    tokens,
    cotangent,
    routes,
    prompt_ids,
    attn_gain,
    query_weight,
    key_weight,
    value_weight,
    output_weight,
    ffn_gain,
    router_weight,
    shared_gate,
    shared_up,
    shared_down,
    expert_gate,
    expert_up_weight,
    expert_down,
):
    contexts = lax.axis_size("context")
    context_here = lax.axis_index("context")
    gain_one, w_query, w_key, w_value, w_out, gain_two, w_router, w_sgate, w_sup, w_sdown = (
        lax.all_gather(attn_gain, "dp", axis=0, tiled=True),
        lax.all_gather(query_weight, "dp", axis=0, tiled=True),
        lax.all_gather(key_weight, "dp", axis=0, tiled=True),
        lax.all_gather(value_weight, "dp", axis=0, tiled=True),
        lax.all_gather(output_weight, "dp", axis=0, tiled=True),
        lax.all_gather(ffn_gain, "dp", axis=0, tiled=True),
        lax.all_gather(router_weight, "dp", axis=0, tiled=True),
        lax.all_gather(shared_gate, "dp", axis=0, tiled=True),
        lax.all_gather(shared_up, "dp", axis=0, tiled=True),
        lax.all_gather(shared_down, "dp", axis=0, tiled=True),
    )
    cos_table, sin_table = rotary_tables(TOK_DEV)
    inputs = tokens.astype(jnp.float32)
    inv_rms1 = lax.rsqrt(jnp.mean(inputs * inputs, -1, keepdims=True) + EPS)
    normed1 = inputs * inv_rms1
    gain1_f = gain_one.astype(jnp.float32)
    hidden1 = (normed1 * gain1_f).astype(jnp.bfloat16)
    query_f = jnp.dot(hidden1, w_query, preferred_element_type=jnp.float32)
    key_f = jnp.dot(hidden1, w_key, preferred_element_type=jnp.float32)
    value_f = jnp.dot(hidden1, w_value, preferred_element_type=jnp.float32)
    query_b = rotate(query_f, cos_table, sin_table).astype(jnp.bfloat16)
    key_b = rotate(key_f, cos_table, sin_table).astype(jnp.bfloat16)
    value_b = value_f.astype(jnp.bfloat16)
    prompt_keys, prompt_values = (
        lax.all_gather(key_b[:PROMPT], "context", axis=0, tiled=True),
        lax.all_gather(value_b[:PROMPT], "context", axis=0, tiled=True),
    )
    keys_h = jnp.concatenate([prompt_keys, key_b[PROMPT:]], 0).reshape(-1, HEADS, HD)
    values_h = jnp.concatenate([prompt_values, value_b[PROMPT:]], 0).reshape(-1, HEADS, HD)
    query_h = query_b.reshape(TOK_DEV, HEADS, HD)
    allowed = key_mask(context_here, prompt_ids, contexts)
    scores = jnp.where(
        allowed[None],
        0.125 * jnp.einsum("qhd,khd->hqk", query_h, keys_h, preferred_element_type=jnp.float32),
        -1e30,
    )
    row_max = jnp.max(scores, -1, keepdims=True)
    exp_scores = jnp.exp(scores - row_max)
    row_total = jnp.sum(exp_scores, -1, keepdims=True)
    log_total = row_max + jnp.log(row_total)
    attn_probs = (exp_scores / row_total).astype(jnp.bfloat16)
    attended = (
        jnp.einsum("hqk,khd->qhd", attn_probs, values_h, preferred_element_type=jnp.float32)
        .reshape(TOK_DEV, D)
        .astype(jnp.bfloat16)
    )
    resid = inputs + jnp.dot(attended, w_out, preferred_element_type=jnp.float32)
    inv_rms2 = lax.rsqrt(jnp.mean(resid * resid, -1, keepdims=True) + EPS)
    normed2 = resid * inv_rms2
    gain2_f = gain_two.astype(jnp.float32)
    hidden2 = (normed2 * gain2_f).astype(jnp.bfloat16)
    logits = jnp.dot(hidden2, w_router, preferred_element_type=jnp.float32)
    route_probs = jax.nn.softmax(logits, -1)
    route_hot = (routes[:, :, None] == jnp.arange(EXPERTS)[None, None, :]).astype(jnp.float32)
    gate_vals = jnp.sum(route_probs[:, None, :] * route_hot, -1)
    shared_gpre = jnp.dot(hidden2, w_sgate, preferred_element_type=jnp.float32)
    shared_upre = jnp.dot(hidden2, w_sup, preferred_element_type=jnp.float32)
    shared_act = (jax.nn.silu(shared_gpre) * shared_upre).astype(jnp.bfloat16)
    shared_res = jnp.dot(shared_act, w_sdown, preferred_element_type=jnp.float32)
    flat_route = routes.reshape(-1)
    flat_hot = (flat_route[:, None] == jnp.arange(EXPERTS)[None, :]).astype(jnp.int32)
    slot_ids = jnp.sum((jnp.cumsum(flat_hot, 0) - flat_hot) * flat_hot, -1)
    slot_index = flat_route * CAP + slot_ids
    send_rows = jnp.repeat(hidden2, TOPK, axis=0)
    outgoing = (
        jnp.zeros((EXPERTS * CAP, D), jnp.bfloat16)
        .at[slot_index]
        .set(send_rows)
        .reshape(EXPERTS, CAP, D)
    )
    received_rows = lax.all_to_all(outgoing, "experts", split_axis=0, concat_axis=1, tiled=True)
    expert_gate_preact = jnp.einsum(
        "mgx,mxp->mgp", received_rows, expert_gate, preferred_element_type=jnp.float32
    )
    expert_up_preact = jnp.einsum(
        "mgx,mxp->mgp", received_rows, expert_up_weight, preferred_element_type=jnp.float32
    )
    expert_activation = (jax.nn.silu(expert_gate_preact) * expert_up_preact).astype(jnp.bfloat16)
    expert_res = jnp.einsum(
        "erf,efd->erd", expert_activation, expert_down, preferred_element_type=jnp.float32
    ).astype(jnp.bfloat16)
    returned = lax.all_to_all(
        expert_res, "experts", split_axis=1, concat_axis=0, tiled=True
    ).reshape(EXPERTS * CAP, D)
    picked = returned[slot_index].astype(jnp.float32).reshape(TOK_DEV, TOPK, D)
    moe_out = jnp.sum(gate_vals[:, :, None] * picked, 1)
    layer_out = (resid + shared_res + moe_out).astype(jnp.bfloat16)
    gain_one, w_query, w_key, w_value, w_out, gain_two, w_router, w_sgate, w_sup, w_sdown = (
        lax.all_gather(attn_gain, "dp", axis=0, tiled=True),
        lax.all_gather(query_weight, "dp", axis=0, tiled=True),
        lax.all_gather(key_weight, "dp", axis=0, tiled=True),
        lax.all_gather(value_weight, "dp", axis=0, tiled=True),
        lax.all_gather(output_weight, "dp", axis=0, tiled=True),
        lax.all_gather(ffn_gain, "dp", axis=0, tiled=True),
        lax.all_gather(router_weight, "dp", axis=0, tiled=True),
        lax.all_gather(shared_gate, "dp", axis=0, tiled=True),
        lax.all_gather(shared_up, "dp", axis=0, tiled=True),
        lax.all_gather(shared_down, "dp", axis=0, tiled=True),
    )
    gain1_f = gain_one.astype(jnp.float32)
    gain2_f = gain_two.astype(jnp.float32)
    grad_total = cotangent.astype(jnp.float32)
    grad_gates = jnp.sum(grad_total[:, None, :] * picked, -1)
    grad_picked = (
        (gate_vals[:, :, None] * grad_total[:, None, :])
        .astype(jnp.bfloat16)
        .reshape(TOK_DEV * TOPK, D)
    )
    grad_back = (
        jnp.zeros((EXPERTS * CAP, D), jnp.bfloat16)
        .at[slot_index]
        .set(grad_picked)
        .reshape(EXPERTS, CAP, D)
    )
    grad_arrived = lax.all_to_all(grad_back, "experts", split_axis=0, concat_axis=1, tiled=True)
    grad_expert_activation = jnp.einsum(
        "erd,efd->erf", grad_arrived, expert_down, preferred_element_type=jnp.float32
    )
    grad_expert_gate_preact = (
        grad_expert_activation * expert_up_preact * swish_derivative(expert_gate_preact)
    ).astype(jnp.bfloat16)
    grad_expert_up_preact = (grad_expert_activation * jax.nn.silu(expert_gate_preact)).astype(
        jnp.bfloat16
    )
    expert_grad_down = jnp.einsum(
        "erf,erd->edf", expert_activation, grad_arrived, preferred_element_type=jnp.float32
    )
    expert_grad_gate = jnp.einsum(
        "xvb,xva->xba", received_rows, grad_expert_gate_preact, preferred_element_type=jnp.float32
    )
    expert_grad_up = jnp.einsum(
        "xvb,xva->xba", received_rows, grad_expert_up_preact, preferred_element_type=jnp.float32
    )
    grad_einputs = jnp.einsum(
        "cgj,clj->cgl", grad_expert_gate_preact, expert_gate, preferred_element_type=jnp.float32
    )
    grad_einputs = (
        grad_einputs
        + jnp.einsum(
            "cgj,clj->cgl",
            grad_expert_up_preact,
            expert_up_weight,
            preferred_element_type=jnp.float32,
        )
    ).astype(jnp.bfloat16)
    grad_returned = lax.all_to_all(
        grad_einputs, "experts", split_axis=1, concat_axis=0, tiled=True
    ).reshape(EXPERTS * CAP, D)
    grad_moe_in = jnp.sum(
        grad_returned[slot_index].astype(jnp.float32).reshape(TOK_DEV, TOPK, D), 1
    )
    grad_rprobs = jnp.sum(grad_gates[:, :, None] * route_hot, 1)
    grad_logits = (
        route_probs * (grad_rprobs - jnp.sum(route_probs * grad_rprobs, -1, keepdims=True))
    ).astype(jnp.bfloat16)
    grad_router_local = inner_rows(hidden2, grad_logits)
    grad_total_b = grad_total.astype(jnp.bfloat16)
    grad_sdown = inner_rows(shared_act, grad_total_b)
    grad_sact = times_transposed(grad_total_b, w_sdown)
    grad_sgpre = (grad_sact * shared_upre * swish_derivative(shared_gpre)).astype(jnp.bfloat16)
    grad_supre = (grad_sact * jax.nn.silu(shared_gpre)).astype(jnp.bfloat16)
    grad_sgate = inner_rows(hidden2, grad_sgpre)
    grad_sup = inner_rows(hidden2, grad_supre)
    grad_hidden2 = (
        grad_moe_in
        + times_transposed(grad_logits, w_router)
        + times_transposed(grad_sgpre, w_sgate)
        + times_transposed(grad_supre, w_sup)
    )
    grad_gain2 = jnp.sum(grad_hidden2 * normed2, 0)
    grad_normed2 = grad_hidden2 * gain2_f
    grad_resid = (
        inv_rms2 * (grad_normed2 - normed2 * jnp.mean(grad_normed2 * normed2, -1, keepdims=True))
        + grad_total
    )
    grad_branch = grad_resid.astype(jnp.bfloat16)
    grad_wout = inner_rows(attended, grad_branch)
    grad_attended = (
        times_transposed(grad_branch, w_out).astype(jnp.bfloat16).reshape(TOK_DEV, HEADS, HD)
    )
    scores_again = jnp.where(
        allowed[None],
        0.125 * jnp.einsum("qhd,khd->hqk", query_h, keys_h, preferred_element_type=jnp.float32),
        -1e30,
    )
    probs_f = jnp.exp(scores_again - log_total)
    probs_b = probs_f.astype(jnp.bfloat16)
    grad_pattn = jnp.einsum(
        "qhd,khd->hqk", grad_attended, values_h, preferred_element_type=jnp.float32
    )
    grad_scores = (
        probs_f * (grad_pattn - jnp.sum(probs_f * grad_pattn, -1, keepdims=True))
    ).astype(jnp.bfloat16)
    grad_query = 0.125 * jnp.einsum(
        "hqk,khd->qhd", grad_scores, keys_h, preferred_element_type=jnp.float32
    ).reshape(TOK_DEV, D)
    grad_keys = 0.125 * jnp.einsum(
        "hqk,qhd->khd", grad_scores, query_h, preferred_element_type=jnp.float32
    ).reshape(-1, D)
    grad_values = jnp.einsum(
        "hqk,qhd->khd", probs_b, grad_attended, preferred_element_type=jnp.float32
    ).reshape(-1, D)
    prompt_span = contexts * PROMPT
    grad_pkeys, grad_pvalues = (
        lax.psum_scatter(
            grad_keys[:prompt_span].astype(jnp.bfloat16), "context", scatter_dimension=0, tiled=True
        ).astype(jnp.float32),
        lax.psum_scatter(
            grad_values[:prompt_span].astype(jnp.bfloat16),
            "context",
            scatter_dimension=0,
            tiled=True,
        ).astype(jnp.float32),
    )
    grad_key_all = jnp.concatenate([grad_pkeys, grad_keys[prompt_span:]], 0)
    grad_value_all = jnp.concatenate([grad_pvalues, grad_values[prompt_span:]], 0)
    grad_qpre = rotate(grad_query, cos_table, -sin_table).astype(jnp.bfloat16)
    grad_kpre = rotate(grad_key_all, cos_table, -sin_table).astype(jnp.bfloat16)
    grad_vpre = grad_value_all.astype(jnp.bfloat16)
    grad_wquery = inner_rows(hidden1, grad_qpre)
    grad_wkey = inner_rows(hidden1, grad_kpre)
    grad_wvalue = inner_rows(hidden1, grad_vpre)
    grad_hidden1 = (
        times_transposed(grad_qpre, w_query)
        + times_transposed(grad_kpre, w_key)
        + times_transposed(grad_vpre, w_value)
    )
    grad_gain1 = jnp.sum(grad_hidden1 * normed1, 0)
    grad_normed1 = grad_hidden1 * gain1_f
    grad_inputs = (
        inv_rms1 * (grad_normed1 - normed1 * jnp.mean(grad_normed1 * normed1, -1, keepdims=True))
        + grad_resid
    )
    shares = (
        lax.psum_scatter(
            grad_gain1.astype(jnp.bfloat16), "dp", scatter_dimension=0, tiled=True
        ).astype(jnp.float32),
        lax.psum_scatter(
            grad_wquery.astype(jnp.bfloat16), "dp", scatter_dimension=0, tiled=True
        ).astype(jnp.float32),
        lax.psum_scatter(
            grad_wkey.astype(jnp.bfloat16), "dp", scatter_dimension=0, tiled=True
        ).astype(jnp.float32),
        lax.psum_scatter(
            grad_wvalue.astype(jnp.bfloat16), "dp", scatter_dimension=0, tiled=True
        ).astype(jnp.float32),
        lax.psum_scatter(
            grad_wout.astype(jnp.bfloat16), "dp", scatter_dimension=0, tiled=True
        ).astype(jnp.float32),
        lax.psum_scatter(
            grad_gain2.astype(jnp.bfloat16), "dp", scatter_dimension=0, tiled=True
        ).astype(jnp.float32),
        lax.psum_scatter(
            grad_router_local.astype(jnp.bfloat16), "dp", scatter_dimension=0, tiled=True
        ).astype(jnp.float32),
        lax.psum_scatter(
            grad_sgate.astype(jnp.bfloat16), "dp", scatter_dimension=0, tiled=True
        ).astype(jnp.float32),
        lax.psum_scatter(
            grad_sup.astype(jnp.bfloat16), "dp", scatter_dimension=0, tiled=True
        ).astype(jnp.float32),
        lax.psum_scatter(
            grad_sdown.astype(jnp.bfloat16), "dp", scatter_dimension=0, tiled=True
        ).astype(jnp.float32),
    )
    totals = (
        lax.psum(shares[0].astype(jnp.bfloat16), ("context", "experts")).astype(jnp.float32),
        lax.psum(shares[1].astype(jnp.bfloat16), ("context", "experts")).astype(jnp.float32),
        lax.psum(shares[2].astype(jnp.bfloat16), ("context", "experts")).astype(jnp.float32),
        lax.psum(shares[3].astype(jnp.bfloat16), ("context", "experts")).astype(jnp.float32),
        lax.psum(shares[4].astype(jnp.bfloat16), ("context", "experts")).astype(jnp.float32),
        lax.psum(shares[5].astype(jnp.bfloat16), ("context", "experts")).astype(jnp.float32),
        lax.psum(shares[6].astype(jnp.bfloat16), ("context", "experts")).astype(jnp.float32),
        lax.psum(shares[7].astype(jnp.bfloat16), ("context", "experts")).astype(jnp.float32),
        lax.psum(shares[8].astype(jnp.bfloat16), ("context", "experts")).astype(jnp.float32),
        lax.psum(shares[9].astype(jnp.bfloat16), ("context", "experts")).astype(jnp.float32),
    )
    summed_gate, summed_up, summed_down = (
        lax.psum_scatter(
            expert_grad_gate.astype(jnp.bfloat16),
            ("dp", "context"),
            scatter_dimension=2,
            tiled=True,
        ).astype(jnp.float32),
        lax.psum_scatter(
            expert_grad_up.astype(jnp.bfloat16), ("dp", "context"), scatter_dimension=2, tiled=True
        ).astype(jnp.float32),
        lax.psum_scatter(
            expert_grad_down.astype(jnp.bfloat16),
            ("dp", "context"),
            scatter_dimension=2,
            tiled=True,
        ).astype(jnp.float32),
    )
    summed_down = jnp.transpose(summed_down, (0, 2, 1))
    return (
        layer_out,
        grad_inputs,
        totals[0],
        totals[1],
        totals[2],
        totals[3],
        totals[4],
        totals[5],
        totals[6],
        totals[7],
        totals[8],
        totals[9],
        summed_gate,
        summed_up,
        summed_down,
    )


TUNED_MESH = {"dp": 4, "context": 2, "experts": 4}
AXES = ("dp", "context", "experts")
SLOT = 72
EXT = 16
ROWS = TOK_DEV + EXT
BF = jnp.bfloat16
F32 = jnp.float32
VMEM_LIMIT = 60 * 1024 * 1024


def microseconds(time):
    return pl.CostEstimate(flops=0, bytes_accessed=int(time * 0.4e6), transcendentals=0)


def moved(value, target):
    pairs = []
    for z in range(4):
        for y in range(2):
            for x in range(2):
                for c in range(2):
                    tz, ty, tx, tc = target(z, y, x, c)
                    pairs.append((((z * 2 + y) * 2 + x) * 2 + c, ((tz * 2 + ty) * 2 + tx) * 2 + tc))
    return lax.ppermute(value, AXES, pairs)


def over_core(value):
    return moved(value, lambda z, y, x, c: (z, y, x, 1 - c))


def over_x(value):
    return moved(value, lambda z, y, x, c: (z, y, 1 - x, c))


def over_a(value):
    return moved(value, lambda z, y, x, c: (z, y, 1 - x, c) if c == 0 else (z, 1 - y, x, c))


def over_b(value):
    return moved(value, lambda z, y, x, c: (z, 1 - y, x, c) if c == 0 else (z, y, 1 - x, c))


def over_z(value, step):
    return moved(value, lambda z, y, x, c: ((z + step) % 4, y, x, c))


def contract(left, right, left_dim, right_dim):
    return lax.dot_general(
        left, right, (((left_dim,), (right_dim,)), ((), ())), preferred_element_type=F32
    )


def one_hot_rows(rank_row):
    slots = lax.broadcasted_iota(jnp.int32, (SLOT, TOK_DEV), 0).astype(F32)
    return (slots == rank_row).astype(F32)


def swish_parts(pre_act):
    sigma = jax.nn.sigmoid(pre_act)
    return pre_act * sigma, sigma * (1.0 + pre_act * (1.0 - sigma))


def group_kernel(
    blocks,
    more,
    base_ref,
    *refs,
):
    block_refs, refs = refs[: 2 * blocks], refs[2 * blocks :]
    more_refs, refs = refs[:more], refs[more:]
    wg_ref, wu_ref, wd_ref = refs[:3]
    results, refs = refs[3 : 3 + 2 * blocks], refs[3 + 2 * blocks :]
    (
        rank_sc,
        prob_sc,
        x_sc,
        gate_sc,
        y_sc,
        acc_sc,
        dgate_sc,
        sel_sc,
        drp_sc,
        in_sc,
        out_sc,
        in_sems,
        out_sems,
    ) = refs[:13]
    e = pl.program_id(0)
    f = pl.program_id(1)
    experts = pl.num_programs(0)
    base = base_ref[0]
    copies = [
        pltpu.make_async_copy(source, into, refs[-1].at[i])
        for i, (source, into) in enumerate(zip(more_refs, refs[13:]))
    ]

    arrivals = [
        pltpu.make_async_copy(
            block_refs[side * blocks + b],
            in_sc.at[b, :, side * D : (side + 1) * D],
            in_sems.at[side, b],
        )
        for b in range(blocks)
        for side in range(2)
    ]

    @pl.when((e == 0) & (f == 0))
    def _():
        for one in arrivals + copies:
            one.start()
        drp_sc[...] = jnp.zeros_like(drp_sc)
        count = x_sc.shape[0]
        rows = []
        for b in range(blocks):
            for one in arrivals[2 * b : 2 * b + 2]:
                one.wait()
            rank_sc[b] = in_sc[b, TOK_DEV:, D : D + TOK_DEV].astype(F32)
            prob_sc[b] = in_sc[b, TOK_DEV:, :TOK_DEV].astype(F32) + in_sc[
                b, TOK_DEV:, TOK_DEV:D
            ].astype(F32)
            hots = []
            for i in range(count):
                hot = one_hot_rows(rank_sc[b, pl.ds(base + i, 1), :])
                gate_sc[i, b * SLOT : (b + 1) * SLOT, :] = jnp.sum(
                    hot * prob_sc[b, pl.ds(base + i, 1), :], -1, keepdims=True
                )
                hots.append(hot)
            hot = jnp.concatenate(hots, 0).astype(BF)
            rows.append(jnp.dot(hot, in_sc[b, :TOK_DEV, :], preferred_element_type=F32))
            if b % 2:
                span = slice((b - 1) * SLOT, (b + 1) * SLOT)
                for i in range(count):
                    of = slice(i * SLOT, (i + 1) * SLOT)
                    x_sc[i, span, :] = jnp.concatenate([v[of] for v in rows[-2:]], 0).astype(BF)

    @pl.when(f == 0)
    def _():
        y_sc[...] = jnp.zeros_like(y_sc)
        acc_sc[...] = jnp.zeros_like(acc_sc)
        dgate_sc[...] = jnp.zeros_like(dgate_sc)

    rows = x_sc[e, :, :D]
    gate_pre = jnp.dot(rows, wg_ref[0], preferred_element_type=F32)
    up_pre = jnp.dot(rows, wu_ref[0], preferred_element_type=F32)
    back = contract(x_sc[e, :, D:], wd_ref[0], 1, 1)
    swish, slope = swish_parts(gate_pre)
    inner = (swish * up_pre).astype(BF)
    dgate_sc[...] += jnp.sum(back * inner.astype(F32), -1, keepdims=True)
    back = back * gate_sc[e]
    dgate_pre = (back * up_pre * slope).astype(BF)
    dup_pre = (back * swish).astype(BF)
    y_sc[...] += jnp.dot(inner, wd_ref[0], preferred_element_type=F32)
    acc_sc[...] += contract(dgate_pre, wg_ref[0], 1, 1) + contract(dup_pre, wu_ref[0], 1, 1)

    @pl.when(f == pl.num_programs(1) - 1)
    def _():
        for b in range(blocks):
            span = slice(b * SLOT, (b + 1) * SLOT)
            into = pl.ds(pl.multiple_of(e * SLOT, 8), SLOT)
            sel_sc[b, into, :D] = y_sc[span, :] * gate_sc[e, span, :]
            sel_sc[b, into, D:] = acc_sc[span, :]
            hot = one_hot_rows(rank_sc[b, pl.ds(base + e, 1), :])
            drp_sc[b, pl.ds(base + e, 1), :] = jnp.sum(hot * dgate_sc[span, :], 0, keepdims=True)

    @pl.when((f == pl.num_programs(1) - 1) & (e == experts - 1))
    def _():
        for one in copies:
            one.wait()
        leaving = []
        for b in range(blocks):
            side, at = divmod(b, blocks // 2)
            moe_out, dx_out = out_sc.at[0, b], out_sc.at[1, b]
            hot = jnp.concatenate(
                [
                    one_hot_rows(rank_sc[b, pl.ds(base + i, 1), :])
                    for i in range(x_sc.shape[0])
                ],
                0,
            ).astype(BF)
            both = contract(hot, sel_sc[b].astype(BF), 0, 0)
            moe, dx = both[:, :D], both[:, D:]
            drp = drp_sc[b]
            if more:
                shared = refs[13 + 2 * at : 15 + 2 * at]
                moe_before, dx_before = refs[17 + b], refs[17 + blocks + b]
                moe = moe + shared[0][side].astype(F32) + moe_before[...].astype(F32)
                dx = dx + shared[1][side].astype(F32) + dx_before[:TOK_DEV, :].astype(F32)
                drp = drp + dx_before[TOK_DEV:, :TOK_DEV].astype(F32)
                drp = drp + dx_before[TOK_DEV:, TOK_DEV:].astype(F32)
            moe_out[:TOK_DEV, :] = moe.astype(BF)
            dx_out[:TOK_DEV, :] = dx.astype(BF)
            high = drp.astype(BF)
            dx_out[TOK_DEV:, :TOK_DEV] = high
            dx_out[TOK_DEV:, TOK_DEV:] = (drp - high.astype(F32)).astype(BF)
            sent = (
                pltpu.make_async_copy(moe_out.at[:TOK_DEV], results[b], out_sems.at[0, b]),
                pltpu.make_async_copy(dx_out, results[blocks + b], out_sems.at[1, b]),
            )
            for one in sent:
                one.start()
            leaving += sent
        for one in leaving:
            one.wait()


def group_experts(base, first, experts, h_group, g_group, more, w_gate, w_up, w_down):
    blocks = len(h_group)
    ff = w_gate.shape[2]
    tile = 512
    results = [(TOK_DEV, D)] * blocks + [(ROWS, D)] * blocks
    return pl.pallas_call(
        functools.partial(group_kernel, blocks, len(more)),
        out_shape=tuple(jax.ShapeDtypeStruct(s, BF) for s in results),
        grid_spec=pltpu.PrefetchScalarGridSpec(
            num_scalar_prefetch=1,
            grid=(experts, ff // tile),
            in_specs=[pl.BlockSpec(memory_space=pl.ANY)] * (2 * blocks + len(more))
            + [
                pl.BlockSpec((1, D, tile), lambda e, f, s: (first + e, 0, f)),
                pl.BlockSpec((1, D, tile), lambda e, f, s: (first + e, 0, f)),
                pl.BlockSpec((1, tile, D), lambda e, f, s: (first + e, f, 0)),
            ],
            out_specs=[pl.BlockSpec(memory_space=pltpu.HBM)] * len(results),
            scratch_shapes=[
                pltpu.VMEM((blocks, EXPERTS, TOK_DEV), F32),
                pltpu.VMEM((blocks, EXPERTS, TOK_DEV), F32),
                pltpu.VMEM((experts, blocks * SLOT, 2 * D), BF),
                pltpu.VMEM((experts, blocks * SLOT, 1), F32),
                pltpu.VMEM((blocks * SLOT, D), F32),
                pltpu.VMEM((blocks * SLOT, D), F32),
                pltpu.VMEM((blocks * SLOT, 1), F32),
                pltpu.VMEM((blocks, experts * SLOT, 2 * D), F32),
                pltpu.VMEM((blocks, EXPERTS, TOK_DEV), F32),
                pltpu.VMEM((blocks, ROWS, 2 * D), BF),
                pltpu.VMEM((2, blocks, ROWS, D), BF),
                pltpu.SemaphoreType.DMA((2, blocks)),
                pltpu.SemaphoreType.DMA((2, blocks)),
            ]
            + [pltpu.VMEM(v.shape, v.dtype) for v in more]
            + [pltpu.SemaphoreType.DMA((max(1, len(more)),))],
        ),
        compiler_params=pltpu.CompilerParams(vmem_limit_bytes=VMEM_LIMIT),
        cost_estimate=microseconds(21),
        name="group_experts",
    )(base, *h_group, *g_group, *more, w_gate, w_up, w_down)


def shared_kernel(h_a_ref, h_b_ref, g_a_ref, g_b_ref, w_a_ref, w_b_ref, out_ref, dh_ref, h_sc, g_sc, out_sc, dh_sc):
    for k, (h_ref, g_ref) in enumerate(((h_a_ref, g_a_ref), (h_b_ref, g_b_ref))):
        h_sc[k * TOK_DEV : (k + 1) * TOK_DEV, :] = h_ref[:TOK_DEV, :]
        g_sc[k * TOK_DEV : (k + 1) * TOK_DEV, :] = g_ref[:TOK_DEV, :]
    for k, w_ref in enumerate((w_a_ref, w_b_ref)):
        w_gate, w_up = w_ref[:, :, :256].reshape(D, 256), w_ref[:, :, 256:512].reshape(D, 256)
        w_down = jnp.concatenate(
            [w_ref[:, 64 * i : 64 * (i + 1), 512:].reshape(256, 256) for i in range(3)], 1
        )
        gate_pre = jnp.dot(h_sc[...], w_gate, preferred_element_type=F32)
        up_pre = jnp.dot(h_sc[...], w_up, preferred_element_type=F32)
        back = contract(g_sc[...], w_down, 1, 1)
        swish, slope = swish_parts(gate_pre)
        inner = (swish * up_pre).astype(BF)
        out = jnp.dot(inner, w_down, preferred_element_type=F32)
        dgate_pre = (back * up_pre * slope).astype(BF)
        dup_pre = (back * swish).astype(BF)
        dh = contract(dgate_pre, w_gate, 1, 1) + contract(dup_pre, w_up, 1, 1)
        if k == 0:
            out_sc[...], dh_sc[...] = out, dh
    for b in range(2):
        rows = slice(b * TOK_DEV, (b + 1) * TOK_DEV)
        out_ref[b] = (out_sc[rows, :] + out[rows]).astype(BF)
        dh_ref[b] = (dh_sc[rows, :] + dh[rows]).astype(BF)


def shared_rows(h_pair, g_pair, w_own, w_far):
    rows = jax.ShapeDtypeStruct((2, TOK_DEV, D), BF)
    vmem = pl.BlockSpec(memory_space=pltpu.VMEM)
    return pl.pallas_call(
        shared_kernel,
        out_shape=(rows, rows),
        in_specs=[vmem] * 6,
        out_specs=(vmem, vmem),
        scratch_shapes=[
            pltpu.VMEM((2 * TOK_DEV, D), BF),
            pltpu.VMEM((2 * TOK_DEV, D), BF),
            pltpu.VMEM((2 * TOK_DEV, D), F32),
            pltpu.VMEM((2 * TOK_DEV, D), F32),
        ],
        compiler_params=pltpu.CompilerParams(vmem_limit_bytes=VMEM_LIMIT),
        cost_estimate=microseconds(8),
        name="shared_rows",
    )(*h_pair, *g_pair, w_own, w_far)


def start_parts(h_parts, g_parts, h_buf, g_buf, sems):
    per = h_parts[0].shape[0]
    copies = []
    for i in range(len(h_parts)):
        for k in range(per // 2):
            at, into = pl.ds(2 * k, 2), pl.ds(i * per + 2 * k, 2)
            number = i * (per // 2) + k
            copies.append(
                (
                    pltpu.make_async_copy(h_parts[i].at[at], h_buf.at[into], sems.at[0, number]),
                    pltpu.make_async_copy(g_parts[i].at[at], g_buf.at[into], sems.at[1, number]),
                )
            )
    for pair in copies:
        for one in pair:
            one.start()
    return copies


def each_pair(copies, work):
    done = 0
    for upto in [1, 2] + list(range(4, len(copies) + 1, 2)):
        for pair in copies[done:upto]:
            for one in pair:
                one.wait()
        lax.fori_loop(done, upto, work, 0, unroll=True)
        done = upto


def expert_slice_kernel(parts, more, pos_ref, *refs):
    h_parts, g_parts = refs[:parts], refs[parts : 2 * parts]
    weights = refs[2 * parts : 2 * parts + 3]
    refs = refs[2 * parts + 3 :]
    sums, refs = refs[: 3 * more], refs[3 * more :]
    outs, (buf, x_sc, gd_sc, rank_sc, prob_sc) = refs[:3], refs[3:8]
    wg_ref, wu_ref, wd_ref, og_ref, ou_ref, od_ref, sems, w_sems, out_sems = refs[8:]
    base = pos_ref[0]
    experts, _, width = wg_ref.shape
    per = h_parts[0].shape[0]
    copies = start_parts(h_parts, g_parts, buf.at[:, :, :D], buf.at[:, :, D:], sems)
    cols = pl.ds(pl.multiple_of(pos_ref[1] * width, width), width)
    loads = [
        pltpu.make_async_copy(weights[0].at[:, :, cols], wg_ref, w_sems.at[0]),
        pltpu.make_async_copy(weights[1].at[:, :, cols], wu_ref, w_sems.at[1]),
        pltpu.make_async_copy(weights[2].at[:, cols, :], wd_ref, w_sems.at[2]),
    ]
    for i in range(3 * more):
        loads.append(
            pltpu.make_async_copy(sums[i], (og_ref, ou_ref, od_ref)[i], w_sems.at[3 + i])
        )
    for one in loads:
        one.start()

    def dispatch(pair, carry):
        both = []
        for k in range(2):
            b = 2 * pair + k
            rank_sc[k] = buf[b, TOK_DEV:, D : D + TOK_DEV].astype(F32)
            prob_sc[k] = buf[b, TOK_DEV:, :TOK_DEV].astype(F32) + buf[
                b, TOK_DEV:, TOK_DEV:D
            ].astype(F32)
            hots, gates = [], []
            for i in range(experts):
                hot = one_hot_rows(rank_sc[k, pl.ds(base + i, 1), :])
                gates.append(
                    jnp.sum(hot * prob_sc[k, pl.ds(base + i, 1), :], -1, keepdims=True)
                )
                hots.append(hot)
            hot = jnp.concatenate(hots, 0).astype(BF)
            rows = jnp.dot(hot, buf[b, :TOK_DEV, :], preferred_element_type=F32)
            both.append((rows[:, :D], rows[:, D:] * jnp.concatenate(gates, 0)))
        into = pl.ds(pl.multiple_of(pair * 2 * SLOT, 2 * SLOT), 2 * SLOT)
        for i in range(experts):
            span = slice(i * SLOT, (i + 1) * SLOT)
            x_sc[i, into, :] = jnp.concatenate([v[0][span] for v in both], 0).astype(BF)
            gd_sc[i, into, :] = jnp.concatenate([v[1][span] for v in both], 0).astype(BF)
        return carry

    each_pair(copies, dispatch)
    for one in loads:
        one.wait()

    def products(i, carry):
        rows = x_sc[i]
        gate_pre = jnp.dot(rows, wg_ref[i], preferred_element_type=F32)
        up_pre = jnp.dot(rows, wu_ref[i], preferred_element_type=F32)
        back = contract(gd_sc[i], wd_ref[i], 1, 1)
        swish, slope = swish_parts(gate_pre)
        inner = (swish * up_pre).astype(BF)
        dgate_pre = (back * up_pre * slope).astype(BF)
        dup_pre = (back * swish).astype(BF)
        add_g = contract(rows, dgate_pre, 0, 0)
        add_u = contract(rows, dup_pre, 0, 0)
        add_d = contract(inner, gd_sc[i], 0, 0)
        if more:
            og_ref[i] += add_g
            ou_ref[i] += add_u
            od_ref[i] += add_d
        else:
            og_ref[i], ou_ref[i], od_ref[i] = add_g, add_u, add_d
        for k, source in enumerate((og_ref, ou_ref, od_ref)):
            pltpu.make_async_copy(source.at[i], outs[k].at[i], out_sems.at[k, i]).start()
        return carry

    lax.fori_loop(0, experts, products, 0, unroll=2 if experts % 2 == 0 else 1)
    for i in range(experts):
        for k, source in enumerate((og_ref, ou_ref, od_ref)):
            pltpu.make_async_copy(source.at[i], outs[k].at[i], out_sems.at[k, i]).wait()


def expert_slice_grads(pos, h_parts, g_parts, w_gate, w_up, w_down, width, sums=()):
    parts, per = len(h_parts), h_parts[0].shape[0]
    experts = w_gate.shape[0]
    blocks = parts * per
    shapes = ((experts, D, width), (experts, D, width), (experts, width, D))
    anywhere = pl.BlockSpec(memory_space=pl.ANY)
    return pl.pallas_call(
        functools.partial(expert_slice_kernel, parts, len(sums) // 3),
        out_shape=tuple(jax.ShapeDtypeStruct(s, F32) for s in shapes),
        in_specs=[pl.BlockSpec(memory_space=pltpu.SMEM)]
        + [anywhere] * (2 * parts + 3 + len(sums)),
        out_specs=(pl.BlockSpec(memory_space=pltpu.HBM),) * 3,
        scratch_shapes=[
            pltpu.VMEM((blocks, ROWS, 2 * D), BF),
            pltpu.VMEM((experts, blocks * SLOT, D), BF),
            pltpu.VMEM((experts, blocks * SLOT, D), BF),
            pltpu.VMEM((2, EXPERTS, TOK_DEV), F32),
            pltpu.VMEM((2, EXPERTS, TOK_DEV), F32),
        ]
        + [pltpu.VMEM(s, BF) for s in shapes]
        + [pltpu.VMEM(s, F32) for s in shapes]
        + [
            pltpu.SemaphoreType.DMA((2, blocks // 2)),
            pltpu.SemaphoreType.DMA((6,)),
            pltpu.SemaphoreType.DMA((3, experts)),
        ],
        compiler_params=pltpu.CompilerParams(vmem_limit_bytes=VMEM_LIMIT),
        cost_estimate=microseconds(31),
        name="expert_slice_grads",
    )(pos, *h_parts, *g_parts, w_gate, w_up, w_down, *sums)


def shared_slice_kernel(parts, more, pos_ref, *refs):
    h_parts, g_parts = refs[:parts], refs[parts : 2 * parts]
    w_ref = refs[2 * parts]
    refs = refs[2 * parts + 1 :]
    sums, refs = refs[: 3 * more], refs[3 * more :]
    if more:
        mine_ref, refs = refs[0], refs[1:]
    og_ref, ou_ref, od_ref, h_buf, g_buf, inner_sc, wg_ref, wu_ref, wd_ref, sems = refs
    per = h_parts[0].shape[0]
    copies = start_parts(h_parts, g_parts, h_buf, g_buf, sems)
    wg_ref[...] = w_ref[:, :, :256].reshape(D, 256)
    wu_ref[...] = w_ref[:, :, 256:512].reshape(D, 256)
    for i in range(3):
        wd_ref[:, 256 * i : 256 * (i + 1)] = w_ref[:, 64 * i : 64 * (i + 1), 512:].reshape(256, 256)
    window = pl.ds(pl.multiple_of(pos_ref[0] * 128, 128), og_ref.shape[0])
    lanes = pl.ds(pl.multiple_of(pos_ref[1] * 128, 128), od_ref.shape[0])
    for i, out_ref in enumerate((og_ref, ou_ref, od_ref)):
        out_ref[...] = sums[i][...] if more else jnp.zeros_like(out_ref)

    def two(buf, pair, cols=slice(None)):
        return jnp.concatenate([buf[2 * pair + k, :TOK_DEV, cols] for k in range(2)], 0)

    def products(pair, carry):
        rows, grads = two(h_buf, pair), two(g_buf, pair)
        gate_pre = jnp.dot(rows, wg_ref[...], preferred_element_type=F32)
        up_pre = jnp.dot(rows, wu_ref[...], preferred_element_type=F32)
        back = contract(grads, wd_ref[...], 1, 1)
        swish, slope = swish_parts(gate_pre)
        inner_sc[...] = (swish * up_pre).astype(BF)
        dgate_pre = (back * up_pre * slope).astype(BF)
        dup_pre = (back * swish).astype(BF)
        picked = two(h_buf, pair, window)
        og_ref[...] += contract(picked, dgate_pre, 0, 0)
        ou_ref[...] += contract(picked, dup_pre, 0, 0)
        od_ref[...] += contract(inner_sc[:, lanes], grads, 0, 0)
        return carry

    each_pair(copies, products)
    if more:
        rows = pl.ds(pl.multiple_of(pos_ref[2], 64), D // 4)
        mine_ref[:, :256] = og_ref[rows, :].astype(BF)
        mine_ref[:, 256:512] = ou_ref[rows, :].astype(BF)
        down = od_ref[pl.ds(pl.multiple_of(pos_ref[3], 64), 64), :].astype(BF)
        for i in range(3):
            mine_ref[64 * i : 64 * (i + 1), 512:] = down[:, 256 * i : 256 * (i + 1)]


def shared_slice_grads(pos, h_parts, g_parts, weights, sums=()):
    parts, per = len(h_parts), h_parts[0].shape[0]
    blocks = parts * per
    width = 256
    shapes = ((256, width), (256, width), (128, D))
    vmem = pl.BlockSpec(memory_space=pltpu.VMEM)
    anywhere = pl.BlockSpec(memory_space=pl.ANY)
    return pl.pallas_call(
        functools.partial(shared_slice_kernel, parts, len(sums) // 3),
        out_shape=jax.ShapeDtypeStruct((D // 4, D), BF)
        if sums
        else tuple(jax.ShapeDtypeStruct(s, F32) for s in shapes),
        in_specs=[pl.BlockSpec(memory_space=pltpu.SMEM)]
        + [anywhere] * (2 * parts)
        + [vmem] * (1 + len(sums)),
        out_specs=vmem if sums else (vmem,) * 3,
        scratch_shapes=[pltpu.VMEM(s, F32) for s in (shapes if sums else ())]
        + [
            pltpu.VMEM((blocks, ROWS, D), BF),
            pltpu.VMEM((blocks, ROWS, D), BF),
            pltpu.VMEM((2 * TOK_DEV, width), BF),
            pltpu.VMEM((D, width), BF),
            pltpu.VMEM((D, width), BF),
            pltpu.VMEM((width, D), BF),
            pltpu.SemaphoreType.DMA((2, blocks // 2)),
        ],
        compiler_params=pltpu.CompilerParams(vmem_limit_bytes=VMEM_LIMIT),
        cost_estimate=microseconds(20),
        name="shared_slice_grads",
    )(pos, *h_parts, *g_parts, weights, *sums)


def pair_sum(kept, received):
    return (kept.astype(F32) + received.astype(F32)).astype(BF)


def halves(value, bit):
    width = value.shape[-1] // 2
    low, high = value[..., :width], value[..., width:]
    return jnp.where(bit == 0, low, high), jnp.where(bit == 0, high, low)


def rejoin(own, other, bit):
    return jnp.where(
        bit == 0, jnp.concatenate([own, other], -1), jnp.concatenate([other, own], -1)
    )


def lane_halves():
    lane = lax.broadcasted_iota(jnp.int32, (1, 128), 1)
    return [(lane < 64).astype(F32).astype(BF), (lane >= 64).astype(F32).astype(BF)]


def pick_lanes(first, second):
    lane = lax.broadcasted_iota(jnp.int32, first.shape, 1)
    return jnp.where(lane < 64, first, second)


def turned(value, cos, sin):
    lane = lax.broadcasted_iota(jnp.int32, value.shape, 1)
    partner = jnp.where(lane % 64 < 32, pltpu.roll(value, 96, 1), pltpu.roll(value, 32, 1))
    return value * cos + partner * sin


def causal_mask(rows, heads):
    row = lax.broadcasted_iota(jnp.int32, (heads * rows, rows), 0) % rows
    col = lax.broadcasted_iota(jnp.int32, (heads * rows, rows), 1)
    return row, col


def stacked(value, masks):
    return jnp.concatenate([value * mask for mask in masks], 0)


def unit_rms(value):
    return lax.rsqrt(jnp.mean(value * value, -1, keepdims=True) + EPS)


def softmax_of(first, second=None):
    top = jnp.max(first, -1, keepdims=True)
    if second is not None:
        top = jnp.maximum(top, jnp.max(second, -1, keepdims=True))
    first = jnp.exp(first - top)
    total = jnp.sum(first, -1, keepdims=True)
    if second is None:
        return first * (1.0 / total)
    second = jnp.exp(second - top)
    scale = 1.0 / (total + jnp.sum(second, -1, keepdims=True))
    return first * scale, second * scale


def attention_kernel(place_ref, *refs):
    w_parts = refs[:8]
    (
        h1_ref,
        own_ref,
        far_ref,
        gain1_ref,
        gain2_ref,
        router_ref,
        cos_ref,
        sin_ref,
        *outs,
        h2_ref,
        w_ref,
        q_ref,
        k_ref,
        v_ref,
        o_ref,
        x1_ref,
        h_sc,
        sems,
        out_sems,
    ) = refs[8:]
    kept = (w_ref, q_ref, k_ref, v_ref, o_ref, x1_ref)
    leaving = [
        pltpu.make_async_copy(kept[i], outs[i], out_sems.at[i]) for i in range(len(kept))
    ]
    copies = []
    for part in range(8):
        for slot in range(4):
            rows = pl.ds(pl.multiple_of(place_ref[8 + slot] * 192, 192), 192)
            copies.append(
                pltpu.make_async_copy(
                    w_parts[part].at[slot, :192, :],
                    w_ref.at[place_ref[part], rows, :],
                    sems.at[part, slot],
                )
            )
    for one in copies:
        one.start()
    h_sc[:TOK_DEV, :] = h1_ref[...]
    far = far_ref[:TOK_DEV, :].astype(F32)
    h_sc[TOK_DEV:, :] = (far * unit_rms(far) * gain1_ref[...]).astype(BF)
    for one in copies:
        one.wait()
    leaving[0].start()
    for i in range(6):
        out_ref = (q_ref, k_ref, v_ref)[i // 2]
        product = jnp.dot(h_sc[...], w_ref[i], preferred_element_type=F32)
        for slab in range(3):
            at = (i % 2) * 384 + slab * 128
            for half in range(2):
                rows = slice(half * TOK_DEV, (half + 1) * TOK_DEV)
                value = product[rows, slab * 128 : (slab + 1) * 128]
                if i < 4:
                    value = turned(value, cos_ref[...], sin_ref[...])
                out_ref[rows, at : at + 128] = value.astype(BF)
        if i % 2:
            leaving[1 + i // 2].start()
    masks = lane_halves()
    row, col = causal_mask(PROMPT, 2)
    prompt_ok = col <= row
    row, col = causal_mask(CONT * CLEN, 2)
    cont_ok = (row // CLEN == col // CLEN) & (col <= row)
    row = lax.broadcasted_iota(jnp.int32, (2 * CONT * CLEN, 1), 0) % (CONT * CLEN)
    reads_far = jnp.where(row < CLEN, place_ref[12], place_ref[13]).astype(F32)
    own_c = slice(PROMPT, TOK_DEV)
    far_p = slice(TOK_DEV, TOK_DEV + PROMPT)

    def heads(pair, carry):
        cols = pl.ds(pl.multiple_of(pair * 128, 128), 128)
        q_p, k_p, v_p = q_ref[:PROMPT, cols], k_ref[:PROMPT, cols], v_ref[:PROMPT, cols]
        q_c, k_c, v_c = q_ref[own_c, cols], k_ref[own_c, cols], v_ref[own_c, cols]
        k_f, v_f = k_ref[far_p, cols], v_ref[far_p, cols]
        score = 0.125 * contract(stacked(q_p, masks), k_p, 1, 1)
        prob = softmax_of(jnp.where(prompt_ok, score, -1e30)).astype(BF)
        out = jnp.dot(prob, v_p, preferred_element_type=F32)
        o_ref[:PROMPT, cols] = pick_lanes(out[:PROMPT], out[PROMPT:]).astype(BF)
        query = stacked(q_c, masks)
        near, far = contract(query, k_p, 1, 1), contract(query, k_f, 1, 1)
        first = 0.125 * jnp.where(reads_far > 0.5, far, near)
        second = jnp.where(cont_ok, 0.125 * contract(query, k_c, 1, 1), -1e30)
        first, second = softmax_of(first, second)
        out = (
            jnp.dot((first * (1.0 - reads_far)).astype(BF), v_p, preferred_element_type=F32)
            + jnp.dot((first * reads_far).astype(BF), v_f, preferred_element_type=F32)
            + jnp.dot(second.astype(BF), v_c, preferred_element_type=F32)
        )
        o_ref[own_c, cols] = pick_lanes(out[: CONT * CLEN], out[CONT * CLEN :]).astype(BF)
        return carry

    lax.fori_loop(0, HEADS // 2, heads, 0, unroll=3)
    leaving[4].start()
    for i in range(2):
        cols = slice(384 * i, 384 * (i + 1))
        x1_ref[:, cols] = own_ref[:TOK_DEV, cols].astype(F32) + jnp.dot(
            o_ref[...], w_ref[6 + i], preferred_element_type=F32
        )
    leaving[5].start()
    resid = x1_ref[...]
    hidden = (resid * unit_rms(resid) * gain2_ref[...]).astype(BF)
    h2_ref[:TOK_DEV, :] = hidden
    logits = contract(router_ref[...], hidden, 1, 1)
    logits = jnp.exp(logits - jnp.max(logits, 0, keepdims=True))
    probs = logits / jnp.sum(logits, 0, keepdims=True)
    high = probs.astype(BF)
    h2_ref[TOK_DEV:, :TOK_DEV] = high
    h2_ref[TOK_DEV:, TOK_DEV:] = (probs - high.astype(F32)).astype(BF)
    for one in leaving:
        one.wait()


def attention_forward(place, w_parts, h1, own, far, gain1, gain2, router_t, cos, sin):
    vmem = pl.BlockSpec(memory_space=pltpu.VMEM)
    hbm = pl.BlockSpec(memory_space=pltpu.HBM)
    kept = (
        ((8, D, 384), BF),
        ((2 * TOK_DEV, D), BF),
        ((2 * TOK_DEV, D), BF),
        ((2 * TOK_DEV, D), BF),
        ((TOK_DEV, D), BF),
        ((TOK_DEV, D), F32),
    )
    return pl.pallas_call(
        attention_kernel,
        out_shape=tuple(jax.ShapeDtypeStruct(*s) for s in kept + (((ROWS, D), BF),)),
        in_specs=[pl.BlockSpec(memory_space=pltpu.SMEM)]
        + [pl.BlockSpec(memory_space=pl.ANY)] * 8
        + [vmem] * 8,
        out_specs=(hbm,) * len(kept) + (vmem,),
        scratch_shapes=[pltpu.VMEM(*s) for s in kept]
        + [
            pltpu.VMEM((2 * TOK_DEV, D), BF),
            pltpu.SemaphoreType.DMA((8, 4)),
            pltpu.SemaphoreType.DMA((len(kept),)),
        ],
        compiler_params=pltpu.CompilerParams(vmem_limit_bytes=VMEM_LIMIT),
        cost_estimate=microseconds(20),
        name="attention_forward",
    )(place, *w_parts, h1, own, far, gain1, gain2, router_t, cos, sin)


def branch_kernel(*refs):
    dx_refs, refs = refs[:3], refs[3:]
    (
        h2_ref,
        x1_ref,
        g_ref,
        gain2_ref,
        router_ref,
        w_ref,
        dx1_ref,
        do_ref,
        do_c_ref,
        grouter_ref,
        ggain_ref,
    ) = refs
    dx = dx_refs[0][...].astype(F32) + dx_refs[1][...].astype(F32) + dx_refs[2][...].astype(F32)
    drp = dx[TOK_DEV:, :TOK_DEV] + dx[TOK_DEV:, TOK_DEV:]
    probs = h2_ref[TOK_DEV:, :TOK_DEV].astype(F32) + h2_ref[TOK_DEV:, TOK_DEV:].astype(F32)
    dlogits = (probs * (drp - jnp.sum(probs * drp, 0, keepdims=True))).astype(BF)
    hidden = h2_ref[:TOK_DEV, :]
    grouter_ref[...] = jnp.dot(dlogits, hidden, preferred_element_type=F32)
    dh2 = (
        dx[:TOK_DEV]
        + contract(dlogits, router_ref[...], 0, 0)
    )
    resid = x1_ref[...]
    scale = unit_rms(resid)
    normed = resid * scale
    ggain_ref[...] = jnp.sum(dh2 * normed, 0, keepdims=True)
    dnormed = dh2 * gain2_ref[...]
    dx1 = scale * (dnormed - normed * jnp.mean(dnormed * normed, -1, keepdims=True)) + g_ref[
        ...
    ].astype(F32)
    dx1_ref[...] = dx1
    datt = dx1.astype(BF)
    do_ref[...] = (
        contract(datt[:, :384], w_ref[0], 1, 1) + contract(datt[:, 384:], w_ref[1], 1, 1)
    ).astype(BF)
    do_c_ref[...] = do_ref[PROMPT:, :]


def branch_backward(dx, h_block, x1, grad, gain2, router_t, w_all):
    shape = jax.ShapeDtypeStruct
    whole = lambda *dims: pl.BlockSpec(dims, lambda i: (0,) * len(dims))
    rows = whole(TOK_DEV, D)
    return pl.pallas_call(
        branch_kernel,
        grid=(1,),
        out_shape=(
            shape((TOK_DEV, D), F32),
            shape((TOK_DEV, D), BF),
            shape((TOK_DEV - PROMPT, D), BF),
            shape((EXPERTS, D), F32),
            shape((1, D), F32),
        ),
        in_specs=[
            whole(ROWS, D),
            whole(ROWS, D),
            whole(ROWS, D),
            whole(ROWS, D),
            rows,
            rows,
            whole(1, D),
            whole(EXPERTS, D),
            pl.BlockSpec((2, D, 384), lambda i: (3, 0, 0)),
        ],
        out_specs=(
            rows,
            rows,
            whole(TOK_DEV - PROMPT, D),
            whole(EXPERTS, D),
            whole(1, D),
        ),
        compiler_params=pltpu.CompilerParams(vmem_limit_bytes=VMEM_LIMIT),
        cost_estimate=microseconds(6),
        name="branch_backward",
    )(*dx, h_block, x1, grad, gain2, router_t, w_all)


def attention_back_kernel(
    flags_ref,
    *refs,
):
    sources = refs[:9]
    do_far_ref, gain1_ref, cos_ref, sin_ref, grouter_ref, ggain2_ref = refs[9:15]
    gtok_ref, keep_ref, send_ref = refs[15:18]
    arrived = refs[18:27]
    q_ref, k_ref, v_ref, do_ref, h1_ref, w_ref, own_ref, dx1_ref, gwo_ref = arrived
    dq_sc, dk_sc, dv_sc, low_sc, product_sc, ext_sc, in_sems, out_sems = refs[27:]
    copies = [
        pltpu.make_async_copy(
            sources[i].at[:6] if i == 5 else sources[i], arrived[i], in_sems.at[i]
        )
        for i in range(9)
    ]
    for one in copies:
        one.start()

    def put(number, source):
        cols = slice((number % 2) * D, (number % 2 + 1) * D)
        copy = lambda out: pltpu.make_async_copy(
            source, out.at[:, : D // 4, cols], out_sems.at[number]
        )

        @pl.when(flags_ref[4] == number // 2)
        def _():
            copy(keep_ref).start()

        @pl.when(flags_ref[4] != number // 2)
        def _():
            copy(send_ref).start()

        return copy(keep_ref)

    for one in copies[:4]:
        one.wait()
    masks = lane_halves()
    row, col = causal_mask(PROMPT, 2)
    prompt_ok = col <= row
    cont_ok = (row // CLEN == col // CLEN) & (col <= row)
    row = lax.broadcasted_iota(jnp.int32, (8 * CLEN, 1), 0) // CLEN % 4
    near = jnp.where(
        row < 2,
        jnp.where(row == 0, flags_ref[0], flags_ref[1]),
        jnp.where(row == 2, flags_ref[2], flags_ref[3]),
    ).astype(F32)
    own_rows = row < 2
    own_c = slice(PROMPT, TOK_DEV)
    far_p = slice(TOK_DEV, TOK_DEV + PROMPT)
    far_c = slice(TOK_DEV + PROMPT, 2 * TOK_DEV)
    cont = CONT * CLEN

    def either(own, other):
        return jnp.where((near > 0.5) | ~own_rows, own, other)

    def heads(pair, carry):
        cols = pl.ds(pl.multiple_of(pair * 128, 128), 128)
        q_p, k_p, v_p = q_ref[:PROMPT, cols], k_ref[:PROMPT, cols], v_ref[:PROMPT, cols]
        k_f, v_f = k_ref[far_p, cols], v_ref[far_p, cols]
        q_c, k_c, v_c = q_ref[own_c, cols], k_ref[own_c, cols], v_ref[own_c, cols]
        do_p, do_c = do_ref[:PROMPT, cols], do_ref[own_c, cols]
        q_4 = jnp.concatenate([q_c, q_ref[far_c, cols]], 0)
        k_4 = jnp.concatenate([k_c, k_ref[far_c, cols]], 0)
        v_4 = jnp.concatenate([v_c, v_ref[far_c, cols]], 0)
        do_4 = jnp.concatenate([do_c, do_far_ref[:, cols]], 0)
        q_all = jnp.concatenate([q_p, q_4], 0)
        do_all = jnp.concatenate([do_p, do_4], 0)
        rows = 4 * CLEN
        query, grad = stacked(q_p, masks), stacked(do_p, masks)
        score = jnp.where(prompt_ok, 0.125 * contract(query, k_p, 1, 1), -1e30)
        prob = softmax_of(score)
        dprob = contract(grad, v_p, 1, 1)
        ds = (prob * (dprob - jnp.sum(prob * dprob, -1, keepdims=True))).astype(BF)
        prob = prob.astype(BF)
        query, grad = stacked(q_4, masks), stacked(do_4, masks)
        first = 0.125 * either(contract(query, k_p, 1, 1), contract(query, k_f, 1, 1))
        second = jnp.where(cont_ok, 0.125 * contract(query, k_4, 1, 1), -1e30)
        first, second = softmax_of(first, second)
        dfirst = either(contract(grad, v_p, 1, 1), contract(grad, v_f, 1, 1))
        dsecond = contract(grad, v_4, 1, 1)
        mean = jnp.sum(first * dfirst, -1, keepdims=True) + jnp.sum(
            second * dsecond, -1, keepdims=True
        )
        ds1 = first * (dfirst - mean)
        ds2 = (second * (dsecond - mean)).astype(BF)
        ds_near = (ds1 * near).astype(BF)
        ds_far = (ds1 * (1.0 - near)).astype(BF)
        p_near = (first * near).astype(BF)
        p_own = second.astype(BF)
        out = jnp.dot(ds, k_p, preferred_element_type=F32)
        dq_sc[:PROMPT, cols] = pick_lanes(out[:PROMPT], out[PROMPT:])
        out = (
            jnp.dot(ds_near, k_p, preferred_element_type=F32)
            + jnp.dot(ds_far, k_f, preferred_element_type=F32)
            + jnp.dot(ds2, k_4, preferred_element_type=F32)
        )
        dq_sc[own_c, cols] = pick_lanes(out[:cont], out[rows : rows + cont])
        for out, left, left_own, right, own in (
            (dk_sc, (ds, ds_near), ds2, q_all, q_c),
            (dv_sc, (prob, p_near), p_own, do_all, do_c),
        ):
            parts = [
                contract(
                    jnp.concatenate([part[h * rows : (h + 1) * rows] for part in left], 0),
                    right,
                    0,
                    0,
                )
                for h in range(2)
            ]
            out[:PROMPT, cols] = pick_lanes(*parts)
            parts = [
                contract(left_own[h * rows : h * rows + cont, :cont], own, 0, 0) for h in range(2)
            ]
            out[own_c, cols] = pick_lanes(*parts)
        return carry

    lax.fori_loop(0, HEADS // 2, heads, 0, unroll=3)
    for one in copies[4:]:
        one.wait()
    leaving = [put(3, gwo_ref)]
    dh1 = None
    for i, source in enumerate((dq_sc, dk_sc, dv_sc)):
        for slab in range(6):
            cols = slice(slab * 128, (slab + 1) * 128)
            value = source[:, cols]
            if i < 2:
                value = turned(0.125 * value, cos_ref[...], -sin_ref[...])
            low_sc[:, cols] = value.astype(BF)
        grads = low_sc[...]
        product = contract(h1_ref[...], grads, 0, 0).astype(BF)
        product_sc[i] = product.reshape(4, D // 4, D)
        leaving.append(put(i, product_sc.at[i]))
        for half in range(2):
            part = contract(grads[:, 384 * half : 384 * (half + 1)], w_ref[2 * i + half], 1, 1)
            dh1 = part if dh1 is None else dh1 + part
    inputs = own_ref[...].astype(F32)
    scale = unit_rms(inputs)
    normed = inputs * scale
    ggain1 = jnp.sum(dh1 * normed, 0, keepdims=True)
    gains = jnp.concatenate([ggain1, ggain2_ref[...], jnp.zeros((EXT - 2, D), F32)], 0)
    ext_sc[...] = jnp.zeros_like(ext_sc)
    for z in range(4):
        cols = slice(z * (D // 4), (z + 1) * (D // 4))
        extras = jnp.concatenate([grouter_ref[:, cols], gains[:, cols]], 1).astype(BF)
        ext_sc[0, z, :, : 2 * (D // 4)] = extras
    for k, out in enumerate((keep_ref, send_ref)):
        which = flags_ref[4] if k == 0 else 1 - flags_ref[4]
        leaving.append(
            pltpu.make_async_copy(ext_sc.at[which], out.at[:, D // 4 :, :], out_sems.at[4 + k])
        )
        leaving[-1].start()
    dnormed = dh1 * gain1_ref[...]
    gtok_ref[...] = (
        scale * (dnormed - normed * jnp.mean(dnormed * normed, -1, keepdims=True)) + dx1_ref[...]
    )
    for one in leaving:
        one.wait()


def attention_backward(
    flags, q, k, v, do, do_far, h1, w_all, own, gain1, cos, sin, dx1, gwo, grouter, ggain2
):
    shape = jax.ShapeDtypeStruct
    vmem = pl.BlockSpec(memory_space=pltpu.VMEM)
    anywhere = pl.BlockSpec(memory_space=pl.ANY)
    hbm = pl.BlockSpec(memory_space=pltpu.HBM)
    packed = (4, D // 4 + EXT, 2 * D)
    late = (q, k, v, do, h1, w_all, own, dx1, gwo.reshape(4, D // 4, D))
    return pl.pallas_call(
        attention_back_kernel,
        out_shape=(shape((TOK_DEV, D), F32), shape(packed, BF), shape(packed, BF)),
        in_specs=[pl.BlockSpec(memory_space=pltpu.SMEM)]
        + [anywhere] * 9
        + [vmem] * 6,
        out_specs=(vmem, hbm, hbm),
        scratch_shapes=[
            pltpu.VMEM((6,) + v.shape[1:] if i == 5 else v.shape, v.dtype)
            for i, v in enumerate(late)
        ]
        + [pltpu.VMEM((TOK_DEV, D), F32)] * 3
        + [
            pltpu.VMEM((TOK_DEV, D), BF),
            pltpu.VMEM((3, 4, D // 4, D), BF),
            pltpu.VMEM((2, 4, EXT, 2 * D), BF),
            pltpu.SemaphoreType.DMA((9,)),
            pltpu.SemaphoreType.DMA((6,)),
        ],
        compiler_params=pltpu.CompilerParams(vmem_limit_bytes=VMEM_LIMIT),
        cost_estimate=microseconds(23),
        name="attention_backward",
    )(flags, *late, do_far, gain1, cos, sin, grouter, ggain2)


def after(value, *earlier):
    return lax.optimization_barrier((value, earlier))[0]


def over_y(value):
    return moved(value, lambda z, y, x, c: (z, 1 - y, x, c))


def beside(results, moving):
    return lax.optimization_barrier((results, moving))


def norm_kernel(rows_ref, gain_ref, out_ref):
    rows = rows_ref[...].astype(F32)
    out_ref[...] = (rows * unit_rms(rows) * gain_ref[...]).astype(BF)


def norm_rows(rows, gain):
    return pl.pallas_call(
        norm_kernel,
        out_shape=jax.ShapeDtypeStruct(rows.shape, BF),
        compiler_params=pltpu.CompilerParams(vmem_limit_bytes=VMEM_LIMIT),
        cost_estimate=microseconds(2),
        name="norm_rows",
    )(rows, gain)


def place_kernel(every_ref, gate_ref, up_ref, down_ref):
    for out_ref, at in ((gate_ref, 0), (up_ref, 256)):
        for k in range(4):
            for p in range(0, 8, 2):
                pair = [
                    every_ref[p + i, :, at + 64 * k : at + 64 * (k + 1)].astype(F32)
                    for i in range(2)
                ]
                to = 512 * k + 64 * p
                out_ref[:, to : to + 128] = jnp.concatenate(pair, 1)
    for p in range(8):
        for i in range(3):
            down_ref[64 * p : 64 * (p + 1), 256 * i : 256 * (i + 1)] = every_ref[
                p, 64 * i : 64 * (i + 1), 512:
            ].astype(F32)


def place_shared(every):
    vmem = pl.BlockSpec(memory_space=pltpu.VMEM)
    return pl.pallas_call(
        place_kernel,
        out_shape=(
            jax.ShapeDtypeStruct((D // 4, 2048), F32),
            jax.ShapeDtypeStruct((D // 4, 2048), F32),
            jax.ShapeDtypeStruct((512, D), F32),
        ),
        in_specs=[vmem],
        out_specs=(vmem,) * 3,
        compiler_params=pltpu.CompilerParams(vmem_limit_bytes=VMEM_LIMIT),
        cost_estimate=microseconds(4),
        name="place_shared",
    )(every)


OTHERS = (
    over_x,
    over_y,
    lambda value: moved(value, lambda z, y, x, c: (z, 1 - y, 1 - x, c)),
)


def plane_pieces(value, x, y):
    width = value.shape[-1] // 4
    quarters = [value[..., width * i : width * (i + 1)] for i in range(4)]

    def pick(column, row):
        left = jnp.where(column == 0, quarters[0], quarters[1])
        right = jnp.where(column == 0, quarters[2], quarters[3])
        return jnp.where(row == 0, left, right)

    return [pick(x, y), pick(1 - x, y), pick(x, 1 - y), pick(1 - x, 1 - y)]


def canonical(slots, z):
    order = [slots[0], slots[3], slots[2], slots[1]]
    return lax.dynamic_slice_in_dim(jnp.stack(order + order), lax.rem(4 - z, 4), 4, 0)


def lane_tables():
    row = np.arange(TOK_DEV)
    position = np.where(row < PROMPT, row, PROMPT + (row - PROMPT) % CLEN).astype(np.float32)
    frequency = (10000.0 ** (-2.0 * np.arange(HD // 2) / HD)).astype(np.float32)
    angles = (position[:, None] * frequency[None, :]).astype(np.float64)
    cos, sin = np.cos(angles).astype(np.float32), np.sin(angles).astype(np.float32)
    return jnp.asarray(np.tile(cos, (1, 4))), jnp.asarray(np.tile(np.concatenate([-sin, sin], 1), (1, 2)))


def tuned_body(
    tokens,
    cotangent,
    routes,
    prompt_ids,
    attn_gain,
    query_weight,
    key_weight,
    value_weight,
    output_weight,
    ffn_gain,
    router_weight,
    shared_gate,
    shared_up,
    shared_down,
    expert_gate,
    expert_up_weight,
    expert_down,
):
    z, y, j = lax.axis_index("dp"), lax.axis_index("context"), lax.axis_index("experts")
    x, core = j // 2, j % 2
    plane = y * 4 + j
    shard = D // 4

    dense = jnp.concatenate([query_weight, key_weight, value_weight, output_weight], 1)
    dense = lax.dynamic_slice_in_dim(dense, plane * 384, 384, 1)
    gains = jnp.concatenate(
        [attn_gain[None], ffn_gain[None], jnp.zeros((EXT - 2, shard), BF)], 0
    )
    dense = jnp.concatenate([dense, jnp.concatenate([router_weight.T, gains], 1)], 0)
    dense_z = [over_z(dense, step) for step in (1, 2, 3)]

    units = lambda w: lax.dynamic_index_in_dim(
        w.reshape(shard, 4, 8, 64), plane, 2, keepdims=False
    ).reshape(shard, 256)
    down = lax.dynamic_slice_in_dim(shared_down, plane * 64, 64, 0)
    down = jnp.concatenate([down[:, 256 * i : 256 * (i + 1)] for i in range(3)], 0)
    shared = jnp.concatenate([units(shared_gate), units(shared_up), down], 1)
    far = over_y(tokens)
    ids = jnp.broadcast_to(prompt_ids.astype(BF)[:, None], (CONT, 128))
    far_ids = over_y(ids)
    dense = jnp.stack([dense] + after(dense_z, far, far_ids))
    small = canonical([dense[i, shard:, :] for i in range(4)], z)
    router_t = small[:, :, :shard].transpose(1, 0, 2).reshape(EXPERTS, D)
    gain1 = small[:, 0, shard:].reshape(1, D).astype(F32)
    gain2 = small[:, 1, shard:].reshape(1, D).astype(F32)
    flip_a, flip_b = jnp.where(core == 0, 2, 4), jnp.where(core == 0, 4, 2)
    flips = [0 * core, flip_a, flip_b, 0 * core + 6]
    flips = flips + [1 + flips[0], 1 + flip_b, 1 + flip_a, 1 + flips[3]]
    place = [jnp.bitwise_xor(plane, flip) for flip in flips]
    place += [lax.rem(z + 4 - slot, 4) for slot in range(4)]
    place += [(prompt_ids[m] != y) for m in range(CONT)]
    place = jnp.stack([v.astype(jnp.int32) for v in place])
    cos, sin = lane_tables()
    gain1, place, gain2, router_t, cos, sin = after((gain1, place, gain2, router_t, cos, sin))
    h1 = norm_rows(tokens, gain1)
    h1, dense_parts = beside(h1, (over_a(dense), over_b(dense)))
    dense_parts = [dense, *dense_parts, over_b(dense_parts[0])]
    dense_parts = dense_parts + [over_core(part) for part in dense_parts]

    expert_ids = jnp.arange(EXPERTS, dtype=jnp.int32)[:, None]
    route_t = routes.T
    member = (route_t[0:1] == expert_ids) | (route_t[1:2] == expert_ids)
    before = (jnp.arange(TOK_DEV)[:, None] < jnp.arange(TOK_DEV)[None, :]).astype(BF)
    ranks = jnp.dot(member.astype(BF), before, preferred_element_type=F32)
    ranks = jnp.where(member, ranks, -1.0).astype(BF)
    g_block = jnp.concatenate([cotangent, jnp.pad(ranks, ((0, 0), (0, D - TOK_DEV)))], 0)
    g_near = after(g_block, h1)
    g_x = over_x(g_near)
    g_group = [g_block, g_x, over_core(g_near), over_core(g_x)]

    g_column = lax.all_gather(after(g_block, dense), "dp", axis=0, tiled=False)

    shared = lax.all_gather(after(shared, dense), "dp", axis=0, tiled=False)
    shared_far = over_y(after(shared, h1))
    place = after(place, shared)
    flags = jnp.concatenate([prompt_ids == y, far_ids[:, 0].astype(jnp.int32) == y, core[None] != 0]).astype(jnp.int32)
    w_all, q, k, v, o, x1, h_block = attention_forward(
        place, dense_parts, h1, tokens, far, gain1, gain2, router_t, cos, sin
    )
    (h_block, x1), (g_x, shared_far) = beside((h_block, x1), (g_x, shared_far))
    g_group = [g_block, g_x, over_core(g_block), over_core(g_x)]

    h_x = over_x(h_block)
    h_near, g_near = [h_block, over_core(h_block)], [g_block, g_group[2]]
    h_column = lax.all_gather(h_block, "dp", axis=0, tiled=False)
    experts_w = (expert_gate, expert_up_weight, expert_down)
    base = (j * 4).astype(jnp.int32)
    more = shared_rows(h_near, g_near, shared, shared_far)
    more, (h_x, g_y) = beside(more, (h_x, over_y(after(g_block, h_block))))
    h_far, g_far = [h_x, over_core(h_x)], [g_x, g_group[3]]
    h_group = [h_near[0], h_far[0], h_near[1], h_far[1]]
    g_second = jnp.where(core == 0, g_y, g_x)
    h_group, g_second = after((h_group, g_second))
    part = group_experts(base[None], 0, 2, h_group, g_group, (), *experts_w)
    (part, h_far), h_b = beside((part, h_far), over_b(after(h_block, h_x)))
    g_first = over_a(after(g_column, h_x))
    more = more + shared_rows(h_far, g_far, shared, shared_far)
    more, g_first = beside(more, g_first)
    g_second = lax.all_gather(g_second, "dp", axis=0, tiled=False)
    results = group_experts(
        base[None] + 2, 2, 2, h_group, g_group, (*more, *part), *experts_w
    )
    g_third = over_b(g_first)
    results, (g_third, g_core) = beside(
        results, (g_third, [over_core(g_column), over_core(g_first)])
    )
    moe, dx = results[:4], results[4:]
    dx_x = pair_sum(dx[1], over_core(dx[3]))
    dx = [dx[0], over_core(dx[2]), over_x(dx_x)]
    h_column = after(h_column, dx_x)
    h_core = [over_core(h_column)]
    window = jnp.array([0, 1, 3, 4], jnp.int32)[z]
    s_pos = jnp.stack([window, z // 2, z * 192 - window * 128, (z % 2) * 64]).astype(jnp.int32)
    e_pos = jnp.stack([base, (z * 2 + y).astype(jnp.int32)])
    s_sums = shared_slice_grads(
        s_pos, [h_column, h_core[0]], [g_column, g_core[0]], shared
    )
    s_sums, dx = beside(s_sums, dx)
    dx1, do, do_c, grad_router_t, grad_gain2 = branch_backward(
        dx, h_block, x1, cotangent, gain2, router_t, w_all
    )
    gwo = inner_rows(o, dx1.astype(BF)).astype(BF)
    gwo, (do_far, g_second) = beside(gwo, (over_y(do_c), g_second))
    h_first = over_a(after(h_column, do_far))
    h_second = lax.all_gather(after(h_b, do_far), "dp", axis=0, tiled=False)
    grad_inputs, keep, send = attention_backward(
        flags,
        q,
        k,
        v,
        do,
        do_far,
        h1,
        w_all,
        tokens,
        gain1,
        cos,
        sin,
        dx1,
        gwo,
        grad_router_t,
        grad_gain2,
    )
    (grad_inputs, keep, send), (h_first, g_far) = beside(
        (grad_inputs, keep, send),
        (h_first, [over_core(after(part, do_far)) for part in (g_second, g_third)]),
    )
    h_core.append(over_core(h_first))
    h_third = over_b(after(h_first, keep))
    h_parts, g_parts = [h_column, h_first] + h_core, [g_column, g_first] + g_core[:2]
    e_pos = after(e_pos, keep)
    e_sums = expert_slice_grads(e_pos, h_parts, g_parts, *experts_w, 256)
    (e_sums, keep), (send, h_second, h_third, g_far) = beside(
        (e_sums, keep),
        (over_core(send), h_second, h_third, g_far),
    )
    h_far = [over_core(h_second), over_core(h_third)]
    h_parts, g_parts = [h_second, h_third] + h_far, [g_second, g_third] + g_far
    pieces = plane_pieces(pair_sum(keep, send), x, y)
    h_parts, pieces = after((h_parts, pieces))
    mine = shared_slice_grads(
        s_pos, [h_first, h_core[1], *h_parts], [g_first, g_core[1], *g_parts], shared, s_sums
    )
    (mine, pieces), there = beside(
        (mine, pieces), [over(piece) for over, piece in zip(OTHERS, pieces[1:])]
    )
    z_own = pieces[0].astype(F32)
    for piece in there:
        z_own = z_own + piece.astype(F32)
    z_own = z_own.astype(BF)
    z_parts = [
        lax.dynamic_index_in_dim(z_own, lax.rem(z + step, 4), 0, keepdims=False)
        for step in (0, 1, 2, 3)
    ]
    moe = after(moe, mine)
    moe_x = pair_sum(moe[1], over_core(moe[3]))
    moe_core = over_core(moe[2])

    mine, z_parts, moe_x, moe_core, h_parts, g_parts = after(
        (mine, z_parts, moe_x, moe_core, h_parts, g_parts)
    )
    every = lax.all_gather(mine, ("context", "experts"), axis=0, tiled=False)
    moving = ([over_z(z_parts[step], step) for step in (1, 2, 3)], over_x(moe_x), every)
    e_gate, e_up, e_down = expert_slice_grads(e_pos, h_parts, g_parts, *experts_w, 256, e_sums)
    (e_gate, e_up, e_down), (there, moe_there, every) = beside((e_gate, e_up, e_down), moving)
    total = z_parts[0].astype(F32)
    for part in there:
        total = total + part.astype(F32)
    total = total.astype(BF)
    total_parts = [over(total) for over in OTHERS]
    layer_out = (
        x1 + (moe[0].astype(F32) + moe_core.astype(F32) + moe_there.astype(F32))
    ).astype(BF)
    s_gate, s_up, s_down = place_shared(every)
    (layer_out, s_gate), total_parts = beside((layer_out, s_gate), total_parts)
    beside_x = rejoin(total, total_parts[0], x)
    total = rejoin(beside_x, rejoin(total_parts[1], total_parts[2], x), y)
    other = over_core(total)
    sum_qk, sum_vo = jnp.where(core == 0, total, other), jnp.where(core == 0, other, total)
    extras = sum_qk[shard:, : 2 * shard].astype(F32)
    sum_qk, sum_vo = sum_qk[:shard].astype(F32), sum_vo[:shard].astype(F32)

    return (
        layer_out,
        grad_inputs,
        extras[0, shard:],
        sum_qk[:, :D],
        sum_qk[:, D:],
        sum_vo[:, :D],
        sum_vo[:, D:],
        extras[1, shard:],
        extras[:, :shard].T,
        s_gate,
        s_up,
        s_down,
        e_gate,
        e_up,
        e_down,
    )


def solution(mesh):
    tuned = dict(mesh.shape) == TUNED_MESH

    return jax.shard_map(
        tuned_body if tuned else plain_body,
        mesh=mesh,
        in_specs=(
            P(("dp", "context", "experts"), None),
            P(("dp", "context", "experts"), None),
            P(("dp", "context", "experts"), None),
            P(("dp", "context", "experts")),
            P("dp"),
            P("dp", None),
            P("dp", None),
            P("dp", None),
            P("dp", None),
            P("dp"),
            P("dp", None),
            P("dp", None),
            P("dp", None),
            P("dp", None),
            P("experts", None, None),
            P("experts", None, None),
            P("experts", None, None),
        ),
        out_specs=(
            P(("dp", "context", "experts"), None),
            P(("dp", "context", "experts"), None),
            P("dp"),
            P("dp", None),
            P("dp", None),
            P("dp", None),
            P("dp", None),
            P("dp"),
            P("dp", None),
            P("dp", None),
            P("dp", None),
            P("dp", None),
            P("experts", None, ("dp", "context")),
            P("experts", None, ("dp", "context")),
            P("experts", ("dp", "context"), None),
        ),
        check_vma=False,
    )
```

```python
import functools

import jax
import jax.numpy as jnp
import numpy as np
from jax import lax
from jax.sharding import PartitionSpec as P

from jax.experimental import pallas as pl
from jax.experimental.pallas import tpu as pltpu

D = 768
HEADS = 12
HD = 64
EXPERTS = 16
TOPK = 2
PROMPT = 256
CONT = 2
CLEN = 64
TOK_DEV = 384
CAP = 66


EPS = 1e-06


def rotary_tables(tok_rows):
    row_ids = jnp.arange(tok_rows)
    position = jnp.where(row_ids < PROMPT, row_ids, PROMPT + (row_ids - PROMPT) % CLEN).astype(
        jnp.float32
    )
    frequency = 10000.0 ** (-2.0 * jnp.arange(HD // 2).astype(jnp.float32) / HD)
    angles = position[:, None] * frequency[None, :]
    return (jnp.cos(angles), jnp.sin(angles))


def rotate(values_in, cos_table, sin_table):
    shaped = values_in.reshape(values_in.shape[:-1] + (HEADS, HD))
    lower_half = shaped[..., : HD // 2]
    upper_half = shaped[..., HD // 2 :]
    cos_part = cos_table[:, None, :]
    sin_part = sin_table[:, None, :]
    turned = jnp.concatenate(
        [
            lower_half * cos_part - upper_half * sin_part,
            upper_half * cos_part + lower_half * sin_part,
        ],
        -1,
    )
    return turned.reshape(values_in.shape)


def key_mask(context_index, prompt_pick, contexts):
    row_ids = jnp.arange(TOK_DEV)[:, None]
    col_ids = jnp.arange(contexts * PROMPT + CONT * CLEN)[None, :]
    prompt_row = row_ids < PROMPT
    cont_row = (row_ids - PROMPT) // CLEN
    within_row = (row_ids - PROMPT) % CLEN
    owner = jnp.sum(
        prompt_pick[None, :] * (jnp.arange(CONT)[None, :] == cont_row), -1, keepdims=True
    )
    target = jnp.where(prompt_row, context_index, owner)
    prompt_keys = col_ids < contexts * PROMPT
    prompt_ok = (
        prompt_keys
        & (col_ids // PROMPT == target)
        & (jnp.logical_not(prompt_row) | (col_ids % PROMPT <= row_ids))
    )
    offset = col_ids - contexts * PROMPT
    cont_ok = (
        jnp.logical_not(prompt_keys)
        & jnp.logical_not(prompt_row)
        & (offset // CLEN == cont_row)
        & (offset % CLEN <= within_row)
    )
    return prompt_ok | cont_ok


def inner_rows(left, right):
    return lax.dot_general(
        left, right, (((0,), (0,)), ((), ())), preferred_element_type=jnp.float32
    )


def times_transposed(left, right):
    return lax.dot_general(
        left, right, (((1,), (1,)), ((), ())), preferred_element_type=jnp.float32
    )


def swish_derivative(pre_act):
    sigma = jax.nn.sigmoid(pre_act)
    return sigma * (1.0 + pre_act * (1.0 - sigma))


def plain_body(
    tokens,
    cotangent,
    routes,
    prompt_ids,
    attn_gain,
    query_weight,
    key_weight,
    value_weight,
    output_weight,
    ffn_gain,
    router_weight,
    shared_gate,
    shared_up,
    shared_down,
    expert_gate,
    expert_up_weight,
    expert_down,
):
    contexts = lax.axis_size("context")
    context_here = lax.axis_index("context")
    gain_one, w_query, w_key, w_value, w_out, gain_two, w_router, w_sgate, w_sup, w_sdown = (
        lax.all_gather(attn_gain, "dp", axis=0, tiled=True),
        lax.all_gather(query_weight, "dp", axis=0, tiled=True),
        lax.all_gather(key_weight, "dp", axis=0, tiled=True),
        lax.all_gather(value_weight, "dp", axis=0, tiled=True),
        lax.all_gather(output_weight, "dp", axis=0, tiled=True),
        lax.all_gather(ffn_gain, "dp", axis=0, tiled=True),
        lax.all_gather(router_weight, "dp", axis=0, tiled=True),
        lax.all_gather(shared_gate, "dp", axis=0, tiled=True),
        lax.all_gather(shared_up, "dp", axis=0, tiled=True),
        lax.all_gather(shared_down, "dp", axis=0, tiled=True),
    )
    cos_table, sin_table = rotary_tables(TOK_DEV)
    inputs = tokens.astype(jnp.float32)
    inv_rms1 = lax.rsqrt(jnp.mean(inputs * inputs, -1, keepdims=True) + EPS)
    normed1 = inputs * inv_rms1
    gain1_f = gain_one.astype(jnp.float32)
    hidden1 = (normed1 * gain1_f).astype(jnp.bfloat16)
    query_f = jnp.dot(hidden1, w_query, preferred_element_type=jnp.float32)
    key_f = jnp.dot(hidden1, w_key, preferred_element_type=jnp.float32)
    value_f = jnp.dot(hidden1, w_value, preferred_element_type=jnp.float32)
    query_b = rotate(query_f, cos_table, sin_table).astype(jnp.bfloat16)
    key_b = rotate(key_f, cos_table, sin_table).astype(jnp.bfloat16)
    value_b = value_f.astype(jnp.bfloat16)
    prompt_keys, prompt_values = (
        lax.all_gather(key_b[:PROMPT], "context", axis=0, tiled=True),
        lax.all_gather(value_b[:PROMPT], "context", axis=0, tiled=True),
    )
    keys_h = jnp.concatenate([prompt_keys, key_b[PROMPT:]], 0).reshape(-1, HEADS, HD)
    values_h = jnp.concatenate([prompt_values, value_b[PROMPT:]], 0).reshape(-1, HEADS, HD)
    query_h = query_b.reshape(TOK_DEV, HEADS, HD)
    allowed = key_mask(context_here, prompt_ids, contexts)
    scores = jnp.where(
        allowed[None],
        0.125 * jnp.einsum("qhd,khd->hqk", query_h, keys_h, preferred_element_type=jnp.float32),
        -1e30,
    )
    row_max = jnp.max(scores, -1, keepdims=True)
    exp_scores = jnp.exp(scores - row_max)
    row_total = jnp.sum(exp_scores, -1, keepdims=True)
    log_total = row_max + jnp.log(row_total)
    attn_probs = (exp_scores / row_total).astype(jnp.bfloat16)
    attended = (
        jnp.einsum("hqk,khd->qhd", attn_probs, values_h, preferred_element_type=jnp.float32)
        .reshape(TOK_DEV, D)
        .astype(jnp.bfloat16)
    )
    resid = inputs + jnp.dot(attended, w_out, preferred_element_type=jnp.float32)
    inv_rms2 = lax.rsqrt(jnp.mean(resid * resid, -1, keepdims=True) + EPS)
    normed2 = resid * inv_rms2
    gain2_f = gain_two.astype(jnp.float32)
    hidden2 = (normed2 * gain2_f).astype(jnp.bfloat16)
    logits = jnp.dot(hidden2, w_router, preferred_element_type=jnp.float32)
    route_probs = jax.nn.softmax(logits, -1)
    route_hot = (routes[:, :, None] == jnp.arange(EXPERTS)[None, None, :]).astype(jnp.float32)
    gate_vals = jnp.sum(route_probs[:, None, :] * route_hot, -1)
    shared_gpre = jnp.dot(hidden2, w_sgate, preferred_element_type=jnp.float32)
    shared_upre = jnp.dot(hidden2, w_sup, preferred_element_type=jnp.float32)
    shared_act = (jax.nn.silu(shared_gpre) * shared_upre).astype(jnp.bfloat16)
    shared_res = jnp.dot(shared_act, w_sdown, preferred_element_type=jnp.float32)
    flat_route = routes.reshape(-1)
    flat_hot = (flat_route[:, None] == jnp.arange(EXPERTS)[None, :]).astype(jnp.int32)
    slot_ids = jnp.sum((jnp.cumsum(flat_hot, 0) - flat_hot) * flat_hot, -1)
    slot_index = flat_route * CAP + slot_ids
    send_rows = jnp.repeat(hidden2, TOPK, axis=0)
    outgoing = (
        jnp.zeros((EXPERTS * CAP, D), jnp.bfloat16)
        .at[slot_index]
        .set(send_rows)
        .reshape(EXPERTS, CAP, D)
    )
    received_rows = lax.all_to_all(outgoing, "experts", split_axis=0, concat_axis=1, tiled=True)
    expert_gate_preact = jnp.einsum(
        "mgx,mxp->mgp", received_rows, expert_gate, preferred_element_type=jnp.float32
    )
    expert_up_preact = jnp.einsum(
        "mgx,mxp->mgp", received_rows, expert_up_weight, preferred_element_type=jnp.float32
    )
    expert_activation = (jax.nn.silu(expert_gate_preact) * expert_up_preact).astype(jnp.bfloat16)
    expert_res = jnp.einsum(
        "erf,efd->erd", expert_activation, expert_down, preferred_element_type=jnp.float32
    ).astype(jnp.bfloat16)
    returned = lax.all_to_all(
        expert_res, "experts", split_axis=1, concat_axis=0, tiled=True
    ).reshape(EXPERTS * CAP, D)
    picked = returned[slot_index].astype(jnp.float32).reshape(TOK_DEV, TOPK, D)
    moe_out = jnp.sum(gate_vals[:, :, None] * picked, 1)
    layer_out = (resid + shared_res + moe_out).astype(jnp.bfloat16)
    gain_one, w_query, w_key, w_value, w_out, gain_two, w_router, w_sgate, w_sup, w_sdown = (
        lax.all_gather(attn_gain, "dp", axis=0, tiled=True),
        lax.all_gather(query_weight, "dp", axis=0, tiled=True),
        lax.all_gather(key_weight, "dp", axis=0, tiled=True),
        lax.all_gather(value_weight, "dp", axis=0, tiled=True),
        lax.all_gather(output_weight, "dp", axis=0, tiled=True),
        lax.all_gather(ffn_gain, "dp", axis=0, tiled=True),
        lax.all_gather(router_weight, "dp", axis=0, tiled=True),
        lax.all_gather(shared_gate, "dp", axis=0, tiled=True),
        lax.all_gather(shared_up, "dp", axis=0, tiled=True),
        lax.all_gather(shared_down, "dp", axis=0, tiled=True),
    )
    gain1_f = gain_one.astype(jnp.float32)
    gain2_f = gain_two.astype(jnp.float32)
    grad_total = cotangent.astype(jnp.float32)
    grad_gates = jnp.sum(grad_total[:, None, :] * picked, -1)
    grad_picked = (
        (gate_vals[:, :, None] * grad_total[:, None, :])
        .astype(jnp.bfloat16)
        .reshape(TOK_DEV * TOPK, D)
    )
    grad_back = (
        jnp.zeros((EXPERTS * CAP, D), jnp.bfloat16)
        .at[slot_index]
        .set(grad_picked)
        .reshape(EXPERTS, CAP, D)
    )
    grad_arrived = lax.all_to_all(grad_back, "experts", split_axis=0, concat_axis=1, tiled=True)
    grad_expert_activation = jnp.einsum(
        "erd,efd->erf", grad_arrived, expert_down, preferred_element_type=jnp.float32
    )
    grad_expert_gate_preact = (
        grad_expert_activation * expert_up_preact * swish_derivative(expert_gate_preact)
    ).astype(jnp.bfloat16)
    grad_expert_up_preact = (grad_expert_activation * jax.nn.silu(expert_gate_preact)).astype(
        jnp.bfloat16
    )
    expert_grad_down = jnp.einsum(
        "erf,erd->edf", expert_activation, grad_arrived, preferred_element_type=jnp.float32
    )
    expert_grad_gate = jnp.einsum(
        "xvb,xva->xba", received_rows, grad_expert_gate_preact, preferred_element_type=jnp.float32
    )
    expert_grad_up = jnp.einsum(
        "xvb,xva->xba", received_rows, grad_expert_up_preact, preferred_element_type=jnp.float32
    )
    grad_einputs = jnp.einsum(
        "cgj,clj->cgl", grad_expert_gate_preact, expert_gate, preferred_element_type=jnp.float32
    )
    grad_einputs = (
        grad_einputs
        + jnp.einsum(
            "cgj,clj->cgl",
            grad_expert_up_preact,
            expert_up_weight,
            preferred_element_type=jnp.float32,
        )
    ).astype(jnp.bfloat16)
    grad_returned = lax.all_to_all(
        grad_einputs, "experts", split_axis=1, concat_axis=0, tiled=True
    ).reshape(EXPERTS * CAP, D)
    grad_moe_in = jnp.sum(
        grad_returned[slot_index].astype(jnp.float32).reshape(TOK_DEV, TOPK, D), 1
    )
    grad_rprobs = jnp.sum(grad_gates[:, :, None] * route_hot, 1)
    grad_logits = (
        route_probs * (grad_rprobs - jnp.sum(route_probs * grad_rprobs, -1, keepdims=True))
    ).astype(jnp.bfloat16)
    grad_router_local = inner_rows(hidden2, grad_logits)
    grad_total_b = grad_total.astype(jnp.bfloat16)
    grad_sdown = inner_rows(shared_act, grad_total_b)
    grad_sact = times_transposed(grad_total_b, w_sdown)
    grad_sgpre = (grad_sact * shared_upre * swish_derivative(shared_gpre)).astype(jnp.bfloat16)
    grad_supre = (grad_sact * jax.nn.silu(shared_gpre)).astype(jnp.bfloat16)
    grad_sgate = inner_rows(hidden2, grad_sgpre)
    grad_sup = inner_rows(hidden2, grad_supre)
    grad_hidden2 = (
        grad_moe_in
        + times_transposed(grad_logits, w_router)
        + times_transposed(grad_sgpre, w_sgate)
        + times_transposed(grad_supre, w_sup)
    )
    grad_gain2 = jnp.sum(grad_hidden2 * normed2, 0)
    grad_normed2 = grad_hidden2 * gain2_f
    grad_resid = (
        inv_rms2 * (grad_normed2 - normed2 * jnp.mean(grad_normed2 * normed2, -1, keepdims=True))
        + grad_total
    )
    grad_branch = grad_resid.astype(jnp.bfloat16)
    grad_wout = inner_rows(attended, grad_branch)
    grad_attended = (
        times_transposed(grad_branch, w_out).astype(jnp.bfloat16).reshape(TOK_DEV, HEADS, HD)
    )
    scores_again = jnp.where(
        allowed[None],
        0.125 * jnp.einsum("qhd,khd->hqk", query_h, keys_h, preferred_element_type=jnp.float32),
        -1e30,
    )
    probs_f = jnp.exp(scores_again - log_total)
    probs_b = probs_f.astype(jnp.bfloat16)
    grad_pattn = jnp.einsum(
        "qhd,khd->hqk", grad_attended, values_h, preferred_element_type=jnp.float32
    )
    grad_scores = (
        probs_f * (grad_pattn - jnp.sum(probs_f * grad_pattn, -1, keepdims=True))
    ).astype(jnp.bfloat16)
    grad_query = 0.125 * jnp.einsum(
        "hqk,khd->qhd", grad_scores, keys_h, preferred_element_type=jnp.float32
    ).reshape(TOK_DEV, D)
    grad_keys = 0.125 * jnp.einsum(
        "hqk,qhd->khd", grad_scores, query_h, preferred_element_type=jnp.float32
    ).reshape(-1, D)
    grad_values = jnp.einsum(
        "hqk,qhd->khd", probs_b, grad_attended, preferred_element_type=jnp.float32
    ).reshape(-1, D)
    prompt_span = contexts * PROMPT
    grad_pkeys, grad_pvalues = (
        lax.psum_scatter(
            grad_keys[:prompt_span].astype(jnp.bfloat16), "context", scatter_dimension=0, tiled=True
        ).astype(jnp.float32),
        lax.psum_scatter(
            grad_values[:prompt_span].astype(jnp.bfloat16),
            "context",
            scatter_dimension=0,
            tiled=True,
        ).astype(jnp.float32),
    )
    grad_key_all = jnp.concatenate([grad_pkeys, grad_keys[prompt_span:]], 0)
    grad_value_all = jnp.concatenate([grad_pvalues, grad_values[prompt_span:]], 0)
    grad_qpre = rotate(grad_query, cos_table, -sin_table).astype(jnp.bfloat16)
    grad_kpre = rotate(grad_key_all, cos_table, -sin_table).astype(jnp.bfloat16)
    grad_vpre = grad_value_all.astype(jnp.bfloat16)
    grad_wquery = inner_rows(hidden1, grad_qpre)
    grad_wkey = inner_rows(hidden1, grad_kpre)
    grad_wvalue = inner_rows(hidden1, grad_vpre)
    grad_hidden1 = (
        times_transposed(grad_qpre, w_query)
        + times_transposed(grad_kpre, w_key)
        + times_transposed(grad_vpre, w_value)
    )
    grad_gain1 = jnp.sum(grad_hidden1 * normed1, 0)
    grad_normed1 = grad_hidden1 * gain1_f
    grad_inputs = (
        inv_rms1 * (grad_normed1 - normed1 * jnp.mean(grad_normed1 * normed1, -1, keepdims=True))
        + grad_resid
    )
    shares = (
        lax.psum_scatter(
            grad_gain1.astype(jnp.bfloat16), "dp", scatter_dimension=0, tiled=True
        ).astype(jnp.float32),
        lax.psum_scatter(
            grad_wquery.astype(jnp.bfloat16), "dp", scatter_dimension=0, tiled=True
        ).astype(jnp.float32),
        lax.psum_scatter(
            grad_wkey.astype(jnp.bfloat16), "dp", scatter_dimension=0, tiled=True
        ).astype(jnp.float32),
        lax.psum_scatter(
            grad_wvalue.astype(jnp.bfloat16), "dp", scatter_dimension=0, tiled=True
        ).astype(jnp.float32),
        lax.psum_scatter(
            grad_wout.astype(jnp.bfloat16), "dp", scatter_dimension=0, tiled=True
        ).astype(jnp.float32),
        lax.psum_scatter(
            grad_gain2.astype(jnp.bfloat16), "dp", scatter_dimension=0, tiled=True
        ).astype(jnp.float32),
        lax.psum_scatter(
            grad_router_local.astype(jnp.bfloat16), "dp", scatter_dimension=0, tiled=True
        ).astype(jnp.float32),
        lax.psum_scatter(
            grad_sgate.astype(jnp.bfloat16), "dp", scatter_dimension=0, tiled=True
        ).astype(jnp.float32),
        lax.psum_scatter(
            grad_sup.astype(jnp.bfloat16), "dp", scatter_dimension=0, tiled=True
        ).astype(jnp.float32),
        lax.psum_scatter(
            grad_sdown.astype(jnp.bfloat16), "dp", scatter_dimension=0, tiled=True
        ).astype(jnp.float32),
    )
    totals = (
        lax.psum(shares[0].astype(jnp.bfloat16), ("context", "experts")).astype(jnp.float32),
        lax.psum(shares[1].astype(jnp.bfloat16), ("context", "experts")).astype(jnp.float32),
        lax.psum(shares[2].astype(jnp.bfloat16), ("context", "experts")).astype(jnp.float32),
        lax.psum(shares[3].astype(jnp.bfloat16), ("context", "experts")).astype(jnp.float32),
        lax.psum(shares[4].astype(jnp.bfloat16), ("context", "experts")).astype(jnp.float32),
        lax.psum(shares[5].astype(jnp.bfloat16), ("context", "experts")).astype(jnp.float32),
        lax.psum(shares[6].astype(jnp.bfloat16), ("context", "experts")).astype(jnp.float32),
        lax.psum(shares[7].astype(jnp.bfloat16), ("context", "experts")).astype(jnp.float32),
        lax.psum(shares[8].astype(jnp.bfloat16), ("context", "experts")).astype(jnp.float32),
        lax.psum(shares[9].astype(jnp.bfloat16), ("context", "experts")).astype(jnp.float32),
    )
    summed_gate, summed_up, summed_down = (
        lax.psum_scatter(
            expert_grad_gate.astype(jnp.bfloat16),
            ("dp", "context"),
            scatter_dimension=2,
            tiled=True,
        ).astype(jnp.float32),
        lax.psum_scatter(
            expert_grad_up.astype(jnp.bfloat16), ("dp", "context"), scatter_dimension=2, tiled=True
        ).astype(jnp.float32),
        lax.psum_scatter(
            expert_grad_down.astype(jnp.bfloat16),
            ("dp", "context"),
            scatter_dimension=2,
            tiled=True,
        ).astype(jnp.float32),
    )
    summed_down = jnp.transpose(summed_down, (0, 2, 1))
    return (
        layer_out,
        grad_inputs,
        totals[0],
        totals[1],
        totals[2],
        totals[3],
        totals[4],
        totals[5],
        totals[6],
        totals[7],
        totals[8],
        totals[9],
        summed_gate,
        summed_up,
        summed_down,
    )


TUNED_MESH = {"dp": 4, "context": 2, "experts": 4}
AXES = ("dp", "context", "experts")
SLOT = 72
EXT = 16
ROWS = TOK_DEV + EXT
BF = jnp.bfloat16
F32 = jnp.float32
VMEM_LIMIT = 60 * 1024 * 1024


def microseconds(time):
    return pl.CostEstimate(flops=0, bytes_accessed=int(time * 0.4e6), transcendentals=0)


def moved(value, target):
    pairs = []
    for z in range(4):
        for y in range(2):
            for x in range(2):
                for c in range(2):
                    tz, ty, tx, tc = target(z, y, x, c)
                    pairs.append((((z * 2 + y) * 2 + x) * 2 + c, ((tz * 2 + ty) * 2 + tx) * 2 + tc))
    return lax.ppermute(value, AXES, pairs)


def over_core(value):
    return moved(value, lambda z, y, x, c: (z, y, x, 1 - c))


def over_x(value):
    return moved(value, lambda z, y, x, c: (z, y, 1 - x, c))


def over_a(value):
    return moved(value, lambda z, y, x, c: (z, y, 1 - x, c) if c == 0 else (z, 1 - y, x, c))


def over_b(value):
    return moved(value, lambda z, y, x, c: (z, 1 - y, x, c) if c == 0 else (z, y, 1 - x, c))


def over_z(value, step):
    return moved(value, lambda z, y, x, c: ((z + step) % 4, y, x, c))


def contract(left, right, left_dim, right_dim):
    return lax.dot_general(
        left, right, (((left_dim,), (right_dim,)), ((), ())), preferred_element_type=F32
    )


def one_hot_rows(rank_row):
    slots = lax.broadcasted_iota(jnp.int32, (SLOT, TOK_DEV), 0).astype(F32)
    return (slots == rank_row).astype(F32)


def swish_parts(pre_act):
    sigma = jax.nn.sigmoid(pre_act)
    return pre_act * sigma, sigma * (1.0 + pre_act * (1.0 - sigma))


def group_kernel(
    blocks,
    more,
    base_ref,
    *refs,
):
    block_refs, refs = refs[: 2 * blocks], refs[2 * blocks :]
    more_refs, refs = refs[:more], refs[more:]
    wg_ref, wu_ref, wd_ref = refs[:3]
    results, refs = refs[3 : 3 + 2 * blocks], refs[3 + 2 * blocks :]
    (
        rank_sc,
        prob_sc,
        x_sc,
        gate_sc,
        y_sc,
        acc_sc,
        dgate_sc,
        sel_sc,
        drp_sc,
        in_sc,
        out_sc,
        in_sems,
        out_sems,
    ) = refs[:13]
    e = pl.program_id(0)
    f = pl.program_id(1)
    experts = pl.num_programs(0)
    base = base_ref[0]
    copies = [
        pltpu.make_async_copy(source, into, refs[-1].at[i])
        for i, (source, into) in enumerate(zip(more_refs, refs[13:]))
    ]

    arrivals = [
        pltpu.make_async_copy(
            block_refs[side * blocks + b],
            in_sc.at[b, : (ROWS, TOK_DEV)[side], side * D : (side + 1) * D],
            in_sems.at[side, b],
        )
        for b in range(blocks)
        for side in range(2)
    ]

    @pl.when((e == 0) & (f == 0))
    def _():
        for one in arrivals + copies:
            one.start()
        drp_sc[...] = jnp.zeros_like(drp_sc)
        count = x_sc.shape[0]
        rows = []
        for b in range(blocks):
            for one in arrivals[2 * b : 2 * b + 2]:
                one.wait()
            rank_sc[b] = in_sc[b, TOK_DEV:, TOK_DEV:D].astype(F32)
            prob_sc[b] = in_sc[b, TOK_DEV:, :TOK_DEV].astype(F32)
            hots = []
            for i in range(count):
                hot = one_hot_rows(rank_sc[b, pl.ds(base + i, 1), :])
                gate_sc[i, b * SLOT : (b + 1) * SLOT, :] = jnp.sum(
                    hot * prob_sc[b, pl.ds(base + i, 1), :], -1, keepdims=True
                )
                hots.append(hot)
            hot = jnp.concatenate(hots, 0).astype(BF)
            rows.append(jnp.dot(hot, in_sc[b, :TOK_DEV, :], preferred_element_type=F32))
            if b % 2:
                span = slice((b - 1) * SLOT, (b + 1) * SLOT)
                for i in range(count):
                    of = slice(i * SLOT, (i + 1) * SLOT)
                    x_sc[i, span, :] = jnp.concatenate([v[of] for v in rows[-2:]], 0).astype(BF)

    @pl.when(f == 0)
    def _():
        y_sc[...] = jnp.zeros_like(y_sc)
        acc_sc[...] = jnp.zeros_like(acc_sc)
        dgate_sc[...] = jnp.zeros_like(dgate_sc)

    rows = x_sc[e, :, :D]
    gate_pre = jnp.dot(rows, wg_ref[0], preferred_element_type=F32)
    up_pre = jnp.dot(rows, wu_ref[0], preferred_element_type=F32)
    back = contract(x_sc[e, :, D:], wd_ref[0], 1, 1)
    swish, slope = swish_parts(gate_pre)
    inner = (swish * up_pre).astype(BF)
    dgate_sc[...] += jnp.sum(back * inner.astype(F32), -1, keepdims=True)
    back = back * gate_sc[e]
    dgate_pre = (back * up_pre * slope).astype(BF)
    dup_pre = (back * swish).astype(BF)
    y_sc[...] += jnp.dot(inner, wd_ref[0], preferred_element_type=F32)
    acc_sc[...] += contract(dgate_pre, wg_ref[0], 1, 1) + contract(dup_pre, wu_ref[0], 1, 1)

    @pl.when(f == pl.num_programs(1) - 1)
    def _():
        for b in range(blocks):
            span = slice(b * SLOT, (b + 1) * SLOT)
            into = pl.ds(pl.multiple_of(e * SLOT, 8), SLOT)
            sel_sc[b, into, :D] = y_sc[span, :] * gate_sc[e, span, :]
            sel_sc[b, into, D:] = acc_sc[span, :]
            hot = one_hot_rows(rank_sc[b, pl.ds(base + e, 1), :])
            drp_sc[b, pl.ds(base + e, 1), :] = jnp.sum(hot * dgate_sc[span, :], 0, keepdims=True)

    @pl.when((f == pl.num_programs(1) - 1) & (e == experts - 1))
    def _():
        for one in copies:
            one.wait()
        leaving = []
        for b in range(blocks):
            side, at = divmod(b, blocks // 2)
            moe_out, dx_out = out_sc.at[0, b], out_sc.at[1, b]
            hot = jnp.concatenate(
                [
                    one_hot_rows(rank_sc[b, pl.ds(base + i, 1), :])
                    for i in range(x_sc.shape[0])
                ],
                0,
            ).astype(BF)
            both = contract(hot, sel_sc[b].astype(BF), 0, 0)
            moe, dx = both[:, :D], both[:, D:]
            drp = drp_sc[b]
            if more:
                shared = refs[13 + 2 * at : 15 + 2 * at]
                moe_before, dx_before = refs[17 + b], refs[17 + blocks + b]
                moe = moe + shared[0][side].astype(F32) + moe_before[...].astype(F32)
                dx = dx + shared[1][side].astype(F32) + dx_before[:TOK_DEV, :].astype(F32)
                drp = drp + dx_before[TOK_DEV:, :TOK_DEV].astype(F32)
                drp = drp + dx_before[TOK_DEV:, TOK_DEV:].astype(F32)
            moe_out[:TOK_DEV, :] = moe.astype(BF)
            dx_out[:TOK_DEV, :] = dx.astype(BF)
            high = drp.astype(BF)
            dx_out[TOK_DEV:, :TOK_DEV] = high
            dx_out[TOK_DEV:, TOK_DEV:] = (drp - high.astype(F32)).astype(BF)
            sent = (
                pltpu.make_async_copy(moe_out.at[:TOK_DEV], results[b], out_sems.at[0, b]),
                pltpu.make_async_copy(dx_out, results[blocks + b], out_sems.at[1, b]),
            )
            for one in sent:
                one.start()
            leaving += sent
        for one in leaving:
            one.wait()


def group_experts(base, first, experts, h_group, g_group, more, w_gate, w_up, w_down):
    blocks = len(h_group)
    ff = w_gate.shape[2]
    tile = 512
    results = [(TOK_DEV, D)] * blocks + [(ROWS, D)] * blocks
    return pl.pallas_call(
        functools.partial(group_kernel, blocks, len(more)),
        out_shape=tuple(jax.ShapeDtypeStruct(s, BF) for s in results),
        grid_spec=pltpu.PrefetchScalarGridSpec(
            num_scalar_prefetch=1,
            grid=(experts, ff // tile),
            in_specs=[pl.BlockSpec(memory_space=pl.ANY)] * (2 * blocks + len(more))
            + [
                pl.BlockSpec((1, D, tile), lambda e, f, s: (first + e, 0, f)),
                pl.BlockSpec((1, D, tile), lambda e, f, s: (first + e, 0, f)),
                pl.BlockSpec((1, tile, D), lambda e, f, s: (first + e, f, 0)),
            ],
            out_specs=[pl.BlockSpec(memory_space=pltpu.HBM)] * len(results),
            scratch_shapes=[
                pltpu.VMEM((blocks, EXPERTS, TOK_DEV), F32),
                pltpu.VMEM((blocks, EXPERTS, TOK_DEV), F32),
                pltpu.VMEM((experts, blocks * SLOT, 2 * D), BF),
                pltpu.VMEM((experts, blocks * SLOT, 1), F32),
                pltpu.VMEM((blocks * SLOT, D), F32),
                pltpu.VMEM((blocks * SLOT, D), F32),
                pltpu.VMEM((blocks * SLOT, 1), F32),
                pltpu.VMEM((blocks, experts * SLOT, 2 * D), F32),
                pltpu.VMEM((blocks, EXPERTS, TOK_DEV), F32),
                pltpu.VMEM((blocks, ROWS, 2 * D), BF),
                pltpu.VMEM((2, blocks, ROWS, D), BF),
                pltpu.SemaphoreType.DMA((2, blocks)),
                pltpu.SemaphoreType.DMA((2, blocks)),
            ]
            + [pltpu.VMEM(v.shape, v.dtype) for v in more]
            + [pltpu.SemaphoreType.DMA((max(1, len(more)),))],
        ),
        compiler_params=pltpu.CompilerParams(vmem_limit_bytes=VMEM_LIMIT),
        cost_estimate=microseconds(21),
        name="group_experts",
    )(base, *h_group, *g_group, *more, w_gate, w_up, w_down)


def shared_kernel(h_a_ref, h_b_ref, g_a_ref, g_b_ref, w_a_ref, w_b_ref, out_ref, dh_ref, h_sc, g_sc, out_sc, dh_sc):
    for k, (h_ref, g_ref) in enumerate(((h_a_ref, g_a_ref), (h_b_ref, g_b_ref))):
        h_sc[k * TOK_DEV : (k + 1) * TOK_DEV, :] = h_ref[:TOK_DEV, :]
        g_sc[k * TOK_DEV : (k + 1) * TOK_DEV, :] = g_ref[:TOK_DEV, :]
    for k, w_ref in enumerate((w_a_ref, w_b_ref)):
        w_gate, w_up = w_ref[:, :, :256].reshape(D, 256), w_ref[:, :, 256:512].reshape(D, 256)
        w_down = jnp.concatenate(
            [w_ref[:, 64 * i : 64 * (i + 1), 512:].reshape(256, 256) for i in range(3)], 1
        )
        gate_pre = jnp.dot(h_sc[...], w_gate, preferred_element_type=F32)
        up_pre = jnp.dot(h_sc[...], w_up, preferred_element_type=F32)
        back = contract(g_sc[...], w_down, 1, 1)
        swish, slope = swish_parts(gate_pre)
        inner = (swish * up_pre).astype(BF)
        out = jnp.dot(inner, w_down, preferred_element_type=F32)
        dgate_pre = (back * up_pre * slope).astype(BF)
        dup_pre = (back * swish).astype(BF)
        dh = contract(dgate_pre, w_gate, 1, 1) + contract(dup_pre, w_up, 1, 1)
        if k == 0:
            out_sc[...], dh_sc[...] = out, dh
    for b in range(2):
        rows = slice(b * TOK_DEV, (b + 1) * TOK_DEV)
        out_ref[b] = (out_sc[rows, :] + out[rows]).astype(BF)
        dh_ref[b] = (dh_sc[rows, :] + dh[rows]).astype(BF)


def shared_rows(h_pair, g_pair, w_own, w_far):
    rows = jax.ShapeDtypeStruct((2, TOK_DEV, D), BF)
    vmem = pl.BlockSpec(memory_space=pltpu.VMEM)
    return pl.pallas_call(
        shared_kernel,
        out_shape=(rows, rows),
        in_specs=[vmem] * 6,
        out_specs=(vmem, vmem),
        scratch_shapes=[
            pltpu.VMEM((2 * TOK_DEV, D), BF),
            pltpu.VMEM((2 * TOK_DEV, D), BF),
            pltpu.VMEM((2 * TOK_DEV, D), F32),
            pltpu.VMEM((2 * TOK_DEV, D), F32),
        ],
        compiler_params=pltpu.CompilerParams(vmem_limit_bytes=VMEM_LIMIT),
        cost_estimate=microseconds(8),
        name="shared_rows",
    )(*h_pair, *g_pair, w_own, w_far)


def start_parts(h_parts, g_parts, h_buf, g_buf, sems):
    per = h_parts[0].shape[0]
    copies = []
    for i in range(len(h_parts)):
        for k in range(per // 2):
            at, into = pl.ds(2 * k, 2), pl.ds(i * per + 2 * k, 2)
            number = i * (per // 2) + k
            copies.append(
                (
                    pltpu.make_async_copy(h_parts[i].at[at], h_buf.at[into], sems.at[0, number]),
                    pltpu.make_async_copy(
                        g_parts[i].at[at, :TOK_DEV], g_buf.at[into, :TOK_DEV], sems.at[1, number]
                    ),
                )
            )
    for pair in copies:
        for one in pair:
            one.start()
    return copies


def each_pair(copies, work):
    done = 0
    for upto in [1, 2] + list(range(4, len(copies) + 1, 2)):
        for pair in copies[done:upto]:
            for one in pair:
                one.wait()
        lax.fori_loop(done, upto, work, 0, unroll=True)
        done = upto


def expert_slice_kernel(parts, more, pos_ref, *refs):
    h_parts, g_parts = refs[:parts], refs[parts : 2 * parts]
    weights = refs[2 * parts : 2 * parts + 3]
    refs = refs[2 * parts + 3 :]
    sums, refs = refs[: 3 * more], refs[3 * more :]
    outs, (buf, x_sc, gd_sc, rank_sc, prob_sc) = refs[:3], refs[3:8]
    wg_ref, wu_ref, wd_ref, og_ref, ou_ref, od_ref, sems, w_sems, out_sems = refs[8:]
    base = pos_ref[0]
    experts, _, width = wg_ref.shape
    per = h_parts[0].shape[0]
    copies = start_parts(h_parts, g_parts, buf.at[:, :, :D], buf.at[:, :, D:], sems)
    cols = pl.ds(pl.multiple_of(pos_ref[1] * width, width), width)
    loads = [
        pltpu.make_async_copy(weights[0].at[:, :, cols], wg_ref, w_sems.at[0]),
        pltpu.make_async_copy(weights[1].at[:, :, cols], wu_ref, w_sems.at[1]),
        pltpu.make_async_copy(weights[2].at[:, cols, :], wd_ref, w_sems.at[2]),
    ]
    for i in range(3 * more):
        loads.append(
            pltpu.make_async_copy(sums[i], (og_ref, ou_ref, od_ref)[i], w_sems.at[3 + i])
        )
    for one in loads:
        one.start()

    def dispatch(pair, carry):
        both = []
        for k in range(2):
            b = 2 * pair + k
            rank_sc[k] = buf[b, TOK_DEV:, TOK_DEV:D].astype(F32)
            prob_sc[k] = buf[b, TOK_DEV:, :TOK_DEV].astype(F32)
            hots, gates = [], []
            for i in range(experts):
                hot = one_hot_rows(rank_sc[k, pl.ds(base + i, 1), :])
                gates.append(
                    jnp.sum(hot * prob_sc[k, pl.ds(base + i, 1), :], -1, keepdims=True)
                )
                hots.append(hot)
            hot = jnp.concatenate(hots, 0).astype(BF)
            rows = jnp.dot(hot, buf[b, :TOK_DEV, :], preferred_element_type=F32)
            both.append((rows[:, :D], rows[:, D:] * jnp.concatenate(gates, 0)))
        into = pl.ds(pl.multiple_of(pair * 2 * SLOT, 2 * SLOT), 2 * SLOT)
        for i in range(experts):
            span = slice(i * SLOT, (i + 1) * SLOT)
            x_sc[i, into, :] = jnp.concatenate([v[0][span] for v in both], 0).astype(BF)
            gd_sc[i, into, :] = jnp.concatenate([v[1][span] for v in both], 0).astype(BF)
        return carry

    each_pair(copies, dispatch)
    for one in loads:
        one.wait()

    def products(i, carry):
        rows = x_sc[i]
        gate_pre = jnp.dot(rows, wg_ref[i], preferred_element_type=F32)
        up_pre = jnp.dot(rows, wu_ref[i], preferred_element_type=F32)
        back = contract(gd_sc[i], wd_ref[i], 1, 1)
        swish, slope = swish_parts(gate_pre)
        inner = (swish * up_pre).astype(BF)
        dgate_pre = (back * up_pre * slope).astype(BF)
        dup_pre = (back * swish).astype(BF)
        add_g = contract(rows, dgate_pre, 0, 0)
        add_u = contract(rows, dup_pre, 0, 0)
        add_d = contract(inner, gd_sc[i], 0, 0)
        if more:
            og_ref[i] += add_g
            ou_ref[i] += add_u
            od_ref[i] += add_d
        else:
            og_ref[i], ou_ref[i], od_ref[i] = add_g, add_u, add_d
        for k, source in enumerate((og_ref, ou_ref, od_ref)):
            pltpu.make_async_copy(source.at[i], outs[k].at[i], out_sems.at[k, i]).start()
        return carry

    lax.fori_loop(0, experts, products, 0, unroll=2 if experts % 2 == 0 else 1)
    for i in range(experts):
        for k, source in enumerate((og_ref, ou_ref, od_ref)):
            pltpu.make_async_copy(source.at[i], outs[k].at[i], out_sems.at[k, i]).wait()


def expert_slice_grads(pos, h_parts, g_parts, w_gate, w_up, w_down, width, sums=()):
    parts, per = len(h_parts), h_parts[0].shape[0]
    experts = w_gate.shape[0]
    blocks = parts * per
    shapes = ((experts, D, width), (experts, D, width), (experts, width, D))
    anywhere = pl.BlockSpec(memory_space=pl.ANY)
    return pl.pallas_call(
        functools.partial(expert_slice_kernel, parts, len(sums) // 3),
        out_shape=tuple(jax.ShapeDtypeStruct(s, F32) for s in shapes),
        in_specs=[pl.BlockSpec(memory_space=pltpu.SMEM)]
        + [anywhere] * (2 * parts + 3 + len(sums)),
        out_specs=(pl.BlockSpec(memory_space=pltpu.HBM),) * 3,
        scratch_shapes=[
            pltpu.VMEM((blocks, ROWS, 2 * D), BF),
            pltpu.VMEM((experts, blocks * SLOT, D), BF),
            pltpu.VMEM((experts, blocks * SLOT, D), BF),
            pltpu.VMEM((2, EXPERTS, TOK_DEV), F32),
            pltpu.VMEM((2, EXPERTS, TOK_DEV), F32),
        ]
        + [pltpu.VMEM(s, BF) for s in shapes]
        + [pltpu.VMEM(s, F32) for s in shapes]
        + [
            pltpu.SemaphoreType.DMA((2, blocks // 2)),
            pltpu.SemaphoreType.DMA((6,)),
            pltpu.SemaphoreType.DMA((3, experts)),
        ],
        compiler_params=pltpu.CompilerParams(vmem_limit_bytes=VMEM_LIMIT),
        cost_estimate=microseconds(31),
        name="expert_slice_grads",
    )(pos, *h_parts, *g_parts, w_gate, w_up, w_down, *sums)


def shared_slice_kernel(parts, more, pos_ref, *refs):
    h_parts, g_parts = refs[:parts], refs[parts : 2 * parts]
    w_ref = refs[2 * parts]
    refs = refs[2 * parts + 1 :]
    sums, refs = refs[: 3 * more], refs[3 * more :]
    if more:
        mine_ref, refs = refs[0], refs[1:]
    og_ref, ou_ref, od_ref, h_buf, g_buf, inner_sc, wg_ref, wu_ref, wd_ref, sems = refs
    per = h_parts[0].shape[0]
    copies = start_parts(h_parts, g_parts, h_buf, g_buf, sems)
    wg_ref[...] = w_ref[:, :, :256].reshape(D, 256)
    wu_ref[...] = w_ref[:, :, 256:512].reshape(D, 256)
    for i in range(3):
        wd_ref[:, 256 * i : 256 * (i + 1)] = w_ref[:, 64 * i : 64 * (i + 1), 512:].reshape(256, 256)
    window = pl.ds(pl.multiple_of(pos_ref[0] * 128, 128), og_ref.shape[0])
    lanes = pl.ds(pl.multiple_of(pos_ref[1] * 128, 128), od_ref.shape[0])
    for i, out_ref in enumerate((og_ref, ou_ref, od_ref)):
        out_ref[...] = sums[i][...] if more else jnp.zeros_like(out_ref)

    def two(buf, pair, cols=slice(None)):
        return jnp.concatenate([buf[2 * pair + k, :TOK_DEV, cols] for k in range(2)], 0)

    def products(pair, carry):
        rows, grads = two(h_buf, pair), two(g_buf, pair)
        gate_pre = jnp.dot(rows, wg_ref[...], preferred_element_type=F32)
        up_pre = jnp.dot(rows, wu_ref[...], preferred_element_type=F32)
        back = contract(grads, wd_ref[...], 1, 1)
        swish, slope = swish_parts(gate_pre)
        inner_sc[...] = (swish * up_pre).astype(BF)
        dgate_pre = (back * up_pre * slope).astype(BF)
        dup_pre = (back * swish).astype(BF)
        picked = two(h_buf, pair, window)
        og_ref[...] += contract(picked, dgate_pre, 0, 0)
        ou_ref[...] += contract(picked, dup_pre, 0, 0)
        od_ref[...] += contract(inner_sc[:, lanes], grads, 0, 0)
        return carry

    each_pair(copies, products)
    if more:
        rows = pl.ds(pl.multiple_of(pos_ref[2], 64), D // 4)
        mine_ref[:, :256] = og_ref[rows, :].astype(BF)
        mine_ref[:, 256:512] = ou_ref[rows, :].astype(BF)
        down = od_ref[pl.ds(pl.multiple_of(pos_ref[3], 64), 64), :].astype(BF)
        for i in range(3):
            mine_ref[64 * i : 64 * (i + 1), 512:] = down[:, 256 * i : 256 * (i + 1)]


def shared_slice_grads(pos, h_parts, g_parts, weights, sums=()):
    parts, per = len(h_parts), h_parts[0].shape[0]
    blocks = parts * per
    width = 256
    shapes = ((256, width), (256, width), (128, D))
    vmem = pl.BlockSpec(memory_space=pltpu.VMEM)
    anywhere = pl.BlockSpec(memory_space=pl.ANY)
    return pl.pallas_call(
        functools.partial(shared_slice_kernel, parts, len(sums) // 3),
        out_shape=jax.ShapeDtypeStruct((D // 4, D), BF)
        if sums
        else tuple(jax.ShapeDtypeStruct(s, F32) for s in shapes),
        in_specs=[pl.BlockSpec(memory_space=pltpu.SMEM)]
        + [anywhere] * (2 * parts)
        + [vmem] * (1 + len(sums)),
        out_specs=vmem if sums else (vmem,) * 3,
        scratch_shapes=[pltpu.VMEM(s, F32) for s in (shapes if sums else ())]
        + [
            pltpu.VMEM((blocks, ROWS, D), BF),
            pltpu.VMEM((blocks, ROWS, D), BF),
            pltpu.VMEM((2 * TOK_DEV, width), BF),
            pltpu.VMEM((D, width), BF),
            pltpu.VMEM((D, width), BF),
            pltpu.VMEM((width, D), BF),
            pltpu.SemaphoreType.DMA((2, blocks // 2)),
        ],
        compiler_params=pltpu.CompilerParams(vmem_limit_bytes=VMEM_LIMIT),
        cost_estimate=microseconds(20),
        name="shared_slice_grads",
    )(pos, *h_parts, *g_parts, weights, *sums)


def pair_sum(kept, received):
    return (kept.astype(F32) + received.astype(F32)).astype(BF)


def halves(value, bit):
    width = value.shape[-1] // 2
    low, high = value[..., :width], value[..., width:]
    return jnp.where(bit == 0, low, high), jnp.where(bit == 0, high, low)


def rejoin(own, other, bit):
    return jnp.where(
        bit == 0, jnp.concatenate([own, other], -1), jnp.concatenate([other, own], -1)
    )


def lane_halves():
    lane = lax.broadcasted_iota(jnp.int32, (1, 128), 1)
    return [(lane < 64).astype(F32).astype(BF), (lane >= 64).astype(F32).astype(BF)]


def pick_lanes(first, second):
    lane = lax.broadcasted_iota(jnp.int32, first.shape, 1)
    return jnp.where(lane < 64, first, second)


def turned(value, cos, sin):
    lane = lax.broadcasted_iota(jnp.int32, value.shape, 1)
    partner = jnp.where(lane % 64 < 32, pltpu.roll(value, 96, 1), pltpu.roll(value, 32, 1))
    return value * cos + partner * sin


def causal_mask(rows, heads):
    row = lax.broadcasted_iota(jnp.int32, (heads * rows, rows), 0) % rows
    col = lax.broadcasted_iota(jnp.int32, (heads * rows, rows), 1)
    return row, col


def stacked(value, masks):
    return jnp.concatenate([value * mask for mask in masks], 0)


def unit_rms(value):
    return lax.rsqrt(jnp.mean(value * value, -1, keepdims=True) + EPS)


def softmax_of(first, second=None):
    top = jnp.max(first, -1, keepdims=True)
    if second is not None:
        top = jnp.maximum(top, jnp.max(second, -1, keepdims=True))
    first = jnp.exp(first - top)
    total = jnp.sum(first, -1, keepdims=True)
    if second is None:
        return first * (1.0 / total)
    second = jnp.exp(second - top)
    scale = 1.0 / (total + jnp.sum(second, -1, keepdims=True))
    return first * scale, second * scale


def attention_kernel(place_ref, *refs):
    w_parts = refs[:8]
    (
        h1_ref,
        own_ref,
        far_ref,
        gain1_ref,
        gain2_ref,
        router_ref,
        cos_ref,
        sin_ref,
        rank_ref,
        *outs,
        h2_ref,
        probs_ref,
        w_ref,
        q_ref,
        k_ref,
        v_ref,
        o_ref,
        x1_ref,
        h_sc,
        sems,
        out_sems,
    ) = refs[8:]
    kept = (w_ref, q_ref, k_ref, v_ref, o_ref, x1_ref)
    leaving = [
        pltpu.make_async_copy(kept[i], outs[i], out_sems.at[i]) for i in range(len(kept))
    ]
    copies = []
    for part in range(8):
        for slot in range(4):
            rows = pl.ds(pl.multiple_of(place_ref[8 + slot] * 192, 192), 192)
            copies.append(
                pltpu.make_async_copy(
                    w_parts[part].at[slot, :192, :],
                    w_ref.at[place_ref[part], rows, :],
                    sems.at[part, slot],
                )
            )
    for one in copies:
        one.start()
    h_sc[:TOK_DEV, :] = h1_ref[...]
    far = far_ref[:TOK_DEV, :].astype(F32)
    h_sc[TOK_DEV:, :] = (far * unit_rms(far) * gain1_ref[...]).astype(BF)
    for one in copies:
        one.wait()
    leaving[0].start()
    for i in range(6):
        out_ref = (q_ref, k_ref, v_ref)[i // 2]
        product = jnp.dot(h_sc[...], w_ref[i], preferred_element_type=F32)
        for slab in range(3):
            at = (i % 2) * 384 + slab * 128
            for half in range(2):
                rows = slice(half * TOK_DEV, (half + 1) * TOK_DEV)
                value = product[rows, slab * 128 : (slab + 1) * 128]
                if i < 4:
                    value = turned(value, cos_ref[...], sin_ref[...])
                out_ref[rows, at : at + 128] = value.astype(BF)
        if i % 2:
            leaving[1 + i // 2].start()
    masks = lane_halves()
    row, col = causal_mask(PROMPT, 2)
    prompt_ok = col <= row
    row, col = causal_mask(CONT * CLEN, 2)
    cont_ok = (row // CLEN == col // CLEN) & (col <= row)
    row = lax.broadcasted_iota(jnp.int32, (2 * CONT * CLEN, 1), 0) % (CONT * CLEN)
    reads_far = jnp.where(row < CLEN, place_ref[12], place_ref[13]).astype(F32)
    own_c = slice(PROMPT, TOK_DEV)
    far_p = slice(TOK_DEV, TOK_DEV + PROMPT)

    def heads(pair, carry):
        cols = pl.ds(pl.multiple_of(pair * 128, 128), 128)
        q_p, k_p, v_p = q_ref[:PROMPT, cols], k_ref[:PROMPT, cols], v_ref[:PROMPT, cols]
        q_c, k_c, v_c = q_ref[own_c, cols], k_ref[own_c, cols], v_ref[own_c, cols]
        k_f, v_f = k_ref[far_p, cols], v_ref[far_p, cols]
        score = 0.125 * contract(stacked(q_p, masks), k_p, 1, 1)
        prob = softmax_of(jnp.where(prompt_ok, score, -1e30)).astype(BF)
        out = jnp.dot(prob, v_p, preferred_element_type=F32)
        o_ref[:PROMPT, cols] = pick_lanes(out[:PROMPT], out[PROMPT:]).astype(BF)
        query = stacked(q_c, masks)
        near, far = contract(query, k_p, 1, 1), contract(query, k_f, 1, 1)
        first = 0.125 * jnp.where(reads_far > 0.5, far, near)
        second = jnp.where(cont_ok, 0.125 * contract(query, k_c, 1, 1), -1e30)
        first, second = softmax_of(first, second)
        out = (
            jnp.dot((first * (1.0 - reads_far)).astype(BF), v_p, preferred_element_type=F32)
            + jnp.dot((first * reads_far).astype(BF), v_f, preferred_element_type=F32)
            + jnp.dot(second.astype(BF), v_c, preferred_element_type=F32)
        )
        o_ref[own_c, cols] = pick_lanes(out[: CONT * CLEN], out[CONT * CLEN :]).astype(BF)
        return carry

    lax.fori_loop(0, HEADS // 2, heads, 0, unroll=3)
    leaving[4].start()
    for i in range(2):
        cols = slice(384 * i, 384 * (i + 1))
        x1_ref[:, cols] = own_ref[:TOK_DEV, cols].astype(F32) + jnp.dot(
            o_ref[...], w_ref[6 + i], preferred_element_type=F32
        )
    leaving[5].start()
    resid = x1_ref[...]
    hidden = (resid * unit_rms(resid) * gain2_ref[...]).astype(BF)
    h2_ref[:TOK_DEV, :] = hidden
    logits = contract(router_ref[...], hidden, 1, 1)
    logits = jnp.exp(logits - jnp.max(logits, 0, keepdims=True))
    probs = logits / jnp.sum(logits, 0, keepdims=True)
    probs_ref[...] = probs
    h2_ref[TOK_DEV:, :TOK_DEV] = probs.astype(BF)
    h2_ref[TOK_DEV:, TOK_DEV:] = rank_ref[...]
    for one in leaving:
        one.wait()


def attention_forward(place, w_parts, h1, own, far, gain1, gain2, router_t, cos, sin, ranks):
    vmem = pl.BlockSpec(memory_space=pltpu.VMEM)
    hbm = pl.BlockSpec(memory_space=pltpu.HBM)
    kept = (
        ((8, D, 384), BF),
        ((2 * TOK_DEV, D), BF),
        ((2 * TOK_DEV, D), BF),
        ((2 * TOK_DEV, D), BF),
        ((TOK_DEV, D), BF),
        ((TOK_DEV, D), F32),
    )
    return pl.pallas_call(
        attention_kernel,
        out_shape=tuple(
            jax.ShapeDtypeStruct(*s)
            for s in kept + (((ROWS, D), BF), ((EXPERTS, TOK_DEV), F32))
        ),
        in_specs=[pl.BlockSpec(memory_space=pltpu.SMEM)]
        + [pl.BlockSpec(memory_space=pl.ANY)] * 8
        + [vmem] * 9,
        out_specs=(hbm,) * len(kept) + (vmem, vmem),
        scratch_shapes=[pltpu.VMEM(*s) for s in kept]
        + [
            pltpu.VMEM((2 * TOK_DEV, D), BF),
            pltpu.SemaphoreType.DMA((8, 4)),
            pltpu.SemaphoreType.DMA((len(kept),)),
        ],
        compiler_params=pltpu.CompilerParams(vmem_limit_bytes=VMEM_LIMIT),
        cost_estimate=microseconds(20),
        name="attention_forward",
    )(place, *w_parts, h1, own, far, gain1, gain2, router_t, cos, sin, ranks)


def branch_kernel(*refs):
    dx_refs, refs = refs[:3], refs[3:]
    (
        h2_ref,
        probs_ref,
        x1_ref,
        g_ref,
        gain2_ref,
        router_ref,
        w_ref,
        dx1_ref,
        do_ref,
        do_c_ref,
        grouter_ref,
        ggain_ref,
    ) = refs
    dx = dx_refs[0][...].astype(F32) + dx_refs[1][...].astype(F32) + dx_refs[2][...].astype(F32)
    drp = dx[TOK_DEV:, :TOK_DEV] + dx[TOK_DEV:, TOK_DEV:]
    probs = probs_ref[...]
    dlogits = (probs * (drp - jnp.sum(probs * drp, 0, keepdims=True))).astype(BF)
    hidden = h2_ref[:TOK_DEV, :]
    grouter_ref[...] = jnp.dot(dlogits, hidden, preferred_element_type=F32)
    dh2 = (
        dx[:TOK_DEV]
        + contract(dlogits, router_ref[...], 0, 0)
    )
    resid = x1_ref[...]
    scale = unit_rms(resid)
    normed = resid * scale
    ggain_ref[...] = jnp.sum(dh2 * normed, 0, keepdims=True)
    dnormed = dh2 * gain2_ref[...]
    dx1 = scale * (dnormed - normed * jnp.mean(dnormed * normed, -1, keepdims=True)) + g_ref[
        ...
    ].astype(F32)
    dx1_ref[...] = dx1
    datt = dx1.astype(BF)
    do_ref[...] = (
        contract(datt[:, :384], w_ref[0], 1, 1) + contract(datt[:, 384:], w_ref[1], 1, 1)
    ).astype(BF)
    do_c_ref[...] = do_ref[PROMPT:, :]


def branch_backward(dx, h_block, probs, x1, grad, gain2, router_t, w_all):
    shape = jax.ShapeDtypeStruct
    whole = lambda *dims: pl.BlockSpec(dims, lambda i: (0,) * len(dims))
    rows = whole(TOK_DEV, D)
    return pl.pallas_call(
        branch_kernel,
        grid=(1,),
        out_shape=(
            shape((TOK_DEV, D), F32),
            shape((TOK_DEV, D), BF),
            shape((TOK_DEV - PROMPT, D), BF),
            shape((EXPERTS, D), F32),
            shape((1, D), F32),
        ),
        in_specs=[
            whole(ROWS, D),
            whole(ROWS, D),
            whole(ROWS, D),
            whole(ROWS, D),
            whole(EXPERTS, TOK_DEV),
            rows,
            rows,
            whole(1, D),
            whole(EXPERTS, D),
            pl.BlockSpec((2, D, 384), lambda i: (3, 0, 0)),
        ],
        out_specs=(
            rows,
            rows,
            whole(TOK_DEV - PROMPT, D),
            whole(EXPERTS, D),
            whole(1, D),
        ),
        compiler_params=pltpu.CompilerParams(vmem_limit_bytes=VMEM_LIMIT),
        cost_estimate=microseconds(6),
        name="branch_backward",
    )(*dx, h_block, probs, x1, grad, gain2, router_t, w_all)


def attention_back_kernel(
    flags_ref,
    *refs,
):
    sources = refs[:9]
    do_far_ref, gain1_ref, cos_ref, sin_ref, grouter_ref, ggain2_ref = refs[9:15]
    gtok_ref, keep_ref, send_ref = refs[15:18]
    arrived = refs[18:27]
    q_ref, k_ref, v_ref, do_ref, h1_ref, w_ref, own_ref, dx1_ref, gwo_ref = arrived
    dq_sc, dk_sc, dv_sc, low_sc, product_sc, ext_sc, in_sems, out_sems = refs[27:]
    copies = [
        pltpu.make_async_copy(
            sources[i].at[:6] if i == 5 else sources[i], arrived[i], in_sems.at[i]
        )
        for i in range(9)
    ]
    for one in copies:
        one.start()

    def put(number, source):
        cols = slice((number % 2) * D, (number % 2 + 1) * D)
        copy = lambda out: pltpu.make_async_copy(
            source, out.at[:, : D // 4, cols], out_sems.at[number]
        )

        @pl.when(flags_ref[4] == number // 2)
        def _():
            copy(keep_ref).start()

        @pl.when(flags_ref[4] != number // 2)
        def _():
            copy(send_ref).start()

        return copy(keep_ref)

    for one in copies[:4]:
        one.wait()
    masks = lane_halves()
    row, col = causal_mask(PROMPT, 2)
    prompt_ok = col <= row
    cont_ok = (row // CLEN == col // CLEN) & (col <= row)
    row = lax.broadcasted_iota(jnp.int32, (8 * CLEN, 1), 0) // CLEN % 4
    near = jnp.where(
        row < 2,
        jnp.where(row == 0, flags_ref[0], flags_ref[1]),
        jnp.where(row == 2, flags_ref[2], flags_ref[3]),
    ).astype(F32)
    own_rows = row < 2
    own_c = slice(PROMPT, TOK_DEV)
    far_p = slice(TOK_DEV, TOK_DEV + PROMPT)
    far_c = slice(TOK_DEV + PROMPT, 2 * TOK_DEV)
    cont = CONT * CLEN

    def either(own, other):
        return jnp.where((near > 0.5) | ~own_rows, own, other)

    def heads(pair, carry):
        cols = pl.ds(pl.multiple_of(pair * 128, 128), 128)
        q_p, k_p, v_p = q_ref[:PROMPT, cols], k_ref[:PROMPT, cols], v_ref[:PROMPT, cols]
        k_f, v_f = k_ref[far_p, cols], v_ref[far_p, cols]
        q_c, k_c, v_c = q_ref[own_c, cols], k_ref[own_c, cols], v_ref[own_c, cols]
        do_p, do_c = do_ref[:PROMPT, cols], do_ref[own_c, cols]
        q_4 = jnp.concatenate([q_c, q_ref[far_c, cols]], 0)
        k_4 = jnp.concatenate([k_c, k_ref[far_c, cols]], 0)
        v_4 = jnp.concatenate([v_c, v_ref[far_c, cols]], 0)
        do_4 = jnp.concatenate([do_c, do_far_ref[:, cols]], 0)
        q_all = jnp.concatenate([q_p, q_4], 0)
        do_all = jnp.concatenate([do_p, do_4], 0)
        rows = 4 * CLEN
        query, grad = stacked(q_p, masks), stacked(do_p, masks)
        score = jnp.where(prompt_ok, 0.125 * contract(query, k_p, 1, 1), -1e30)
        prob = softmax_of(score)
        dprob = contract(grad, v_p, 1, 1)
        ds = (prob * (dprob - jnp.sum(prob * dprob, -1, keepdims=True))).astype(BF)
        prob = prob.astype(BF)
        query, grad = stacked(q_4, masks), stacked(do_4, masks)
        first = 0.125 * either(contract(query, k_p, 1, 1), contract(query, k_f, 1, 1))
        second = jnp.where(cont_ok, 0.125 * contract(query, k_4, 1, 1), -1e30)
        first, second = softmax_of(first, second)
        dfirst = either(contract(grad, v_p, 1, 1), contract(grad, v_f, 1, 1))
        dsecond = contract(grad, v_4, 1, 1)
        mean = jnp.sum(first * dfirst, -1, keepdims=True) + jnp.sum(
            second * dsecond, -1, keepdims=True
        )
        ds1 = first * (dfirst - mean)
        ds2 = (second * (dsecond - mean)).astype(BF)
        ds_near = (ds1 * near).astype(BF)
        ds_far = (ds1 * (1.0 - near)).astype(BF)
        p_near = (first * near).astype(BF)
        p_own = second.astype(BF)
        out = jnp.dot(ds, k_p, preferred_element_type=F32)
        dq_sc[:PROMPT, cols] = pick_lanes(out[:PROMPT], out[PROMPT:])
        out = (
            jnp.dot(ds_near, k_p, preferred_element_type=F32)
            + jnp.dot(ds_far, k_f, preferred_element_type=F32)
            + jnp.dot(ds2, k_4, preferred_element_type=F32)
        )
        dq_sc[own_c, cols] = pick_lanes(out[:cont], out[rows : rows + cont])
        for out, left, left_own, right, own in (
            (dk_sc, (ds, ds_near), ds2, q_all, q_c),
            (dv_sc, (prob, p_near), p_own, do_all, do_c),
        ):
            parts = [
                contract(
                    jnp.concatenate([part[h * rows : (h + 1) * rows] for part in left], 0),
                    right,
                    0,
                    0,
                )
                for h in range(2)
            ]
            out[:PROMPT, cols] = pick_lanes(*parts)
            parts = [
                contract(left_own[h * rows : h * rows + cont, :cont], own, 0, 0) for h in range(2)
            ]
            out[own_c, cols] = pick_lanes(*parts)
        return carry

    lax.fori_loop(0, HEADS // 2, heads, 0, unroll=3)
    for one in copies[4:]:
        one.wait()
    leaving = [put(3, gwo_ref)]
    dh1 = None
    for i, source in enumerate((dq_sc, dk_sc, dv_sc)):
        for slab in range(6):
            cols = slice(slab * 128, (slab + 1) * 128)
            value = source[:, cols]
            if i < 2:
                value = turned(0.125 * value, cos_ref[...], -sin_ref[...])
            low_sc[:, cols] = value.astype(BF)
        grads = low_sc[...]
        product = contract(h1_ref[...], grads, 0, 0).astype(BF)
        product_sc[i] = product.reshape(4, D // 4, D)
        leaving.append(put(i, product_sc.at[i]))
        for half in range(2):
            part = contract(grads[:, 384 * half : 384 * (half + 1)], w_ref[2 * i + half], 1, 1)
            dh1 = part if dh1 is None else dh1 + part
    inputs = own_ref[...].astype(F32)
    scale = unit_rms(inputs)
    normed = inputs * scale
    ggain1 = jnp.sum(dh1 * normed, 0, keepdims=True)
    gains = jnp.concatenate([ggain1, ggain2_ref[...], jnp.zeros((EXT - 2, D), F32)], 0)
    ext_sc[...] = jnp.zeros_like(ext_sc)
    for z in range(4):
        cols = slice(z * (D // 4), (z + 1) * (D // 4))
        extras = jnp.concatenate([grouter_ref[:, cols], gains[:, cols]], 1).astype(BF)
        ext_sc[0, z, :, : 2 * (D // 4)] = extras
    for k, out in enumerate((keep_ref, send_ref)):
        which = flags_ref[4] if k == 0 else 1 - flags_ref[4]
        leaving.append(
            pltpu.make_async_copy(ext_sc.at[which], out.at[:, D // 4 :, :], out_sems.at[4 + k])
        )
        leaving[-1].start()
    dnormed = dh1 * gain1_ref[...]
    gtok_ref[...] = (
        scale * (dnormed - normed * jnp.mean(dnormed * normed, -1, keepdims=True)) + dx1_ref[...]
    )
    for one in leaving:
        one.wait()


def attention_backward(
    flags, q, k, v, do, do_far, h1, w_all, own, gain1, cos, sin, dx1, gwo, grouter, ggain2
):
    shape = jax.ShapeDtypeStruct
    vmem = pl.BlockSpec(memory_space=pltpu.VMEM)
    anywhere = pl.BlockSpec(memory_space=pl.ANY)
    hbm = pl.BlockSpec(memory_space=pltpu.HBM)
    packed = (4, D // 4 + EXT, 2 * D)
    late = (q, k, v, do, h1, w_all, own, dx1, gwo.reshape(4, D // 4, D))
    return pl.pallas_call(
        attention_back_kernel,
        out_shape=(shape((TOK_DEV, D), F32), shape(packed, BF), shape(packed, BF)),
        in_specs=[pl.BlockSpec(memory_space=pltpu.SMEM)]
        + [anywhere] * 9
        + [vmem] * 6,
        out_specs=(vmem, hbm, hbm),
        scratch_shapes=[
            pltpu.VMEM((6,) + v.shape[1:] if i == 5 else v.shape, v.dtype)
            for i, v in enumerate(late)
        ]
        + [pltpu.VMEM((TOK_DEV, D), F32)] * 3
        + [
            pltpu.VMEM((TOK_DEV, D), BF),
            pltpu.VMEM((3, 4, D // 4, D), BF),
            pltpu.VMEM((2, 4, EXT, 2 * D), BF),
            pltpu.SemaphoreType.DMA((9,)),
            pltpu.SemaphoreType.DMA((6,)),
        ],
        compiler_params=pltpu.CompilerParams(vmem_limit_bytes=VMEM_LIMIT),
        cost_estimate=microseconds(23),
        name="attention_backward",
    )(flags, *late, do_far, gain1, cos, sin, grouter, ggain2)


def after(value, *earlier):
    return lax.optimization_barrier((value, earlier))[0]


def over_y(value):
    return moved(value, lambda z, y, x, c: (z, 1 - y, x, c))


def beside(results, moving):
    return lax.optimization_barrier((results, moving))


def norm_kernel(rows_ref, gain_ref, out_ref):
    rows = rows_ref[...].astype(F32)
    out_ref[...] = (rows * unit_rms(rows) * gain_ref[...]).astype(BF)


def norm_rows(rows, gain):
    return pl.pallas_call(
        norm_kernel,
        out_shape=jax.ShapeDtypeStruct(rows.shape, BF),
        compiler_params=pltpu.CompilerParams(vmem_limit_bytes=VMEM_LIMIT),
        cost_estimate=microseconds(2),
        name="norm_rows",
    )(rows, gain)


def place_kernel(every_ref, gate_ref, up_ref, down_ref):
    for out_ref, at in ((gate_ref, 0), (up_ref, 256)):
        for k in range(4):
            for p in range(0, 8, 2):
                pair = [
                    every_ref[p + i, :, at + 64 * k : at + 64 * (k + 1)].astype(F32)
                    for i in range(2)
                ]
                to = 512 * k + 64 * p
                out_ref[:, to : to + 128] = jnp.concatenate(pair, 1)
    for p in range(8):
        for i in range(3):
            down_ref[64 * p : 64 * (p + 1), 256 * i : 256 * (i + 1)] = every_ref[
                p, 64 * i : 64 * (i + 1), 512:
            ].astype(F32)


def place_shared(every):
    vmem = pl.BlockSpec(memory_space=pltpu.VMEM)
    return pl.pallas_call(
        place_kernel,
        out_shape=(
            jax.ShapeDtypeStruct((D // 4, 2048), F32),
            jax.ShapeDtypeStruct((D // 4, 2048), F32),
            jax.ShapeDtypeStruct((512, D), F32),
        ),
        in_specs=[vmem],
        out_specs=(vmem,) * 3,
        compiler_params=pltpu.CompilerParams(vmem_limit_bytes=VMEM_LIMIT),
        cost_estimate=microseconds(4),
        name="place_shared",
    )(every)


OTHERS = (
    over_x,
    over_y,
    lambda value: moved(value, lambda z, y, x, c: (z, 1 - y, 1 - x, c)),
)


def plane_pieces(value, x, y):
    width = value.shape[-1] // 4
    quarters = [value[..., width * i : width * (i + 1)] for i in range(4)]

    def pick(column, row):
        left = jnp.where(column == 0, quarters[0], quarters[1])
        right = jnp.where(column == 0, quarters[2], quarters[3])
        return jnp.where(row == 0, left, right)

    return [pick(x, y), pick(1 - x, y), pick(x, 1 - y), pick(1 - x, 1 - y)]


def canonical(slots, z):
    order = [slots[0], slots[3], slots[2], slots[1]]
    return lax.dynamic_slice_in_dim(jnp.stack(order + order), lax.rem(4 - z, 4), 4, 0)


def lane_tables():
    row = np.arange(TOK_DEV)
    position = np.where(row < PROMPT, row, PROMPT + (row - PROMPT) % CLEN).astype(np.float32)
    frequency = (10000.0 ** (-2.0 * np.arange(HD // 2) / HD)).astype(np.float32)
    angles = (position[:, None] * frequency[None, :]).astype(np.float64)
    cos, sin = np.cos(angles).astype(np.float32), np.sin(angles).astype(np.float32)
    return jnp.asarray(np.tile(cos, (1, 4))), jnp.asarray(np.tile(np.concatenate([-sin, sin], 1), (1, 2)))


def tuned_body(
    tokens,
    cotangent,
    routes,
    prompt_ids,
    attn_gain,
    query_weight,
    key_weight,
    value_weight,
    output_weight,
    ffn_gain,
    router_weight,
    shared_gate,
    shared_up,
    shared_down,
    expert_gate,
    expert_up_weight,
    expert_down,
):
    z, y, j = lax.axis_index("dp"), lax.axis_index("context"), lax.axis_index("experts")
    x, core = j // 2, j % 2
    plane = y * 4 + j
    shard = D // 4

    dense = jnp.concatenate([query_weight, key_weight, value_weight, output_weight], 1)
    dense = lax.dynamic_slice_in_dim(dense, plane * 384, 384, 1)
    gains = jnp.concatenate(
        [attn_gain[None], ffn_gain[None], jnp.zeros((EXT - 2, shard), BF)], 0
    )
    dense = jnp.concatenate([dense, jnp.concatenate([router_weight.T, gains], 1)], 0)
    dense_z = [over_z(dense, step) for step in (1, 2, 3)]

    units = lambda w: lax.dynamic_index_in_dim(
        w.reshape(shard, 4, 8, 64), plane, 2, keepdims=False
    ).reshape(shard, 256)
    down = lax.dynamic_slice_in_dim(shared_down, plane * 64, 64, 0)
    down = jnp.concatenate([down[:, 256 * i : 256 * (i + 1)] for i in range(3)], 0)
    shared = jnp.concatenate([units(shared_gate), units(shared_up), down], 1)
    far = over_y(tokens)
    ids = jnp.broadcast_to(prompt_ids.astype(BF)[:, None], (CONT, 128))
    far_ids = over_y(ids)
    dense = jnp.stack([dense] + after(dense_z, far, far_ids))
    small = canonical([dense[i, shard:, :] for i in range(4)], z)
    router_t = small[:, :, :shard].transpose(1, 0, 2).reshape(EXPERTS, D)
    gain1 = small[:, 0, shard:].reshape(1, D).astype(F32)
    gain2 = small[:, 1, shard:].reshape(1, D).astype(F32)
    flip_a, flip_b = jnp.where(core == 0, 2, 4), jnp.where(core == 0, 4, 2)
    flips = [0 * core, flip_a, flip_b, 0 * core + 6]
    flips = flips + [1 + flips[0], 1 + flip_b, 1 + flip_a, 1 + flips[3]]
    place = [jnp.bitwise_xor(plane, flip) for flip in flips]
    place += [lax.rem(z + 4 - slot, 4) for slot in range(4)]
    place += [(prompt_ids[m] != y) for m in range(CONT)]
    place = jnp.stack([v.astype(jnp.int32) for v in place])
    cos, sin = lane_tables()
    gain1, place, gain2, router_t, cos, sin = after((gain1, place, gain2, router_t, cos, sin))
    h1 = norm_rows(tokens, gain1)
    h1, dense_parts = beside(h1, (over_a(dense), over_b(dense)))
    dense_parts = [dense, *dense_parts, over_b(dense_parts[0])]
    dense_parts = dense_parts + [over_core(part) for part in dense_parts]

    expert_ids = jnp.arange(EXPERTS, dtype=jnp.int32)[:, None]
    route_t = routes.T
    member = (route_t[0:1] == expert_ids) | (route_t[1:2] == expert_ids)
    before = (jnp.arange(TOK_DEV)[:, None] < jnp.arange(TOK_DEV)[None, :]).astype(BF)
    ranks = jnp.dot(member.astype(BF), before, preferred_element_type=F32)
    ranks = jnp.where(member, ranks, -1.0).astype(BF)
    g_block = cotangent
    g_near = after(g_block, h1)
    g_x = over_x(g_near)
    g_group = [g_block, g_x, over_core(g_near), over_core(g_x)]

    g_column = lax.all_gather(after(g_block, dense), "dp", axis=0, tiled=False)

    shared = lax.all_gather(after(shared, dense), "dp", axis=0, tiled=False)
    shared_far = over_y(after(shared, h1))
    place = after(place, shared)
    flags = jnp.concatenate([prompt_ids == y, far_ids[:, 0].astype(jnp.int32) == y, core[None] != 0]).astype(jnp.int32)
    w_all, q, k, v, o, x1, h_block, probs = attention_forward(
        place, dense_parts, h1, tokens, far, gain1, gain2, router_t, cos, sin, ranks
    )
    (h_block, x1), (g_x, shared_far) = beside((h_block, x1), (g_x, shared_far))
    g_group = [g_block, g_x, over_core(g_block), over_core(g_x)]

    h_x = over_x(h_block)
    h_near, g_near = [h_block, over_core(h_block)], [g_block, g_group[2]]
    h_column = lax.all_gather(h_block, "dp", axis=0, tiled=False)
    experts_w = (expert_gate, expert_up_weight, expert_down)
    base = (j * 4).astype(jnp.int32)
    more = shared_rows(h_near, g_near, shared, shared_far)
    more, (h_x, g_y) = beside(more, (h_x, over_y(after(g_block, h_block))))
    h_far, g_far = [h_x, over_core(h_x)], [g_x, g_group[3]]
    h_group = [h_near[0], h_far[0], h_near[1], h_far[1]]
    g_second = jnp.pad(jnp.where(core == 0, g_y, g_x), ((0, EXT), (0, 0)))
    h_group, g_second = after((h_group, g_second))
    part = group_experts(base[None], 0, 2, h_group, g_group, (), *experts_w)
    (part, h_far), h_b = beside((part, h_far), over_b(after(h_block, h_x)))
    g_first = over_a(after(g_column, h_x))
    more = more + shared_rows(h_far, g_far, shared, shared_far)
    more, g_first = beside(more, g_first)
    g_second = lax.all_gather(g_second, "dp", axis=0, tiled=False)
    results = group_experts(
        base[None] + 2, 2, 2, h_group, g_group, (*more, *part), *experts_w
    )
    g_third = over_b(g_first)
    results, (g_third, g_core) = beside(
        results, (g_third, [over_core(g_column), over_core(g_first)])
    )
    moe, dx = results[:4], results[4:]
    dx_x = pair_sum(dx[1], over_core(dx[3]))
    dx = [dx[0], over_core(dx[2]), over_x(dx_x)]
    h_column = after(h_column, dx_x)
    h_core = [over_core(h_column)]
    window = jnp.array([0, 1, 3, 4], jnp.int32)[z]
    s_pos = jnp.stack([window, z // 2, z * 192 - window * 128, (z % 2) * 64]).astype(jnp.int32)
    e_pos = jnp.stack([base, (z * 2 + y).astype(jnp.int32)])
    s_sums = shared_slice_grads(
        s_pos, [h_column, h_core[0]], [g_column, g_core[0]], shared
    )
    s_sums, dx = beside(s_sums, dx)
    dx1, do, do_c, grad_router_t, grad_gain2 = branch_backward(
        dx, h_block, probs, x1, cotangent, gain2, router_t, w_all
    )
    gwo = inner_rows(o, dx1.astype(BF)).astype(BF)
    gwo, (do_far, g_second) = beside(gwo, (over_y(do_c), g_second))
    h_first = over_a(after(h_column, do_far))
    h_second = lax.all_gather(after(h_b, do_far), "dp", axis=0, tiled=False)
    grad_inputs, keep, send = attention_backward(
        flags,
        q,
        k,
        v,
        do,
        do_far,
        h1,
        w_all,
        tokens,
        gain1,
        cos,
        sin,
        dx1,
        gwo,
        grad_router_t,
        grad_gain2,
    )
    (grad_inputs, keep, send), (h_first, g_far) = beside(
        (grad_inputs, keep, send),
        (h_first, [over_core(after(part, do_far)) for part in (g_second, g_third)]),
    )
    h_core.append(over_core(h_first))
    h_third = over_b(after(h_first, keep))
    h_parts, g_parts = [h_column, h_first] + h_core, [g_column, g_first] + g_core[:2]
    e_pos = after(e_pos, keep)
    e_sums = expert_slice_grads(e_pos, h_parts, g_parts, *experts_w, 256)
    (e_sums, keep), (send, h_second, h_third, g_far) = beside(
        (e_sums, keep),
        (over_core(send), h_second, h_third, g_far),
    )
    h_far = [over_core(h_second), over_core(h_third)]
    h_parts, g_parts = [h_second, h_third] + h_far, [g_second, g_third] + g_far
    pieces = plane_pieces(pair_sum(keep, send), x, y)
    h_parts, pieces = after((h_parts, pieces))
    mine = shared_slice_grads(
        s_pos, [h_first, h_core[1], *h_parts], [g_first, g_core[1], *g_parts], shared, s_sums
    )
    (mine, pieces), there = beside(
        (mine, pieces), [over(piece) for over, piece in zip(OTHERS, pieces[1:])]
    )
    z_own = pieces[0].astype(F32)
    for piece in there:
        z_own = z_own + piece.astype(F32)
    z_own = z_own.astype(BF)
    z_parts = [
        lax.dynamic_index_in_dim(z_own, lax.rem(z + step, 4), 0, keepdims=False)
        for step in (0, 1, 2, 3)
    ]
    moe = after(moe, mine)
    moe_x = pair_sum(moe[1], over_core(moe[3]))
    moe_core = over_core(moe[2])

    mine, z_parts, moe_x, moe_core, h_parts, g_parts = after(
        (mine, z_parts, moe_x, moe_core, h_parts, g_parts)
    )
    every = lax.all_gather(mine, ("context", "experts"), axis=0, tiled=False)
    moving = ([over_z(z_parts[step], step) for step in (1, 2, 3)], over_x(moe_x), every)
    e_gate, e_up, e_down = expert_slice_grads(e_pos, h_parts, g_parts, *experts_w, 256, e_sums)
    (e_gate, e_up, e_down), (there, moe_there, every) = beside((e_gate, e_up, e_down), moving)
    total = z_parts[0].astype(F32)
    for part in there:
        total = total + part.astype(F32)
    total = total.astype(BF)
    total_parts = [over(total) for over in OTHERS]
    layer_out = (
        x1 + (moe[0].astype(F32) + moe_core.astype(F32) + moe_there.astype(F32))
    ).astype(BF)
    s_gate, s_up, s_down = place_shared(every)
    (layer_out, s_gate), total_parts = beside((layer_out, s_gate), total_parts)
    beside_x = rejoin(total, total_parts[0], x)
    total = rejoin(beside_x, rejoin(total_parts[1], total_parts[2], x), y)
    other = over_core(total)
    sum_qk, sum_vo = jnp.where(core == 0, total, other), jnp.where(core == 0, other, total)
    extras = sum_qk[shard:, : 2 * shard].astype(F32)
    sum_qk, sum_vo = sum_qk[:shard].astype(F32), sum_vo[:shard].astype(F32)

    return (
        layer_out,
        grad_inputs,
        extras[0, shard:],
        sum_qk[:, :D],
        sum_qk[:, D:],
        sum_vo[:, :D],
        sum_vo[:, D:],
        extras[1, shard:],
        extras[:, :shard].T,
        s_gate,
        s_up,
        s_down,
        e_gate,
        e_up,
        e_down,
    )


def solution(mesh):
    tuned = dict(mesh.shape) == TUNED_MESH

    return jax.shard_map(
        tuned_body if tuned else plain_body,
        mesh=mesh,
        in_specs=(
            P(("dp", "context", "experts"), None),
            P(("dp", "context", "experts"), None),
            P(("dp", "context", "experts"), None),
            P(("dp", "context", "experts")),
            P("dp"),
            P("dp", None),
            P("dp", None),
            P("dp", None),
            P("dp", None),
            P("dp"),
            P("dp", None),
            P("dp", None),
            P("dp", None),
            P("dp", None),
            P("experts", None, None),
            P("experts", None, None),
            P("experts", None, None),
        ),
        out_specs=(
            P(("dp", "context", "experts"), None),
            P(("dp", "context", "experts"), None),
            P("dp"),
            P("dp", None),
            P("dp", None),
            P("dp", None),
            P("dp", None),
            P("dp"),
            P("dp", None),
            P("dp", None),
            P("dp", None),
            P("dp", None),
            P("experts", None, ("dp", "context")),
            P("experts", None, ("dp", "context")),
            P("experts", ("dp", "context"), None),
        ),
        check_vma=False,
    )
```

```python
import functools

import jax
import jax.numpy as jnp
import numpy as np
from jax import lax
from jax.sharding import PartitionSpec as P

from jax.experimental import pallas as pl
from jax.experimental.pallas import tpu as pltpu

D = 768
HEADS = 12
HD = 64
EXPERTS = 16
TOPK = 2
PROMPT = 256
CONT = 2
CLEN = 64
TOK_DEV = 384
CAP = 66


EPS = 1e-06


def rotary_tables(tok_rows):
    row_ids = jnp.arange(tok_rows)
    position = jnp.where(row_ids < PROMPT, row_ids, PROMPT + (row_ids - PROMPT) % CLEN).astype(
        jnp.float32
    )
    frequency = 10000.0 ** (-2.0 * jnp.arange(HD // 2).astype(jnp.float32) / HD)
    angles = position[:, None] * frequency[None, :]
    return (jnp.cos(angles), jnp.sin(angles))


def rotate(values_in, cos_table, sin_table):
    shaped = values_in.reshape(values_in.shape[:-1] + (HEADS, HD))
    lower_half = shaped[..., : HD // 2]
    upper_half = shaped[..., HD // 2 :]
    cos_part = cos_table[:, None, :]
    sin_part = sin_table[:, None, :]
    turned = jnp.concatenate(
        [
            lower_half * cos_part - upper_half * sin_part,
            upper_half * cos_part + lower_half * sin_part,
        ],
        -1,
    )
    return turned.reshape(values_in.shape)


def key_mask(context_index, prompt_pick, contexts):
    row_ids = jnp.arange(TOK_DEV)[:, None]
    col_ids = jnp.arange(contexts * PROMPT + CONT * CLEN)[None, :]
    prompt_row = row_ids < PROMPT
    cont_row = (row_ids - PROMPT) // CLEN
    within_row = (row_ids - PROMPT) % CLEN
    owner = jnp.sum(
        prompt_pick[None, :] * (jnp.arange(CONT)[None, :] == cont_row), -1, keepdims=True
    )
    target = jnp.where(prompt_row, context_index, owner)
    prompt_keys = col_ids < contexts * PROMPT
    prompt_ok = (
        prompt_keys
        & (col_ids // PROMPT == target)
        & (jnp.logical_not(prompt_row) | (col_ids % PROMPT <= row_ids))
    )
    offset = col_ids - contexts * PROMPT
    cont_ok = (
        jnp.logical_not(prompt_keys)
        & jnp.logical_not(prompt_row)
        & (offset // CLEN == cont_row)
        & (offset % CLEN <= within_row)
    )
    return prompt_ok | cont_ok


def inner_rows(left, right):
    return lax.dot_general(
        left, right, (((0,), (0,)), ((), ())), preferred_element_type=jnp.float32
    )


def times_transposed(left, right):
    return lax.dot_general(
        left, right, (((1,), (1,)), ((), ())), preferred_element_type=jnp.float32
    )


def swish_derivative(pre_act):
    sigma = jax.nn.sigmoid(pre_act)
    return sigma * (1.0 + pre_act * (1.0 - sigma))


def plain_body(
    tokens,
    cotangent,
    routes,
    prompt_ids,
    attn_gain,
    query_weight,
    key_weight,
    value_weight,
    output_weight,
    ffn_gain,
    router_weight,
    shared_gate,
    shared_up,
    shared_down,
    expert_gate,
    expert_up_weight,
    expert_down,
):
    contexts = lax.axis_size("context")
    context_here = lax.axis_index("context")
    gain_one, w_query, w_key, w_value, w_out, gain_two, w_router, w_sgate, w_sup, w_sdown = (
        lax.all_gather(attn_gain, "dp", axis=0, tiled=True),
        lax.all_gather(query_weight, "dp", axis=0, tiled=True),
        lax.all_gather(key_weight, "dp", axis=0, tiled=True),
        lax.all_gather(value_weight, "dp", axis=0, tiled=True),
        lax.all_gather(output_weight, "dp", axis=0, tiled=True),
        lax.all_gather(ffn_gain, "dp", axis=0, tiled=True),
        lax.all_gather(router_weight, "dp", axis=0, tiled=True),
        lax.all_gather(shared_gate, "dp", axis=0, tiled=True),
        lax.all_gather(shared_up, "dp", axis=0, tiled=True),
        lax.all_gather(shared_down, "dp", axis=0, tiled=True),
    )
    cos_table, sin_table = rotary_tables(TOK_DEV)
    inputs = tokens.astype(jnp.float32)
    inv_rms1 = lax.rsqrt(jnp.mean(inputs * inputs, -1, keepdims=True) + EPS)
    normed1 = inputs * inv_rms1
    gain1_f = gain_one.astype(jnp.float32)
    hidden1 = (normed1 * gain1_f).astype(jnp.bfloat16)
    query_f = jnp.dot(hidden1, w_query, preferred_element_type=jnp.float32)
    key_f = jnp.dot(hidden1, w_key, preferred_element_type=jnp.float32)
    value_f = jnp.dot(hidden1, w_value, preferred_element_type=jnp.float32)
    query_b = rotate(query_f, cos_table, sin_table).astype(jnp.bfloat16)
    key_b = rotate(key_f, cos_table, sin_table).astype(jnp.bfloat16)
    value_b = value_f.astype(jnp.bfloat16)
    prompt_keys, prompt_values = (
        lax.all_gather(key_b[:PROMPT], "context", axis=0, tiled=True),
        lax.all_gather(value_b[:PROMPT], "context", axis=0, tiled=True),
    )
    keys_h = jnp.concatenate([prompt_keys, key_b[PROMPT:]], 0).reshape(-1, HEADS, HD)
    values_h = jnp.concatenate([prompt_values, value_b[PROMPT:]], 0).reshape(-1, HEADS, HD)
    query_h = query_b.reshape(TOK_DEV, HEADS, HD)
    allowed = key_mask(context_here, prompt_ids, contexts)
    scores = jnp.where(
        allowed[None],
        0.125 * jnp.einsum("qhd,khd->hqk", query_h, keys_h, preferred_element_type=jnp.float32),
        -1e30,
    )
    row_max = jnp.max(scores, -1, keepdims=True)
    exp_scores = jnp.exp(scores - row_max)
    row_total = jnp.sum(exp_scores, -1, keepdims=True)
    log_total = row_max + jnp.log(row_total)
    attn_probs = (exp_scores / row_total).astype(jnp.bfloat16)
    attended = (
        jnp.einsum("hqk,khd->qhd", attn_probs, values_h, preferred_element_type=jnp.float32)
        .reshape(TOK_DEV, D)
        .astype(jnp.bfloat16)
    )
    resid = inputs + jnp.dot(attended, w_out, preferred_element_type=jnp.float32)
    inv_rms2 = lax.rsqrt(jnp.mean(resid * resid, -1, keepdims=True) + EPS)
    normed2 = resid * inv_rms2
    gain2_f = gain_two.astype(jnp.float32)
    hidden2 = (normed2 * gain2_f).astype(jnp.bfloat16)
    logits = jnp.dot(hidden2, w_router, preferred_element_type=jnp.float32)
    route_probs = jax.nn.softmax(logits, -1)
    route_hot = (routes[:, :, None] == jnp.arange(EXPERTS)[None, None, :]).astype(jnp.float32)
    gate_vals = jnp.sum(route_probs[:, None, :] * route_hot, -1)
    shared_gpre = jnp.dot(hidden2, w_sgate, preferred_element_type=jnp.float32)
    shared_upre = jnp.dot(hidden2, w_sup, preferred_element_type=jnp.float32)
    shared_act = (jax.nn.silu(shared_gpre) * shared_upre).astype(jnp.bfloat16)
    shared_res = jnp.dot(shared_act, w_sdown, preferred_element_type=jnp.float32)
    flat_route = routes.reshape(-1)
    flat_hot = (flat_route[:, None] == jnp.arange(EXPERTS)[None, :]).astype(jnp.int32)
    slot_ids = jnp.sum((jnp.cumsum(flat_hot, 0) - flat_hot) * flat_hot, -1)
    slot_index = flat_route * CAP + slot_ids
    send_rows = jnp.repeat(hidden2, TOPK, axis=0)
    outgoing = (
        jnp.zeros((EXPERTS * CAP, D), jnp.bfloat16)
        .at[slot_index]
        .set(send_rows)
        .reshape(EXPERTS, CAP, D)
    )
    received_rows = lax.all_to_all(outgoing, "experts", split_axis=0, concat_axis=1, tiled=True)
    expert_gate_preact = jnp.einsum(
        "mgx,mxp->mgp", received_rows, expert_gate, preferred_element_type=jnp.float32
    )
    expert_up_preact = jnp.einsum(
        "mgx,mxp->mgp", received_rows, expert_up_weight, preferred_element_type=jnp.float32
    )
    expert_activation = (jax.nn.silu(expert_gate_preact) * expert_up_preact).astype(jnp.bfloat16)
    expert_res = jnp.einsum(
        "erf,efd->erd", expert_activation, expert_down, preferred_element_type=jnp.float32
    ).astype(jnp.bfloat16)
    returned = lax.all_to_all(
        expert_res, "experts", split_axis=1, concat_axis=0, tiled=True
    ).reshape(EXPERTS * CAP, D)
    picked = returned[slot_index].astype(jnp.float32).reshape(TOK_DEV, TOPK, D)
    moe_out = jnp.sum(gate_vals[:, :, None] * picked, 1)
    layer_out = (resid + shared_res + moe_out).astype(jnp.bfloat16)
    gain_one, w_query, w_key, w_value, w_out, gain_two, w_router, w_sgate, w_sup, w_sdown = (
        lax.all_gather(attn_gain, "dp", axis=0, tiled=True),
        lax.all_gather(query_weight, "dp", axis=0, tiled=True),
        lax.all_gather(key_weight, "dp", axis=0, tiled=True),
        lax.all_gather(value_weight, "dp", axis=0, tiled=True),
        lax.all_gather(output_weight, "dp", axis=0, tiled=True),
        lax.all_gather(ffn_gain, "dp", axis=0, tiled=True),
        lax.all_gather(router_weight, "dp", axis=0, tiled=True),
        lax.all_gather(shared_gate, "dp", axis=0, tiled=True),
        lax.all_gather(shared_up, "dp", axis=0, tiled=True),
        lax.all_gather(shared_down, "dp", axis=0, tiled=True),
    )
    gain1_f = gain_one.astype(jnp.float32)
    gain2_f = gain_two.astype(jnp.float32)
    grad_total = cotangent.astype(jnp.float32)
    grad_gates = jnp.sum(grad_total[:, None, :] * picked, -1)
    grad_picked = (
        (gate_vals[:, :, None] * grad_total[:, None, :])
        .astype(jnp.bfloat16)
        .reshape(TOK_DEV * TOPK, D)
    )
    grad_back = (
        jnp.zeros((EXPERTS * CAP, D), jnp.bfloat16)
        .at[slot_index]
        .set(grad_picked)
        .reshape(EXPERTS, CAP, D)
    )
    grad_arrived = lax.all_to_all(grad_back, "experts", split_axis=0, concat_axis=1, tiled=True)
    grad_expert_activation = jnp.einsum(
        "erd,efd->erf", grad_arrived, expert_down, preferred_element_type=jnp.float32
    )
    grad_expert_gate_preact = (
        grad_expert_activation * expert_up_preact * swish_derivative(expert_gate_preact)
    ).astype(jnp.bfloat16)
    grad_expert_up_preact = (grad_expert_activation * jax.nn.silu(expert_gate_preact)).astype(
        jnp.bfloat16
    )
    expert_grad_down = jnp.einsum(
        "erf,erd->edf", expert_activation, grad_arrived, preferred_element_type=jnp.float32
    )
    expert_grad_gate = jnp.einsum(
        "xvb,xva->xba", received_rows, grad_expert_gate_preact, preferred_element_type=jnp.float32
    )
    expert_grad_up = jnp.einsum(
        "xvb,xva->xba", received_rows, grad_expert_up_preact, preferred_element_type=jnp.float32
    )
    grad_einputs = jnp.einsum(
        "cgj,clj->cgl", grad_expert_gate_preact, expert_gate, preferred_element_type=jnp.float32
    )
    grad_einputs = (
        grad_einputs
        + jnp.einsum(
            "cgj,clj->cgl",
            grad_expert_up_preact,
            expert_up_weight,
            preferred_element_type=jnp.float32,
        )
    ).astype(jnp.bfloat16)
    grad_returned = lax.all_to_all(
        grad_einputs, "experts", split_axis=1, concat_axis=0, tiled=True
    ).reshape(EXPERTS * CAP, D)
    grad_moe_in = jnp.sum(
        grad_returned[slot_index].astype(jnp.float32).reshape(TOK_DEV, TOPK, D), 1
    )
    grad_rprobs = jnp.sum(grad_gates[:, :, None] * route_hot, 1)
    grad_logits = (
        route_probs * (grad_rprobs - jnp.sum(route_probs * grad_rprobs, -1, keepdims=True))
    ).astype(jnp.bfloat16)
    grad_router_local = inner_rows(hidden2, grad_logits)
    grad_total_b = grad_total.astype(jnp.bfloat16)
    grad_sdown = inner_rows(shared_act, grad_total_b)
    grad_sact = times_transposed(grad_total_b, w_sdown)
    grad_sgpre = (grad_sact * shared_upre * swish_derivative(shared_gpre)).astype(jnp.bfloat16)
    grad_supre = (grad_sact * jax.nn.silu(shared_gpre)).astype(jnp.bfloat16)
    grad_sgate = inner_rows(hidden2, grad_sgpre)
    grad_sup = inner_rows(hidden2, grad_supre)
    grad_hidden2 = (
        grad_moe_in
        + times_transposed(grad_logits, w_router)
        + times_transposed(grad_sgpre, w_sgate)
        + times_transposed(grad_supre, w_sup)
    )
    grad_gain2 = jnp.sum(grad_hidden2 * normed2, 0)
    grad_normed2 = grad_hidden2 * gain2_f
    grad_resid = (
        inv_rms2 * (grad_normed2 - normed2 * jnp.mean(grad_normed2 * normed2, -1, keepdims=True))
        + grad_total
    )
    grad_branch = grad_resid.astype(jnp.bfloat16)
    grad_wout = inner_rows(attended, grad_branch)
    grad_attended = (
        times_transposed(grad_branch, w_out).astype(jnp.bfloat16).reshape(TOK_DEV, HEADS, HD)
    )
    scores_again = jnp.where(
        allowed[None],
        0.125 * jnp.einsum("qhd,khd->hqk", query_h, keys_h, preferred_element_type=jnp.float32),
        -1e30,
    )
    probs_f = jnp.exp(scores_again - log_total)
    probs_b = probs_f.astype(jnp.bfloat16)
    grad_pattn = jnp.einsum(
        "qhd,khd->hqk", grad_attended, values_h, preferred_element_type=jnp.float32
    )
    grad_scores = (
        probs_f * (grad_pattn - jnp.sum(probs_f * grad_pattn, -1, keepdims=True))
    ).astype(jnp.bfloat16)
    grad_query = 0.125 * jnp.einsum(
        "hqk,khd->qhd", grad_scores, keys_h, preferred_element_type=jnp.float32
    ).reshape(TOK_DEV, D)
    grad_keys = 0.125 * jnp.einsum(
        "hqk,qhd->khd", grad_scores, query_h, preferred_element_type=jnp.float32
    ).reshape(-1, D)
    grad_values = jnp.einsum(
        "hqk,qhd->khd", probs_b, grad_attended, preferred_element_type=jnp.float32
    ).reshape(-1, D)
    prompt_span = contexts * PROMPT
    grad_pkeys, grad_pvalues = (
        lax.psum_scatter(
            grad_keys[:prompt_span].astype(jnp.bfloat16), "context", scatter_dimension=0, tiled=True
        ).astype(jnp.float32),
        lax.psum_scatter(
            grad_values[:prompt_span].astype(jnp.bfloat16),
            "context",
            scatter_dimension=0,
            tiled=True,
        ).astype(jnp.float32),
    )
    grad_key_all = jnp.concatenate([grad_pkeys, grad_keys[prompt_span:]], 0)
    grad_value_all = jnp.concatenate([grad_pvalues, grad_values[prompt_span:]], 0)
    grad_qpre = rotate(grad_query, cos_table, -sin_table).astype(jnp.bfloat16)
    grad_kpre = rotate(grad_key_all, cos_table, -sin_table).astype(jnp.bfloat16)
    grad_vpre = grad_value_all.astype(jnp.bfloat16)
    grad_wquery = inner_rows(hidden1, grad_qpre)
    grad_wkey = inner_rows(hidden1, grad_kpre)
    grad_wvalue = inner_rows(hidden1, grad_vpre)
    grad_hidden1 = (
        times_transposed(grad_qpre, w_query)
        + times_transposed(grad_kpre, w_key)
        + times_transposed(grad_vpre, w_value)
    )
    grad_gain1 = jnp.sum(grad_hidden1 * normed1, 0)
    grad_normed1 = grad_hidden1 * gain1_f
    grad_inputs = (
        inv_rms1 * (grad_normed1 - normed1 * jnp.mean(grad_normed1 * normed1, -1, keepdims=True))
        + grad_resid
    )
    shares = (
        lax.psum_scatter(
            grad_gain1.astype(jnp.bfloat16), "dp", scatter_dimension=0, tiled=True
        ).astype(jnp.float32),
        lax.psum_scatter(
            grad_wquery.astype(jnp.bfloat16), "dp", scatter_dimension=0, tiled=True
        ).astype(jnp.float32),
        lax.psum_scatter(
            grad_wkey.astype(jnp.bfloat16), "dp", scatter_dimension=0, tiled=True
        ).astype(jnp.float32),
        lax.psum_scatter(
            grad_wvalue.astype(jnp.bfloat16), "dp", scatter_dimension=0, tiled=True
        ).astype(jnp.float32),
        lax.psum_scatter(
            grad_wout.astype(jnp.bfloat16), "dp", scatter_dimension=0, tiled=True
        ).astype(jnp.float32),
        lax.psum_scatter(
            grad_gain2.astype(jnp.bfloat16), "dp", scatter_dimension=0, tiled=True
        ).astype(jnp.float32),
        lax.psum_scatter(
            grad_router_local.astype(jnp.bfloat16), "dp", scatter_dimension=0, tiled=True
        ).astype(jnp.float32),
        lax.psum_scatter(
            grad_sgate.astype(jnp.bfloat16), "dp", scatter_dimension=0, tiled=True
        ).astype(jnp.float32),
        lax.psum_scatter(
            grad_sup.astype(jnp.bfloat16), "dp", scatter_dimension=0, tiled=True
        ).astype(jnp.float32),
        lax.psum_scatter(
            grad_sdown.astype(jnp.bfloat16), "dp", scatter_dimension=0, tiled=True
        ).astype(jnp.float32),
    )
    totals = (
        lax.psum(shares[0].astype(jnp.bfloat16), ("context", "experts")).astype(jnp.float32),
        lax.psum(shares[1].astype(jnp.bfloat16), ("context", "experts")).astype(jnp.float32),
        lax.psum(shares[2].astype(jnp.bfloat16), ("context", "experts")).astype(jnp.float32),
        lax.psum(shares[3].astype(jnp.bfloat16), ("context", "experts")).astype(jnp.float32),
        lax.psum(shares[4].astype(jnp.bfloat16), ("context", "experts")).astype(jnp.float32),
        lax.psum(shares[5].astype(jnp.bfloat16), ("context", "experts")).astype(jnp.float32),
        lax.psum(shares[6].astype(jnp.bfloat16), ("context", "experts")).astype(jnp.float32),
        lax.psum(shares[7].astype(jnp.bfloat16), ("context", "experts")).astype(jnp.float32),
        lax.psum(shares[8].astype(jnp.bfloat16), ("context", "experts")).astype(jnp.float32),
        lax.psum(shares[9].astype(jnp.bfloat16), ("context", "experts")).astype(jnp.float32),
    )
    summed_gate, summed_up, summed_down = (
        lax.psum_scatter(
            expert_grad_gate.astype(jnp.bfloat16),
            ("dp", "context"),
            scatter_dimension=2,
            tiled=True,
        ).astype(jnp.float32),
        lax.psum_scatter(
            expert_grad_up.astype(jnp.bfloat16), ("dp", "context"), scatter_dimension=2, tiled=True
        ).astype(jnp.float32),
        lax.psum_scatter(
            expert_grad_down.astype(jnp.bfloat16),
            ("dp", "context"),
            scatter_dimension=2,
            tiled=True,
        ).astype(jnp.float32),
    )
    summed_down = jnp.transpose(summed_down, (0, 2, 1))
    return (
        layer_out,
        grad_inputs,
        totals[0],
        totals[1],
        totals[2],
        totals[3],
        totals[4],
        totals[5],
        totals[6],
        totals[7],
        totals[8],
        totals[9],
        summed_gate,
        summed_up,
        summed_down,
    )


TUNED_MESH = {"dp": 4, "context": 2, "experts": 4}
AXES = ("dp", "context", "experts")
SLOT = 72
EXT = 16
ROWS = TOK_DEV + EXT
BF = jnp.bfloat16
F32 = jnp.float32
VMEM_LIMIT = 60 * 1024 * 1024


def microseconds(time):
    return pl.CostEstimate(flops=0, bytes_accessed=int(time * 0.4e6), transcendentals=0)


def moved(value, target):
    pairs = []
    for z in range(4):
        for y in range(2):
            for x in range(2):
                for c in range(2):
                    tz, ty, tx, tc = target(z, y, x, c)
                    pairs.append((((z * 2 + y) * 2 + x) * 2 + c, ((tz * 2 + ty) * 2 + tx) * 2 + tc))
    return lax.ppermute(value, AXES, pairs)


def over_core(value):
    return moved(value, lambda z, y, x, c: (z, y, x, 1 - c))


def over_x(value):
    return moved(value, lambda z, y, x, c: (z, y, 1 - x, c))


def over_a(value):
    return moved(value, lambda z, y, x, c: (z, y, 1 - x, c) if c == 0 else (z, 1 - y, x, c))


def over_b(value):
    return moved(value, lambda z, y, x, c: (z, 1 - y, x, c) if c == 0 else (z, y, 1 - x, c))


def over_z(value, step):
    return moved(value, lambda z, y, x, c: ((z + step) % 4, y, x, c))


def contract(left, right, left_dim, right_dim):
    return lax.dot_general(
        left, right, (((left_dim,), (right_dim,)), ((), ())), preferred_element_type=F32
    )


def one_hot_rows(rank_row):
    slots = lax.broadcasted_iota(jnp.int32, (SLOT, TOK_DEV), 0).astype(F32)
    return (slots == rank_row).astype(F32)


def swish_parts(pre_act):
    sigma = jax.nn.sigmoid(pre_act)
    return pre_act * sigma, sigma * (1.0 + pre_act * (1.0 - sigma))


def group_kernel(
    blocks,
    more,
    base_ref,
    *refs,
):
    block_refs, refs = refs[: 2 * blocks], refs[2 * blocks :]
    more_refs, refs = refs[:more], refs[more:]
    wg_ref, wu_ref, wd_ref = refs[:3]
    results, refs = refs[3 : 3 + 2 * blocks], refs[3 + 2 * blocks :]
    (
        rank_sc,
        prob_sc,
        x_sc,
        gate_sc,
        y_sc,
        acc_sc,
        dgate_sc,
        sel_sc,
        drp_sc,
        in_sc,
        out_sc,
        in_sems,
        out_sems,
    ) = refs[:13]
    e = pl.program_id(0)
    f = pl.program_id(1)
    experts = pl.num_programs(0)
    base = base_ref[0]
    copies = [
        pltpu.make_async_copy(source, into, refs[-1].at[i])
        for i, (source, into) in enumerate(zip(more_refs, refs[13:]))
    ]

    arrivals = [
        pltpu.make_async_copy(
            block_refs[side * blocks + b],
            in_sc.at[b, : (ROWS, TOK_DEV)[side], side * D : (side + 1) * D],
            in_sems.at[side, b],
        )
        for b in range(blocks)
        for side in range(2)
    ]

    @pl.when((e == 0) & (f == 0))
    def _():
        for one in arrivals + copies:
            one.start()
        drp_sc[...] = jnp.zeros_like(drp_sc)
        count = x_sc.shape[0]
        rows = []
        for b in range(blocks):
            for one in arrivals[2 * b : 2 * b + 2]:
                one.wait()
            rank_sc[b] = in_sc[b, TOK_DEV:, TOK_DEV:D].astype(F32)
            prob_sc[b] = in_sc[b, TOK_DEV:, :TOK_DEV].astype(F32)
            hots = []
            for i in range(count):
                hot = one_hot_rows(rank_sc[b, pl.ds(base + i, 1), :])
                gate_sc[i, b * SLOT : (b + 1) * SLOT, :] = jnp.sum(
                    hot * prob_sc[b, pl.ds(base + i, 1), :], -1, keepdims=True
                )
                hots.append(hot)
            hot = jnp.concatenate(hots, 0).astype(BF)
            rows.append(jnp.dot(hot, in_sc[b, :TOK_DEV, :], preferred_element_type=F32))
            if b % 2:
                span = slice((b - 1) * SLOT, (b + 1) * SLOT)
                for i in range(count):
                    of = slice(i * SLOT, (i + 1) * SLOT)
                    x_sc[i, span, :] = jnp.concatenate([v[of] for v in rows[-2:]], 0).astype(BF)

    @pl.when(f == 0)
    def _():
        y_sc[...] = jnp.zeros_like(y_sc)
        acc_sc[...] = jnp.zeros_like(acc_sc)
        dgate_sc[...] = jnp.zeros_like(dgate_sc)

    rows = x_sc[e, :, :D]
    gate_pre = jnp.dot(rows, wg_ref[0], preferred_element_type=F32)
    up_pre = jnp.dot(rows, wu_ref[0], preferred_element_type=F32)
    back = contract(x_sc[e, :, D:], wd_ref[0], 1, 1)
    swish, slope = swish_parts(gate_pre)
    inner = (swish * up_pre).astype(BF)
    dgate_sc[...] += jnp.sum(back * inner.astype(F32), -1, keepdims=True)
    back = back * gate_sc[e]
    dgate_pre = (back * up_pre * slope).astype(BF)
    dup_pre = (back * swish).astype(BF)
    y_sc[...] += jnp.dot(inner, wd_ref[0], preferred_element_type=F32)
    acc_sc[...] += contract(dgate_pre, wg_ref[0], 1, 1) + contract(dup_pre, wu_ref[0], 1, 1)

    @pl.when(f == pl.num_programs(1) - 1)
    def _():
        for b in range(blocks):
            span = slice(b * SLOT, (b + 1) * SLOT)
            into = pl.ds(pl.multiple_of(e * SLOT, 8), SLOT)
            sel_sc[b, into, :D] = y_sc[span, :] * gate_sc[e, span, :]
            sel_sc[b, into, D:] = acc_sc[span, :]
            hot = one_hot_rows(rank_sc[b, pl.ds(base + e, 1), :])
            drp_sc[b, pl.ds(base + e, 1), :] = jnp.sum(hot * dgate_sc[span, :], 0, keepdims=True)

    @pl.when((f == pl.num_programs(1) - 1) & (e == experts - 1))
    def _():
        for one in copies:
            one.wait()
        leaving = []
        for b in range(blocks):
            side, at = divmod(b, blocks // 2)
            moe_out, dx_out = out_sc.at[0, b], out_sc.at[1, b]
            hot = jnp.concatenate(
                [
                    one_hot_rows(rank_sc[b, pl.ds(base + i, 1), :])
                    for i in range(x_sc.shape[0])
                ],
                0,
            ).astype(BF)
            both = contract(hot, sel_sc[b].astype(BF), 0, 0)
            moe, dx = both[:, :D], both[:, D:]
            drp = drp_sc[b]
            if more:
                shared = refs[13 + 2 * at : 15 + 2 * at]
                moe_before, dx_before = refs[17 + b], refs[17 + blocks + b]
                moe = moe + shared[0][side].astype(F32) + moe_before[...].astype(F32)
                dx = dx + shared[1][side].astype(F32) + dx_before[:TOK_DEV, :].astype(F32)
                drp = drp + dx_before[TOK_DEV:, :TOK_DEV].astype(F32)
                drp = drp + dx_before[TOK_DEV:, TOK_DEV:].astype(F32)
            moe_out[:TOK_DEV, :] = moe.astype(BF)
            dx_out[:TOK_DEV, :] = dx.astype(BF)
            high = drp.astype(BF)
            dx_out[TOK_DEV:, :TOK_DEV] = high
            dx_out[TOK_DEV:, TOK_DEV:] = (drp - high.astype(F32)).astype(BF)
            sent = (
                pltpu.make_async_copy(moe_out.at[:TOK_DEV], results[b], out_sems.at[0, b]),
                pltpu.make_async_copy(dx_out, results[blocks + b], out_sems.at[1, b]),
            )
            for one in sent:
                one.start()
            leaving += sent
        for one in leaving:
            one.wait()


def group_experts(base, first, experts, h_group, g_group, more, w_gate, w_up, w_down):
    blocks = len(h_group)
    ff = w_gate.shape[2]
    tile = 512
    results = [(TOK_DEV, D)] * blocks + [(ROWS, D)] * blocks
    return pl.pallas_call(
        functools.partial(group_kernel, blocks, len(more)),
        out_shape=tuple(jax.ShapeDtypeStruct(s, BF) for s in results),
        grid_spec=pltpu.PrefetchScalarGridSpec(
            num_scalar_prefetch=1,
            grid=(experts, ff // tile),
            in_specs=[pl.BlockSpec(memory_space=pl.ANY)] * (2 * blocks + len(more))
            + [
                pl.BlockSpec((1, D, tile), lambda e, f, s: (first + e, 0, f)),
                pl.BlockSpec((1, D, tile), lambda e, f, s: (first + e, 0, f)),
                pl.BlockSpec((1, tile, D), lambda e, f, s: (first + e, f, 0)),
            ],
            out_specs=[pl.BlockSpec(memory_space=pltpu.HBM)] * len(results),
            scratch_shapes=[
                pltpu.VMEM((blocks, EXPERTS, TOK_DEV), F32),
                pltpu.VMEM((blocks, EXPERTS, TOK_DEV), F32),
                pltpu.VMEM((experts, blocks * SLOT, 2 * D), BF),
                pltpu.VMEM((experts, blocks * SLOT, 1), F32),
                pltpu.VMEM((blocks * SLOT, D), F32),
                pltpu.VMEM((blocks * SLOT, D), F32),
                pltpu.VMEM((blocks * SLOT, 1), F32),
                pltpu.VMEM((blocks, experts * SLOT, 2 * D), F32),
                pltpu.VMEM((blocks, EXPERTS, TOK_DEV), F32),
                pltpu.VMEM((blocks, ROWS, 2 * D), BF),
                pltpu.VMEM((2, blocks, ROWS, D), BF),
                pltpu.SemaphoreType.DMA((2, blocks)),
                pltpu.SemaphoreType.DMA((2, blocks)),
            ]
            + [pltpu.VMEM(v.shape, v.dtype) for v in more]
            + [pltpu.SemaphoreType.DMA((max(1, len(more)),))],
        ),
        compiler_params=pltpu.CompilerParams(vmem_limit_bytes=VMEM_LIMIT),
        cost_estimate=microseconds(21),
        name="group_experts",
    )(base, *h_group, *g_group, *more, w_gate, w_up, w_down)


def shared_kernel(h_a_ref, h_b_ref, g_a_ref, g_b_ref, w_a_ref, w_b_ref, out_ref, dh_ref, h_sc, g_sc, out_sc, dh_sc):
    for k, (h_ref, g_ref) in enumerate(((h_a_ref, g_a_ref), (h_b_ref, g_b_ref))):
        h_sc[k * TOK_DEV : (k + 1) * TOK_DEV, :] = h_ref[:TOK_DEV, :]
        g_sc[k * TOK_DEV : (k + 1) * TOK_DEV, :] = g_ref[:TOK_DEV, :]
    for k, w_ref in enumerate((w_a_ref, w_b_ref)):
        w_gate, w_up = w_ref[:, :, :256].reshape(D, 256), w_ref[:, :, 256:512].reshape(D, 256)
        w_down = jnp.concatenate(
            [w_ref[:, 64 * i : 64 * (i + 1), 512:].reshape(256, 256) for i in range(3)], 1
        )
        gate_pre = jnp.dot(h_sc[...], w_gate, preferred_element_type=F32)
        up_pre = jnp.dot(h_sc[...], w_up, preferred_element_type=F32)
        back = contract(g_sc[...], w_down, 1, 1)
        swish, slope = swish_parts(gate_pre)
        inner = (swish * up_pre).astype(BF)
        out = jnp.dot(inner, w_down, preferred_element_type=F32)
        dgate_pre = (back * up_pre * slope).astype(BF)
        dup_pre = (back * swish).astype(BF)
        dh = contract(dgate_pre, w_gate, 1, 1) + contract(dup_pre, w_up, 1, 1)
        if k == 0:
            out_sc[...], dh_sc[...] = out, dh
    for b in range(2):
        rows = slice(b * TOK_DEV, (b + 1) * TOK_DEV)
        out_ref[b] = (out_sc[rows, :] + out[rows]).astype(BF)
        dh_ref[b] = (dh_sc[rows, :] + dh[rows]).astype(BF)


def shared_rows(h_pair, g_pair, w_own, w_far):
    rows = jax.ShapeDtypeStruct((2, TOK_DEV, D), BF)
    vmem = pl.BlockSpec(memory_space=pltpu.VMEM)
    return pl.pallas_call(
        shared_kernel,
        out_shape=(rows, rows),
        in_specs=[vmem] * 6,
        out_specs=(vmem, vmem),
        scratch_shapes=[
            pltpu.VMEM((2 * TOK_DEV, D), BF),
            pltpu.VMEM((2 * TOK_DEV, D), BF),
            pltpu.VMEM((2 * TOK_DEV, D), F32),
            pltpu.VMEM((2 * TOK_DEV, D), F32),
        ],
        compiler_params=pltpu.CompilerParams(vmem_limit_bytes=VMEM_LIMIT),
        cost_estimate=microseconds(8),
        name="shared_rows",
    )(*h_pair, *g_pair, w_own, w_far)


def start_parts(h_parts, g_parts, h_buf, g_buf, sems):
    per = h_parts[0].shape[0]
    copies = []
    for i in range(len(h_parts)):
        for k in range(per // 2):
            at, into = pl.ds(2 * k, 2), pl.ds(i * per + 2 * k, 2)
            number = i * (per // 2) + k
            copies.append(
                (
                    pltpu.make_async_copy(h_parts[i].at[at], h_buf.at[into], sems.at[0, number]),
                    pltpu.make_async_copy(
                        g_parts[i].at[at, :TOK_DEV], g_buf.at[into, :TOK_DEV], sems.at[1, number]
                    ),
                )
            )
    for pair in copies:
        for one in pair:
            one.start()
    return copies


def each_pair(copies, work):
    done = 0
    for upto in [1, 2] + list(range(4, len(copies) + 1, 2)):
        for pair in copies[done:upto]:
            for one in pair:
                one.wait()
        lax.fori_loop(done, upto, work, 0, unroll=True)
        done = upto


def expert_slice_kernel(parts, more, pos_ref, *refs):
    h_parts, g_parts = refs[:parts], refs[parts : 2 * parts]
    weights = refs[2 * parts : 2 * parts + 3]
    refs = refs[2 * parts + 3 :]
    sums, refs = refs[: 3 * more], refs[3 * more :]
    outs, (buf, x_sc, gd_sc, rank_sc, prob_sc) = refs[:3], refs[3:8]
    wg_ref, wu_ref, wd_ref, og_ref, ou_ref, od_ref, sems, w_sems, out_sems = refs[8:]
    base = pos_ref[0]
    experts, _, width = wg_ref.shape
    per = h_parts[0].shape[0]
    copies = start_parts(h_parts, g_parts, buf.at[:, :, :D], buf.at[:, :, D:], sems)
    cols = pl.ds(pl.multiple_of(pos_ref[1] * width, width), width)
    loads = [
        pltpu.make_async_copy(weights[0].at[:, :, cols], wg_ref, w_sems.at[0]),
        pltpu.make_async_copy(weights[1].at[:, :, cols], wu_ref, w_sems.at[1]),
        pltpu.make_async_copy(weights[2].at[:, cols, :], wd_ref, w_sems.at[2]),
    ]
    for i in range(3 * more):
        loads.append(
            pltpu.make_async_copy(sums[i], (og_ref, ou_ref, od_ref)[i], w_sems.at[3 + i])
        )
    for one in loads:
        one.start()

    def dispatch(pair, carry):
        both = []
        for k in range(2):
            b = 2 * pair + k
            rank_sc[k] = buf[b, TOK_DEV:, TOK_DEV:D].astype(F32)
            prob_sc[k] = buf[b, TOK_DEV:, :TOK_DEV].astype(F32)
            hots, gates = [], []
            for i in range(experts):
                hot = one_hot_rows(rank_sc[k, pl.ds(base + i, 1), :])
                gates.append(
                    jnp.sum(hot * prob_sc[k, pl.ds(base + i, 1), :], -1, keepdims=True)
                )
                hots.append(hot)
            hot = jnp.concatenate(hots, 0).astype(BF)
            rows = jnp.dot(hot, buf[b, :TOK_DEV, :], preferred_element_type=F32)
            both.append((rows[:, :D], rows[:, D:] * jnp.concatenate(gates, 0)))
        into = pl.ds(pl.multiple_of(pair * 2 * SLOT, 2 * SLOT), 2 * SLOT)
        for i in range(experts):
            span = slice(i * SLOT, (i + 1) * SLOT)
            x_sc[i, into, :] = jnp.concatenate([v[0][span] for v in both], 0).astype(BF)
            gd_sc[i, into, :] = jnp.concatenate([v[1][span] for v in both], 0).astype(BF)
        return carry

    each_pair(copies, dispatch)
    for one in loads:
        one.wait()

    def products(i, carry):
        rows = x_sc[i]
        gate_pre = jnp.dot(rows, wg_ref[i], preferred_element_type=F32)
        up_pre = jnp.dot(rows, wu_ref[i], preferred_element_type=F32)
        back = contract(gd_sc[i], wd_ref[i], 1, 1)
        swish, slope = swish_parts(gate_pre)
        inner = (swish * up_pre).astype(BF)
        dgate_pre = (back * up_pre * slope).astype(BF)
        dup_pre = (back * swish).astype(BF)
        add_g = contract(rows, dgate_pre, 0, 0)
        add_u = contract(rows, dup_pre, 0, 0)
        add_d = contract(inner, gd_sc[i], 0, 0)
        if more:
            og_ref[i] += add_g
            ou_ref[i] += add_u
            od_ref[i] += add_d
        else:
            og_ref[i], ou_ref[i], od_ref[i] = add_g, add_u, add_d
        for k, source in enumerate((og_ref, ou_ref, od_ref)):
            pltpu.make_async_copy(source.at[i], outs[k].at[i], out_sems.at[k, i]).start()
        return carry

    lax.fori_loop(0, experts, products, 0, unroll=2 if experts % 2 == 0 else 1)
    for i in range(experts):
        for k, source in enumerate((og_ref, ou_ref, od_ref)):
            pltpu.make_async_copy(source.at[i], outs[k].at[i], out_sems.at[k, i]).wait()


def expert_slice_grads(pos, h_parts, g_parts, w_gate, w_up, w_down, width, sums=()):
    parts, per = len(h_parts), h_parts[0].shape[0]
    experts = w_gate.shape[0]
    blocks = parts * per
    shapes = ((experts, D, width), (experts, D, width), (experts, width, D))
    anywhere = pl.BlockSpec(memory_space=pl.ANY)
    return pl.pallas_call(
        functools.partial(expert_slice_kernel, parts, len(sums) // 3),
        out_shape=tuple(jax.ShapeDtypeStruct(s, F32) for s in shapes),
        in_specs=[pl.BlockSpec(memory_space=pltpu.SMEM)]
        + [anywhere] * (2 * parts + 3 + len(sums)),
        out_specs=(pl.BlockSpec(memory_space=pltpu.HBM),) * 3,
        scratch_shapes=[
            pltpu.VMEM((blocks, ROWS, 2 * D), BF),
            pltpu.VMEM((experts, blocks * SLOT, D), BF),
            pltpu.VMEM((experts, blocks * SLOT, D), BF),
            pltpu.VMEM((2, EXPERTS, TOK_DEV), F32),
            pltpu.VMEM((2, EXPERTS, TOK_DEV), F32),
        ]
        + [pltpu.VMEM(s, BF) for s in shapes]
        + [pltpu.VMEM(s, F32) for s in shapes]
        + [
            pltpu.SemaphoreType.DMA((2, blocks // 2)),
            pltpu.SemaphoreType.DMA((6,)),
            pltpu.SemaphoreType.DMA((3, experts)),
        ],
        compiler_params=pltpu.CompilerParams(vmem_limit_bytes=VMEM_LIMIT),
        cost_estimate=microseconds(31),
        name="expert_slice_grads",
    )(pos, *h_parts, *g_parts, w_gate, w_up, w_down, *sums)


def shared_slice_kernel(parts, more, pos_ref, *refs):
    h_parts, g_parts = refs[:parts], refs[parts : 2 * parts]
    w_ref = refs[2 * parts]
    refs = refs[2 * parts + 1 :]
    sums, refs = refs[: 3 * more], refs[3 * more :]
    if more:
        mine_ref, refs = refs[0], refs[1:]
    og_ref, ou_ref, od_ref, h_buf, g_buf, inner_sc, wg_ref, wu_ref, wd_ref, sems = refs
    per = h_parts[0].shape[0]
    copies = start_parts(h_parts, g_parts, h_buf, g_buf, sems)
    wg_ref[...] = w_ref[:, :, :256].reshape(D, 256)
    wu_ref[...] = w_ref[:, :, 256:512].reshape(D, 256)
    for i in range(3):
        wd_ref[:, 256 * i : 256 * (i + 1)] = w_ref[:, 64 * i : 64 * (i + 1), 512:].reshape(256, 256)
    window = pl.ds(pl.multiple_of(pos_ref[0] * 128, 128), og_ref.shape[0])
    lanes = pl.ds(pl.multiple_of(pos_ref[1] * 128, 128), od_ref.shape[0])
    for i, out_ref in enumerate((og_ref, ou_ref, od_ref)):
        out_ref[...] = sums[i][...] if more else jnp.zeros_like(out_ref)

    def two(buf, pair, cols=slice(None)):
        return jnp.concatenate([buf[2 * pair + k, :TOK_DEV, cols] for k in range(2)], 0)

    def products(pair, carry):
        rows, grads = two(h_buf, pair), two(g_buf, pair)
        gate_pre = jnp.dot(rows, wg_ref[...], preferred_element_type=F32)
        up_pre = jnp.dot(rows, wu_ref[...], preferred_element_type=F32)
        back = contract(grads, wd_ref[...], 1, 1)
        swish, slope = swish_parts(gate_pre)
        inner_sc[...] = (swish * up_pre).astype(BF)
        dgate_pre = (back * up_pre * slope).astype(BF)
        dup_pre = (back * swish).astype(BF)
        picked = two(h_buf, pair, window)
        og_ref[...] += contract(picked, dgate_pre, 0, 0)
        ou_ref[...] += contract(picked, dup_pre, 0, 0)
        od_ref[...] += contract(inner_sc[:, lanes], grads, 0, 0)
        return carry

    each_pair(copies, products)
    if more:
        rows = pl.ds(pl.multiple_of(pos_ref[2], 64), D // 4)
        mine_ref[:, :256] = og_ref[rows, :].astype(BF)
        mine_ref[:, 256:512] = ou_ref[rows, :].astype(BF)
        down = od_ref[pl.ds(pl.multiple_of(pos_ref[3], 64), 64), :].astype(BF)
        for i in range(3):
            mine_ref[64 * i : 64 * (i + 1), 512:] = down[:, 256 * i : 256 * (i + 1)]


def shared_slice_grads(pos, h_parts, g_parts, weights, sums=()):
    parts, per = len(h_parts), h_parts[0].shape[0]
    blocks = parts * per
    width = 256
    shapes = ((256, width), (256, width), (128, D))
    vmem = pl.BlockSpec(memory_space=pltpu.VMEM)
    anywhere = pl.BlockSpec(memory_space=pl.ANY)
    return pl.pallas_call(
        functools.partial(shared_slice_kernel, parts, len(sums) // 3),
        out_shape=jax.ShapeDtypeStruct((D // 4, D), BF)
        if sums
        else tuple(jax.ShapeDtypeStruct(s, F32) for s in shapes),
        in_specs=[pl.BlockSpec(memory_space=pltpu.SMEM)]
        + [anywhere] * (2 * parts)
        + [vmem] * (1 + len(sums)),
        out_specs=vmem if sums else (vmem,) * 3,
        scratch_shapes=[pltpu.VMEM(s, F32) for s in (shapes if sums else ())]
        + [
            pltpu.VMEM((blocks, ROWS, D), BF),
            pltpu.VMEM((blocks, ROWS, D), BF),
            pltpu.VMEM((2 * TOK_DEV, width), BF),
            pltpu.VMEM((D, width), BF),
            pltpu.VMEM((D, width), BF),
            pltpu.VMEM((width, D), BF),
            pltpu.SemaphoreType.DMA((2, blocks // 2)),
        ],
        compiler_params=pltpu.CompilerParams(vmem_limit_bytes=VMEM_LIMIT),
        cost_estimate=microseconds(20),
        name="shared_slice_grads",
    )(pos, *h_parts, *g_parts, weights, *sums)


def pair_sum(kept, received):
    return (kept.astype(F32) + received.astype(F32)).astype(BF)


def halves(value, bit):
    width = value.shape[-1] // 2
    low, high = value[..., :width], value[..., width:]
    return jnp.where(bit == 0, low, high), jnp.where(bit == 0, high, low)


def rejoin(own, other, bit):
    return jnp.where(
        bit == 0, jnp.concatenate([own, other], -1), jnp.concatenate([other, own], -1)
    )


def lane_halves():
    lane = lax.broadcasted_iota(jnp.int32, (1, 128), 1)
    return [(lane < 64).astype(F32).astype(BF), (lane >= 64).astype(F32).astype(BF)]


def pick_lanes(first, second):
    lane = lax.broadcasted_iota(jnp.int32, first.shape, 1)
    return jnp.where(lane < 64, first, second)


def turned(value, cos, sin):
    lane = lax.broadcasted_iota(jnp.int32, value.shape, 1)
    partner = jnp.where(lane % 64 < 32, pltpu.roll(value, 96, 1), pltpu.roll(value, 32, 1))
    return value * cos + partner * sin


def causal_mask(rows, heads):
    row = lax.broadcasted_iota(jnp.int32, (heads * rows, rows), 0) % rows
    col = lax.broadcasted_iota(jnp.int32, (heads * rows, rows), 1)
    return row, col


def stacked(value, masks):
    return jnp.concatenate([value * mask for mask in masks], 0)


def unit_rms(value):
    return lax.rsqrt(jnp.mean(value * value, -1, keepdims=True) + EPS)


def softmax_of(first, second=None):
    top = jnp.max(first, -1, keepdims=True)
    if second is not None:
        top = jnp.maximum(top, jnp.max(second, -1, keepdims=True))
    first = jnp.exp(first - top)
    total = jnp.sum(first, -1, keepdims=True)
    if second is None:
        return first * (1.0 / total)
    second = jnp.exp(second - top)
    scale = 1.0 / (total + jnp.sum(second, -1, keepdims=True))
    return first * scale, second * scale


def attention_kernel(place_ref, *refs):
    w_parts = refs[:8]
    (
        h1_ref,
        own_ref,
        far_ref,
        gain1_ref,
        gain2_ref,
        router_ref,
        cos_ref,
        sin_ref,
        rank_ref,
        *outs,
        h2_ref,
        probs_ref,
        w_ref,
        q_ref,
        k_ref,
        v_ref,
        o_ref,
        x1_ref,
        h_sc,
        sems,
        out_sems,
    ) = refs[8:]
    kept = (w_ref, q_ref, k_ref, v_ref, o_ref, x1_ref)
    leaving = [
        pltpu.make_async_copy(kept[i], outs[i], out_sems.at[i]) for i in range(len(kept))
    ]
    copies = []
    for part in range(8):
        for slot in range(4):
            rows = pl.ds(pl.multiple_of(place_ref[8 + slot] * 192, 192), 192)
            copies.append(
                pltpu.make_async_copy(
                    w_parts[part].at[slot, :192, :],
                    w_ref.at[place_ref[part], rows, :],
                    sems.at[part, slot],
                )
            )
    for one in copies:
        one.start()
    h_sc[:TOK_DEV, :] = h1_ref[...]
    far = far_ref[:TOK_DEV, :].astype(F32)
    h_sc[TOK_DEV:, :] = (far * unit_rms(far) * gain1_ref[...]).astype(BF)
    for one in copies:
        one.wait()
    leaving[0].start()
    for i in range(6):
        out_ref = (q_ref, k_ref, v_ref)[i // 2]
        product = jnp.dot(h_sc[...], w_ref[i], preferred_element_type=F32)
        for slab in range(3):
            at = (i % 2) * 384 + slab * 128
            for half in range(2):
                rows = slice(half * TOK_DEV, (half + 1) * TOK_DEV)
                value = product[rows, slab * 128 : (slab + 1) * 128]
                if i < 4:
                    value = turned(value, cos_ref[...], sin_ref[...])
                out_ref[rows, at : at + 128] = value.astype(BF)
        if i % 2:
            leaving[1 + i // 2].start()
    masks = lane_halves()
    row, col = causal_mask(PROMPT, 2)
    prompt_ok = col <= row
    row, col = causal_mask(CONT * CLEN, 2)
    cont_ok = (row // CLEN == col // CLEN) & (col <= row)
    row = lax.broadcasted_iota(jnp.int32, (2 * CONT * CLEN, 1), 0) % (CONT * CLEN)
    reads_far = jnp.where(row < CLEN, place_ref[12], place_ref[13]).astype(F32)
    own_c = slice(PROMPT, TOK_DEV)
    far_p = slice(TOK_DEV, TOK_DEV + PROMPT)

    def heads(pair, carry):
        cols = pl.ds(pl.multiple_of(pair * 128, 128), 128)
        q_p, k_p, v_p = q_ref[:PROMPT, cols], k_ref[:PROMPT, cols], v_ref[:PROMPT, cols]
        q_c, k_c, v_c = q_ref[own_c, cols], k_ref[own_c, cols], v_ref[own_c, cols]
        k_f, v_f = k_ref[far_p, cols], v_ref[far_p, cols]
        score = 0.125 * contract(stacked(q_p, masks), k_p, 1, 1)
        prob = softmax_of(jnp.where(prompt_ok, score, -1e30)).astype(BF)
        out = jnp.dot(prob, v_p, preferred_element_type=F32)
        o_ref[:PROMPT, cols] = pick_lanes(out[:PROMPT], out[PROMPT:]).astype(BF)
        query = stacked(q_c, masks)
        near, far = contract(query, k_p, 1, 1), contract(query, k_f, 1, 1)
        first = 0.125 * jnp.where(reads_far > 0.5, far, near)
        second = jnp.where(cont_ok, 0.125 * contract(query, k_c, 1, 1), -1e30)
        first, second = softmax_of(first, second)
        out = (
            jnp.dot((first * (1.0 - reads_far)).astype(BF), v_p, preferred_element_type=F32)
            + jnp.dot((first * reads_far).astype(BF), v_f, preferred_element_type=F32)
            + jnp.dot(second.astype(BF), v_c, preferred_element_type=F32)
        )
        o_ref[own_c, cols] = pick_lanes(out[: CONT * CLEN], out[CONT * CLEN :]).astype(BF)
        return carry

    lax.fori_loop(0, HEADS // 2, heads, 0, unroll=3)
    leaving[4].start()
    for i in range(2):
        cols = slice(384 * i, 384 * (i + 1))
        x1_ref[:, cols] = own_ref[:TOK_DEV, cols].astype(F32) + jnp.dot(
            o_ref[...], w_ref[6 + i], preferred_element_type=F32
        )
    leaving[5].start()
    resid = x1_ref[...]
    hidden = (resid * unit_rms(resid) * gain2_ref[...]).astype(BF)
    h2_ref[:TOK_DEV, :] = hidden
    logits = contract(router_ref[...], hidden, 1, 1)
    logits = jnp.exp(logits - jnp.max(logits, 0, keepdims=True))
    probs = logits / jnp.sum(logits, 0, keepdims=True)
    probs_ref[...] = probs
    h2_ref[TOK_DEV:, :TOK_DEV] = probs.astype(BF)
    h2_ref[TOK_DEV:, TOK_DEV:] = rank_ref[...]
    for one in leaving:
        one.wait()


def attention_forward(place, w_parts, h1, own, far, gain1, gain2, router_t, cos, sin, ranks):
    vmem = pl.BlockSpec(memory_space=pltpu.VMEM)
    hbm = pl.BlockSpec(memory_space=pltpu.HBM)
    kept = (
        ((8, D, 384), BF),
        ((2 * TOK_DEV, D), BF),
        ((2 * TOK_DEV, D), BF),
        ((2 * TOK_DEV, D), BF),
        ((TOK_DEV, D), BF),
        ((TOK_DEV, D), F32),
    )
    return pl.pallas_call(
        attention_kernel,
        out_shape=tuple(
            jax.ShapeDtypeStruct(*s)
            for s in kept + (((ROWS, D), BF), ((EXPERTS, TOK_DEV), F32))
        ),
        in_specs=[pl.BlockSpec(memory_space=pltpu.SMEM)]
        + [pl.BlockSpec(memory_space=pl.ANY)] * 8
        + [vmem] * 9,
        out_specs=(hbm,) * len(kept) + (vmem, vmem),
        scratch_shapes=[pltpu.VMEM(*s) for s in kept]
        + [
            pltpu.VMEM((2 * TOK_DEV, D), BF),
            pltpu.SemaphoreType.DMA((8, 4)),
            pltpu.SemaphoreType.DMA((len(kept),)),
        ],
        compiler_params=pltpu.CompilerParams(vmem_limit_bytes=VMEM_LIMIT),
        cost_estimate=microseconds(20),
        name="attention_forward",
    )(place, *w_parts, h1, own, far, gain1, gain2, router_t, cos, sin, ranks)


def branch_kernel(*refs):
    dx_refs, refs = refs[:3], refs[3:]
    (
        h2_ref,
        probs_ref,
        x1_ref,
        g_ref,
        gain2_ref,
        router_ref,
        w_ref,
        dx1_ref,
        do_ref,
        do_c_ref,
        grouter_ref,
        ggain_ref,
    ) = refs
    dx = dx_refs[0][...].astype(F32) + dx_refs[1][...].astype(F32) + dx_refs[2][...].astype(F32)
    drp = dx[TOK_DEV:, :TOK_DEV] + dx[TOK_DEV:, TOK_DEV:]
    probs = probs_ref[...]
    dlogits = (probs * (drp - jnp.sum(probs * drp, 0, keepdims=True))).astype(BF)
    hidden = h2_ref[:TOK_DEV, :]
    grouter_ref[...] = jnp.dot(dlogits, hidden, preferred_element_type=F32)
    dh2 = (
        dx[:TOK_DEV]
        + contract(dlogits, router_ref[...], 0, 0)
    )
    resid = x1_ref[...]
    scale = unit_rms(resid)
    normed = resid * scale
    ggain_ref[...] = jnp.sum(dh2 * normed, 0, keepdims=True)
    dnormed = dh2 * gain2_ref[...]
    dx1 = scale * (dnormed - normed * jnp.mean(dnormed * normed, -1, keepdims=True)) + g_ref[
        ...
    ].astype(F32)
    dx1_ref[...] = dx1
    datt = dx1.astype(BF)
    do_ref[...] = (
        contract(datt[:, :384], w_ref[0], 1, 1) + contract(datt[:, 384:], w_ref[1], 1, 1)
    ).astype(BF)
    do_c_ref[...] = do_ref[PROMPT:, :]


def branch_backward(dx, h_block, probs, x1, grad, gain2, router_t, w_all):
    shape = jax.ShapeDtypeStruct
    whole = lambda *dims: pl.BlockSpec(dims, lambda i: (0,) * len(dims))
    rows = whole(TOK_DEV, D)
    return pl.pallas_call(
        branch_kernel,
        grid=(1,),
        out_shape=(
            shape((TOK_DEV, D), F32),
            shape((TOK_DEV, D), BF),
            shape((TOK_DEV - PROMPT, D), BF),
            shape((EXPERTS, D), F32),
            shape((1, D), F32),
        ),
        in_specs=[
            whole(ROWS, D),
            whole(ROWS, D),
            whole(ROWS, D),
            whole(ROWS, D),
            whole(EXPERTS, TOK_DEV),
            rows,
            rows,
            whole(1, D),
            whole(EXPERTS, D),
            pl.BlockSpec((2, D, 384), lambda i: (3, 0, 0)),
        ],
        out_specs=(
            rows,
            rows,
            whole(TOK_DEV - PROMPT, D),
            whole(EXPERTS, D),
            whole(1, D),
        ),
        compiler_params=pltpu.CompilerParams(vmem_limit_bytes=VMEM_LIMIT),
        cost_estimate=microseconds(6),
        name="branch_backward",
    )(*dx, h_block, probs, x1, grad, gain2, router_t, w_all)


def attention_back_kernel(
    flags_ref,
    *refs,
):
    sources = refs[:9]
    do_far_ref, gain1_ref, cos_ref, sin_ref, grouter_ref, ggain2_ref = refs[9:15]
    gtok_ref, keep_ref, send_ref = refs[15:18]
    arrived = refs[18:27]
    q_ref, k_ref, v_ref, do_ref, h1_ref, w_ref, own_ref, dx1_ref, gwo_ref = arrived
    dq_sc, dk_sc, dv_sc, low_sc, product_sc, ext_sc, in_sems, out_sems = refs[27:]
    copies = [
        pltpu.make_async_copy(
            sources[i].at[:6] if i == 5 else sources[i], arrived[i], in_sems.at[i]
        )
        for i in range(9)
    ]
    for one in copies:
        one.start()

    def put(number, source):
        cols = slice((number % 2) * D, (number % 2 + 1) * D)
        copy = lambda out: pltpu.make_async_copy(
            source, out.at[:, : D // 4, cols], out_sems.at[number]
        )

        @pl.when(flags_ref[4] == number // 2)
        def _():
            copy(keep_ref).start()

        @pl.when(flags_ref[4] != number // 2)
        def _():
            copy(send_ref).start()

        return copy(keep_ref)

    for one in copies[:4]:
        one.wait()
    masks = lane_halves()
    row, col = causal_mask(PROMPT, 2)
    prompt_ok = col <= row
    cont_ok = (row // CLEN == col // CLEN) & (col <= row)
    row = lax.broadcasted_iota(jnp.int32, (8 * CLEN, 1), 0) // CLEN % 4
    near = jnp.where(
        row < 2,
        jnp.where(row == 0, flags_ref[0], flags_ref[1]),
        jnp.where(row == 2, flags_ref[2], flags_ref[3]),
    ).astype(F32)
    own_rows = row < 2
    own_c = slice(PROMPT, TOK_DEV)
    far_p = slice(TOK_DEV, TOK_DEV + PROMPT)
    far_c = slice(TOK_DEV + PROMPT, 2 * TOK_DEV)
    cont = CONT * CLEN

    def either(own, other):
        return jnp.where((near > 0.5) | ~own_rows, own, other)

    def heads(pair, carry):
        cols = pl.ds(pl.multiple_of(pair * 128, 128), 128)
        q_p, k_p, v_p = q_ref[:PROMPT, cols], k_ref[:PROMPT, cols], v_ref[:PROMPT, cols]
        k_f, v_f = k_ref[far_p, cols], v_ref[far_p, cols]
        q_c, k_c, v_c = q_ref[own_c, cols], k_ref[own_c, cols], v_ref[own_c, cols]
        do_p, do_c = do_ref[:PROMPT, cols], do_ref[own_c, cols]
        q_4 = jnp.concatenate([q_c, q_ref[far_c, cols]], 0)
        k_4 = jnp.concatenate([k_c, k_ref[far_c, cols]], 0)
        v_4 = jnp.concatenate([v_c, v_ref[far_c, cols]], 0)
        do_4 = jnp.concatenate([do_c, do_far_ref[:, cols]], 0)
        q_all = jnp.concatenate([q_p, q_4], 0)
        do_all = jnp.concatenate([do_p, do_4], 0)
        rows = 4 * CLEN
        query, grad = stacked(q_p, masks), stacked(do_p, masks)
        score = jnp.where(prompt_ok, 0.125 * contract(query, k_p, 1, 1), -1e30)
        prob = softmax_of(score)
        dprob = contract(grad, v_p, 1, 1)
        ds = (prob * (dprob - jnp.sum(prob * dprob, -1, keepdims=True))).astype(BF)
        prob = prob.astype(BF)
        query, grad = stacked(q_4, masks), stacked(do_4, masks)
        first = 0.125 * either(contract(query, k_p, 1, 1), contract(query, k_f, 1, 1))
        second = jnp.where(cont_ok, 0.125 * contract(query, k_4, 1, 1), -1e30)
        first, second = softmax_of(first, second)
        dfirst = either(contract(grad, v_p, 1, 1), contract(grad, v_f, 1, 1))
        dsecond = contract(grad, v_4, 1, 1)
        mean = jnp.sum(first * dfirst, -1, keepdims=True) + jnp.sum(
            second * dsecond, -1, keepdims=True
        )
        ds1 = first * (dfirst - mean)
        ds2 = (second * (dsecond - mean)).astype(BF)
        ds_near = (ds1 * near).astype(BF)
        ds_far = (ds1 * (1.0 - near)).astype(BF)
        p_near = (first * near).astype(BF)
        p_own = second.astype(BF)
        out = jnp.dot(ds, k_p, preferred_element_type=F32)
        dq_sc[:PROMPT, cols] = pick_lanes(out[:PROMPT], out[PROMPT:])
        out = (
            jnp.dot(ds_near, k_p, preferred_element_type=F32)
            + jnp.dot(ds_far, k_f, preferred_element_type=F32)
            + jnp.dot(ds2, k_4, preferred_element_type=F32)
        )
        dq_sc[own_c, cols] = pick_lanes(out[:cont], out[rows : rows + cont])
        for out, left, left_own, right, own in (
            (dk_sc, (ds, ds_near), ds2, q_all, q_c),
            (dv_sc, (prob, p_near), p_own, do_all, do_c),
        ):
            parts = [
                contract(
                    jnp.concatenate([part[h * rows : (h + 1) * rows] for part in left], 0),
                    right,
                    0,
                    0,
                )
                for h in range(2)
            ]
            out[:PROMPT, cols] = pick_lanes(*parts)
            parts = [
                contract(left_own[h * rows : h * rows + cont, :cont], own, 0, 0) for h in range(2)
            ]
            out[own_c, cols] = pick_lanes(*parts)
        return carry

    lax.fori_loop(0, HEADS // 2, heads, 0, unroll=3)
    for one in copies[4:]:
        one.wait()
    leaving = [put(3, gwo_ref)]
    dh1 = None
    for i, source in enumerate((dq_sc, dk_sc, dv_sc)):
        for slab in range(6):
            cols = slice(slab * 128, (slab + 1) * 128)
            value = source[:, cols]
            if i < 2:
                value = turned(0.125 * value, cos_ref[...], -sin_ref[...])
            low_sc[:, cols] = value.astype(BF)
        grads = low_sc[...]
        product = contract(h1_ref[...], grads, 0, 0).astype(BF)
        product_sc[i] = product.reshape(4, D // 4, D)
        leaving.append(put(i, product_sc.at[i]))
        for half in range(2):
            part = contract(grads[:, 384 * half : 384 * (half + 1)], w_ref[2 * i + half], 1, 1)
            dh1 = part if dh1 is None else dh1 + part
    inputs = own_ref[...].astype(F32)
    scale = unit_rms(inputs)
    normed = inputs * scale
    ggain1 = jnp.sum(dh1 * normed, 0, keepdims=True)
    gains = jnp.concatenate([ggain1, ggain2_ref[...], jnp.zeros((EXT - 2, D), F32)], 0)
    ext_sc[...] = jnp.zeros_like(ext_sc)
    for z in range(4):
        cols = slice(z * (D // 4), (z + 1) * (D // 4))
        extras = jnp.concatenate([grouter_ref[:, cols], gains[:, cols]], 1).astype(BF)
        ext_sc[0, z, :, : 2 * (D // 4)] = extras
    for k, out in enumerate((keep_ref, send_ref)):
        which = flags_ref[4] if k == 0 else 1 - flags_ref[4]
        leaving.append(
            pltpu.make_async_copy(ext_sc.at[which], out.at[:, D // 4 :, :], out_sems.at[4 + k])
        )
        leaving[-1].start()
    dnormed = dh1 * gain1_ref[...]
    gtok_ref[...] = (
        scale * (dnormed - normed * jnp.mean(dnormed * normed, -1, keepdims=True)) + dx1_ref[...]
    )
    for one in leaving:
        one.wait()


def attention_backward(
    flags, q, k, v, do, do_far, h1, w_all, own, gain1, cos, sin, dx1, gwo, grouter, ggain2
):
    shape = jax.ShapeDtypeStruct
    vmem = pl.BlockSpec(memory_space=pltpu.VMEM)
    anywhere = pl.BlockSpec(memory_space=pl.ANY)
    hbm = pl.BlockSpec(memory_space=pltpu.HBM)
    packed = (4, D // 4 + EXT, 2 * D)
    late = (q, k, v, do, h1, w_all, own, dx1, gwo.reshape(4, D // 4, D))
    return pl.pallas_call(
        attention_back_kernel,
        out_shape=(shape((TOK_DEV, D), F32), shape(packed, BF), shape(packed, BF)),
        in_specs=[pl.BlockSpec(memory_space=pltpu.SMEM)]
        + [anywhere] * 9
        + [vmem] * 6,
        out_specs=(vmem, hbm, hbm),
        scratch_shapes=[
            pltpu.VMEM((6,) + v.shape[1:] if i == 5 else v.shape, v.dtype)
            for i, v in enumerate(late)
        ]
        + [pltpu.VMEM((TOK_DEV, D), F32)] * 3
        + [
            pltpu.VMEM((TOK_DEV, D), BF),
            pltpu.VMEM((3, 4, D // 4, D), BF),
            pltpu.VMEM((2, 4, EXT, 2 * D), BF),
            pltpu.SemaphoreType.DMA((9,)),
            pltpu.SemaphoreType.DMA((6,)),
        ],
        compiler_params=pltpu.CompilerParams(vmem_limit_bytes=VMEM_LIMIT),
        cost_estimate=microseconds(23),
        name="attention_backward",
    )(flags, *late, do_far, gain1, cos, sin, grouter, ggain2)


def after(value, *earlier):
    return lax.optimization_barrier((value, earlier))[0]


def over_y(value):
    return moved(value, lambda z, y, x, c: (z, 1 - y, x, c))


def beside(results, moving):
    return lax.optimization_barrier((results, moving))


def norm_kernel(rows_ref, gain_ref, out_ref):
    rows = rows_ref[...].astype(F32)
    out_ref[...] = (rows * unit_rms(rows) * gain_ref[...]).astype(BF)


def norm_rows(rows, gain):
    return pl.pallas_call(
        norm_kernel,
        out_shape=jax.ShapeDtypeStruct(rows.shape, BF),
        compiler_params=pltpu.CompilerParams(vmem_limit_bytes=VMEM_LIMIT),
        cost_estimate=microseconds(2),
        name="norm_rows",
    )(rows, gain)


def place_kernel(every_ref, gate_ref, up_ref, down_ref):
    for out_ref, at in ((gate_ref, 0), (up_ref, 256)):
        for k in range(4):
            for p in range(0, 8, 2):
                pair = [
                    every_ref[p + i, :, at + 64 * k : at + 64 * (k + 1)].astype(F32)
                    for i in range(2)
                ]
                to = 512 * k + 64 * p
                out_ref[:, to : to + 128] = jnp.concatenate(pair, 1)
    for p in range(8):
        for i in range(3):
            down_ref[64 * p : 64 * (p + 1), 256 * i : 256 * (i + 1)] = every_ref[
                p, 64 * i : 64 * (i + 1), 512:
            ].astype(F32)


def place_shared(every):
    vmem = pl.BlockSpec(memory_space=pltpu.VMEM)
    return pl.pallas_call(
        place_kernel,
        out_shape=(
            jax.ShapeDtypeStruct((D // 4, 2048), F32),
            jax.ShapeDtypeStruct((D // 4, 2048), F32),
            jax.ShapeDtypeStruct((512, D), F32),
        ),
        in_specs=[vmem],
        out_specs=(vmem,) * 3,
        compiler_params=pltpu.CompilerParams(vmem_limit_bytes=VMEM_LIMIT),
        cost_estimate=microseconds(4),
        name="place_shared",
    )(every)


OTHERS = (
    over_x,
    over_y,
    lambda value: moved(value, lambda z, y, x, c: (z, 1 - y, 1 - x, c)),
)


def plane_pieces(value, x, y):
    width = value.shape[-1] // 4
    quarters = [value[..., width * i : width * (i + 1)] for i in range(4)]

    def pick(column, row):
        left = jnp.where(column == 0, quarters[0], quarters[1])
        right = jnp.where(column == 0, quarters[2], quarters[3])
        return jnp.where(row == 0, left, right)

    return [pick(x, y), pick(1 - x, y), pick(x, 1 - y), pick(1 - x, 1 - y)]


def canonical(slots, z):
    order = [slots[0], slots[3], slots[2], slots[1]]
    return lax.dynamic_slice_in_dim(jnp.stack(order + order), lax.rem(4 - z, 4), 4, 0)


def lane_tables():
    row = np.arange(TOK_DEV)
    position = np.where(row < PROMPT, row, PROMPT + (row - PROMPT) % CLEN).astype(np.float32)
    frequency = (10000.0 ** (-2.0 * np.arange(HD // 2) / HD)).astype(np.float32)
    angles = (position[:, None] * frequency[None, :]).astype(np.float64)
    cos, sin = np.cos(angles).astype(np.float32), np.sin(angles).astype(np.float32)
    return jnp.asarray(np.tile(cos, (1, 4))), jnp.asarray(np.tile(np.concatenate([-sin, sin], 1), (1, 2)))


def tuned_body(
    tokens,
    cotangent,
    routes,
    prompt_ids,
    attn_gain,
    query_weight,
    key_weight,
    value_weight,
    output_weight,
    ffn_gain,
    router_weight,
    shared_gate,
    shared_up,
    shared_down,
    expert_gate,
    expert_up_weight,
    expert_down,
):
    z, y, j = lax.axis_index("dp"), lax.axis_index("context"), lax.axis_index("experts")
    x, core = j // 2, j % 2
    plane = y * 4 + j
    shard = D // 4

    dense = jnp.concatenate([query_weight, key_weight, value_weight, output_weight], 1)
    dense = lax.dynamic_slice_in_dim(dense, plane * 384, 384, 1)
    gains = jnp.concatenate(
        [attn_gain[None], ffn_gain[None], jnp.zeros((EXT - 2, shard), BF)], 0
    )
    dense = jnp.concatenate([dense, jnp.concatenate([router_weight.T, gains], 1)], 0)
    dense_z = [over_z(dense, step) for step in (1, 2, 3)]

    units = lambda w: lax.dynamic_index_in_dim(
        w.reshape(shard, 4, 8, 64), plane, 2, keepdims=False
    ).reshape(shard, 256)
    down = lax.dynamic_slice_in_dim(shared_down, plane * 64, 64, 0)
    down = jnp.concatenate([down[:, 256 * i : 256 * (i + 1)] for i in range(3)], 0)
    shared = jnp.concatenate([units(shared_gate), units(shared_up), down], 1)
    far = over_y(tokens)
    ids = jnp.broadcast_to(prompt_ids.astype(BF)[:, None], (CONT, 128))
    far_ids = over_y(ids)
    dense = jnp.stack([dense] + after(dense_z, far, far_ids))
    small = canonical([dense[i, shard:, :] for i in range(4)], z)
    router_t = small[:, :, :shard].transpose(1, 0, 2).reshape(EXPERTS, D)
    gain1 = small[:, 0, shard:].reshape(1, D).astype(F32)
    gain2 = small[:, 1, shard:].reshape(1, D).astype(F32)
    flip_a, flip_b = jnp.where(core == 0, 2, 4), jnp.where(core == 0, 4, 2)
    flips = [0 * core, flip_a, flip_b, 0 * core + 6]
    flips = flips + [1 + flips[0], 1 + flip_b, 1 + flip_a, 1 + flips[3]]
    place = [jnp.bitwise_xor(plane, flip) for flip in flips]
    place += [lax.rem(z + 4 - slot, 4) for slot in range(4)]
    place += [(prompt_ids[m] != y) for m in range(CONT)]
    place = jnp.stack([v.astype(jnp.int32) for v in place])
    cos, sin = lane_tables()
    gain1, place, gain2, router_t, cos, sin = after((gain1, place, gain2, router_t, cos, sin))
    h1 = norm_rows(tokens, gain1)
    h1, dense_parts = beside(h1, (over_a(dense), over_b(dense)))
    dense_parts = [dense, *dense_parts, over_b(dense_parts[0])]
    dense_parts = dense_parts + [over_core(part) for part in dense_parts]

    expert_ids = jnp.arange(EXPERTS, dtype=jnp.int32)[:, None]
    route_t = routes.T
    member = (route_t[0:1] == expert_ids) | (route_t[1:2] == expert_ids)
    before = (jnp.arange(TOK_DEV)[:, None] < jnp.arange(TOK_DEV)[None, :]).astype(BF)
    ranks = jnp.dot(member.astype(BF), before, preferred_element_type=F32)
    ranks = jnp.where(member, ranks, -1.0).astype(BF)
    g_block = cotangent
    g_near = after(g_block, h1)
    g_x = over_x(g_near)
    g_group = [g_block, g_x, over_core(g_near), over_core(g_x)]

    g_column = lax.all_gather(after(g_block, dense), "dp", axis=0, tiled=False)

    shared = lax.all_gather(shared, "dp", axis=0, tiled=False)
    shared_far = over_y(after(shared, h1))
    place = after(place, shared)
    flags = jnp.concatenate([prompt_ids == y, far_ids[:, 0].astype(jnp.int32) == y, core[None] != 0]).astype(jnp.int32)
    w_all, q, k, v, o, x1, h_block, probs = attention_forward(
        place, dense_parts, h1, tokens, far, gain1, gain2, router_t, cos, sin, ranks
    )
    (h_block, x1), (g_x, shared_far) = beside((h_block, x1), (g_x, shared_far))
    g_group = [g_block, g_x, over_core(g_block), over_core(g_x)]

    h_x = over_x(h_block)
    h_near, g_near = [h_block, over_core(h_block)], [g_block, g_group[2]]
    h_column = lax.all_gather(h_block, "dp", axis=0, tiled=False)
    experts_w = (expert_gate, expert_up_weight, expert_down)
    base = (j * 4).astype(jnp.int32)
    more = shared_rows(h_near, g_near, shared, shared_far)
    more, (h_x, g_y) = beside(more, (h_x, over_y(after(g_block, h_block))))
    h_far, g_far = [h_x, over_core(h_x)], [g_x, g_group[3]]
    h_group = [h_near[0], h_far[0], h_near[1], h_far[1]]
    g_second = jnp.pad(jnp.where(core == 0, g_y, g_x), ((0, EXT), (0, 0)))
    h_group, g_second = after((h_group, g_second))
    part = group_experts(base[None], 0, 2, h_group, g_group, (), *experts_w)
    (part, h_far), h_b = beside((part, h_far), over_b(after(h_block, h_x)))
    g_first = over_a(after(g_column, h_x))
    more = more + shared_rows(h_far, g_far, shared, shared_far)
    more, g_first = beside(more, g_first)
    g_second = lax.all_gather(g_second, "dp", axis=0, tiled=False)
    results = group_experts(
        base[None] + 2, 2, 2, h_group, g_group, (*more, *part), *experts_w
    )
    g_third = over_b(g_first)
    results, (g_third, g_core) = beside(
        results, (g_third, [over_core(g_column), over_core(g_first)])
    )
    moe, dx = results[:4], results[4:]
    dx_x = pair_sum(dx[1], over_core(dx[3]))
    dx = [dx[0], over_core(dx[2]), over_x(dx_x)]
    h_column = after(h_column, dx_x)
    h_core = [over_core(h_column)]
    window = jnp.array([0, 1, 3, 4], jnp.int32)[z]
    s_pos = jnp.stack([window, z // 2, z * 192 - window * 128, (z % 2) * 64]).astype(jnp.int32)
    e_pos = jnp.stack([base, (z * 2 + y).astype(jnp.int32)])
    s_sums = shared_slice_grads(
        s_pos, [h_column, h_core[0]], [g_column, g_core[0]], shared
    )
    s_sums, dx = beside(s_sums, dx)
    dx1, do, do_c, grad_router_t, grad_gain2 = branch_backward(
        dx, h_block, probs, x1, cotangent, gain2, router_t, w_all
    )
    gwo = inner_rows(o, dx1.astype(BF)).astype(BF)
    gwo, (do_far, g_second) = beside(gwo, (over_y(do_c), g_second))
    h_first = over_a(after(h_column, do_far))
    h_second = lax.all_gather(after(h_b, do_far), "dp", axis=0, tiled=False)
    grad_inputs, keep, send = attention_backward(
        flags,
        q,
        k,
        v,
        do,
        do_far,
        h1,
        w_all,
        tokens,
        gain1,
        cos,
        sin,
        dx1,
        gwo,
        grad_router_t,
        grad_gain2,
    )
    (grad_inputs, keep, send), (h_first, g_far) = beside(
        (grad_inputs, keep, send),
        (h_first, [over_core(after(part, do_far)) for part in (g_second, g_third)]),
    )
    h_core.append(over_core(h_first))
    h_third = over_b(after(h_first, keep))
    h_parts, g_parts = [h_column, h_first] + h_core, [g_column, g_first] + g_core[:2]
    e_pos = after(e_pos, keep)
    e_sums = expert_slice_grads(e_pos, h_parts, g_parts, *experts_w, 256)
    (e_sums, keep), (send, h_second, h_third, g_far) = beside(
        (e_sums, keep),
        (over_core(send), h_second, h_third, g_far),
    )
    h_far = [over_core(h_second), over_core(h_third)]
    h_parts, g_parts = [h_second, h_third] + h_far, [g_second, g_third] + g_far
    pieces = plane_pieces(pair_sum(keep, send), x, y)
    h_parts, pieces = after((h_parts, pieces))
    mine = shared_slice_grads(
        s_pos, [h_first, h_core[1], *h_parts], [g_first, g_core[1], *g_parts], shared, s_sums
    )
    (mine, pieces), there = beside(
        (mine, pieces), [over(piece) for over, piece in zip(OTHERS, pieces[1:])]
    )
    z_own = pieces[0].astype(F32)
    for piece in there:
        z_own = z_own + piece.astype(F32)
    z_own = z_own.astype(BF)
    z_parts = [
        lax.dynamic_index_in_dim(z_own, lax.rem(z + step, 4), 0, keepdims=False)
        for step in (0, 1, 2, 3)
    ]
    moe = after(moe, mine)
    moe_x = pair_sum(moe[1], over_core(moe[3]))
    moe_core = over_core(moe[2])

    mine, z_parts, moe_x, moe_core, h_parts, g_parts = after(
        (mine, z_parts, moe_x, moe_core, h_parts, g_parts)
    )
    every = lax.all_gather(mine, ("context", "experts"), axis=0, tiled=False)
    moving = ([over_z(z_parts[step], step) for step in (1, 2, 3)], over_x(moe_x), every)
    e_gate, e_up, e_down = expert_slice_grads(e_pos, h_parts, g_parts, *experts_w, 256, e_sums)
    (e_gate, e_up, e_down), (there, moe_there, every) = beside((e_gate, e_up, e_down), moving)
    total = z_parts[0].astype(F32)
    for part in there:
        total = total + part.astype(F32)
    total = total.astype(BF)
    total_parts = [over(total) for over in OTHERS]
    layer_out = (
        x1 + (moe[0].astype(F32) + moe_core.astype(F32) + moe_there.astype(F32))
    ).astype(BF)
    s_gate, s_up, s_down = place_shared(every)
    (layer_out, s_gate), total_parts = beside((layer_out, s_gate), total_parts)
    beside_x = rejoin(total, total_parts[0], x)
    total = rejoin(beside_x, rejoin(total_parts[1], total_parts[2], x), y)
    other = over_core(total)
    sum_qk, sum_vo = jnp.where(core == 0, total, other), jnp.where(core == 0, other, total)
    extras = sum_qk[shard:, : 2 * shard].astype(F32)
    sum_qk, sum_vo = sum_qk[:shard].astype(F32), sum_vo[:shard].astype(F32)

    return (
        layer_out,
        grad_inputs,
        extras[0, shard:],
        sum_qk[:, :D],
        sum_qk[:, D:],
        sum_vo[:, :D],
        sum_vo[:, D:],
        extras[1, shard:],
        extras[:, :shard].T,
        s_gate,
        s_up,
        s_down,
        e_gate,
        e_up,
        e_down,
    )


def solution(mesh):
    tuned = dict(mesh.shape) == TUNED_MESH

    return jax.shard_map(
        tuned_body if tuned else plain_body,
        mesh=mesh,
        in_specs=(
            P(("dp", "context", "experts"), None),
            P(("dp", "context", "experts"), None),
            P(("dp", "context", "experts"), None),
            P(("dp", "context", "experts")),
            P("dp"),
            P("dp", None),
            P("dp", None),
            P("dp", None),
            P("dp", None),
            P("dp"),
            P("dp", None),
            P("dp", None),
            P("dp", None),
            P("dp", None),
            P("experts", None, None),
            P("experts", None, None),
            P("experts", None, None),
        ),
        out_specs=(
            P(("dp", "context", "experts"), None),
            P(("dp", "context", "experts"), None),
            P("dp"),
            P("dp", None),
            P("dp", None),
            P("dp", None),
            P("dp", None),
            P("dp"),
            P("dp", None),
            P("dp", None),
            P("dp", None),
            P("dp", None),
            P("experts", None, ("dp", "context")),
            P("experts", None, ("dp", "context")),
            P("experts", ("dp", "context"), None),
        ),
        check_vma=False,
    )
```
